32 devices in a mesh: pipe: 2 (over core), dp: 16 (over z, y, x).
Axes of the slice: x: 2, y: 2, z: 4, core: 2. Of those that a mesh axis runs over, the one named last changes fastest.
Arguments:
- images: bfloat16 [64, 24, 24, 320], P('dp'), may hold values from -6 to 6
- masks: int32 [64, 24, 24], P('dp'), may hold values from 0 to 1, as said below
- conv_weight: bfloat16 [2, 9, 320], P('pipe'), may hold values from -2 to 2
- batch_gain: float32 [2, 320], P('pipe'), may hold values from 0.5 to 1.5
- batch_bias: float32 [2, 320], P('pipe'), may hold values from -3 to 3
- width_weight: bfloat16 [2, 24, 24], P('pipe'), may hold values from -1.25 to 1.25
- width_bias: float32 [2, 24], P('pipe'), may hold values from -3 to 3
- height_weight: bfloat16 [2, 24, 24], P('pipe'), may hold values from -1.25 to 1.25
- height_bias: float32 [2, 24], P('pipe'), may hold values from -3 to 3
- merge_weight: bfloat16 [2, 960, 320], P('pipe'), may hold values from -0.1875 to 0.1875
- merge_bias: float32 [2, 320], P('pipe'), may hold values from -3 to 3
- norm_gain: float32 [2, 320], P('pipe'), may hold values from 0.5 to 1.5
- norm_bias: float32 [2, 320], P('pipe'), may hold values from -3 to 3
- up_weight: bfloat16 [2, 320, 1280], P('pipe'), may hold values from -0.3125 to 0.3125
- up_bias: float32 [2, 1280], P('pipe'), may hold values from -3 to 3
- down_weight: bfloat16 [2, 1280, 320], P('pipe'), may hold values from -0.25 to 0.25
- down_bias: float32 [2, 320], P('pipe'), may hold values from -3 to 3
- out_grad: bfloat16 [64, 24, 24, 320], P('dp'), may hold values from -6 to 6
Outputs:
- section_outputs: bfloat16 [2, 64, 24, 24, 320], P('pipe', 'dp')
- input_grads: bfloat16 [2, 64, 24, 24, 320], P('pipe', 'dp')
- conv_grad: float32 [2, 9, 320], P('pipe')
- batch_gain_grad: float32 [2, 320], P('pipe')
- batch_bias_grad: float32 [2, 320], P('pipe')
- width_grad: float32 [2, 24, 24], P('pipe')
- width_bias_grad: float32 [2, 24], P('pipe')
- height_grad: float32 [2, 24, 24], P('pipe')
- height_bias_grad: float32 [2, 24], P('pipe')
- merge_grad: float32 [2, 960, 320], P('pipe')
- merge_bias_grad: float32 [2, 320], P('pipe')
- norm_gain_grad: float32 [2, 320], P('pipe')
- norm_bias_grad: float32 [2, 320], P('pipe')
- up_grad: float32 [2, 320, 1280], P('pipe')
- up_bias_grad: float32 [2, 1280], P('pipe')
- down_grad: float32 [2, 1280, 320], P('pipe')
- down_bias_grad: float32 [2, 320], P('pipe')
The draws below stay inside these ranges and needn't reach their ends.
Inputs may be any that keep to these rules, and one draw needn't show every extreme that they name: `masks`: each image's valid patches are its first h rows and first w columns, h and w between 8 and 24.
All inputs are finite; a program needn't handle non-finite values.
Results may differ from the reference program's by a relative error of at most 0.014.
Values may be sent and summed in bfloat16 or wider, within the bound.
A program may use at most 128 MiB of HBM per device.

```python
import jax
import jax.numpy as jnp
from jax import lax

C = 320
FF = 1280
SIDE = 24
IMAGES = 64
N_DP = 16


def draw_masks(key, part):
    key = jax.random.fold_in(key, 11)
    first_key, second_key = jax.random.split(key)
    rows = jax.random.randint(first_key, (IMAGES,), SIDE // 3, SIDE + 1)
    cols = jax.random.randint(second_key, (IMAGES,), SIDE // 3, SIDE + 1)
    places = jnp.arange(SIDE)
    inside = (places[None, :, None] < rows[:, None, None]) & (places[None, None, :] < cols[:, None, None])
    return inside.astype(jnp.int32)


def block_scale(rng, dims, pieces, least, top_value):
    factor_of = 1.0
    for position, shards_of in pieces:
        draws = jax.random.uniform(jax.random.fold_in(jax.random.fold_in(rng, 6), position), (shards_of,), jnp.float32, least / len(pieces), top_value / len(pieces))
        factor_of = factor_of * jnp.repeat(jnp.exp(draws), dims[position] // shards_of).reshape((-1,) + (1,) * (len(dims) - 1 - position))
    return factor_of


def scatter_about(stream_key, shape, scale, reach, cuts=(), held_as=jnp.bfloat16):
    gain = block_scale(stream_key, shape, cuts, -0.22, 0.18) if cuts else 1.0
    entries = jax.random.normal(stream_key, shape, jnp.float32) * scale * gain
    return jnp.minimum(jnp.maximum(entries, -reach), reach).astype(held_as)


def setup_inputs(seed: int = 0) -> dict:
    arg_keys = jax.random.split(jax.random.key(seed), 19)
    images = scatter_about(arg_keys[0], (IMAGES, SIDE, SIDE, C), 1.0, 6.0, ((0, 16),))
    masks = draw_masks(jax.random.fold_in(arg_keys[18], 71), 0)
    conv_weight = scatter_about(arg_keys[2], (2, 9, C), 9 ** -0.5, 2.0, ((0, 2),))
    batch_gain = jnp.clip(0.5 + 1.0 * jax.random.uniform(arg_keys[3], (2, C), jnp.float32) ** block_scale(arg_keys[3], (2, C), ((0, 2),), -0.2, 0.2), 0.5, 1.5)
    batch_bias = scatter_about(arg_keys[4], (2, C), 0.5, 3.0, ((0, 2),), jnp.float32)
    width_weight = scatter_about(arg_keys[5], (2, SIDE, SIDE), SIDE ** -0.5, 1.25, ((0, 2),))
    width_bias = scatter_about(arg_keys[6], (2, SIDE), 0.5, 3.0, ((0, 2),), jnp.float32)
    height_weight = scatter_about(arg_keys[7], (2, SIDE, SIDE), SIDE ** -0.5, 1.25, ((0, 2),))
    height_bias = scatter_about(arg_keys[8], (2, SIDE), 0.5, 3.0, ((0, 2),), jnp.float32)
    merge_weight = scatter_about(arg_keys[9], (2, 3 * C, C), (3 * C) ** -0.5, 0.1875, ((0, 2),))
    merge_bias = scatter_about(arg_keys[10], (2, C), 0.5, 3.0, ((0, 2),), jnp.float32)
    norm_gain = jnp.clip(0.5 + 1.0 * jax.random.uniform(arg_keys[11], (2, C), jnp.float32) ** block_scale(arg_keys[11], (2, C), ((0, 2),), -0.2, 0.2), 0.5, 1.5)
    norm_bias = scatter_about(arg_keys[12], (2, C), 0.5, 3.0, ((0, 2),), jnp.float32)
    up_weight = scatter_about(arg_keys[13], (2, C, FF), C ** -0.5, 0.3125, ((0, 2),))
    up_bias = scatter_about(arg_keys[14], (2, FF), 0.5, 3.0, ((0, 2),), jnp.float32)
    down_weight = scatter_about(arg_keys[15], (2, FF, C), (FF // 2) ** -0.5, 0.25, ((0, 2),))
    down_bias = scatter_about(arg_keys[16], (2, C), 0.5, 3.0, ((0, 2),), jnp.float32)
    out_grad = scatter_about(arg_keys[17], (IMAGES, SIDE, SIDE, C), 1.0, 6.0, ((0, 16),))
    return {"images": images, "masks": masks, "conv_weight": conv_weight, "batch_gain": batch_gain, "batch_bias": batch_bias, "width_weight": width_weight, "width_bias": width_bias, "height_weight": height_weight, "height_bias": height_bias, "merge_weight": merge_weight, "merge_bias": merge_bias, "norm_gain": norm_gain, "norm_bias": norm_bias, "up_weight": up_weight, "up_bias": up_bias, "down_weight": down_weight, "down_bias": down_bias, "out_grad": out_grad}


EPS = 1e-05
HIGH = lax.Precision.HIGHEST

@jax.custom_vjp
def low(v):
    return lax.optimization_barrier(v.astype(jnp.bfloat16)).astype(jnp.float32)

@jax.custom_vjp
def low_back(v):
    return v

def low_keep(v):
    return (low(v), None)

def low_pass(kept_rows, grad):
    return (grad,)

def back_keep(v):
    return (v, None)

def back_low(kept_rows, grad):
    return (low(grad),)
low.defvjp(low_keep, low_pass)
low_back.defvjp(back_keep, back_low)

def conv_taps(field, kernel):
    side = field.shape[1]
    padded = jnp.pad(field, ((0, 0), (1, 1), (1, 1), (0, 0)))
    total = jnp.zeros(field.shape, jnp.float32)
    for row in range(3):
        for col in range(3):
            total = total + padded[:, row:row + side, col:col + side, :] * kernel[3 * row + col]
    return total

def block(field, row_mask, weights):
    conv_w, batchnorm_factor, batchnorm_shift, width_w, width_b, height_w, height_b, merge_w, merge_b, norm_g, norm_b, up_w, up_b, down_w, down_b = weights
    spatial_filtered = conv_taps(field, conv_w)
    column_mask = row_mask[..., None]
    kept_count = jnp.sum(row_mask)
    batch_mean = lax.optimization_barrier(jnp.sum(column_mask * spatial_filtered, axis=(0, 1, 2))) / kept_count
    centred = spatial_filtered - batch_mean
    var = lax.optimization_barrier(jnp.sum(column_mask * centred * centred, axis=(0, 1, 2))) / kept_count
    mixed_output = low((centred * lax.rsqrt(var + EPS) * batchnorm_factor + batchnorm_shift) * column_mask)
    along_w = low(low_back(jnp.einsum('gikc,jk->gijc', mixed_output, width_w, precision=HIGH) + width_b[None, None, :, None]))
    along_h = low(low_back(jnp.einsum('gkjc,ik->gijc', mixed_output, height_w, precision=HIGH) + height_b[None, :, None, None]))
    joined_output = jnp.concatenate([along_w, along_h, mixed_output], -1)
    merged = low_back(jnp.einsum('gijd,dc->gijc', joined_output, merge_w, precision=HIGH) + merge_b)
    first_output = field + merged
    centre = lax.optimization_barrier(jnp.mean(first_output, -1, keepdims=True))
    spread = first_output - centre
    nvar = lax.optimization_barrier(jnp.mean(spread * spread, -1, keepdims=True))
    normalized_input = low(spread * lax.rsqrt(nvar + EPS) * norm_g + norm_b)
    preactivation = low_back(jnp.einsum('gijc,ch->gijh', normalized_input, up_w, precision=HIGH) + up_b)
    hidden_units = low(jax.nn.gelu(preactivation, approximate=False))
    final_output = low_back(jnp.einsum('gijh,hc->gijc', hidden_units, down_w, precision=HIGH) + down_b)
    return first_output + final_output

def reference(images, masks, conv_weight, batch_gain, batch_bias, width_weight, width_bias, height_weight, height_bias, merge_weight, merge_bias, norm_gain, norm_bias, up_weight, up_bias, down_weight, down_bias, out_grad):
    micro = images.shape[0] // N_DP

    def regroup(value):
        return jnp.swapaxes(value.reshape((N_DP, micro) + value.shape[1:]), 0, 1)

    def ungroup(value):
        return jnp.swapaxes(value, 0, 1).reshape((-1,) + value.shape[2:])
    inputs = regroup(images.astype(jnp.float32))
    groups = regroup(masks.astype(jnp.float32))
    cotangent = regroup(out_grad.astype(jnp.float32))
    stacked = tuple((w.astype(jnp.float32) for w in (conv_weight, batch_gain, batch_bias, width_weight, width_bias, height_weight, height_bias, merge_weight, merge_bias, norm_gain, norm_bias, up_weight, up_bias, down_weight, down_bias)))
    lead = tuple((w[0] for w in stacked))
    trail = tuple((w[1] for w in stacked))

    def forward(inputs, probe, lead, trail):

        def single(item):
            field, row_mask, extra = item
            output_one = block(low_back(field), row_mask, lead)
            output_two = block(low_back(low(output_one) + extra), row_mask, trail)
            return (output_one, output_two)
        return lax.map(jax.checkpoint(single), (inputs, groups, probe))
    probe = jnp.zeros_like(inputs)
    (output_one, output_two), pull = jax.vjp(forward, inputs, probe, lead, trail)
    grad_in, grad_probe, grad_lead, grad_trail = pull((jnp.zeros_like(output_one), cotangent))
    section_outputs = jnp.stack([ungroup(output_one), ungroup(output_two)]).astype(jnp.bfloat16)
    input_grads = jnp.stack([ungroup(grad_in), ungroup(grad_probe)]).astype(jnp.bfloat16)
    pairs = [jnp.stack([one, two]) for one, two in zip(grad_lead, grad_trail)]
    return (section_outputs, input_grads, pairs[0], pairs[1], pairs[2], pairs[3], pairs[4], pairs[5], pairs[6], pairs[7], pairs[8], pairs[9], pairs[10], pairs[11], pairs[12], pairs[13], pairs[14])
```

```python
import functools

import jax
import jax.numpy as jnp
from jax import lax
from jax.experimental import pallas as pl
from jax.experimental.pallas import tpu as pltpu
from jax.sharding import PartitionSpec as P

EPS = 1e-05
MESH = pl.DeviceIdType.MESH
F32 = jnp.float32
BF16 = jnp.bfloat16

SIDE = 24
ROWS = SIDE * SIDE
C = 320
CP = 384
FF = 1280
FT = 256
CHUNK = 48
GROUP = 8 * SIDE

CONV, BGAIN, BBIAS, MBIAS, NGAIN, NBIAS, DBIAS, WBIAS, HBIAS, UBIAS, WW, HW, PACK = (
    0, 9, 10, 11, 12, 13, 14, 15, 16, 17, 24, 48, 72)


def dot(a, b, contract=(1, 0), precision=None):
    return lax.dot_general(
        a, b, (((contract[0],), (contract[1],)), ((), ())),
        preferred_element_type=F32, precision=precision)


def fold(value):
    rows = value.shape[0]
    return jnp.sum(value.reshape(rows // 8, 8, value.shape[1]), 0)


def total(partial):
    return jnp.sum(partial, 0, keepdims=True)


def grid_row(index):
    return (index * 2731) >> 16


def one_hots(rows):
    place = lax.broadcasted_iota(jnp.int32, (rows, SIDE), 0)
    lane = lax.broadcasted_iota(jnp.int32, (rows, SIDE), 1)
    i = grid_row(place)
    return i == lane, place - SIDE * i == lane


def gelu_both(x):
    ax = jnp.abs(x)
    e = jnp.exp(-0.5 * x * x)
    t = 1.0 / (1.0 + (0.3275911 * 0.7071067811865476) * ax)
    poly = t * (0.127414796 + t * (-0.142248368 + t * (0.7107068705 + t * (-0.7265760135 + t * 0.5307027145))))
    tail = poly * e
    phi = jnp.where(x >= 0, 1.0 - tail, tail)
    return x * phi, phi + x * e * 0.3989422804014327


def kernel(
    n_dp,
    images, mask_h, pack_h, wm_h, wu_h, wd_h, og_h,
    so_h, ig_h, gm, gu, gd, gs,
    mask_cols, pack, wm, wu, wd, ub, uf, cv, joined, normal, xl, rstd, hidden, gp,
    gf, gb, gbt, gpre, gmix, gwh, gsh, kw, kh, wbcol, hbcol,
    gw_acc, gh_acc, wcol, hcol, ybuf, msg, land,
    local_sems, pack_sems, w_send, w_recv, st_send, st_recv,
    so_local, so_send, so_recv, ig_local, ig_send, ig_recv,
):
    me_p = lax.axis_index("pipe")
    me_d = lax.axis_index("dp")
    other = 1 - me_p
    first = gsh.at[2, pl.ds(SIDE, ROWS)]
    igbuf = ybuf
    gnorm = gsh.at[0, pl.ds(SIDE, ROWS)]
    pre_s = gsh.at[1, pl.ds(SIDE, ROWS), pl.ds(0, FT)]

    def local_w(k_src, n):
        return pltpu.make_async_copy(wm_h.at[0, pl.ds(C * n, C)], wm.at[me_p, pl.ds(CP * n, C)], local_sems.at[n])

    image_in = [pltpu.make_async_copy(images.at[2 * me_p + t], ub.at[t], local_sems.at[5 + t]) for t in range(2)]
    grad_in = [pltpu.make_async_copy(og_h.at[2 * me_p + t], ub.at[t], local_sems.at[7 + t]) for t in range(2)]
    pack_in = pltpu.make_async_copy(pack_h, pack.at[me_p], local_sems.at[9])
    weights_in = [local_w(0, n) for n in range(3)] + [
        pltpu.make_async_copy(wu_h.at[0], wu.at[me_p], local_sems.at[3]),
        pltpu.make_async_copy(wd_h.at[0], wd.at[me_p], local_sems.at[4]),
    ]
    mask_in = pltpu.make_async_copy(mask_h.at[pl.ds(2 * me_p, 2)], mask_cols, local_sems.at[10])
    mask_in.start()
    pack_in.start()
    for copy in image_in + weights_in:
        copy.start()

    barrier = pltpu.get_barrier_semaphore()

    def greet(step, carry):
        pl.semaphore_signal(barrier, inc=1, device_id={"dp": lax.rem(me_d + step, n_dp)}, device_id_type=MESH)
        return carry

    lax.fori_loop(1, n_dp, greet, 0)
    pl.semaphore_signal(barrier, inc=1, device_id={"pipe": other}, device_id_type=MESH)
    pl.semaphore_wait(barrier, n_dp)

    def across(src, dst, send, recv):
        return pltpu.make_async_remote_copy(
            src_ref=src, dst_ref=dst, send_sem=send, recv_sem=recv,
            device_id={"pipe": other}, device_id_type=MESH)

    pack_over = across(pack_h, pack.at[me_p], pack_sems.at[0], pack_sems.at[1])
    weights_over = [
        across(wm_h.at[0, pl.ds(C * n, C)], wm.at[me_p, pl.ds(CP * n, C)], w_send.at[n], w_recv.at[n]) for n in range(3)
    ] + [
        across(wu_h.at[0], wu.at[me_p], w_send.at[3], w_recv.at[3]),
        across(wd_h.at[0], wd.at[me_p], w_send.at[4], w_recv.at[4]),
    ]
    pack_over.start()
    for copy in weights_over:
        copy.start()

    msg[...] = jnp.zeros(msg.shape, F32)
    for k in range(2):
        for n in range(3):
            wm[k, CP * n + C : CP * n + CP, :] = jnp.zeros((CP - C, C), BF16)
        gm[k] = jnp.zeros(gm.shape[1:], F32)
        gu[k] = jnp.zeros(gu.shape[1:], F32)
        gd[k] = jnp.zeros(gd.shape[1:], F32)
        gs[k] = jnp.zeros(gs.shape[1:], F32)
    for n in range(4):
        for b in range(3):
            joined[n, :, CP * b + 2 * 128 : CP * b + CP] = jnp.zeros((ROWS, 128), BF16)
        uf[n, 0:SIDE, :] = jnp.zeros((SIDE, C), F32)
        uf[n, SIDE + ROWS : 2 * SIDE + ROWS, :] = jnp.zeros((SIDE, C), F32)
    for n in range(3):
        gsh[n, 0:SIDE, :] = jnp.zeros((SIDE, C), F32)
        gsh[n, SIDE + ROWS : 2 * SIDE + ROWS, :] = jnp.zeros((SIDE, C), F32)

    column = lax.broadcasted_iota(jnp.int32, (CHUNK, C), 0)
    column = column - SIDE * grid_row(column)
    not_first = column != 0
    not_last = column != SIDE - 1

    def later(value):
        return jnp.where(not_first, pltpu.roll(value, 1, 0), 0.0)

    def sooner(value):
        return jnp.where(not_last, pltpu.roll(value, CHUNK - 1, 0), 0.0)

    def mask_chunk(t, start):
        return mask_cols[t, pl.ds(start, CHUNK), :]

    def chunks(body, init):
        def step(c, carry):
            return body(pl.multiple_of(c * CHUNK, CHUNK), carry)
        return lax.fori_loop(0, ROWS // CHUNK, step, init)

    def send_stats(r):
        def one(step, carry):
            pltpu.make_async_remote_copy(
                src_ref=msg.at[r], dst_ref=land.at[r, n_dp - 1 - step],
                send_sem=st_send.at[r], recv_sem=st_recv.at[r],
                device_id={"dp": lax.rem(me_d + step, n_dp)}, device_id_type=MESH).start()
            return carry
        lax.fori_loop(1, n_dp, one, 0)

    def wait_stats(r):
        whole = pltpu.make_async_remote_copy(
            src_ref=land.at[r], dst_ref=land.at[r], send_sem=st_send.at[r], recv_sem=st_recv.at[r],
            device_id={"dp": lax.rem(me_d + 1, n_dp)}, device_id_type=MESH)
        whole.wait_send()
        whole.wait_recv()

    def conv_stage(t, k):
        z = 2 * k + t
        taps = [pack[k, CONV + n : CONV + n + 1, :] for n in range(9)]

        def conv(start, acc):
            rows = [uf[z, pl.ds(start + SIDE * r, CHUNK), :] for r in range(3)]
            part = [rows[0] * taps[s] + rows[1] * taps[3 + s] + rows[2] * taps[6 + s] for s in range(3)]
            out = part[1] + later(part[0]) + sooner(part[2])
            cv[z, pl.ds(start, CHUNK), :] = out
            m = mask_chunk(t, start)
            return acc[0] + fold(out * m), acc[1] + fold(m)

        acc, n_acc = chunks(conv, (jnp.zeros((8, C), F32), jnp.zeros((8, 1), F32)))
        sums, n_own = total(acc), total(n_acc)
        mean = sums / n_own

        def centred(start, acc):
            d = cv[z, pl.ds(start, CHUNK), :] - mean
            return acc + fold(d * d * mask_chunk(t, start))

        m2 = total(chunks(centred, jnp.zeros((8, C), F32)))
        msg[z, 0:1, 0:C] = sums
        msg[z, 0:1, C:CP] = jnp.broadcast_to(n_own, (1, CP - C))
        msg[z, 1:2, 0:C] = m2
        send_stats(z)

    def gather_stats(r):
        def add(d, carry):
            return carry + land[r, d]
        return lax.fori_loop(0, n_dp - 1, add, msg[r])

    def norm_stats(z):
        sums = gather_stats(z)[0:1, :]
        count = sums[:, CP - 1 : CP]
        mean = sums[:, 0:C] / count

        def spread(values):
            n = values[0:1, CP - 1 : CP]
            off = values[0:1, 0:C] / n - mean
            return values[1:2, 0:C] + n * off * off

        def add(d, carry):
            return carry + spread(land[z, d])
        m2 = lax.fori_loop(0, n_dp - 1, add, spread(msg[z]))
        return mean, lax.rsqrt(m2 / count + EPS), count

    def mixers(k, backward):
        _, j_g = one_hots(GROUP)
        i_r, j_r = one_hots(ROWS)
        ww = pack[k, WW : WW + SIDE, 0:SIDE].astype(BF16)
        hw = pack[k, HW : HW + SIDE, 0:SIDE].astype(BF16)
        side_of = 0 if backward else 1
        j_b = jnp.where(j_g, 1.0, 0.0).astype(BF16)
        i_b = jnp.where(i_r, 1.0, 0.0).astype(BF16)
        left = dot(j_b, ww, (1, 1 - side_of)).astype(BF16)
        p = grid_row(lax.broadcasted_iota(jnp.int32, (GROUP, GROUP), 0))
        q = grid_row(lax.broadcasted_iota(jnp.int32, (GROUP, GROUP), 1))
        kw[...] = jnp.where(p == q, dot(left, j_b, (1, 1)), 0.0).astype(BF16)
        left = dot(i_b, hw, (1, 1 - side_of)).astype(BF16)
        for piece in range(3):
            rows = slice(piece * GROUP, piece * GROUP + GROUP)
            p = lax.broadcasted_iota(jnp.int32, (GROUP, ROWS), 0) + piece * GROUP
            q = lax.broadcasted_iota(jnp.int32, (GROUP, ROWS), 1)
            same = p - SIDE * grid_row(p) == q - SIDE * grid_row(q)
            kh[rows, :] = jnp.where(same, dot(left[rows, :], i_b, (1, 1)), 0.0).astype(BF16)
        if not backward:
            wb = pack[k, WBIAS : WBIAS + 1, 0:SIDE]
            hb = pack[k, HBIAS : HBIAS + 1, 0:SIDE]
            wbcol[...] = jnp.sum(jnp.where(j_r, wb, 0.0), 1, keepdims=True)
            hbcol[...] = jnp.sum(jnp.where(i_r, hb, 0.0), 1, keepdims=True)

    def forward_stage(t, k):
        z = 2 * k + t
        wait_stats(z)
        mean, scale, _ = norm_stats(z)
        gain = pack[k, BGAIN : BGAIN + 1, :]
        bias = pack[k, BBIAS : BBIAS + 1, :]

        def standardize(start, carry):
            x = (cv[z, pl.ds(start, CHUNK), :] - mean) * scale
            cv[z, pl.ds(start, CHUNK), :] = x
            mixed = (x * gain + bias) * mask_chunk(t, start)
            joined[z, pl.ds(start, CHUNK), 2 * CP : 2 * CP + C] = mixed.astype(BF16)
            return carry
        chunks(standardize, 0)

        for g in range(3):
            rows = slice(g * GROUP, g * GROUP + GROUP)
            along = dot(kw[...], joined[z, rows, 2 * CP : 2 * CP + C]) + wbcol[rows, :]
            joined[z, rows, 0:C] = along.astype(BF16)
        along = dot(kh[...], joined[z, :, 2 * CP : 2 * CP + C]) + hbcol[...]
        joined[z, :, CP : CP + C] = along.astype(BF16)
        first[...] = dot(joined[z], wm[k])

        m_bias = pack[k, MBIAS : MBIAS + 1, :]
        n_gain = pack[k, NGAIN : NGAIN + 1, :]
        n_bias = pack[k, NBIAS : NBIAS + 1, :]

        def layer_norm(start, carry):
            rows = pl.ds(start, CHUNK)
            f = uf[z, pl.ds(start + SIDE, CHUNK), :] + first[rows, :] + m_bias
            d = f - jnp.mean(f, 1, keepdims=True)
            rs = lax.rsqrt(jnp.mean(d * d, 1, keepdims=True) + EPS)
            x = d * rs
            first[rows, :] = f
            rstd[z, rows, :] = rs
            xl[z, rows, :] = x.astype(BF16)
            normal[z, rows, :] = (x * n_gain + n_bias).astype(BF16)
            return carry
        chunks(layer_norm, 0)

        for n in range(FF // FT):
            cols = slice(n * FT, n * FT + FT)
            u_row = UBIAS + n
            u_bias = pack[k, u_row : u_row + 1, 0:FT]
            pre_s[...] = dot(normal[z], wu[k, :, cols])

            def act(start, carry):
                rows = pl.ds(start, CHUNK)
                h, dh = gelu_both(pre_s[rows, :] + u_bias)
                hidden[z, rows, cols] = h.astype(BF16)
                gp[z, rows, cols] = dh.astype(BF16)
                return carry
            chunks(act, 0)

        gnorm[...] = dot(hidden[z], wd[k])
        d_bias = pack[k, DBIAS : DBIAS + 1, :]

        def finish(i, carry):
            rows = pl.ds(pl.multiple_of(i * SIDE, SIDE), SIDE)
            y = (first[rows, :] + gnorm[rows, :] + d_bias).astype(BF16)
            ybuf[z, i] = y

            @pl.when(k == 0)
            def _():
                uf[2 + t, pl.ds(pl.multiple_of(i * SIDE + SIDE, SIDE), SIDE), :] = y.astype(F32)
            return carry
        lax.fori_loop(0, SIDE, finish, 0)

        @pl.when(me_p == k)
        def _():
            pltpu.make_async_copy(ybuf.at[z], so_h.at[0, 2 * me_p + t], so_local.at[t]).start()

        @pl.when(me_p != k)
        def _():
            across(ybuf.at[z], so_h.at[0, 2 * me_p + t], so_send.at[t], so_recv.at[t]).start()

    def backward_stage(t, k):
        z = 2 * k + t

        def round_grad(start, acc):
            rows = pl.ds(start, CHUNK)
            g = gf[t, rows, :]
            gb[rows, :] = g.astype(BF16)
            return acc + fold(g)
        d_bias_acc = chunks(round_grad, jnp.zeros((8, C), F32))
        gs[k, DBIAS : DBIAS + 1, :] += total(d_bias_acc)

        gbt[...] = gb[...].T
        for n in range(FF // FT):
            cols = slice(n * FT, n * FT + FT)
            gd[k, :, cols] += dot(gbt[...], hidden[z, :, cols])
            pre_s[...] = dot(gb[...], wd[k, cols, :], (1, 1))

            def act(start, acc):
                rows = pl.ds(start, CHUNK)
                g = (pre_s[rows, :] * gp[z, rows, cols].astype(F32)).astype(BF16)
                gpre[rows, cols] = g
                return acc + fold(g.astype(F32))
            u_acc = chunks(act, jnp.zeros((8, FT), F32))
            u_row = UBIAS + n
            gs[k, u_row : u_row + 1, 0:FT] += total(u_acc)

        gnorm[...] = dot(gpre[...], wu[k], (1, 1))
        gbt[...] = normal[z].T
        for n in range(FF // FT):
            cols = slice(n * FT, n * FT + FT)
            gu[k, :, cols] += dot(gbt[...], gpre[:, cols])

        n_gain = pack[k, NGAIN : NGAIN + 1, :]

        def norm_back(start, acc):
            rows = pl.ds(start, CHUNK)
            g = gnorm[rows, :]
            x = xl[z, rows, :].astype(F32)
            gn = g * n_gain
            mean_g = jnp.mean(gn, 1, keepdims=True)
            mean_gx = jnp.mean(gn * x, 1, keepdims=True)
            out = gf[t, rows, :] + rstd[z, rows, :] * (gn - mean_g - x * mean_gx)
            gf[t, rows, :] = out
            low = out.astype(BF16)
            gb[rows, :] = low
            return acc[0] + fold(g * x), acc[1] + fold(g), acc[2] + fold(low.astype(F32))
        zero = jnp.zeros((8, C), F32)
        acc = chunks(norm_back, (zero, zero, zero))
        gs[k, NGAIN : NGAIN + 1, :] += total(acc[0])
        gs[k, NBIAS : NBIAS + 1, :] += total(acc[1])
        gs[k, MBIAS : MBIAS + 1, :] += total(acc[2])

        gbt[...] = gb[...].T
        for n in range(3):
            cols = slice(n * CP, n * CP + CP)
            gm[k, :, cols] += dot(gbt[...], joined[z, :, cols])
        for n in range(2):
            gnorm[...] = dot(gb[...], wm[k, n * CP : n * CP + C, :], (1, 1))
            col = (wcol, hcol)[n]

            def branch(start, carry):
                rows = pl.ds(start, CHUNK)
                g = gnorm[rows, :].astype(BF16)
                gwh[n, rows, :] = g
                col[rows, :] += jnp.sum(g.astype(F32), 1, keepdims=True)
                return carry
            chunks(branch, 0)
        gnorm[...] = dot(gb[...], wm[k, 2 * CP : 2 * CP + C, :], (1, 1))
        for g in range(3):
            rows = slice(g * GROUP, g * GROUP + GROUP)
            gw_acc[...] += dot(gwh[0, rows, :], joined[z, rows, 2 * CP : 2 * CP + C], (1, 1))
            gnorm[rows, :] += dot(kw[...], gwh[0, rows, :])
        gh_acc[...] += dot(gwh[1], joined[z, :, 2 * CP : 2 * CP + C], (1, 1))
        gnorm[...] += dot(kh[...], gwh[1])

        def batch_sums(start, acc):
            rows = pl.ds(start, CHUNK)
            g = gnorm[rows, :] * mask_chunk(t, start)
            gmix[t, rows, :] = g
            return acc[0] + fold(g), acc[1] + fold(g * cv[z, rows, :])
        acc = chunks(batch_sums, (zero, zero))
        plain, cross = total(acc[0]), total(acc[1])
        gs[k, BBIAS : BBIAS + 1, :] += plain
        gs[k, BGAIN : BGAIN + 1, :] += cross
        r = 4 + z
        msg[r, 0:1, 0:C] = plain
        msg[r, 1:2, 0:C] = cross
        send_stats(r)

    def input_stage(t, k):
        z = 2 * k + t
        r = 4 + z
        wait_stats(r)
        _, scale, count = norm_stats(z)
        both = gather_stats(r)
        plain, cross = both[0:1, 0:C], both[1:2, 0:C]
        gain = pack[k, BGAIN : BGAIN + 1, :]
        out_scale = gain * scale
        plain = plain / count
        cross = cross / count

        def shifted(start, carry):
            rows = pl.ds(start, CHUNK)
            g = (gmix[t, rows, :] - plain - cv[z, rows, :] * cross) * (mask_chunk(t, start) * out_scale)
            rows = pl.ds(start + SIDE, CHUNK)
            gsh[0, rows, :] = sooner(g)
            gsh[1, rows, :] = g
            gsh[2, rows, :] = later(g)
            return carry
        chunks(shifted, 0)
        taps = [pack[k, CONV + n : CONV + n + 1, :] for n in range(9)]

        def pull(start, acc):
            start = pl.multiple_of(start, SIDE)
            rows = pl.ds(start, SIDE)
            u = [uf[z, pl.ds(start + SIDE * r, SIDE), :] for r in range(3)]
            out = gf[t, rows, :]
            new = []
            for s in range(3):
                here = gsh[s, pl.ds(start + SIDE, SIDE), :]
                for r in range(3):
                    out += gsh[s, pl.ds(start + SIDE * (2 - r), SIDE), :] * taps[3 * r + s]
                new.append([acc[s][r] + fold(here * u[r]) for r in range(3)])
            y = out.astype(BF16)
            igbuf[z, lax.div(start, SIDE)] = y

            @pl.when(k == 1)
            def _():
                gf[t, rows, :] = y.astype(F32)
            return new

        def step(i, acc):
            return pull(i * SIDE, acc)
        acc = lax.fori_loop(0, SIDE, step, [[jnp.zeros((8, C), F32) for _ in range(3)] for _ in range(3)])
        for r in range(3):
            for s in range(3):
                row = CONV + 3 * r + s
                gs[k, row : row + 1, :] += total(acc[s][r])

        @pl.when(me_p == k)
        def _():
            pltpu.make_async_copy(igbuf.at[z], ig_h.at[0, 2 * me_p + t], ig_local.at[t]).start()

        @pl.when(me_p != k)
        def _():
            across(igbuf.at[z], ig_h.at[0, 2 * me_p + t], ig_send.at[t], ig_recv.at[t]).start()

    def clear_mix():
        gw_acc[...] = jnp.zeros(gw_acc.shape, F32)
        gh_acc[...] = jnp.zeros(gh_acc.shape, F32)
        wcol[...] = jnp.zeros(wcol.shape, F32)
        hcol[...] = jnp.zeros(hcol.shape, F32)

    def close_mix(k):
        i_r, j_r = one_hots(ROWS)
        _, j_g = one_hots(GROUP)
        gs[k, WBIAS : WBIAS + 1, 0:SIDE] = total(jnp.where(j_r, wcol[...], 0.0))
        gs[k, HBIAS : HBIAS + 1, 0:SIDE] = total(jnp.where(i_r, hcol[...], 0.0))
        highest = lax.Precision.HIGHEST
        p = grid_row(lax.broadcasted_iota(jnp.int32, (GROUP, GROUP), 0))
        q = grid_row(lax.broadcasted_iota(jnp.int32, (GROUP, GROUP), 1))
        own = jnp.where(p == q, gw_acc[...], 0.0)
        own = jnp.sum(own.reshape(GROUP // SIDE, SIDE, GROUP), 0)
        gs[k, WW : WW + SIDE, 0:SIDE] = dot(own, jnp.where(j_g, 1.0, 0.0), precision=highest)
        i_f = jnp.where(i_r, 1.0, 0.0)
        for i in range(SIDE):
            rows = slice(i * SIDE, i * SIDE + SIDE)
            p = lax.broadcasted_iota(jnp.int32, (SIDE, ROWS), 0)
            q = lax.broadcasted_iota(jnp.int32, (SIDE, ROWS), 1)
            own = jnp.where(p == q - SIDE * grid_row(q), gh_acc[rows, :], 0.0)
            first[i : i + 1, :] = jnp.sum(own, 0, keepdims=True)[:, 0:C]
            gnorm[i : i + 1, 0 : ROWS - C] = jnp.sum(own, 0, keepdims=True)[:, C:ROWS]
        value = dot(first[0:SIDE, :], i_f[0:C, :], precision=highest)
        value += dot(gnorm[0:SIDE, 0 : ROWS - C], i_f[C:ROWS, :], precision=highest)
        gs[k, HW : HW + SIDE, 0:SIDE] = value

    mask_in.wait()
    pack_in.wait()
    pack_over.wait()
    for t in range(2):
        image_in[t].wait()

    def start_image(t, carry):
        def widen(i, inner):
            uf[t, pl.ds(pl.multiple_of(i * SIDE + SIDE, SIDE), SIDE), :] = ub[t, i].astype(F32)
            return inner
        lax.fori_loop(0, SIDE, widen, 0)
        conv_stage(t, 0)
        return carry
    lax.fori_loop(0, 2, start_image, 0)
    for t in range(2):
        grad_in[t].start()

    for copy in weights_in + weights_over:
        copy.wait()

    def forward_block(k, carry):
        mixers(k, False)

        def one(t, inner):
            forward_stage(t, k)

            @pl.when(k == 0)
            def _():
                conv_stage(t, 1)
            return inner
        lax.fori_loop(0, 2, one, 0)
        return carry
    lax.fori_loop(0, 2, forward_block, 0)

    for t in range(2):
        grad_in[t].wait()
        pltpu.make_async_copy(ybuf.at[t], so_h.at[0, t], so_local.at[t]).wait()
        across(ybuf.at[t], so_h.at[0, t], so_send.at[t], so_recv.at[t]).wait_send()

    def load_grad(t, carry):
        def widen(i, inner):
            gf[t, pl.ds(pl.multiple_of(i * SIDE, SIDE), SIDE), :] = ub[t, i].astype(F32)
            return inner
        lax.fori_loop(0, SIDE, widen, 0)
        return carry
    lax.fori_loop(0, 2, load_grad, 0)

    def backward_block(step, carry):
        k = 1 - step
        mixers(k, True)
        clear_mix()

        def one(t, inner):
            @pl.when(k == 0)
            def _():
                input_stage(t, 1)
            backward_stage(t, k)
            return inner
        lax.fori_loop(0, 2, one, 0)
        close_mix(k)
        return carry
    lax.fori_loop(0, 2, backward_block, 0)

    def last(t, carry):
        input_stage(t, 0)
        return carry
    lax.fori_loop(0, 2, last, 0)

    for t in range(2):
        pltpu.make_async_copy(igbuf.at[t], ig_h.at[0, t], ig_local.at[t]).wait()
        across(ybuf.at[t], so_h.at[0, t], so_send.at[t], so_recv.at[t]).wait_recv()
        across(igbuf.at[t], ig_h.at[0, t], ig_send.at[t], ig_recv.at[t]).wait()


def on_device(
    images, masks, conv_weight, batch_gain, batch_bias, width_weight, width_bias,
    height_weight, height_bias, merge_weight, merge_bias, norm_gain, norm_bias,
    up_weight, up_bias, down_weight, down_bias, out_grad,
):
    n_dp = lax.axis_size("dp")
    micro = images.shape[0]

    def wide(value):
        return jnp.pad(value.astype(F32), ((0, 0), (0, C - value.shape[1])))

    pack = jnp.concatenate([
        conv_weight[0].astype(F32), batch_gain, batch_bias, merge_bias, norm_gain, norm_bias, down_bias,
        wide(width_bias), wide(height_bias), wide(up_bias.reshape(FF // FT, FT)),
        jnp.zeros((WW - UBIAS - FF // FT, C), F32), wide(width_weight[0]), wide(height_weight[0])], 0)
    mask_cols = masks.astype(F32).reshape(micro, ROWS, 1)

    any_space = pl.BlockSpec(memory_space=pl.ANY)
    vmem = pl.BlockSpec(memory_space=pltpu.VMEM)
    dma = pltpu.SemaphoreType.DMA
    grid = (SIDE, SIDE, C)
    outs = pl.pallas_call(
        functools.partial(kernel, n_dp),
        out_shape=(
            jax.ShapeDtypeStruct((1, micro) + grid, BF16),
            jax.ShapeDtypeStruct((1, micro) + grid, BF16),
            jax.ShapeDtypeStruct((2, C, 3 * CP), F32),
            jax.ShapeDtypeStruct((2, C, FF), F32),
            jax.ShapeDtypeStruct((2, C, FF), F32),
            jax.ShapeDtypeStruct((2, PACK, C), F32),
        ),
        in_specs=[any_space] * 7,
        out_specs=(any_space, any_space, vmem, vmem, vmem, vmem),
        scratch_shapes=[
            pltpu.VMEM((2, ROWS, 1), F32),
            pltpu.VMEM((2, PACK, C), F32),
            pltpu.VMEM((2, 3 * CP, C), BF16),
            pltpu.VMEM((2, C, FF), BF16),
            pltpu.VMEM((2, FF, C), BF16),
            pltpu.VMEM((2,) + grid, BF16),
            pltpu.VMEM((4, ROWS + 2 * SIDE, C), F32),
            pltpu.VMEM((4, ROWS, C), F32),
            pltpu.VMEM((4, ROWS, 3 * CP), BF16),
            pltpu.VMEM((4, ROWS, C), BF16),
            pltpu.VMEM((4, ROWS, C), BF16),
            pltpu.VMEM((4, ROWS, 1), F32),
            pltpu.VMEM((4, ROWS, FF), BF16),
            pltpu.VMEM((4, ROWS, FF), BF16),
            pltpu.VMEM((2, ROWS, C), F32),
            pltpu.VMEM((ROWS, C), BF16),
            pltpu.VMEM((C, ROWS), BF16),
            pltpu.VMEM((ROWS, FF), BF16),
            pltpu.VMEM((2, ROWS, C), F32),
            pltpu.VMEM((2, ROWS, C), BF16),
            pltpu.VMEM((3, ROWS + 2 * SIDE, C), F32),
            pltpu.VMEM((GROUP, GROUP), BF16),
            pltpu.VMEM((ROWS, ROWS), BF16),
            pltpu.VMEM((ROWS, 1), F32),
            pltpu.VMEM((ROWS, 1), F32),
            pltpu.VMEM((GROUP, GROUP), F32),
            pltpu.VMEM((ROWS, ROWS), F32),
            pltpu.VMEM((ROWS, 1), F32),
            pltpu.VMEM((ROWS, 1), F32),
            pltpu.VMEM((4,) + grid, BF16),
            pltpu.VMEM((8, 2, CP), F32),
            pltpu.VMEM((8, n_dp - 1, 2, CP), F32),
            dma((11,)), dma((2,)), dma((5,)), dma((5,)), dma((8,)), dma((8,)),
            dma((2,)), dma((2,)), dma((2,)), dma((2,)), dma((2,)), dma((2,)),
        ],
        compiler_params=pltpu.CompilerParams(
            collective_id=0, has_side_effects=True, vmem_limit_bytes=65400 * 1024),
    )(images, mask_cols, pack, merge_weight, up_weight, down_weight, out_grad)
    so, ig, gm, gu, gd, gs = outs

    def reduce(value):
        return lax.psum(lax.psum_scatter(value, "pipe", scatter_dimension=0), "dp")

    gm, gu, gd, gs = reduce(gm), reduce(gu), reduce(gd), reduce(gs)
    gm = gm.reshape(C, 3, CP)[:, :, :C].reshape(C, 3 * C).T
    return (
        so, ig,
        gs[None, CONV : CONV + 9], gs[None, BGAIN], gs[None, BBIAS],
        gs[None, WW : WW + SIDE, :SIDE], gs[None, WBIAS, :SIDE],
        gs[None, HW : HW + SIDE, :SIDE], gs[None, HBIAS, :SIDE],
        gm[None], gs[None, MBIAS], gs[None, NGAIN], gs[None, NBIAS],
        gu[None], gs[UBIAS : UBIAS + FF // FT, :FT].reshape(1, FF), gd.T[None], gs[None, DBIAS],
    )


def solution(mesh):
    data4 = P("dp", None, None, None)
    p1, p2, p3 = P("pipe"), P("pipe", None), P("pipe", None, None)
    out5 = P("pipe", "dp", None, None, None)
    return jax.shard_map(
        on_device,
        mesh=mesh,
        in_specs=(data4, P("dp", None, None), p3, p2, p2, p3, p2, p3, p2, p3, p2, p2, p2, p3, p2, p3, p2, data4),
        out_specs=(out5, out5, p3, p2, p2, p3, p2, p3, p2, p3, p2, p2, p2, p3, p2, p3, p2),
        check_vma=False,
    )
```

```python
import functools

import jax
import jax.numpy as jnp
from jax import lax
from jax.experimental import pallas as pl
from jax.experimental.pallas import tpu as pltpu
from jax.sharding import PartitionSpec as P

EPS = 1e-05
MESH = pl.DeviceIdType.MESH
F32 = jnp.float32
BF16 = jnp.bfloat16

SIDE = 24
ROWS = SIDE * SIDE
C = 320
CP = 384
FF = 1280
FT = 256
CHUNK = 48
GROUP = 8 * SIDE

HALF = C // 2
SHARD = HALF // 2
WIDE = FF // 2
SHARDS = 8

CONV, BGAIN, BBIAS, MBIAS, NGAIN, NBIAS, DBIAS, WBIAS, HBIAS, UBIAS, WW, HW, PACK = (
    0, 16, 17, 18, 19, 20, 21, 22, 23, 24, 32, 56, 80)
SMALL = 16


def dot(a, b, contract=(1, 0), precision=None):
    return lax.dot_general(
        a, b, (((contract[0],), (contract[1],)), ((), ())),
        preferred_element_type=F32, precision=precision)


def fold(value):
    rows = value.shape[0]
    return jnp.sum(value.reshape(rows // 8, 8, value.shape[1]), 0)


def total(partial):
    return jnp.sum(partial, 0, keepdims=True)


def grid_row(index):
    return (index * 2731) >> 16


def one_hots(rows):
    place = lax.broadcasted_iota(jnp.int32, (rows, SIDE), 0)
    lane = lax.broadcasted_iota(jnp.int32, (rows, SIDE), 1)
    i = grid_row(place)
    return i == lane, place - SIDE * i == lane


def gelu_both(x):
    ax = jnp.abs(x)
    e = jnp.exp(-0.5 * x * x)
    t = 1.0 / (1.0 + (0.3275911 * 0.7071067811865476) * ax)
    poly = t * (0.127414796 + t * (-0.142248368 + t * (0.7107068705 + t * (-0.7265760135 + t * 0.5307027145))))
    tail = poly * e
    phi = jnp.where(x >= 0, 1.0 - tail, tail)
    return x * phi, phi + x * e * 0.3989422804014327


def kernel(
    n_dp,
    images, masks, conv_w, bgain, bbias, wwt, wb, hwt, hb, wm_h, mbias, ngain, nbias, wu_h, ubias, wd_h, dbias, og_h,
    so_h, ig_h, ga_h, gb_h, gs_h, sp_hidden, sp_gp, sp_joined, sp_normal, sp_xl,
    mask_cols, pack, wm, wmid, wu, wd, ub, uf, cv, joined, normal, xl, rstd, hidden, gp,
    gf, gb, gbt, gpre, gmix, gwh, gsh, kw, kh, wbcol, hbcol,
    gw_acc, gh_acc, wcol, hcol, ybuf, msg, land, acc_a, acc_b, gs,
    sb_a, lb_a, rl_a, sb_b, lb_b, rl_b, small_land, conv_land,
    local_sems, again_sems, pack_sems, w_send, w_recv, st_send, st_recv,
    so_local, so_send, so_recv, ig_local, ig_send, ig_recv, spill_sems, fetch_sems,
    red_send, red_recv, small_send, small_recv, conv_send, conv_recv, out_local, out_send, out_recv, gs_sem,
):
    me_p = lax.axis_index("pipe")
    me_d = lax.axis_index("dp")
    other = 1 - me_p
    first = gsh.at[2, pl.ds(SIDE, ROWS)]
    igbuf = ybuf
    gnorm = gsh.at[0, pl.ds(SIDE, ROWS)]
    pre_s = gsh.at[1, pl.ds(SIDE, ROWS), pl.ds(0, FT)]

    def image_copy(t, sems):
        return pltpu.make_async_copy(images.at[2 * me_p + t], ub.at[t], sems)

    image_in = [image_copy(t, local_sems.at[5 + t]) for t in range(2)]
    grad_in = [pltpu.make_async_copy(og_h.at[2 * me_p + t], ub.at[t], local_sems.at[7 + t]) for t in range(2)]
    weights = ((wm_h, wm), (wu_h, wu), (wd_h, wd))
    weights_in = [pltpu.make_async_copy(src, dst.at[me_p], local_sems.at[n]) for n, (src, dst) in enumerate(weights)]
    for copy in image_in + weights_in:
        copy.start()

    barrier = pltpu.get_barrier_semaphore()

    def greet(step, carry):
        pl.semaphore_signal(barrier, inc=1, device_id={"dp": lax.rem(me_d + step, n_dp)}, device_id_type=MESH)
        return carry

    lax.fori_loop(1, n_dp, greet, 0)
    pl.semaphore_signal(barrier, inc=1, device_id={"pipe": other}, device_id_type=MESH)

    pack[me_p] = jnp.zeros(pack.shape[1:], F32)
    pack[me_p, CONV : CONV + 9, :] = conv_w[0].astype(F32)
    for row, ref in ((BGAIN, bgain), (BBIAS, bbias), (MBIAS, mbias), (NGAIN, ngain), (NBIAS, nbias), (DBIAS, dbias)):
        pack[me_p, row : row + 1, :] = ref[...]
    for row, ref in ((WBIAS, wb), (HBIAS, hb)):
        pack[me_p, row : row + 1, 0:SIDE] = ref[...]
    for n in range(FF // FT):
        pack[me_p, UBIAS + n : UBIAS + n + 1, 0:FT] = ubias[:, n * FT : n * FT + FT]
    for row, ref in ((WW, wwt), (HW, hwt)):
        pack[me_p, row : row + SIDE, 0:SIDE] = ref[0].astype(F32)

    pl.semaphore_wait(barrier, n_dp)

    def across(src, dst, send, recv):
        return pltpu.make_async_remote_copy(
            src_ref=src, dst_ref=dst, send_sem=send, recv_sem=recv,
            device_id={"pipe": other}, device_id_type=MESH)

    pack_over = across(pack.at[me_p], pack.at[me_p], pack_sems.at[0], pack_sems.at[1])
    weights_over = [across(src, dst.at[me_p], w_send.at[n], w_recv.at[n]) for n, (src, dst) in enumerate(weights)]
    pack_over.start()
    for copy in weights_over:
        copy.start()

    msg[...] = jnp.zeros(msg.shape, F32)
    for k in range(2):
        for n in range(4):
            acc_a[k, n] = jnp.zeros(acc_a.shape[2:], F32)
            acc_b[k, n] = jnp.zeros(acc_b.shape[2:], F32)
        gs[k] = jnp.zeros(gs.shape[1:], F32)
    for n in range(2):
        uf[n, 0:SIDE, :] = jnp.zeros((SIDE, C), F32)
        uf[n, SIDE + ROWS : 2 * SIDE + ROWS, :] = jnp.zeros((SIDE, C), F32)
    for n in range(3):
        gsh[n, 0:SIDE, :] = jnp.zeros((SIDE, C), F32)
        gsh[n, SIDE + ROWS : 2 * SIDE + ROWS, :] = jnp.zeros((SIDE, C), F32)

    i_r, j_r = one_hots(ROWS)
    i_b = jnp.where(i_r, 1.0, 0.0).astype(BF16)
    for t in range(2):
        chosen = dot(i_b, masks[2 * me_p + t].astype(F32).astype(BF16))
        mask_cols[t] = jnp.sum(jnp.where(j_r, chosen, 0.0), 1, keepdims=True)

    column = lax.broadcasted_iota(jnp.int32, (CHUNK, C), 0)
    column = column - SIDE * grid_row(column)
    not_first = column != 0
    not_last = column != SIDE - 1

    def later(value):
        return jnp.where(not_first, pltpu.roll(value, 1, 0), 0.0)

    def sooner(value):
        return jnp.where(not_last, pltpu.roll(value, CHUNK - 1, 0), 0.0)

    def mask_chunk(t, start):
        return mask_cols[t, pl.ds(start, CHUNK), :]

    def chunks(body, init):
        def step(c, carry):
            return body(pl.multiple_of(c * CHUNK, CHUNK), carry)
        return lax.fori_loop(0, ROWS // CHUNK, step, init)

    def send_stats(r):
        def one(step, carry):
            pltpu.make_async_remote_copy(
                src_ref=msg.at[r], dst_ref=land.at[r, n_dp - 1 - step],
                send_sem=st_send.at[r], recv_sem=st_recv.at[r],
                device_id={"dp": lax.rem(me_d + step, n_dp)}, device_id_type=MESH).start()
            return carry
        lax.fori_loop(1, n_dp, one, 0)

    def wait_stats(r):
        whole = pltpu.make_async_remote_copy(
            src_ref=land.at[r], dst_ref=land.at[r], send_sem=st_send.at[r], recv_sem=st_recv.at[r],
            device_id={"dp": lax.rem(me_d + 1, n_dp)}, device_id_type=MESH)
        whole.wait_send()
        whole.wait_recv()

    def conv_stage(t, k):
        z = 2 * k + t
        taps = [pack[k, CONV + n : CONV + n + 1, :] for n in range(9)]

        def conv(start, acc):
            rows = [uf[t, pl.ds(start + SIDE * r, CHUNK), :] for r in range(3)]
            part = [rows[0] * taps[s] + rows[1] * taps[3 + s] + rows[2] * taps[6 + s] for s in range(3)]
            out = part[1] + later(part[0]) + sooner(part[2])
            cv[z, pl.ds(start, CHUNK), :] = out
            m = mask_chunk(t, start)
            return acc[0] + fold(out * m), acc[1] + fold(m)

        acc, n_acc = chunks(conv, (jnp.zeros((8, C), F32), jnp.zeros((8, 1), F32)))
        sums, n_own = total(acc), total(n_acc)
        mean = sums / n_own

        def centred(start, acc):
            d = cv[z, pl.ds(start, CHUNK), :] - mean
            return acc + fold(d * d * mask_chunk(t, start))

        m2 = total(chunks(centred, jnp.zeros((8, C), F32)))
        msg[z, 0:1, 0:C] = sums
        msg[z, 0:1, C:CP] = jnp.broadcast_to(n_own, (1, CP - C))
        msg[z, 1:2, 0:C] = m2
        send_stats(z)

    def gather_stats(r):
        def add(d, carry):
            return carry + land[r, d]
        return lax.fori_loop(0, n_dp - 1, add, msg[r])

    def norm_stats(z):
        sums = gather_stats(z)[0:1, :]
        count = sums[:, CP - 1 : CP]
        mean = sums[:, 0:C] / count

        def spread(values):
            n = values[0:1, CP - 1 : CP]
            off = values[0:1, 0:C] / n - mean
            return values[1:2, 0:C] + n * off * off

        def add(d, carry):
            return carry + spread(land[z, d])
        m2 = lax.fori_loop(0, n_dp - 1, add, spread(msg[z]))
        return mean, lax.rsqrt(m2 / count + EPS), count

    def mixers(k, backward):
        _, j_g = one_hots(GROUP)
        i_r, j_r = one_hots(ROWS)
        ww = pack[k, WW : WW + SIDE, 0:SIDE].astype(BF16)
        hw = pack[k, HW : HW + SIDE, 0:SIDE].astype(BF16)
        side_of = 0 if backward else 1
        j_b = jnp.where(j_g, 1.0, 0.0).astype(BF16)
        i_b = jnp.where(i_r, 1.0, 0.0).astype(BF16)
        left = dot(j_b, ww, (1, 1 - side_of)).astype(BF16)
        p = grid_row(lax.broadcasted_iota(jnp.int32, (GROUP, GROUP), 0))
        q = grid_row(lax.broadcasted_iota(jnp.int32, (GROUP, GROUP), 1))
        kw[...] = jnp.where(p == q, dot(left, j_b, (1, 1)), 0.0).astype(BF16)
        left = dot(i_b, hw, (1, 1 - side_of)).astype(BF16)
        for piece in range(3):
            rows = slice(piece * GROUP, piece * GROUP + GROUP)
            p = lax.broadcasted_iota(jnp.int32, (GROUP, ROWS), 0) + piece * GROUP
            q = lax.broadcasted_iota(jnp.int32, (GROUP, ROWS), 1)
            same = p - SIDE * grid_row(p) == q - SIDE * grid_row(q)
            kh[rows, :] = jnp.where(same, dot(left[rows, :], i_b, (1, 1)), 0.0).astype(BF16)
        if not backward:
            wb = pack[k, WBIAS : WBIAS + 1, 0:SIDE]
            hb = pack[k, HBIAS : HBIAS + 1, 0:SIDE]
            wbcol[...] = jnp.sum(jnp.where(j_r, wb, 0.0), 1, keepdims=True)
            hbcol[...] = jnp.sum(jnp.where(i_r, hb, 0.0), 1, keepdims=True)

    stored = ((hidden, sp_hidden), (gp, sp_gp), (joined, sp_joined), (normal, sp_normal), (xl, sp_xl))

    def spill(t):
        return [pltpu.make_async_copy(v.at[t], h.at[t], spill_sems.at[t, n]) for n, (v, h) in enumerate(stored)]

    def fetch(t):
        return [pltpu.make_async_copy(h.at[t], v.at[t], fetch_sems.at[t, n]) for n, (v, h) in enumerate(stored)]

    def forward_stage(t, k):
        z = 2 * k + t

        @pl.when(k == 1)
        def _():
            for copy in spill(t):
                copy.wait()

        wait_stats(z)
        mean, scale, _ = norm_stats(z)
        gain = pack[k, BGAIN : BGAIN + 1, :]
        bias = pack[k, BBIAS : BBIAS + 1, :]

        def standardize(start, carry):
            x = (cv[z, pl.ds(start, CHUNK), :] - mean) * scale
            cv[z, pl.ds(start, CHUNK), :] = x
            mixed = (x * gain + bias) * mask_chunk(t, start)
            joined[t, pl.ds(start, CHUNK), 2 * C : 3 * C] = mixed.astype(BF16)
            return carry
        chunks(standardize, 0)

        for g in range(3):
            rows = slice(g * GROUP, g * GROUP + GROUP)
            along = dot(kw[...], joined[t, rows, 2 * C : 3 * C]) + wbcol[rows, :]
            joined[t, rows, 0:C] = along.astype(BF16)
        along = dot(kh[...], joined[t, :, 2 * C : 3 * C]) + hbcol[...]
        joined[t, :, C : 2 * C] = along.astype(BF16)
        first[...] = dot(joined[t], wm[k], (1, 1))

        m_bias = pack[k, MBIAS : MBIAS + 1, :]
        n_gain = pack[k, NGAIN : NGAIN + 1, :]
        n_bias = pack[k, NBIAS : NBIAS + 1, :]

        def layer_norm(start, carry):
            rows = pl.ds(start, CHUNK)
            f = uf[t, pl.ds(start + SIDE, CHUNK), :] + first[rows, :] + m_bias
            d = f - jnp.mean(f, 1, keepdims=True)
            rs = lax.rsqrt(jnp.mean(d * d, 1, keepdims=True) + EPS)
            x = d * rs
            first[rows, :] = f
            rstd[z, rows, :] = rs
            xl[t, rows, :] = x.astype(BF16)
            normal[t, rows, :] = (x * n_gain + n_bias).astype(BF16)
            return carry
        chunks(layer_norm, 0)

        for n in range(FF // FT):
            cols = slice(n * FT, n * FT + FT)
            u_row = UBIAS + n
            u_bias = pack[k, u_row : u_row + 1, 0:FT]
            pre_s[...] = dot(normal[t], wu[k, :, cols])

            def act(start, carry):
                rows = pl.ds(start, CHUNK)
                h, dh = gelu_both(pre_s[rows, :] + u_bias)
                hidden[t, rows, cols] = h.astype(BF16)
                gp[t, rows, cols] = dh.astype(BF16)
                return carry
            chunks(act, 0)

        gnorm[...] = dot(hidden[t], wd[k], (1, 1))
        d_bias = pack[k, DBIAS : DBIAS + 1, :]

        def finish(i, carry):
            rows = pl.ds(pl.multiple_of(i * SIDE, SIDE), SIDE)
            y = (first[rows, :] + gnorm[rows, :] + d_bias).astype(BF16)
            ybuf[z, i] = y

            @pl.when(k == 0)
            def _():
                uf[t, pl.ds(pl.multiple_of(i * SIDE + SIDE, SIDE), SIDE), :] = y.astype(F32)
            return carry
        lax.fori_loop(0, SIDE, finish, 0)

        @pl.when(me_p == k)
        def _():
            pltpu.make_async_copy(ybuf.at[z], so_h.at[0, 2 * me_p + t], so_local.at[t]).start()

        @pl.when(me_p != k)
        def _():
            across(ybuf.at[z], so_h.at[0, 2 * me_p + t], so_send.at[t], so_recv.at[t]).start()

    def backward_stage(t, k, tick):
        z = 2 * k + t

        def round_grad(start, acc):
            rows = pl.ds(start, CHUNK)
            g = gf[t, rows, :]
            gb[rows, :] = g.astype(BF16)
            return acc + fold(g)
        d_bias_acc = chunks(round_grad, jnp.zeros((8, C), F32))
        gs[k, DBIAS : DBIAS + 1, :] += total(d_bias_acc)

        gbt[...] = gb[...].T
        for n in range(2):
            acc_a[k, n] += dot(gbt[...], hidden[t, :, n * WIDE : n * WIDE + WIDE])
        tick(1)
        for n in range(FF // FT):
            cols = slice(n * FT, n * FT + FT)
            pre_s[...] = dot(gb[...], wd[k, :, cols])

            def act(start, acc):
                rows = pl.ds(start, CHUNK)
                g = (pre_s[rows, :] * gp[t, rows, cols].astype(F32)).astype(BF16)
                gpre[rows, cols] = g
                return acc + fold(g.astype(F32))
            u_acc = chunks(act, jnp.zeros((8, FT), F32))
            u_row = UBIAS + n
            gs[k, u_row : u_row + 1, 0:FT] += total(u_acc)

        tick(2)
        gnorm[...] = dot(gpre[...], wu[k], (1, 1))
        gbt[...] = normal[t].T
        for n in range(2):
            acc_a[k, 2 + n] += dot(gbt[...], gpre[:, n * WIDE : n * WIDE + WIDE])
        tick(3)

        n_gain = pack[k, NGAIN : NGAIN + 1, :]

        def norm_back(start, acc):
            rows = pl.ds(start, CHUNK)
            g = gnorm[rows, :]
            x = xl[t, rows, :].astype(F32)
            gn = g * n_gain
            mean_g = jnp.mean(gn, 1, keepdims=True)
            mean_gx = jnp.mean(gn * x, 1, keepdims=True)
            out = gf[t, rows, :] + rstd[z, rows, :] * (gn - mean_g - x * mean_gx)
            gf[t, rows, :] = out
            low = out.astype(BF16)
            gb[rows, :] = low
            return acc[0] + fold(g * x), acc[1] + fold(g), acc[2] + fold(low.astype(F32))
        zero = jnp.zeros((8, C), F32)
        acc = chunks(norm_back, (zero, zero, zero))
        gs[k, NGAIN : NGAIN + 1, :] += total(acc[0])
        gs[k, NBIAS : NBIAS + 1, :] += total(acc[1])
        gs[k, MBIAS : MBIAS + 1, :] += total(acc[2])

        gbt[...] = gb[...].T
        for n in range(4):
            width = min(FT, 3 * C - n * FT)
            acc_b[k, n, :, 0:width] += dot(gbt[...], joined[t, :, n * FT : n * FT + width])
        tick(4)
        for n in range(2):
            gnorm[...] = dot(gb[...], wmid[k] if n else wm[k, :, 0:C])
            col = (wcol, hcol)[n]

            def branch(start, carry):
                rows = pl.ds(start, CHUNK)
                g = gnorm[rows, :].astype(BF16)
                gwh[n, rows, :] = g
                col[rows, :] += jnp.sum(g.astype(F32), 1, keepdims=True)
                return carry
            chunks(branch, 0)
        tick(5)
        gnorm[...] = dot(gb[...], wm[k, :, 2 * C : 3 * C])
        for g in range(3):
            rows = slice(g * GROUP, g * GROUP + GROUP)
            gw_acc[...] += dot(gwh[0, rows, :], joined[t, rows, 2 * C : 3 * C], (1, 1))
            gnorm[rows, :] += dot(kw[...], gwh[0, rows, :])
        gh_acc[...] += dot(gwh[1], joined[t, :, 2 * C : 3 * C], (1, 1))
        gnorm[...] += dot(kh[...], gwh[1])

        def batch_sums(start, acc):
            rows = pl.ds(start, CHUNK)
            g = gnorm[rows, :] * mask_chunk(t, start)
            gmix[t, rows, :] = g
            return acc[0] + fold(g), acc[1] + fold(g * cv[z, rows, :])
        acc = chunks(batch_sums, (zero, zero))
        plain, cross = total(acc[0]), total(acc[1])
        gs[k, BBIAS : BBIAS + 1, :] += plain
        gs[k, BGAIN : BGAIN + 1, :] += cross
        r = 4 + z
        msg[r, 0:1, 0:C] = plain
        msg[r, 1:2, 0:C] = cross
        send_stats(r)

    def input_stage(t, k, tick):
        z = 2 * k + t
        r = 4 + z
        wait_stats(r)
        _, scale, count = norm_stats(z)
        both = gather_stats(r)
        plain, cross = both[0:1, 0:C], both[1:2, 0:C]
        gain = pack[k, BGAIN : BGAIN + 1, :]
        out_scale = gain * scale
        plain = plain / count
        cross = cross / count

        def shifted(start, carry):
            rows = pl.ds(start, CHUNK)
            g = (gmix[t, rows, :] - plain - cv[z, rows, :] * cross) * (mask_chunk(t, start) * out_scale)
            rows = pl.ds(start + SIDE, CHUNK)
            gsh[0, rows, :] = sooner(g)
            gsh[1, rows, :] = g
            gsh[2, rows, :] = later(g)
            return carry
        chunks(shifted, 0)
        tick(8)
        taps = [pack[k, CONV + n : CONV + n + 1, :] for n in range(9)]

        def pull(start, acc):
            start = pl.multiple_of(start, SIDE)
            rows = pl.ds(start, SIDE)
            u = [uf[t, pl.ds(start + SIDE * r, SIDE), :] for r in range(3)]
            out = gf[t, rows, :]
            new = []
            for s in range(3):
                here = gsh[s, pl.ds(start + SIDE, SIDE), :]
                for r in range(3):
                    out += gsh[s, pl.ds(start + SIDE * (2 - r), SIDE), :] * taps[3 * r + s]
                new.append([acc[s][r] + fold(here * u[r]) for r in range(3)])
            y = out.astype(BF16)
            igbuf[z, lax.div(start, SIDE)] = y

            @pl.when(k == 1)
            def _():
                gf[t, rows, :] = y.astype(F32)
            return new

        def step(i, acc):
            return pull(i * SIDE, acc)
        acc = lax.fori_loop(0, SIDE, step, [[jnp.zeros((8, C), F32) for _ in range(3)] for _ in range(3)])
        for r in range(3):
            for s in range(3):
                row = CONV + 3 * r + s
                gs[k, row : row + 1, :] += total(acc[s][r])

        @pl.when(me_p == k)
        def _():
            pltpu.make_async_copy(igbuf.at[z], ig_h.at[0, 2 * me_p + t], ig_local.at[t]).start()

        @pl.when(me_p != k)
        def _():
            across(igbuf.at[z], ig_h.at[0, 2 * me_p + t], ig_send.at[t], ig_recv.at[t]).start()

    def clear_mix():
        gw_acc[...] = jnp.zeros(gw_acc.shape, F32)
        gh_acc[...] = jnp.zeros(gh_acc.shape, F32)
        wcol[...] = jnp.zeros(wcol.shape, F32)
        hcol[...] = jnp.zeros(hcol.shape, F32)

    def close_mix(k):
        i_r, j_r = one_hots(ROWS)
        _, j_g = one_hots(GROUP)
        gs[k, WBIAS : WBIAS + 1, 0:SIDE] = total(jnp.where(j_r, wcol[...], 0.0))
        gs[k, HBIAS : HBIAS + 1, 0:SIDE] = total(jnp.where(i_r, hcol[...], 0.0))
        highest = lax.Precision.HIGHEST
        p = grid_row(lax.broadcasted_iota(jnp.int32, (GROUP, GROUP), 0))
        q = grid_row(lax.broadcasted_iota(jnp.int32, (GROUP, GROUP), 1))
        own = jnp.where(p == q, gw_acc[...], 0.0)
        own = jnp.sum(own.reshape(GROUP // SIDE, SIDE, GROUP), 0)
        gs[k, WW : WW + SIDE, 0:SIDE] = dot(own, jnp.where(j_g, 1.0, 0.0), precision=highest)
        i_f = jnp.where(i_r, 1.0, 0.0)
        for i in range(SIDE):
            rows = slice(i * SIDE, i * SIDE + SIDE)
            p = lax.broadcasted_iota(jnp.int32, (SIDE, ROWS), 0)
            q = lax.broadcasted_iota(jnp.int32, (SIDE, ROWS), 1)
            own = jnp.where(p == q - SIDE * grid_row(q), gh_acc[rows, :], 0.0)
            first[i : i + 1, :] = jnp.sum(own, 0, keepdims=True)[:, 0:C]
            gnorm[i : i + 1, 0 : ROWS - C] = jnp.sum(own, 0, keepdims=True)[:, C:ROWS]
        value = dot(first[0:SIDE, :], i_f[0:C, :], precision=highest)
        value += dot(gnorm[0:SIDE, 0 : ROWS - C], i_f[C:ROWS, :], precision=highest)
        gs[k, HW : HW + SIDE, 0:SIDE] = value

    bits = [1, 2, 4]
    while 2 * bits[-1] < n_dp:
        bits.append(2 * bits[-1])

    def partner(bit):
        return me_d + bit * (1 - 2 * lax.rem(me_d // bit, 2))

    def side(bit):
        return lax.rem(me_d // bit, 2)

    halving = [1 + me_p, 2 - me_p, 4]

    def along(bit, src, dst, send, recv):
        return pltpu.make_async_remote_copy(
            src_ref=src, dst_ref=dst, send_sem=send, recv_sem=recv,
            device_id={"dp": partner(bit)}, device_id_type=MESH)

    n_steps = 4 + len(bits) - 3 + 3

    def reduction(phase):
        k, which = 1 - phase // 2, phase % 2
        acc, out_h = ((acc_a, ga_h), (acc_b, gb_h))[which]
        slot = phase // 2
        sb, lb, rl = ((sb_a, lb_a, rl_a), (sb_b, lb_b, rl_b))[which]
        sb, lb, rl = sb.at[slot], lb.at[slot], rl.at[slot]

        def sems(step):
            return red_send.at[phase, step], red_recv.at[phase, step]

        def own(q):
            return k, lax.div(q, 2), pl.ds(pl.multiple_of(me_p * HALF + lax.rem(q, 2) * SHARD, 16), SHARD), slice(None)

        def each(count, body):
            def step(n, carry):
                body(n)
                return carry
            lax.fori_loop(0, count, step, 0)

        in_chip = across(sb.at[pl.ds(0, SHARDS)], lb, *sems(0))
        base = [0]
        for n, bit in enumerate(halving):
            base.append(base[n] + side(bit) * (4 >> n))
        mine = base[3]

        def half_copy(n):
            count, at = 4 >> n, 8 - (8 >> n)
            return along(halving[n], sb.at[pl.ds(at, count)], rl.at[pl.ds(at, count)], *sems(1 + n))

        def swap_copy(n):
            return along(bits[3 + n], sb.at[7 + n], rl.at[7 + n], *sems(4 + n))

        def double_copy(n):
            count = 4 >> n
            here = lb.at[pl.ds(base[n + 1], count)]
            return along(halving[n], here, here, *sems(n_steps - 1 - n))

        def send_half(n, landed):
            count, at = 4 >> n, 8 - (8 >> n)
            give = base[n] + (1 - side(halving[n])) * count
            keep = base[n + 1]

            def one(q):
                sb[at + q] = (acc[own(give + q)] + landed(give + q).astype(F32)).astype(BF16)
            each(count, one)
            half_copy(n).start()

            def two(q):
                acc[own(keep + q)] += landed(keep + q).astype(F32)
            each(count, two)

        def start():
            def one(q):
                rows = pl.ds(pl.multiple_of(other * HALF + lax.rem(q, 2) * SHARD, 16), SHARD)
                sb[q] = acc[k, lax.div(q, 2), rows, :].astype(BF16)
            each(SHARDS, one)
            in_chip.start()

        def first_half():
            in_chip.wait()
            send_half(0, lambda q: lb[q])

        def next_half(n):
            def run():
                half_copy(n - 1).wait()
                at = 8 - (8 >> (n - 1))
                send_half(n, lambda q: rl[at + q - base[n]])
            return run

        def swap(n):
            def run():
                if n == 0:
                    half_copy(2).wait()
                    acc[own(mine)] += rl[6].astype(F32)
                else:
                    swap_copy(n - 1).wait()
                    acc[own(mine)] = sb[6 + n].astype(F32) + rl[6 + n].astype(F32)
                sb[7 + n] = acc[own(mine)].astype(BF16)
                swap_copy(n).start()
            return run

        def double(n):
            def run():
                if n == 2:
                    last = len(bits) - 4
                    swap_copy(last).wait()
                    lb[mine] = (sb[7 + last].astype(F32) + rl[7 + last].astype(F32)).astype(BF16)
                else:
                    double_copy(n + 1).wait()
                double_copy(n).start()
            return run

        def hand_over():
            double_copy(0).wait()

            @pl.when(me_p == k)
            def _():
                pltpu.make_async_copy(lb, out_h.at[me_p], out_local.at[which]).start()

            @pl.when(me_p != k)
            def _():
                across(lb, out_h.at[me_p], out_send.at[which], out_recv.at[which]).start()

        return ([start, first_half, next_half(1), next_half(2)] + [swap(n) for n in range(len(bits) - 3)]
                + [double(2), double(1), double(0), hand_over])

    def small_sum(rows, landing, send, recv):
        count = rows.stop - rows.start
        rows = pl.ds(rows.start, count)
        in_chip = across(gs.at[other, rows], landing.at[0], send.at[0], recv.at[0])

        def swap_copy(n):
            return along(bits[n], gs.at[me_p, rows], landing.at[1 + n], send.at[1 + n], recv.at[1 + n])

        def step(n):
            def run():
                (swap_copy(n - 1) if n else in_chip).wait()
                gs[me_p, rows, :] += landing[n]
                if n < len(bits):
                    swap_copy(n).start()
            return run
        return [in_chip.start] + [step(n) for n in range(len(bits) + 1)]

    block2 = [reduction(0), reduction(1)]
    block1 = [reduction(2), reduction(3)]
    small = small_sum(slice(SMALL, PACK), small_land, small_send, small_recv)
    taps_sum = small_sum(slice(0, SMALL), conv_land, conv_send, conv_recv)

    plan = {}

    def put(places, pair):
        left = [list(pair[0]), list(pair[1])]
        plan.setdefault(places[0], []).append(left[0].pop(0))
        plan.setdefault(places[1], []).append(left[1].pop(0))
        turn = 0
        for place in places[2:]:
            if left[turn]:
                plan.setdefault(place, []).append(left[turn].pop(0))
            turn = 1 - turn
        rest = []
        while left[0] or left[1]:
            if left[turn]:
                rest.append(left[turn].pop(0))
            turn = 1 - turn
        return rest

    inner = [7, 8, 9, 0, 1, 2, 3, 4, 5, 6]
    tail = put([(1, 3), (1, 4), (1, 5), (1, 6)] + [(2, p) for p in inner] + [(3, p) for p in inner], block2)
    assert not tail
    tail = put([(3, 3), (3, 4), (3, 5), (3, 6)] + [(4, 7), (4, 8), (4, 9), (5, 7), (5, 8), (5, 9)], block1)
    for place, step in zip([(4, 7), (4, 8), (4, 9), (5, 7), (5, 8), (5, 9)], small):
        plan.setdefault(place, []).append(step)
    tail += small[6:]

    pack_over.wait()
    for t in range(2):
        image_in[t].wait()

    def widen_image(t):
        def widen(i, inner):
            uf[t, pl.ds(pl.multiple_of(i * SIDE + SIDE, SIDE), SIDE), :] = ub[t, i].astype(F32)
            return inner
        lax.fori_loop(0, SIDE, widen, 0)

    def start_image(t, carry):
        widen_image(t)
        conv_stage(t, 0)
        return carry
    lax.fori_loop(0, 2, start_image, 0)
    for t in range(2):
        grad_in[t].start()

    for copy in weights_in + weights_over:
        copy.wait()
    for k in range(2):
        wmid[k] = wm[k, :, C : 2 * C]

    def forward_block(k, carry):
        mixers(k, False)

        def one(t, inner):
            forward_stage(t, k)

            @pl.when(k == 0)
            def _():
                for copy in spill(t):
                    copy.start()
                conv_stage(t, 1)
            return inner
        lax.fori_loop(0, 2, one, 0)
        return carry
    lax.fori_loop(0, 2, forward_block, 0)

    for t in range(2):
        grad_in[t].wait()
        pltpu.make_async_copy(ybuf.at[t], so_h.at[0, t], so_local.at[t]).wait()
        across(ybuf.at[t], so_h.at[0, t], so_send.at[t], so_recv.at[t]).wait_send()

    def load_grad(t, carry):
        def widen(i, inner):
            gf[t, pl.ds(pl.multiple_of(i * SIDE, SIDE), SIDE), :] = ub[t, i].astype(F32)
            return inner
        lax.fori_loop(0, SIDE, widen, 0)
        return carry
    lax.fori_loop(0, 2, load_grad, 0)
    for t in range(2):
        image_copy(t, again_sems.at[t]).start()

    def turn(s, carry):
        t = lax.rem(s, 2)

        def tick(place):
            for n in range(6):
                steps = plan.get((n, place), [])
                if steps:
                    @pl.when(s == n)
                    def _():
                        for step in steps:
                            step()

        @pl.when(lax.rem(s, 2) == 0)
        def _():
            @pl.when(s > 0)
            def _():
                close_mix(2 - lax.div(s, 2))

            @pl.when(s < 4)
            def _():
                mixers(1 - lax.div(s, 2), True)
                clear_mix()

        @pl.when(s > 1)
        def _():
            @pl.when(s > 3)
            def _():
                image_copy(t, again_sems.at[t]).wait()
                widen_image(t)
            tick(7)
            input_stage(t, 2 - lax.div(s, 2), tick)
            tick(9)

        @pl.when(s < 4)
        def _():
            @pl.when(s > 1)
            def _():
                for copy in fetch(t):
                    copy.wait()
            tick(0)
            backward_stage(t, 1 - lax.div(s, 2), tick)
            tick(6)

            @pl.when(s < 2)
            def _():
                for copy in fetch(t):
                    copy.start()
        return carry
    lax.fori_loop(0, 6, turn, 0)

    taps_left = list(taps_sum)
    taps_left.pop(0)()
    while tail or taps_left:
        if tail:
            tail.pop(0)()
        if taps_left:
            taps_left.pop(0)()

    gs_out = pltpu.make_async_copy(gs.at[me_p], gs_h, gs_sem.at[0])
    gs_out.start()
    for t in range(2):
        pltpu.make_async_copy(igbuf.at[t], ig_h.at[0, t], ig_local.at[t]).wait()
        across(ybuf.at[t], so_h.at[0, t], so_send.at[t], so_recv.at[t]).wait_recv()
        across(igbuf.at[t], ig_h.at[0, t], ig_send.at[t], ig_recv.at[t]).wait()
    for lb, out_h, n in ((lb_a, ga_h, 0), (lb_b, gb_h, 1)):
        pltpu.make_async_copy(lb.at[0], out_h.at[0], out_local.at[n]).wait()
        across(lb.at[0], out_h.at[0], out_send.at[n], out_recv.at[n]).wait()
    gs_out.wait()


def finish_kernel(
    so_in, ig_in, ga, gb, gs,
    so, ig, conv, bgain, bbias, ww, wb, hw, hb, gm, mbias, ngain, nbias, gu, ubias, gd, dbias, sems,
):
    copies = [pltpu.make_async_copy(so_in, so, sems.at[0]), pltpu.make_async_copy(ig_in, ig, sems.at[1])]
    for copy in copies:
        copy.start()
    for p in range(2):
        for q in range(SHARDS):
            start = p * HALF + (q % 2) * SHARD
            rows = slice(start, start + SHARD)
            out, at = (gd, gu)[q // 4], WIDE * (q // 2 % 2)
            out[rows, at : at + WIDE] = ga[p, q].astype(F32)
            at = FT * (q // 2)
            width = min(FT, 3 * C - at)
            gm[rows, at : at + width] = gb[p, q, :, 0:width].astype(F32)
    for n in range(9):
        conv[n] = gs[CONV + n : CONV + n + 1, :]
    for row, ref in ((BGAIN, bgain), (BBIAS, bbias), (MBIAS, mbias), (NGAIN, ngain), (NBIAS, nbias), (DBIAS, dbias)):
        ref[...] = gs[row : row + 1, :]
    for row, ref in ((WBIAS, wb), (HBIAS, hb)):
        ref[...] = gs[row : row + 1, 0:SIDE]
    for n in range(FF // FT):
        ubias[:, n * FT : n * FT + FT] = gs[UBIAS + n : UBIAS + n + 1, 0:FT]
    for row, ref in ((WW, ww), (HW, hw)):
        ref[0] = gs[row : row + SIDE, 0:SIDE]
    for copy in copies:
        copy.wait()


def on_device(
    images, masks, conv_weight, batch_gain, batch_bias, width_weight, width_bias,
    height_weight, height_bias, merge_weight, merge_bias, norm_gain, norm_bias,
    up_weight, up_bias, down_weight, down_bias, out_grad,
):
    n_dp = lax.axis_size("dp")
    micro = images.shape[0]
    steps = max(n_dp.bit_length() - 1, 4)
    any_space = pl.BlockSpec(memory_space=pl.ANY)
    vmem = pl.BlockSpec(memory_space=pltpu.VMEM)
    dma = pltpu.SemaphoreType.DMA
    grid = (SIDE, SIDE, C)
    shape = jax.ShapeDtypeStruct
    outs = pl.pallas_call(
        functools.partial(kernel, n_dp),
        out_shape=(
            shape((1, micro) + grid, BF16),
            shape((1, micro) + grid, BF16),
            shape((2, SHARDS, SHARD, WIDE), BF16),
            shape((2, SHARDS, SHARD, FT), BF16),
            shape((PACK, C), F32),
            shape((2, ROWS, FF), BF16),
            shape((2, ROWS, FF), BF16),
            shape((2, ROWS, 3 * C), BF16),
            shape((2, ROWS, C), BF16),
            shape((2, ROWS, C), BF16),
        ),
        in_specs=[any_space] + [vmem] * 8 + [any_space] + [vmem] * 3 + [any_space, vmem, any_space, vmem, any_space],
        out_specs=(any_space,) * 10,
        scratch_shapes=[
            pltpu.VMEM((2, ROWS, 1), F32),
            pltpu.VMEM((2, PACK, C), F32),
            pltpu.VMEM((2, C, 3 * C), BF16),
            pltpu.VMEM((2, C, C), BF16),
            pltpu.VMEM((2, C, FF), BF16),
            pltpu.VMEM((2, C, FF), BF16),
            pltpu.VMEM((2,) + grid, BF16),
            pltpu.VMEM((2, ROWS + 2 * SIDE, C), F32),
            pltpu.VMEM((4, ROWS, C), F32),
            pltpu.VMEM((2, ROWS, 3 * C), BF16),
            pltpu.VMEM((2, ROWS, C), BF16),
            pltpu.VMEM((2, ROWS, C), BF16),
            pltpu.VMEM((4, ROWS, 1), F32),
            pltpu.VMEM((2, ROWS, FF), BF16),
            pltpu.VMEM((2, ROWS, FF), BF16),
            pltpu.VMEM((2, ROWS, C), F32),
            pltpu.VMEM((ROWS, C), BF16),
            pltpu.VMEM((C, ROWS), BF16),
            pltpu.VMEM((ROWS, FF), BF16),
            pltpu.VMEM((2, ROWS, C), F32),
            pltpu.VMEM((2, ROWS, C), BF16),
            pltpu.VMEM((3, ROWS + 2 * SIDE, C), F32),
            pltpu.VMEM((GROUP, GROUP), BF16),
            pltpu.VMEM((ROWS, ROWS), BF16),
            pltpu.VMEM((ROWS, 1), F32),
            pltpu.VMEM((ROWS, 1), F32),
            pltpu.VMEM((GROUP, GROUP), F32),
            pltpu.VMEM((ROWS, ROWS), F32),
            pltpu.VMEM((ROWS, 1), F32),
            pltpu.VMEM((ROWS, 1), F32),
            pltpu.VMEM((4,) + grid, BF16),
            pltpu.VMEM((8, 2, CP), F32),
            pltpu.VMEM((8, n_dp - 1, 2, CP), F32),
            pltpu.VMEM((2, 4, C, WIDE), F32),
            pltpu.VMEM((2, 4, C, FT), F32),
            pltpu.VMEM((2, PACK, C), F32),
            pltpu.VMEM((2, 4 + steps, SHARD, WIDE), BF16),
            pltpu.VMEM((2, SHARDS, SHARD, WIDE), BF16),
            pltpu.VMEM((2, 4 + steps, SHARD, WIDE), BF16),
            pltpu.VMEM((2, 4 + steps, SHARD, FT), BF16),
            pltpu.VMEM((2, SHARDS, SHARD, FT), BF16),
            pltpu.VMEM((2, 4 + steps, SHARD, FT), BF16),
            pltpu.VMEM((1 + steps, PACK - SMALL, C), F32),
            pltpu.VMEM((1 + steps, SMALL, C), F32),
            dma((9,)), dma((2,)), dma((2,)), dma((3,)), dma((3,)), dma((8,)), dma((8,)),
            dma((2,)), dma((2,)), dma((2,)), dma((2,)), dma((2,)), dma((2,)), dma((2, 5)), dma((2, 5)),
            dma((4, 4 + steps)), dma((4, 4 + steps)), dma((1 + steps,)), dma((1 + steps,)),
            dma((1 + steps,)), dma((1 + steps,)), dma((2,)), dma((2,)), dma((2,)), dma((1,)),
        ],
        compiler_params=pltpu.CompilerParams(
            collective_id=0, has_side_effects=True, vmem_limit_bytes=65400 * 1024),
    )(
        images, masks, conv_weight, batch_gain, batch_bias, width_weight, width_bias, height_weight, height_bias,
        merge_weight[0].T, merge_bias, norm_gain, norm_bias, up_weight[0], up_bias, down_weight[0].T, down_bias, out_grad)

    row = shape((1, C), F32)
    square, line = shape((1, SIDE, SIDE), F32), shape((1, SIDE), F32)
    so, ig, conv, bgain, bbias, ww, wb, hw, hb, gm, mbias, ngain, nbias, gu, ubias, gd, dbias = pl.pallas_call(
        finish_kernel,
        out_shape=(
            shape((1, micro) + grid, BF16), shape((1, micro) + grid, BF16), shape((9, 1, C), F32), row, row,
            square, line, square, line, shape((C, 3 * C), F32), row, row, row,
            shape((C, FF), F32), shape((1, FF), F32), shape((C, FF), F32), row),
        in_specs=[any_space] * 2 + [vmem] * 3,
        out_specs=(any_space,) * 2 + (vmem,) * 15,
        scratch_shapes=[dma((2,))],
        compiler_params=pltpu.CompilerParams(vmem_limit_bytes=32 * 1024 * 1024),
    )(*outs[:5])
    return (
        so, ig, jnp.swapaxes(conv, 0, 1), bgain, bbias, ww, wb, hw, hb, gm.T[None], mbias, ngain, nbias,
        gu[None], ubias, gd.T[None], dbias)


def solution(mesh):
    data4 = P("dp", None, None, None)
    p1, p2, p3 = P("pipe"), P("pipe", None), P("pipe", None, None)
    out5 = P("pipe", "dp", None, None, None)
    return jax.shard_map(
        on_device,
        mesh=mesh,
        in_specs=(data4, P("dp", None, None), p3, p2, p2, p3, p2, p3, p2, p3, p2, p2, p2, p3, p2, p3, p2, data4),
        out_specs=(out5, out5, p3, p2, p2, p3, p2, p3, p2, p3, p2, p2, p2, p3, p2, p3, p2),
        check_vma=False,
    )
```

```python
import functools

import jax
import jax.numpy as jnp
from jax import lax
from jax.experimental import pallas as pl
from jax.experimental.pallas import tpu as pltpu
from jax.sharding import PartitionSpec as P

EPS = 1e-05
MESH = pl.DeviceIdType.MESH
F32 = jnp.float32
BF16 = jnp.bfloat16

SIDE = 24
ROWS = SIDE * SIDE
C = 320
CP = 384
FF = 1280
FT = 256
CHUNK = 48
GROUP = 8 * SIDE

HALF = C // 2
SHARD = HALF // 2
WIDE = FF // 2
SHARDS = 8

CONV, BGAIN, BBIAS, MBIAS, NGAIN, NBIAS, DBIAS, WBIAS, HBIAS, UBIAS, WW, HW, PACK = (
    0, 16, 17, 18, 19, 20, 21, 22, 23, 24, 32, 56, 80)
SMALL = 16


def dot(a, b, contract=(1, 0), precision=None):
    return lax.dot_general(
        a, b, (((contract[0],), (contract[1],)), ((), ())),
        preferred_element_type=F32, precision=precision)


def fold(value):
    rows = value.shape[0]
    return jnp.sum(value.reshape(rows // 8, 8, value.shape[1]), 0)


def total(partial):
    return jnp.sum(partial, 0, keepdims=True)


def grid_row(index):
    return (index * 2731) >> 16


def one_hots(rows):
    place = lax.broadcasted_iota(jnp.int32, (rows, SIDE), 0)
    lane = lax.broadcasted_iota(jnp.int32, (rows, SIDE), 1)
    i = grid_row(place)
    return i == lane, place - SIDE * i == lane


def gelu_both(x):
    e = jnp.exp2(x * x * -0.7213475204444817)
    d = 1.0 + 0.23164189 * jnp.abs(x)
    t = pl.reciprocal(d, approx=True)
    t = t * (2.0 - d * t)
    poly = t * (0.127414796 + t * (-0.142248368 + t * (0.7107068705 + t * (-0.7265760135 + t * 0.5307027145))))
    tail = poly * e
    phi = jnp.where(x >= 0, 1.0 - tail, tail)
    return x * phi, phi + x * e * 0.3989422804014327


def kernel(
    n_dp,
    images, masks, conv_w, bgain, bbias, wwt, wb, hwt, hb, wm_h, mbias, ngain, nbias, wu_h, ubias, wd_h, dbias, og_h,
    so_h, ig_h, ga_h, gb_h, gs_h, sp_hidden, sp_gp, sp_joined, sp_normal, sp_xl,
    mask_cols, pack, wm, wmid, wu, wd, ub, uf, cv, joined, normal, xl, rstd, hidden, gp,
    gf, gb, gmb, gbt, gpre, gmix, gwh, gsh, kw, kh, wbcol, hbcol,
    gw_acc, gh_acc, wcol, hcol, ybuf, msg, land, acc_a, acc_b, gs,
    sb_a, lb_a, rl_a, sb_b, lb_b, rl_b, small_land, conv_land,
    local_sems, again_sems, pack_sems, w_send, w_recv, st_send, st_recv,
    so_local, so_send, so_recv, ig_local, ig_send, ig_recv, spill_sems, fetch_sems,
    red_send, red_recv, small_send, small_recv, conv_send, conv_recv, out_local, out_send, out_recv, gs_sem,
):
    me_p = lax.axis_index("pipe")
    me_d = lax.axis_index("dp")
    other = 1 - me_p
    first = gsh.at[2, pl.ds(SIDE, ROWS)]
    igbuf = ybuf
    gnorm = gsh.at[0, pl.ds(SIDE, ROWS)]

    def image_copy(t, sems):
        return pltpu.make_async_copy(images.at[2 * me_p + t], ub.at[t], sems)

    image_in = [image_copy(t, local_sems.at[5 + t]) for t in range(2)]
    grad_in = [pltpu.make_async_copy(og_h.at[2 * me_p + t], ub.at[t], local_sems.at[7 + t]) for t in range(2)]
    weights = ((wm_h, wm), (wu_h, wu), (wd_h, wd))
    weights_in = [pltpu.make_async_copy(src, dst.at[me_p], local_sems.at[n]) for n, (src, dst) in enumerate(weights)]
    for copy in image_in + weights_in:
        copy.start()

    barrier = pltpu.get_barrier_semaphore()

    def greet(step, carry):
        pl.semaphore_signal(barrier, inc=1, device_id={"dp": lax.rem(me_d + step, n_dp)}, device_id_type=MESH)
        return carry

    lax.fori_loop(1, n_dp, greet, 0)
    pl.semaphore_signal(barrier, inc=1, device_id={"pipe": other}, device_id_type=MESH)

    pack[me_p] = jnp.zeros(pack.shape[1:], F32)
    pack[me_p, CONV : CONV + 9, :] = conv_w[0].astype(F32)
    for row, ref in ((BGAIN, bgain), (BBIAS, bbias), (MBIAS, mbias), (NGAIN, ngain), (NBIAS, nbias), (DBIAS, dbias)):
        pack[me_p, row : row + 1, :] = ref[...]
    for row, ref in ((WBIAS, wb), (HBIAS, hb)):
        pack[me_p, row : row + 1, 0:SIDE] = ref[...]
    for n in range(FF // FT):
        pack[me_p, UBIAS + n : UBIAS + n + 1, 0:FT] = ubias[:, n * FT : n * FT + FT]
    for row, ref in ((WW, wwt), (HW, hwt)):
        pack[me_p, row : row + SIDE, 0:SIDE] = ref[0].astype(F32)

    pl.semaphore_wait(barrier, n_dp)

    def across(src, dst, send, recv):
        return pltpu.make_async_remote_copy(
            src_ref=src, dst_ref=dst, send_sem=send, recv_sem=recv,
            device_id={"pipe": other}, device_id_type=MESH)

    pack_over = across(pack.at[me_p], pack.at[me_p], pack_sems.at[0], pack_sems.at[1])
    weights_over = [across(src, dst.at[me_p], w_send.at[n], w_recv.at[n]) for n, (src, dst) in enumerate(weights)]
    pack_over.start()
    for copy in weights_over:
        copy.start()

    msg[...] = jnp.zeros(msg.shape, F32)
    for k in range(2):
        for n in range(4):
            acc_a[k, n] = jnp.zeros(acc_a.shape[2:], F32)
            acc_b[k, n] = jnp.zeros(acc_b.shape[2:], F32)
        gs[k] = jnp.zeros(gs.shape[1:], F32)
    for n in range(2):
        uf[n, 0:SIDE, :] = jnp.zeros((SIDE, C), F32)
        uf[n, SIDE + ROWS : 2 * SIDE + ROWS, :] = jnp.zeros((SIDE, C), F32)
    for n in range(3):
        gsh[n, 0:SIDE, :] = jnp.zeros((SIDE, C), F32)
        gsh[n, SIDE + ROWS : 2 * SIDE + ROWS, :] = jnp.zeros((SIDE, C), F32)

    i_r, j_r = one_hots(ROWS)
    i_b = jnp.where(i_r, 1.0, 0.0).astype(BF16)
    for t in range(2):
        chosen = dot(i_b, masks[2 * me_p + t].astype(F32).astype(BF16))
        mask_cols[t] = jnp.sum(jnp.where(j_r, chosen, 0.0), 1, keepdims=True)

    column = lax.broadcasted_iota(jnp.int32, (CHUNK, C), 0)
    column = column - SIDE * grid_row(column)
    not_first = column != 0
    not_last = column != SIDE - 1

    def later(value):
        return jnp.where(not_first, pltpu.roll(value, 1, 0), 0.0)

    def sooner(value):
        return jnp.where(not_last, pltpu.roll(value, CHUNK - 1, 0), 0.0)

    def mask_chunk(t, start):
        return mask_cols[t, pl.ds(start, CHUNK), :]

    def chunks(body, init):
        def step(c, carry):
            return body(pl.multiple_of(c * CHUNK, CHUNK), carry)
        return lax.fori_loop(0, ROWS // CHUNK, step, init)

    def groups(body, init):
        def step(g, carry):
            return body(pl.multiple_of(g * GROUP, GROUP), carry)
        return lax.fori_loop(0, ROWS // GROUP, step, init)

    def send_stats(r):
        def one(step, carry):
            pltpu.make_async_remote_copy(
                src_ref=msg.at[r], dst_ref=land.at[r, n_dp - 1 - step],
                send_sem=st_send.at[r], recv_sem=st_recv.at[r],
                device_id={"dp": lax.rem(me_d + step, n_dp)}, device_id_type=MESH).start()
            return carry
        lax.fori_loop(1, n_dp, one, 0)

    def wait_stats(r):
        whole = pltpu.make_async_remote_copy(
            src_ref=land.at[r], dst_ref=land.at[r], send_sem=st_send.at[r], recv_sem=st_recv.at[r],
            device_id={"dp": lax.rem(me_d + 1, n_dp)}, device_id_type=MESH)
        whole.wait_send()
        whole.wait_recv()

    def conv_stage(t, k):
        z = 2 * k + t
        taps = [pack[k, CONV + n : CONV + n + 1, :] for n in range(9)]

        def conv(start, acc):
            rows = [uf[t, pl.ds(start + SIDE * r, CHUNK), :] for r in range(3)]
            part = [rows[0] * taps[s] + rows[1] * taps[3 + s] + rows[2] * taps[6 + s] for s in range(3)]
            out = part[1] + later(part[0]) + sooner(part[2])
            cv[z, pl.ds(start, CHUNK), :] = out
            m = mask_chunk(t, start)
            return acc[0] + fold(out * m), acc[1] + fold(m)

        acc, n_acc = chunks(conv, (jnp.zeros((8, C), F32), jnp.zeros((8, 1), F32)))
        sums, n_own = total(acc), total(n_acc)
        mean = sums / n_own

        def centred(start, acc):
            d = cv[z, pl.ds(start, CHUNK), :] - mean
            return acc + fold(d * d * mask_chunk(t, start))

        m2 = total(chunks(centred, jnp.zeros((8, C), F32)))
        msg[z, 0:1, 0:C] = sums
        msg[z, 0:1, C:CP] = jnp.broadcast_to(n_own, (1, CP - C))
        msg[z, 1:2, 0:C] = m2
        send_stats(z)

    def gather_stats(r):
        def add(d, carry):
            return carry + land[r, d]
        return lax.fori_loop(0, n_dp - 1, add, msg[r])

    def norm_stats(z):
        sums = gather_stats(z)[0:1, :]
        count = sums[:, CP - 1 : CP]
        mean = sums[:, 0:C] / count

        def spread(values):
            n = values[0:1, CP - 1 : CP]
            off = values[0:1, 0:C] / n - mean
            return values[1:2, 0:C] + n * off * off

        def add(d, carry):
            return carry + spread(land[z, d])
        m2 = lax.fori_loop(0, n_dp - 1, add, spread(msg[z]))
        return mean, lax.rsqrt(m2 / count + EPS), count

    def mixers(k, backward):
        _, j_g = one_hots(GROUP)
        i_r, j_r = one_hots(ROWS)
        ww = pack[k, WW : WW + SIDE, 0:SIDE].astype(BF16)
        hw = pack[k, HW : HW + SIDE, 0:SIDE].astype(BF16)
        side_of = 0 if backward else 1
        j_b = jnp.where(j_g, 1.0, 0.0).astype(BF16)
        i_b = jnp.where(i_r, 1.0, 0.0).astype(BF16)
        left = dot(j_b, ww, (1, 1 - side_of)).astype(BF16)
        p = grid_row(lax.broadcasted_iota(jnp.int32, (GROUP, GROUP), 0))
        q = grid_row(lax.broadcasted_iota(jnp.int32, (GROUP, GROUP), 1))
        kw[...] = jnp.where(p == q, dot(left, j_b, (1, 1)), 0.0).astype(BF16)
        left = dot(i_b, hw, (1, 1 - side_of)).astype(BF16)
        for piece in range(3):
            rows = slice(piece * GROUP, piece * GROUP + GROUP)
            p = lax.broadcasted_iota(jnp.int32, (GROUP, ROWS), 0) + piece * GROUP
            q = lax.broadcasted_iota(jnp.int32, (GROUP, ROWS), 1)
            same = p - SIDE * grid_row(p) == q - SIDE * grid_row(q)
            kh[rows, :] = jnp.where(same, dot(left[rows, :], i_b, (1, 1)), 0.0).astype(BF16)
        if not backward:
            wb = pack[k, WBIAS : WBIAS + 1, 0:SIDE]
            hb = pack[k, HBIAS : HBIAS + 1, 0:SIDE]
            wbcol[...] = jnp.sum(jnp.where(j_r, wb, 0.0), 1, keepdims=True)
            hbcol[...] = jnp.sum(jnp.where(i_r, hb, 0.0), 1, keepdims=True)

    stored = ((hidden, sp_hidden), (gp, sp_gp), (joined, sp_joined), (normal, sp_normal), (xl, sp_xl))

    def spill(t):
        return [pltpu.make_async_copy(v.at[t], h.at[t], spill_sems.at[t, n]) for n, (v, h) in enumerate(stored)]

    def fetch(t):
        return [pltpu.make_async_copy(h.at[t], v.at[t], fetch_sems.at[t, n]) for n, (v, h) in enumerate(stored)]

    def forward_stage(t, k):
        z = 2 * k + t

        @pl.when(k == 1)
        def _():
            for copy in spill(t):
                copy.wait()

        wait_stats(z)
        mean, scale, _ = norm_stats(z)
        gain = pack[k, BGAIN : BGAIN + 1, :]
        bias = pack[k, BBIAS : BBIAS + 1, :]

        def standardize(start, carry):
            rows = pl.ds(start, GROUP)
            x = (cv[z, rows, :] - mean) * scale
            cv[z, rows, :] = x
            mixed = ((x * gain + bias) * mask_cols[t, rows, :]).astype(BF16)
            joined[t, rows, 2 * C : 3 * C] = mixed
            joined[t, rows, 0:C] = (dot(kw[...], mixed) + wbcol[rows, :]).astype(BF16)
            return carry
        groups(standardize, 0)

        m_bias = pack[k, MBIAS : MBIAS + 1, :]
        n_gain = pack[k, NGAIN : NGAIN + 1, :]
        n_bias = pack[k, NBIAS : NBIAS + 1, :]
        d_bias = pack[k, DBIAS : DBIAS + 1, :]
        u_bias = [pack[k, UBIAS + n : UBIAS + n + 1, 0:FT] for n in range(FF // FT)]

        def rest(start, carry):
            rows = pl.ds(start, GROUP)
            along = dot(kh[rows, :], joined[t, :, 2 * C : 3 * C]) + hbcol[rows, :]
            joined[t, rows, C : 2 * C] = along.astype(BF16)
            f = uf[t, pl.ds(start + SIDE, GROUP), :] + dot(joined[t, rows, :], wm[k], (1, 1)) + m_bias
            d = f - jnp.mean(f, 1, keepdims=True)
            rs = lax.rsqrt(jnp.mean(d * d, 1, keepdims=True) + EPS)
            x = d * rs
            first[rows, :] = f
            rstd[z, rows, :] = rs
            xl[t, rows, :] = x.astype(BF16)
            norm = (x * n_gain + n_bias).astype(BF16)
            normal[t, rows, :] = norm
            pre = dot(norm, wu[k, :, 0:FT])
            for n in range(FF // FT):
                cols = slice(n * FT, n * FT + FT)
                now = pre + u_bias[n]
                if n + 1 < FF // FT:
                    pre = dot(norm, wu[k, :, n * FT + FT : n * FT + 2 * FT])
                h, dh = gelu_both(now)
                hidden[t, rows, cols] = h.astype(BF16)
                gp[t, rows, cols] = dh.astype(BF16)
            y = first[rows, :] + dot(hidden[t, rows, :], wd[k], (1, 1)) + d_bias
            y = y.reshape(GROUP // SIDE, SIDE, C).astype(BF16)
            i = pl.ds(lax.div(start, SIDE), GROUP // SIDE)
            ybuf[z, i] = y

            @pl.when(k == 0)
            def _():
                uf[t, pl.ds(start + SIDE, GROUP), :] = ybuf[z, i].astype(F32).reshape(GROUP, C)
            return carry
        groups(rest, 0)

        @pl.when(me_p == k)
        def _():
            pltpu.make_async_copy(ybuf.at[z], so_h.at[0, 2 * me_p + t], so_local.at[t]).start()

        @pl.when(me_p != k)
        def _():
            across(ybuf.at[z], so_h.at[0, 2 * me_p + t], so_send.at[t], so_recv.at[t]).start()

    def backward_stage(t, k, tick):
        z = 2 * k + t
        zero = jnp.zeros((8, C), F32)
        n_gain = pack[k, NGAIN : NGAIN + 1, :]

        def chain(start, acc):
            rows = pl.ds(start, GROUP)
            g = gf[t, rows, :]
            low = g.astype(BF16)
            gb[rows, :] = low
            d_acc = acc[0] + fold(g)
            u_acc = []
            raw = dot(low, wd[k, :, 0:FT])
            for n in range(FF // FT):
                cols = slice(n * FT, n * FT + FT)
                now = raw
                if n + 1 < FF // FT:
                    raw = dot(low, wd[k, :, n * FT + FT : n * FT + 2 * FT])
                gpn = (now * gp[t, rows, cols].astype(F32)).astype(BF16)
                gpre[rows, cols] = gpn
                u_acc.append(acc[4][n] + fold(gpn.astype(F32)))
            g = dot(gpre[rows, :], wu[k], (1, 1))
            x = xl[t, rows, :].astype(F32)
            gn = g * n_gain
            mean_g = jnp.mean(gn, 1, keepdims=True)
            mean_gx = jnp.mean(gn * x, 1, keepdims=True)
            out = gf[t, rows, :] + rstd[z, rows, :] * (gn - mean_g - x * mean_gx)
            gf[t, rows, :] = out
            low = out.astype(BF16)
            gmb[rows, :] = low
            g_w = dot(low, wm[k, :, 0:C]).astype(BF16)
            g_h = dot(low, wmid[k]).astype(BF16)
            gwh[rows, :] = g_h
            wcol[rows, :] += jnp.sum(g_w.astype(F32), 1, keepdims=True)
            hcol[rows, :] += jnp.sum(g_h.astype(F32), 1, keepdims=True)
            gmix[t, rows, :] = dot(low, wm[k, :, 2 * C : 3 * C]) + dot(kw[...], g_w)
            gw_acc[...] += dot(g_w, joined[t, rows, 2 * C : 3 * C], (1, 1))
            return (d_acc, acc[1] + fold(g * x), acc[2] + fold(g), acc[3] + fold(low.astype(F32)), u_acc)
        acc = groups(chain, (zero, zero, zero, zero, [jnp.zeros((8, FT), F32) for _ in range(FF // FT)]))
        gs[k, DBIAS : DBIAS + 1, :] += total(acc[0])
        gs[k, NGAIN : NGAIN + 1, :] += total(acc[1])
        gs[k, NBIAS : NBIAS + 1, :] += total(acc[2])
        gs[k, MBIAS : MBIAS + 1, :] += total(acc[3])
        for n in range(FF // FT):
            gs[k, UBIAS + n : UBIAS + n + 1, 0:FT] += total(acc[4][n])
        tick(1)
        gbt[...] = gb[...].T
        for n in range(2):
            acc_a[k, n] += dot(gbt[...], hidden[t, :, n * WIDE : n * WIDE + WIDE])
        tick(2)
        gbt[...] = normal[t].T
        for n in range(2):
            acc_a[k, 2 + n] += dot(gbt[...], gpre[:, n * WIDE : n * WIDE + WIDE])
        tick(3)
        gbt[...] = gmb[...].T
        for n in range(4):
            width = min(FT, 3 * C - n * FT)
            acc_b[k, n, :, 0:width] += dot(gbt[...], joined[t, :, n * FT : n * FT + width])
        tick(4)
        gh_acc[...] += dot(gwh[...], joined[t, :, 2 * C : 3 * C], (1, 1))
        tick(5)

        def batch_sums(start, acc):
            rows = pl.ds(start, GROUP)
            g = (gmix[t, rows, :] + dot(kh[rows, :], gwh[...])) * mask_cols[t, rows, :]
            gmix[t, rows, :] = g
            return acc[0] + fold(g), acc[1] + fold(g * cv[z, rows, :])
        acc = groups(batch_sums, (zero, zero))
        plain, cross = total(acc[0]), total(acc[1])
        gs[k, BBIAS : BBIAS + 1, :] += plain
        gs[k, BGAIN : BGAIN + 1, :] += cross
        r = 4 + z
        msg[r, 0:1, 0:C] = plain
        msg[r, 1:2, 0:C] = cross
        send_stats(r)

    def input_stage(t, k, tick):
        z = 2 * k + t
        r = 4 + z
        wait_stats(r)
        _, scale, count = norm_stats(z)
        both = gather_stats(r)
        plain, cross = both[0:1, 0:C], both[1:2, 0:C]
        gain = pack[k, BGAIN : BGAIN + 1, :]
        out_scale = gain * scale
        plain = plain / count
        cross = cross / count

        def shifted(start, carry):
            rows = pl.ds(start, CHUNK)
            g = (gmix[t, rows, :] - plain - cv[z, rows, :] * cross) * (mask_chunk(t, start) * out_scale)
            rows = pl.ds(start + SIDE, CHUNK)
            gsh[0, rows, :] = sooner(g)
            gsh[1, rows, :] = g
            gsh[2, rows, :] = later(g)
            return carry
        chunks(shifted, 0)
        tick(8)
        taps = [pack[k, CONV + n : CONV + n + 1, :] for n in range(9)]

        def pull(start, acc):
            start = pl.multiple_of(start, SIDE)
            rows = pl.ds(start, SIDE)
            u = [uf[t, pl.ds(start + SIDE * r, SIDE), :] for r in range(3)]
            out = gf[t, rows, :]
            new = []
            for s in range(3):
                here = gsh[s, pl.ds(start + SIDE, SIDE), :]
                for r in range(3):
                    out += gsh[s, pl.ds(start + SIDE * (2 - r), SIDE), :] * taps[3 * r + s]
                new.append([acc[s][r] + fold(here * u[r]) for r in range(3)])
            y = out.astype(BF16)
            igbuf[z, lax.div(start, SIDE)] = y

            @pl.when(k == 1)
            def _():
                gf[t, rows, :] = y.astype(F32)
            return new

        def step(i, acc):
            return pull(i * SIDE, acc)
        acc = lax.fori_loop(0, SIDE, step, [[jnp.zeros((8, C), F32) for _ in range(3)] for _ in range(3)])
        for r in range(3):
            for s in range(3):
                row = CONV + 3 * r + s
                gs[k, row : row + 1, :] += total(acc[s][r])

        @pl.when(me_p == k)
        def _():
            pltpu.make_async_copy(igbuf.at[z], ig_h.at[0, 2 * me_p + t], ig_local.at[t]).start()

        @pl.when(me_p != k)
        def _():
            across(igbuf.at[z], ig_h.at[0, 2 * me_p + t], ig_send.at[t], ig_recv.at[t]).start()

    def clear_mix():
        gw_acc[...] = jnp.zeros(gw_acc.shape, F32)
        gh_acc[...] = jnp.zeros(gh_acc.shape, F32)
        wcol[...] = jnp.zeros(wcol.shape, F32)
        hcol[...] = jnp.zeros(hcol.shape, F32)

    def close_mix(k):
        i_r, j_r = one_hots(ROWS)
        _, j_g = one_hots(GROUP)
        gs[k, WBIAS : WBIAS + 1, 0:SIDE] = total(jnp.where(j_r, wcol[...], 0.0))
        gs[k, HBIAS : HBIAS + 1, 0:SIDE] = total(jnp.where(i_r, hcol[...], 0.0))
        highest = lax.Precision.HIGHEST
        p = grid_row(lax.broadcasted_iota(jnp.int32, (GROUP, GROUP), 0))
        q = grid_row(lax.broadcasted_iota(jnp.int32, (GROUP, GROUP), 1))
        own = jnp.where(p == q, gw_acc[...], 0.0)
        own = jnp.sum(own.reshape(GROUP // SIDE, SIDE, GROUP), 0)
        gs[k, WW : WW + SIDE, 0:SIDE] = dot(own, jnp.where(j_g, 1.0, 0.0), precision=highest)
        i_f = jnp.where(i_r, 1.0, 0.0)
        for i in range(SIDE):
            rows = slice(i * SIDE, i * SIDE + SIDE)
            p = lax.broadcasted_iota(jnp.int32, (SIDE, ROWS), 0)
            q = lax.broadcasted_iota(jnp.int32, (SIDE, ROWS), 1)
            own = jnp.where(p == q - SIDE * grid_row(q), gh_acc[rows, :], 0.0)
            first[i : i + 1, :] = jnp.sum(own, 0, keepdims=True)[:, 0:C]
            gnorm[i : i + 1, 0 : ROWS - C] = jnp.sum(own, 0, keepdims=True)[:, C:ROWS]
        value = dot(first[0:SIDE, :], i_f[0:C, :], precision=highest)
        value += dot(gnorm[0:SIDE, 0 : ROWS - C], i_f[C:ROWS, :], precision=highest)
        gs[k, HW : HW + SIDE, 0:SIDE] = value

    bits = [1, 2, 4]
    while 2 * bits[-1] < n_dp:
        bits.append(2 * bits[-1])

    def partner(bit):
        return me_d + bit * (1 - 2 * lax.rem(me_d // bit, 2))

    def side(bit):
        return lax.rem(me_d // bit, 2)

    halving = [1 + me_p, 2 - me_p, 4]

    def along(bit, src, dst, send, recv):
        return pltpu.make_async_remote_copy(
            src_ref=src, dst_ref=dst, send_sem=send, recv_sem=recv,
            device_id={"dp": partner(bit)}, device_id_type=MESH)

    n_steps = 4 + len(bits) - 3 + 3

    def reduction(phase):
        k, which = 1 - phase // 2, phase % 2
        acc, out_h = ((acc_a, ga_h), (acc_b, gb_h))[which]
        slot = phase // 2
        sb, lb, rl = ((sb_a, lb_a, rl_a), (sb_b, lb_b, rl_b))[which]
        sb, lb, rl = sb.at[slot], lb.at[slot], rl.at[slot]

        def sems(step):
            return red_send.at[phase, step], red_recv.at[phase, step]

        def own(q):
            return k, lax.div(q, 2), pl.ds(pl.multiple_of(me_p * HALF + lax.rem(q, 2) * SHARD, 16), SHARD), slice(None)

        def each(count, body):
            def step(n, carry):
                body(n)
                return carry
            lax.fori_loop(0, count, step, 0)

        in_chip = across(sb.at[pl.ds(0, SHARDS)], lb, *sems(0))
        base = [0]
        for n, bit in enumerate(halving):
            base.append(base[n] + side(bit) * (4 >> n))
        mine = base[3]

        def half_copy(n):
            count, at = 4 >> n, 8 - (8 >> n)
            return along(halving[n], sb.at[pl.ds(at, count)], rl.at[pl.ds(at, count)], *sems(1 + n))

        def swap_copy(n):
            return along(bits[3 + n], sb.at[7 + n], rl.at[7 + n], *sems(4 + n))

        def double_copy(n):
            count = 4 >> n
            here = lb.at[pl.ds(base[n + 1], count)]
            return along(halving[n], here, here, *sems(n_steps - 1 - n))

        def send_half(n, landed):
            count, at = 4 >> n, 8 - (8 >> n)
            give = base[n] + (1 - side(halving[n])) * count
            keep = base[n + 1]

            def one(q):
                sb[at + q] = (acc[own(give + q)] + landed(give + q).astype(F32)).astype(BF16)
            each(count, one)
            half_copy(n).start()

            def two(q):
                acc[own(keep + q)] += landed(keep + q).astype(F32)
            each(count, two)

        def start():
            def one(q):
                rows = pl.ds(pl.multiple_of(other * HALF + lax.rem(q, 2) * SHARD, 16), SHARD)
                sb[q] = acc[k, lax.div(q, 2), rows, :].astype(BF16)
            each(SHARDS, one)
            in_chip.start()

        def first_half():
            in_chip.wait()
            send_half(0, lambda q: lb[q])

        def next_half(n):
            def run():
                half_copy(n - 1).wait()
                at = 8 - (8 >> (n - 1))
                send_half(n, lambda q: rl[at + q - base[n]])
            return run

        def swap(n):
            def run():
                if n == 0:
                    half_copy(2).wait()
                    acc[own(mine)] += rl[6].astype(F32)
                else:
                    swap_copy(n - 1).wait()
                    acc[own(mine)] = sb[6 + n].astype(F32) + rl[6 + n].astype(F32)
                sb[7 + n] = acc[own(mine)].astype(BF16)
                swap_copy(n).start()
            return run

        def double(n):
            def run():
                if n == 2:
                    last = len(bits) - 4
                    swap_copy(last).wait()
                    lb[mine] = (sb[7 + last].astype(F32) + rl[7 + last].astype(F32)).astype(BF16)
                else:
                    double_copy(n + 1).wait()
                double_copy(n).start()
            return run

        def hand_over():
            double_copy(0).wait()

            @pl.when(me_p == k)
            def _():
                pltpu.make_async_copy(lb, out_h.at[me_p], out_local.at[which]).start()

            @pl.when(me_p != k)
            def _():
                across(lb, out_h.at[me_p], out_send.at[which], out_recv.at[which]).start()

        return ([start, first_half, next_half(1), next_half(2)] + [swap(n) for n in range(len(bits) - 3)]
                + [double(2), double(1), double(0), hand_over])

    def small_sum(rows, landing, send, recv):
        count = rows.stop - rows.start
        rows = pl.ds(rows.start, count)
        in_chip = across(gs.at[other, rows], landing.at[0], send.at[0], recv.at[0])

        def swap_copy(n):
            return along(bits[n], gs.at[me_p, rows], landing.at[1 + n], send.at[1 + n], recv.at[1 + n])

        def step(n):
            def run():
                (swap_copy(n - 1) if n else in_chip).wait()
                gs[me_p, rows, :] += landing[n]
                if n < len(bits):
                    swap_copy(n).start()
            return run
        return [in_chip.start] + [step(n) for n in range(len(bits) + 1)]

    block2 = [reduction(0), reduction(1)]
    block1 = [reduction(2), reduction(3)]
    small = small_sum(slice(SMALL, PACK), small_land, small_send, small_recv)
    taps_sum = small_sum(slice(0, SMALL), conv_land, conv_send, conv_recv)

    plan = {}

    def put(places, pair):
        left = [list(pair[0]), list(pair[1])]
        plan.setdefault(places[0], []).append(left[0].pop(0))
        plan.setdefault(places[1], []).append(left[1].pop(0))
        turn = 0
        for place in places[2:]:
            if left[turn]:
                plan.setdefault(place, []).append(left[turn].pop(0))
            turn = 1 - turn
        rest = []
        while left[0] or left[1]:
            if left[turn]:
                rest.append(left[turn].pop(0))
            turn = 1 - turn
        return rest

    inner = [7, 8, 9, 0, 1, 2, 3, 4, 5, 6]
    tail = put([(1, 3), (1, 4), (1, 5), (1, 6)] + [(2, p) for p in inner] + [(3, p) for p in inner], block2)
    assert not tail
    tail = put([(3, 3), (3, 4), (3, 5), (3, 6)] + [(4, 7), (4, 8), (4, 9), (5, 7), (5, 8), (5, 9)], block1)
    for place, step in zip([(4, 7), (4, 8), (4, 9), (5, 7), (5, 8), (5, 9)], small):
        plan.setdefault(place, []).append(step)
    tail += small[6:]

    pack_over.wait()
    for t in range(2):
        image_in[t].wait()

    def widen_image(t):
        def widen(i, inner):
            uf[t, pl.ds(pl.multiple_of(i * SIDE + SIDE, SIDE), SIDE), :] = ub[t, i].astype(F32)
            return inner
        lax.fori_loop(0, SIDE, widen, 0)

    def start_image(t, carry):
        widen_image(t)
        conv_stage(t, 0)
        return carry
    lax.fori_loop(0, 2, start_image, 0)
    for t in range(2):
        grad_in[t].start()

    for copy in weights_in + weights_over:
        copy.wait()
    for k in range(2):
        wmid[k] = wm[k, :, C : 2 * C]

    def forward_block(k, carry):
        mixers(k, False)

        def one(t, inner):
            forward_stage(t, k)

            @pl.when(k == 0)
            def _():
                for copy in spill(t):
                    copy.start()
                conv_stage(t, 1)
            return inner
        lax.fori_loop(0, 2, one, 0)
        return carry
    lax.fori_loop(0, 2, forward_block, 0)

    for t in range(2):
        grad_in[t].wait()
        pltpu.make_async_copy(ybuf.at[t], so_h.at[0, t], so_local.at[t]).wait()
        across(ybuf.at[t], so_h.at[0, t], so_send.at[t], so_recv.at[t]).wait_send()

    def load_grad(t, carry):
        def widen(i, inner):
            gf[t, pl.ds(pl.multiple_of(i * SIDE, SIDE), SIDE), :] = ub[t, i].astype(F32)
            return inner
        lax.fori_loop(0, SIDE, widen, 0)
        return carry
    lax.fori_loop(0, 2, load_grad, 0)
    for t in range(2):
        image_copy(t, again_sems.at[t]).start()

    def turn(s, carry):
        t = lax.rem(s, 2)

        def tick(place):
            for n in range(6):
                steps = plan.get((n, place), [])
                if steps:
                    @pl.when(s == n)
                    def _():
                        for step in steps:
                            step()

        @pl.when(lax.rem(s, 2) == 0)
        def _():
            @pl.when(s > 0)
            def _():
                close_mix(2 - lax.div(s, 2))

            @pl.when(s < 4)
            def _():
                mixers(1 - lax.div(s, 2), True)
                clear_mix()

        @pl.when(s > 1)
        def _():
            @pl.when(s > 3)
            def _():
                image_copy(t, again_sems.at[t]).wait()
                widen_image(t)
            tick(7)
            input_stage(t, 2 - lax.div(s, 2), tick)
            tick(9)

        @pl.when(s < 4)
        def _():
            @pl.when(s > 1)
            def _():
                for copy in fetch(t):
                    copy.wait()
            tick(0)
            backward_stage(t, 1 - lax.div(s, 2), tick)
            tick(6)

            @pl.when(s < 2)
            def _():
                for copy in fetch(t):
                    copy.start()
        return carry
    lax.fori_loop(0, 6, turn, 0)

    taps_left = list(taps_sum)
    taps_left.pop(0)()
    while tail or taps_left:
        if tail:
            tail.pop(0)()
        if taps_left:
            taps_left.pop(0)()

    gs_out = pltpu.make_async_copy(gs.at[me_p], gs_h, gs_sem.at[0])
    gs_out.start()
    for t in range(2):
        pltpu.make_async_copy(igbuf.at[t], ig_h.at[0, t], ig_local.at[t]).wait()
        across(ybuf.at[t], so_h.at[0, t], so_send.at[t], so_recv.at[t]).wait_recv()
        across(igbuf.at[t], ig_h.at[0, t], ig_send.at[t], ig_recv.at[t]).wait()
    for lb, out_h, n in ((lb_a, ga_h, 0), (lb_b, gb_h, 1)):
        pltpu.make_async_copy(lb.at[0], out_h.at[0], out_local.at[n]).wait()
        across(lb.at[0], out_h.at[0], out_send.at[n], out_recv.at[n]).wait()
    gs_out.wait()


def finish_kernel(
    so_in, ig_in, ga, gb, gs,
    so, ig, conv, bgain, bbias, ww, wb, hw, hb, gm, mbias, ngain, nbias, gu, ubias, gd, dbias, sems,
):
    copies = [pltpu.make_async_copy(so_in, so, sems.at[0]), pltpu.make_async_copy(ig_in, ig, sems.at[1])]
    for copy in copies:
        copy.start()
    for p in range(2):
        for q in range(SHARDS):
            start = p * HALF + (q % 2) * SHARD
            rows = slice(start, start + SHARD)
            out, at = (gd, gu)[q // 4], WIDE * (q // 2 % 2)
            out[rows, at : at + WIDE] = ga[p, q].astype(F32)
            at = FT * (q // 2)
            width = min(FT, 3 * C - at)
            gm[rows, at : at + width] = gb[p, q, :, 0:width].astype(F32)
    for n in range(9):
        conv[n] = gs[CONV + n : CONV + n + 1, :]
    for row, ref in ((BGAIN, bgain), (BBIAS, bbias), (MBIAS, mbias), (NGAIN, ngain), (NBIAS, nbias), (DBIAS, dbias)):
        ref[...] = gs[row : row + 1, :]
    for row, ref in ((WBIAS, wb), (HBIAS, hb)):
        ref[...] = gs[row : row + 1, 0:SIDE]
    for n in range(FF // FT):
        ubias[:, n * FT : n * FT + FT] = gs[UBIAS + n : UBIAS + n + 1, 0:FT]
    for row, ref in ((WW, ww), (HW, hw)):
        ref[0] = gs[row : row + SIDE, 0:SIDE]
    for copy in copies:
        copy.wait()


def on_device(
    images, masks, conv_weight, batch_gain, batch_bias, width_weight, width_bias,
    height_weight, height_bias, merge_weight, merge_bias, norm_gain, norm_bias,
    up_weight, up_bias, down_weight, down_bias, out_grad,
):
    n_dp = lax.axis_size("dp")
    micro = images.shape[0]
    steps = max(n_dp.bit_length() - 1, 4)
    any_space = pl.BlockSpec(memory_space=pl.ANY)
    vmem = pl.BlockSpec(memory_space=pltpu.VMEM)
    dma = pltpu.SemaphoreType.DMA
    grid = (SIDE, SIDE, C)
    shape = jax.ShapeDtypeStruct
    outs = pl.pallas_call(
        functools.partial(kernel, n_dp),
        out_shape=(
            shape((1, micro) + grid, BF16),
            shape((1, micro) + grid, BF16),
            shape((2, SHARDS, SHARD, WIDE), BF16),
            shape((2, SHARDS, SHARD, FT), BF16),
            shape((PACK, C), F32),
            shape((2, ROWS, FF), BF16),
            shape((2, ROWS, FF), BF16),
            shape((2, ROWS, 3 * C), BF16),
            shape((2, ROWS, C), BF16),
            shape((2, ROWS, C), BF16),
        ),
        in_specs=[any_space] + [vmem] * 8 + [any_space] + [vmem] * 3 + [any_space, vmem, any_space, vmem, any_space],
        out_specs=(any_space,) * 10,
        scratch_shapes=[
            pltpu.VMEM((2, ROWS, 1), F32),
            pltpu.VMEM((2, PACK, C), F32),
            pltpu.VMEM((2, C, 3 * C), BF16),
            pltpu.VMEM((2, C, C), BF16),
            pltpu.VMEM((2, C, FF), BF16),
            pltpu.VMEM((2, C, FF), BF16),
            pltpu.VMEM((2,) + grid, BF16),
            pltpu.VMEM((2, ROWS + 2 * SIDE, C), F32),
            pltpu.VMEM((4, ROWS, C), F32),
            pltpu.VMEM((2, ROWS, 3 * C), BF16),
            pltpu.VMEM((2, ROWS, C), BF16),
            pltpu.VMEM((2, ROWS, C), BF16),
            pltpu.VMEM((4, ROWS, 1), F32),
            pltpu.VMEM((2, ROWS, FF), BF16),
            pltpu.VMEM((2, ROWS, FF), BF16),
            pltpu.VMEM((2, ROWS, C), F32),
            pltpu.VMEM((ROWS, C), BF16),
            pltpu.VMEM((ROWS, C), BF16),
            pltpu.VMEM((C, ROWS), BF16),
            pltpu.VMEM((ROWS, FF), BF16),
            pltpu.VMEM((2, ROWS, C), F32),
            pltpu.VMEM((ROWS, C), BF16),
            pltpu.VMEM((3, ROWS + 2 * SIDE, C), F32),
            pltpu.VMEM((GROUP, GROUP), BF16),
            pltpu.VMEM((ROWS, ROWS), BF16),
            pltpu.VMEM((ROWS, 1), F32),
            pltpu.VMEM((ROWS, 1), F32),
            pltpu.VMEM((GROUP, GROUP), F32),
            pltpu.VMEM((ROWS, ROWS), F32),
            pltpu.VMEM((ROWS, 1), F32),
            pltpu.VMEM((ROWS, 1), F32),
            pltpu.VMEM((4,) + grid, BF16),
            pltpu.VMEM((8, 2, CP), F32),
            pltpu.VMEM((8, n_dp - 1, 2, CP), F32),
            pltpu.VMEM((2, 4, C, WIDE), F32),
            pltpu.VMEM((2, 4, C, FT), F32),
            pltpu.VMEM((2, PACK, C), F32),
            pltpu.VMEM((2, 4 + steps, SHARD, WIDE), BF16),
            pltpu.VMEM((2, SHARDS, SHARD, WIDE), BF16),
            pltpu.VMEM((2, 4 + steps, SHARD, WIDE), BF16),
            pltpu.VMEM((2, 4 + steps, SHARD, FT), BF16),
            pltpu.VMEM((2, SHARDS, SHARD, FT), BF16),
            pltpu.VMEM((2, 4 + steps, SHARD, FT), BF16),
            pltpu.VMEM((1 + steps, PACK - SMALL, C), F32),
            pltpu.VMEM((1 + steps, SMALL, C), F32),
            dma((9,)), dma((2,)), dma((2,)), dma((3,)), dma((3,)), dma((8,)), dma((8,)),
            dma((2,)), dma((2,)), dma((2,)), dma((2,)), dma((2,)), dma((2,)), dma((2, 5)), dma((2, 5)),
            dma((4, 4 + steps)), dma((4, 4 + steps)), dma((1 + steps,)), dma((1 + steps,)),
            dma((1 + steps,)), dma((1 + steps,)), dma((2,)), dma((2,)), dma((2,)), dma((1,)),
        ],
        compiler_params=pltpu.CompilerParams(
            collective_id=0, has_side_effects=True, vmem_limit_bytes=65400 * 1024),
    )(
        images, masks, conv_weight, batch_gain, batch_bias, width_weight, width_bias, height_weight, height_bias,
        merge_weight[0].T, merge_bias, norm_gain, norm_bias, up_weight[0], up_bias, down_weight[0].T, down_bias, out_grad)

    row = shape((1, C), F32)
    square, line = shape((1, SIDE, SIDE), F32), shape((1, SIDE), F32)
    so, ig, conv, bgain, bbias, ww, wb, hw, hb, gm, mbias, ngain, nbias, gu, ubias, gd, dbias = pl.pallas_call(
        finish_kernel,
        out_shape=(
            shape((1, micro) + grid, BF16), shape((1, micro) + grid, BF16), shape((9, 1, C), F32), row, row,
            square, line, square, line, shape((C, 3 * C), F32), row, row, row,
            shape((C, FF), F32), shape((1, FF), F32), shape((C, FF), F32), row),
        in_specs=[any_space] * 2 + [vmem] * 3,
        out_specs=(any_space,) * 2 + (vmem,) * 15,
        scratch_shapes=[dma((2,))],
        compiler_params=pltpu.CompilerParams(vmem_limit_bytes=32 * 1024 * 1024),
    )(*outs[:5])
    return (
        so, ig, jnp.swapaxes(conv, 0, 1), bgain, bbias, ww, wb, hw, hb, gm.T[None], mbias, ngain, nbias,
        gu[None], ubias, gd.T[None], dbias)


def solution(mesh):
    data4 = P("dp", None, None, None)
    p1, p2, p3 = P("pipe"), P("pipe", None), P("pipe", None, None)
    out5 = P("pipe", "dp", None, None, None)
    return jax.shard_map(
        on_device,
        mesh=mesh,
        in_specs=(data4, P("dp", None, None), p3, p2, p2, p3, p2, p3, p2, p3, p2, p2, p2, p3, p2, p3, p2, data4),
        out_specs=(out5, out5, p3, p2, p2, p3, p2, p3, p2, p3, p2, p2, p2, p3, p2, p3, p2),
        check_vma=False,
    )
```

```python
import functools

import jax
import jax.numpy as jnp
from jax import lax
from jax.experimental import pallas as pl
from jax.experimental.pallas import tpu as pltpu
from jax.sharding import PartitionSpec as P

EPS = 1e-05
MESH = pl.DeviceIdType.MESH
F32 = jnp.float32
BF16 = jnp.bfloat16

SIDE = 24
ROWS = SIDE * SIDE
C = 320
CP = 384
FF = 1280
FT = 256
CHUNK = 48
TILE = 32
LANES = ((0, 128), (128, 256), (256, 320))
GROUP = 8 * SIDE

HALF = C // 2
SHARD = HALF // 2
WIDE = FF // 2
SHARDS = 8

CONV, BGAIN, BBIAS, MBIAS, NGAIN, NBIAS, DBIAS, WBIAS, HBIAS, UBIAS, WW, HW, PACK = (
    0, 16, 17, 18, 19, 20, 21, 22, 23, 24, 32, 56, 80)
SMALL = 16


def dot(a, b, contract=(1, 0), precision=None):
    return lax.dot_general(
        a, b, (((contract[0],), (contract[1],)), ((), ())),
        preferred_element_type=F32, precision=precision)


def fold(value):
    rows = value.shape[0]
    return jnp.sum(value.reshape(rows // 8, 8, value.shape[1]), 0)


def total(partial):
    return jnp.sum(partial, 0, keepdims=True)


def grid_row(index):
    return (index * 2731) >> 16


def one_hots(rows):
    place = lax.broadcasted_iota(jnp.int32, (rows, SIDE), 0)
    lane = lax.broadcasted_iota(jnp.int32, (rows, SIDE), 1)
    i = grid_row(place)
    return i == lane, place - SIDE * i == lane


def gelu_both(x):
    e = jnp.exp2(x * x * -0.7213475204444817)
    d = 1.0 + 0.23164189 * jnp.abs(x)
    t = pl.reciprocal(d, approx=True)
    t = t * (2.0 - d * t)
    poly = t * (0.127414796 + t * (-0.142248368 + t * (0.7107068705 + t * (-0.7265760135 + t * 0.5307027145))))
    tail = poly * e
    phi = jnp.where(x >= 0, 1.0 - tail, tail)
    return x * phi, phi + x * e * 0.3989422804014327


def kernel(
    n_dp,
    images, masks, conv_w, bgain, bbias, wwt, wb, hwt, hb, wm_h, mbias, ngain, nbias, wu_h, ubias, wd_h, dbias, og_h,
    so_h, ig_h, ga_h, gb_h, gs_h, sp_hidden, sp_gp, sp_joined, sp_normal, sp_xl,
    mask_cols, pack, wm, wmid, wu, wd, ub, uf, cv, joined, normal, xl, rstd, hidden, gp,
    gf, gb, gmb, gwb, gbt, gpre, gmix, gwh, gsh, kw, kh, wbcol, hbcol,
    gw_acc, gh_acc, wcol, hcol, ybuf, msg, land, acc_a, acc_b, gs,
    sb_a, lb_a, rl_a, sb_b, lb_b, rl_b, small_land, conv_land,
    local_sems, again_sems, pack_sems, w_send, w_recv, st_send, st_recv,
    so_local, so_send, so_recv, ig_local, ig_send, ig_recv, spill_sems, fetch_sems,
    red_send, red_recv, small_send, small_recv, conv_send, conv_recv, out_local, out_send, out_recv, gs_sem,
):
    me_p = lax.axis_index("pipe")
    me_d = lax.axis_index("dp")
    other = 1 - me_p
    first = gsh.at[2, pl.ds(SIDE, ROWS)]
    igbuf = ybuf
    gnorm = gsh.at[0, pl.ds(SIDE, ROWS)]

    def image_copy(t, sems):
        return pltpu.make_async_copy(images.at[2 * me_p + t], ub.at[t], sems)

    image_in = [image_copy(t, local_sems.at[5 + t]) for t in range(2)]
    grad_in = [pltpu.make_async_copy(og_h.at[2 * me_p + t], ub.at[t], local_sems.at[7 + t]) for t in range(2)]
    weights = ((wm_h, wm), (wu_h, wu), (wd_h, wd))
    weights_in = [pltpu.make_async_copy(src, dst.at[me_p], local_sems.at[n]) for n, (src, dst) in enumerate(weights)]
    for copy in image_in + weights_in:
        copy.start()

    barrier = pltpu.get_barrier_semaphore()

    def greet(step, carry):
        pl.semaphore_signal(barrier, inc=1, device_id={"dp": lax.rem(me_d + step, n_dp)}, device_id_type=MESH)
        return carry

    lax.fori_loop(1, n_dp, greet, 0)
    pl.semaphore_signal(barrier, inc=1, device_id={"pipe": other}, device_id_type=MESH)

    pack[me_p] = jnp.zeros(pack.shape[1:], F32)
    pack[me_p, CONV : CONV + 9, :] = conv_w[0].astype(F32)
    for row, ref in ((BGAIN, bgain), (BBIAS, bbias), (MBIAS, mbias), (NGAIN, ngain), (NBIAS, nbias), (DBIAS, dbias)):
        pack[me_p, row : row + 1, :] = ref[...]
    for row, ref in ((WBIAS, wb), (HBIAS, hb)):
        pack[me_p, row : row + 1, 0:SIDE] = ref[...]
    for n in range(FF // FT):
        pack[me_p, UBIAS + n : UBIAS + n + 1, 0:FT] = ubias[:, n * FT : n * FT + FT]
    for row, ref in ((WW, wwt), (HW, hwt)):
        pack[me_p, row : row + SIDE, 0:SIDE] = ref[0].astype(F32)

    pl.semaphore_wait(barrier, n_dp)

    def across(src, dst, send, recv):
        return pltpu.make_async_remote_copy(
            src_ref=src, dst_ref=dst, send_sem=send, recv_sem=recv,
            device_id={"pipe": other}, device_id_type=MESH)

    pack_over = across(pack.at[me_p], pack.at[me_p], pack_sems.at[0], pack_sems.at[1])
    weights_over = [across(src, dst.at[me_p], w_send.at[n], w_recv.at[n]) for n, (src, dst) in enumerate(weights)]
    pack_over.start()
    for copy in weights_over:
        copy.start()

    msg[...] = jnp.zeros(msg.shape, F32)
    for k in range(2):
        for n in range(4):
            acc_a[k, n] = jnp.zeros(acc_a.shape[2:], F32)
            acc_b[k, n] = jnp.zeros(acc_b.shape[2:], F32)
        gs[k] = jnp.zeros(gs.shape[1:], F32)
    for n in range(2):
        uf[n, 0:SIDE, :] = jnp.zeros((SIDE, C), F32)
        uf[n, SIDE + ROWS : 2 * SIDE + ROWS, :] = jnp.zeros((SIDE, C), F32)
    for n in range(3):
        gsh[n, 0:SIDE, :] = jnp.zeros((SIDE, C), F32)
        gsh[n, SIDE + ROWS : 2 * SIDE + ROWS, :] = jnp.zeros((SIDE, C), F32)

    i_r, j_r = one_hots(ROWS)
    i_b = jnp.where(i_r, 1.0, 0.0).astype(BF16)
    for t in range(2):
        chosen = dot(i_b, masks[2 * me_p + t].astype(F32).astype(BF16))
        mask_cols[t] = jnp.sum(jnp.where(j_r, chosen, 0.0), 1, keepdims=True)

    def later(value):
        at = lax.broadcasted_iota(jnp.int32, value.shape, 0)
        return jnp.where(at != 0, pltpu.roll(value, 1, 0), 0.0)

    def sooner(value):
        at = lax.broadcasted_iota(jnp.int32, value.shape, 0)
        return jnp.where(at != SIDE - 1, pltpu.roll(value, SIDE - 1, 0), 0.0)

    def grid_rows(body, init):
        def step(c, carry):
            for half in range(2):
                carry = body(pl.multiple_of(c * CHUNK, CHUNK) + half * SIDE, carry)
            return carry
        return lax.fori_loop(0, SIDE // 2, step, init)

    def groups(body, init):
        def step(g, carry):
            return body(pl.multiple_of(g * GROUP, GROUP), carry)
        return lax.fori_loop(0, ROWS // GROUP, step, init)

    def send_stats(r):
        def one(step, carry):
            pltpu.make_async_remote_copy(
                src_ref=msg.at[r], dst_ref=land.at[r, n_dp - 1 - step],
                send_sem=st_send.at[r], recv_sem=st_recv.at[r],
                device_id={"dp": lax.rem(me_d + step, n_dp)}, device_id_type=MESH).start()
            return carry
        lax.fori_loop(1, n_dp, one, 0)

    def wait_stats(r):
        whole = pltpu.make_async_remote_copy(
            src_ref=land.at[r], dst_ref=land.at[r], send_sem=st_send.at[r], recv_sem=st_recv.at[r],
            device_id={"dp": lax.rem(me_d + 1, n_dp)}, device_id_type=MESH)
        whole.wait_send()
        whole.wait_recv()

    def conv_stage(t, k):
        z = 2 * k + t
        n_own = total(mask_cols[t])
        parts = []
        for l, m in LANES:
            taps = [pack[k, CONV + n : CONV + n + 1, l:m] for n in range(9)]

            def conv(start, acc):
                rows = [uf[t, pl.ds(start + SIDE * r, SIDE), l:m] for r in range(3)]
                part = [rows[0] * taps[s] + rows[1] * taps[3 + s] + rows[2] * taps[6 + s] for s in range(3)]
                out = part[1] + later(part[0]) + sooner(part[2])
                rows = pl.ds(start, SIDE)
                cv[z, rows, l:m] = out
                return acc + fold(out * mask_cols[t, rows, :])
            parts.append(total(grid_rows(conv, jnp.zeros((8, m - l), F32))))
        sums = jnp.concatenate(parts, 1)
        mean = sums / n_own

        def centred(start, acc):
            rows = pl.ds(start, SIDE)
            d = cv[z, rows, :] - mean
            return acc + fold(d * d * mask_cols[t, rows, :])

        m2 = total(grid_rows(centred, jnp.zeros((8, C), F32)))
        msg[z, 0:1, 0:C] = sums
        msg[z, 0:1, C:CP] = jnp.broadcast_to(n_own, (1, CP - C))
        msg[z, 1:2, 0:C] = m2
        send_stats(z)

    def gather_stats(r):
        def add(d, carry):
            return carry + land[r, d]
        return lax.fori_loop(0, n_dp - 1, add, msg[r])

    def norm_stats(z):
        sums = gather_stats(z)[0:1, :]
        count = sums[:, CP - 1 : CP]
        mean = sums[:, 0:C] / count

        def spread(values):
            n = values[0:1, CP - 1 : CP]
            off = values[0:1, 0:C] / n - mean
            return values[1:2, 0:C] + n * off * off

        def add(d, carry):
            return carry + spread(land[z, d])
        m2 = lax.fori_loop(0, n_dp - 1, add, spread(msg[z]))
        return mean, lax.rsqrt(m2 / count + EPS), count

    def mixers(k, backward):
        _, j_g = one_hots(GROUP)
        i_r, j_r = one_hots(ROWS)
        ww = pack[k, WW : WW + SIDE, 0:SIDE].astype(BF16)
        hw = pack[k, HW : HW + SIDE, 0:SIDE].astype(BF16)
        side_of = 0 if backward else 1
        j_b = jnp.where(j_g, 1.0, 0.0).astype(BF16)
        i_b = jnp.where(i_r, 1.0, 0.0).astype(BF16)
        left = dot(j_b, ww, (1, 1 - side_of)).astype(BF16)
        p = grid_row(lax.broadcasted_iota(jnp.int32, (GROUP, GROUP), 0))
        q = grid_row(lax.broadcasted_iota(jnp.int32, (GROUP, GROUP), 1))
        kw[...] = jnp.where(p == q, dot(left, j_b, (1, 1)), 0.0).astype(BF16)
        left = dot(i_b, hw, (1, 1 - side_of)).astype(BF16)
        for piece in range(3):
            rows = slice(piece * GROUP, piece * GROUP + GROUP)
            p = lax.broadcasted_iota(jnp.int32, (GROUP, ROWS), 0) + piece * GROUP
            q = lax.broadcasted_iota(jnp.int32, (GROUP, ROWS), 1)
            same = p - SIDE * grid_row(p) == q - SIDE * grid_row(q)
            kh[rows, :] = jnp.where(same, dot(left[rows, :], i_b, (1, 1)), 0.0).astype(BF16)
        if not backward:
            wb = pack[k, WBIAS : WBIAS + 1, 0:SIDE]
            hb = pack[k, HBIAS : HBIAS + 1, 0:SIDE]
            wbcol[...] = jnp.sum(jnp.where(j_r, wb, 0.0), 1, keepdims=True)
            hbcol[...] = jnp.sum(jnp.where(i_r, hb, 0.0), 1, keepdims=True)

    stored = ((hidden, sp_hidden), (gp, sp_gp), (joined, sp_joined), (normal, sp_normal), (xl, sp_xl))

    def spill(t):
        return [pltpu.make_async_copy(v.at[t], h.at[t], spill_sems.at[t, n]) for n, (v, h) in enumerate(stored)]

    def fetch(t):
        return [pltpu.make_async_copy(h.at[t], v.at[t], fetch_sems.at[t, n]) for n, (v, h) in enumerate(stored)]

    def forward_stage(t, k):
        z = 2 * k + t

        @pl.when(k == 1)
        def _():
            for copy in spill(t):
                copy.wait()

        wait_stats(z)
        mean, scale, _ = norm_stats(z)
        gain = pack[k, BGAIN : BGAIN + 1, :]
        bias = pack[k, BBIAS : BBIAS + 1, :]

        def standardize(start, carry):
            for o in range(0, GROUP, TILE):
                rows = pl.ds(start + o, TILE)
                x = (cv[z, rows, :] - mean) * scale
                cv[z, rows, :] = x
                joined[t, rows, 2 * C : 3 * C] = ((x * gain + bias) * mask_cols[t, rows, :]).astype(BF16)
            along = dot(kw[...], joined[t, pl.ds(start, GROUP), 2 * C : 3 * C])
            for o in range(0, GROUP, TILE):
                rows = pl.ds(start + o, TILE)
                joined[t, rows, 0:C] = (along[o : o + TILE] + wbcol[rows, :]).astype(BF16)
            return carry
        groups(standardize, 0)

        m_bias = pack[k, MBIAS : MBIAS + 1, :]
        n_gain = pack[k, NGAIN : NGAIN + 1, :]
        n_bias = pack[k, NBIAS : NBIAS + 1, :]
        d_bias = pack[k, DBIAS : DBIAS + 1, :]
        u_bias = [pack[k, UBIAS + n : UBIAS + n + 1, 0:FT] for n in range(FF // FT)]

        def rest(start, carry):
            rows = pl.ds(start, GROUP)
            along = dot(kh[rows, :], joined[t, :, 2 * C : 3 * C])
            for o in range(0, GROUP, TILE):
                part = pl.ds(start + o, TILE)
                joined[t, part, C : 2 * C] = (along[o : o + TILE] + hbcol[part, :]).astype(BF16)
            merged = dot(joined[t, rows, :], wm[k], (1, 1))
            for o in range(0, GROUP, TILE):
                part = pl.ds(start + o, TILE)
                f = uf[t, pl.ds(start + SIDE + o, TILE), :] + merged[o : o + TILE] + m_bias
                d = f - jnp.mean(f, 1, keepdims=True)
                rs = lax.rsqrt(jnp.mean(d * d, 1, keepdims=True) + EPS)
                x = d * rs
                first[part, :] = f
                rstd[z, part, :] = rs
                xl[t, part, :] = x.astype(BF16)
                normal[t, part, :] = (x * n_gain + n_bias).astype(BF16)
            norm = normal[t, rows, :]
            pre = dot(norm, wu[k, :, 0:FT])
            for n in range(FF // FT):
                cols = slice(n * FT, n * FT + FT)
                now = pre
                if n + 1 < FF // FT:
                    pre = dot(norm, wu[k, :, n * FT + FT : n * FT + 2 * FT])
                for o in range(0, GROUP, TILE):
                    part = pl.ds(start + o, TILE)
                    h, dh = gelu_both(now[o : o + TILE] + u_bias[n])
                    hidden[t, part, cols] = h.astype(BF16)
                    gp[t, part, cols] = dh.astype(BF16)
            down = dot(hidden[t, rows, :], wd[k], (1, 1))
            i = lax.div(start, SIDE)
            for r in range(GROUP // SIDE):
                y = first[pl.ds(start + r * SIDE, SIDE), :] + down[r * SIDE : r * SIDE + SIDE] + d_bias
                ybuf[z, i + r] = y.astype(BF16)

            @pl.when(k == 0)
            def _():
                for r in range(GROUP // SIDE):
                    uf[t, pl.ds(start + SIDE + r * SIDE, SIDE), :] = ybuf[z, i + r].astype(F32)
            return carry
        groups(rest, 0)

        @pl.when(me_p == k)
        def _():
            pltpu.make_async_copy(ybuf.at[z], so_h.at[0, 2 * me_p + t], so_local.at[t]).start()

        @pl.when(me_p != k)
        def _():
            across(ybuf.at[z], so_h.at[0, 2 * me_p + t], so_send.at[t], so_recv.at[t]).start()

    def backward_stage(t, k, tick):
        z = 2 * k + t
        zero = jnp.zeros((8, C), F32)
        n_gain = pack[k, NGAIN : NGAIN + 1, :]

        def chain(start, acc):
            rows = pl.ds(start, GROUP)
            d_acc, x_acc, n_acc, m_acc, u_acc = acc
            u_acc = list(u_acc)
            for o in range(0, GROUP, TILE):
                part = pl.ds(start + o, TILE)
                g = gf[t, part, :]
                gb[part, :] = g.astype(BF16)
                d_acc = d_acc + fold(g)
            low = gb[rows, :]
            raw = dot(low, wd[k, :, 0:FT])
            for n in range(FF // FT):
                cols = slice(n * FT, n * FT + FT)
                now = raw
                if n + 1 < FF // FT:
                    raw = dot(low, wd[k, :, n * FT + FT : n * FT + 2 * FT])
                for o in range(0, GROUP, TILE):
                    part = pl.ds(start + o, TILE)
                    gpn = (now[o : o + TILE] * gp[t, part, cols].astype(F32)).astype(BF16)
                    gpre[part, cols] = gpn
                    u_acc[n] = u_acc[n] + fold(gpn.astype(F32))
            back = dot(gpre[rows, :], wu[k], (1, 1))
            for o in range(0, GROUP, TILE):
                part = pl.ds(start + o, TILE)
                g = back[o : o + TILE]
                x = xl[t, part, :].astype(F32)
                gn = g * n_gain
                mean_g = jnp.mean(gn, 1, keepdims=True)
                mean_gx = jnp.mean(gn * x, 1, keepdims=True)
                out = gf[t, part, :] + rstd[z, part, :] * (gn - mean_g - x * mean_gx)
                gf[t, part, :] = out
                low = out.astype(BF16)
                gmb[part, :] = low
                x_acc = x_acc + fold(g * x)
                n_acc = n_acc + fold(g)
                m_acc = m_acc + fold(low.astype(F32))
            low = gmb[rows, :]
            g_w = dot(low, wm[k, :, 0:C])
            g_h = dot(low, wmid[k])
            for o in range(0, GROUP, TILE):
                part = pl.ds(start + o, TILE)
                one = g_w[o : o + TILE].astype(BF16)
                gwb[o : o + TILE, :] = one
                wcol[part, :] += jnp.sum(one.astype(F32), 1, keepdims=True)
                one = g_h[o : o + TILE].astype(BF16)
                gwh[part, :] = one
                hcol[part, :] += jnp.sum(one.astype(F32), 1, keepdims=True)
            third = dot(low, wm[k, :, 2 * C : 3 * C])
            crossed = dot(kw[...], gwb[...])
            for o in range(0, GROUP, TILE):
                gmix[t, pl.ds(start + o, TILE), :] = third[o : o + TILE] + crossed[o : o + TILE]
            gw_acc[...] += dot(gwb[...], joined[t, rows, 2 * C : 3 * C], (1, 1))
            return (d_acc, x_acc, n_acc, m_acc, u_acc)
        acc = groups(chain, (zero, zero, zero, zero, [jnp.zeros((8, FT), F32) for _ in range(FF // FT)]))
        gs[k, DBIAS : DBIAS + 1, :] += total(acc[0])
        gs[k, NGAIN : NGAIN + 1, :] += total(acc[1])
        gs[k, NBIAS : NBIAS + 1, :] += total(acc[2])
        gs[k, MBIAS : MBIAS + 1, :] += total(acc[3])
        for n in range(FF // FT):
            gs[k, UBIAS + n : UBIAS + n + 1, 0:FT] += total(acc[4][n])
        tick(1)
        gbt[...] = gb[...].T
        for n in range(2):
            acc_a[k, n] += dot(gbt[...], hidden[t, :, n * WIDE : n * WIDE + WIDE])
        tick(2)
        gbt[...] = normal[t].T
        for n in range(2):
            acc_a[k, 2 + n] += dot(gbt[...], gpre[:, n * WIDE : n * WIDE + WIDE])
        tick(3)
        gbt[...] = gmb[...].T
        for n in range(4):
            width = min(FT, 3 * C - n * FT)
            acc_b[k, n, :, 0:width] += dot(gbt[...], joined[t, :, n * FT : n * FT + width])
        tick(4)
        gh_acc[...] += dot(gwh[...], joined[t, :, 2 * C : 3 * C], (1, 1))
        tick(5)

        def batch_sums(start, acc):
            plain, cross = acc
            crossed = dot(kh[pl.ds(start, GROUP), :], gwh[...])
            for o in range(0, GROUP, TILE):
                rows = pl.ds(start + o, TILE)
                g = (gmix[t, rows, :] + crossed[o : o + TILE]) * mask_cols[t, rows, :]
                gmix[t, rows, :] = g
                plain = plain + fold(g)
                cross = cross + fold(g * cv[z, rows, :])
            return plain, cross
        acc = groups(batch_sums, (zero, zero))
        plain, cross = total(acc[0]), total(acc[1])
        gs[k, BBIAS : BBIAS + 1, :] += plain
        gs[k, BGAIN : BGAIN + 1, :] += cross
        r = 4 + z
        msg[r, 0:1, 0:C] = plain
        msg[r, 1:2, 0:C] = cross
        send_stats(r)

    def input_stage(t, k, tick):
        z = 2 * k + t
        r = 4 + z
        wait_stats(r)
        _, scale, count = norm_stats(z)
        both = gather_stats(r)
        plain, cross = both[0:1, 0:C], both[1:2, 0:C]
        gain = pack[k, BGAIN : BGAIN + 1, :]
        out_scale = gain * scale
        plain = plain / count
        cross = cross / count

        def shifted(start, carry):
            rows = pl.ds(start, SIDE)
            g = (gmix[t, rows, :] - plain - cv[z, rows, :] * cross) * (mask_cols[t, rows, :] * out_scale)
            rows = pl.ds(start + SIDE, SIDE)
            gsh[0, rows, :] = sooner(g)
            gsh[1, rows, :] = g
            gsh[2, rows, :] = later(g)
            return carry
        grid_rows(shifted, 0)
        tick(8)
        for l, m in LANES:
            taps = [pack[k, CONV + n : CONV + n + 1, l:m] for n in range(9)]

            def pull(start, acc):
                u = [uf[t, pl.ds(start + SIDE * r, SIDE), l:m] for r in range(3)]
                out = gf[t, pl.ds(start, SIDE), l:m]
                new = []
                for s in range(3):
                    around = [gsh[s, pl.ds(start + SIDE * r, SIDE), l:m] for r in range(3)]
                    out = out + around[2] * taps[s] + around[1] * taps[3 + s] + around[0] * taps[6 + s]
                    new.append([acc[s][r] + fold(around[1] * u[r]) for r in range(3)])
                igbuf[z, lax.div(start, SIDE), :, l:m] = out.astype(BF16)
                return new
            acc = grid_rows(pull, [[jnp.zeros((8, m - l), F32) for _ in range(3)] for _ in range(3)])
            for r in range(3):
                for s in range(3):
                    row = CONV + 3 * r + s
                    gs[k, row : row + 1, l:m] += total(acc[s][r])

        @pl.when(k == 1)
        def _():
            def reread(start, carry):
                gf[t, pl.ds(start, SIDE), :] = igbuf[z, lax.div(start, SIDE)].astype(F32)
                return carry
            grid_rows(reread, 0)

        @pl.when(me_p == k)
        def _():
            pltpu.make_async_copy(igbuf.at[z], ig_h.at[0, 2 * me_p + t], ig_local.at[t]).start()

        @pl.when(me_p != k)
        def _():
            across(igbuf.at[z], ig_h.at[0, 2 * me_p + t], ig_send.at[t], ig_recv.at[t]).start()

    def clear_mix():
        gw_acc[...] = jnp.zeros(gw_acc.shape, F32)
        gh_acc[...] = jnp.zeros(gh_acc.shape, F32)
        wcol[...] = jnp.zeros(wcol.shape, F32)
        hcol[...] = jnp.zeros(hcol.shape, F32)

    def close_mix(k):
        i_r, j_r = one_hots(ROWS)
        _, j_g = one_hots(GROUP)
        gs[k, WBIAS : WBIAS + 1, 0:SIDE] = total(jnp.where(j_r, wcol[...], 0.0))
        gs[k, HBIAS : HBIAS + 1, 0:SIDE] = total(jnp.where(i_r, hcol[...], 0.0))
        highest = lax.Precision.HIGHEST
        p = grid_row(lax.broadcasted_iota(jnp.int32, (GROUP, GROUP), 0))
        q = grid_row(lax.broadcasted_iota(jnp.int32, (GROUP, GROUP), 1))
        own = jnp.where(p == q, gw_acc[...], 0.0)
        own = jnp.sum(own.reshape(GROUP // SIDE, SIDE, GROUP), 0)
        gs[k, WW : WW + SIDE, 0:SIDE] = dot(own, jnp.where(j_g, 1.0, 0.0), precision=highest)
        i_f = jnp.where(i_r, 1.0, 0.0)
        for i in range(SIDE):
            rows = slice(i * SIDE, i * SIDE + SIDE)
            p = lax.broadcasted_iota(jnp.int32, (SIDE, ROWS), 0)
            q = lax.broadcasted_iota(jnp.int32, (SIDE, ROWS), 1)
            own = jnp.where(p == q - SIDE * grid_row(q), gh_acc[rows, :], 0.0)
            first[i : i + 1, :] = jnp.sum(own, 0, keepdims=True)[:, 0:C]
            gnorm[i : i + 1, 0 : ROWS - C] = jnp.sum(own, 0, keepdims=True)[:, C:ROWS]
        value = dot(first[0:SIDE, :], i_f[0:C, :], precision=highest)
        value += dot(gnorm[0:SIDE, 0 : ROWS - C], i_f[C:ROWS, :], precision=highest)
        gs[k, HW : HW + SIDE, 0:SIDE] = value

    bits = [1, 2, 4]
    while 2 * bits[-1] < n_dp:
        bits.append(2 * bits[-1])

    def partner(bit):
        return me_d + bit * (1 - 2 * lax.rem(me_d // bit, 2))

    def side(bit):
        return lax.rem(me_d // bit, 2)

    halving = [1 + me_p, 2 - me_p, 4]

    def along(bit, src, dst, send, recv):
        return pltpu.make_async_remote_copy(
            src_ref=src, dst_ref=dst, send_sem=send, recv_sem=recv,
            device_id={"dp": partner(bit)}, device_id_type=MESH)

    n_steps = 4 + len(bits) - 3 + 3

    def reduction(phase):
        k, which = 1 - phase // 2, phase % 2
        acc, out_h = ((acc_a, ga_h), (acc_b, gb_h))[which]
        slot = phase // 2
        sb, lb, rl = ((sb_a, lb_a, rl_a), (sb_b, lb_b, rl_b))[which]
        sb, lb, rl = sb.at[slot], lb.at[slot], rl.at[slot]

        def sems(step):
            return red_send.at[phase, step], red_recv.at[phase, step]

        def own(q):
            return k, lax.div(q, 2), pl.ds(pl.multiple_of(me_p * HALF + lax.rem(q, 2) * SHARD, 16), SHARD), slice(None)

        def each(count, body):
            def step(n, carry):
                body(n)
                return carry
            lax.fori_loop(0, count, step, 0)

        in_chip = across(sb.at[pl.ds(0, SHARDS)], lb, *sems(0))
        base = [0]
        for n, bit in enumerate(halving):
            base.append(base[n] + side(bit) * (4 >> n))
        mine = base[3]

        def half_copy(n):
            count, at = 4 >> n, 8 - (8 >> n)
            return along(halving[n], sb.at[pl.ds(at, count)], rl.at[pl.ds(at, count)], *sems(1 + n))

        def swap_copy(n):
            return along(bits[3 + n], sb.at[7 + n], rl.at[7 + n], *sems(4 + n))

        def double_copy(n):
            count = 4 >> n
            here = lb.at[pl.ds(base[n + 1], count)]
            return along(halving[n], here, here, *sems(n_steps - 1 - n))

        def send_half(n, landed):
            count, at = 4 >> n, 8 - (8 >> n)
            give = base[n] + (1 - side(halving[n])) * count
            keep = base[n + 1]

            def one(q):
                sb[at + q] = (acc[own(give + q)] + landed(give + q).astype(F32)).astype(BF16)
            each(count, one)
            half_copy(n).start()

            def two(q):
                acc[own(keep + q)] += landed(keep + q).astype(F32)
            each(count, two)

        def start():
            def one(q):
                rows = pl.ds(pl.multiple_of(other * HALF + lax.rem(q, 2) * SHARD, 16), SHARD)
                sb[q] = acc[k, lax.div(q, 2), rows, :].astype(BF16)
            each(SHARDS, one)
            in_chip.start()

        def first_half():
            in_chip.wait()
            send_half(0, lambda q: lb[q])

        def next_half(n):
            def run():
                half_copy(n - 1).wait()
                at = 8 - (8 >> (n - 1))
                send_half(n, lambda q: rl[at + q - base[n]])
            return run

        def swap(n):
            def run():
                if n == 0:
                    half_copy(2).wait()
                    acc[own(mine)] += rl[6].astype(F32)
                else:
                    swap_copy(n - 1).wait()
                    acc[own(mine)] = sb[6 + n].astype(F32) + rl[6 + n].astype(F32)
                sb[7 + n] = acc[own(mine)].astype(BF16)
                swap_copy(n).start()
            return run

        def double(n):
            def run():
                if n == 2:
                    last = len(bits) - 4
                    swap_copy(last).wait()
                    lb[mine] = (sb[7 + last].astype(F32) + rl[7 + last].astype(F32)).astype(BF16)
                else:
                    double_copy(n + 1).wait()
                double_copy(n).start()
            return run

        def hand_over():
            double_copy(0).wait()

            @pl.when(me_p == k)
            def _():
                pltpu.make_async_copy(lb, out_h.at[me_p], out_local.at[which]).start()

            @pl.when(me_p != k)
            def _():
                across(lb, out_h.at[me_p], out_send.at[which], out_recv.at[which]).start()

        return ([start, first_half, next_half(1), next_half(2)] + [swap(n) for n in range(len(bits) - 3)]
                + [double(2), double(1), double(0), hand_over])

    def small_sum(rows, landing, send, recv):
        count = rows.stop - rows.start
        rows = pl.ds(rows.start, count)
        in_chip = across(gs.at[other, rows], landing.at[0], send.at[0], recv.at[0])

        def swap_copy(n):
            return along(bits[n], gs.at[me_p, rows], landing.at[1 + n], send.at[1 + n], recv.at[1 + n])

        def step(n):
            def run():
                (swap_copy(n - 1) if n else in_chip).wait()
                gs[me_p, rows, :] += landing[n]
                if n < len(bits):
                    swap_copy(n).start()
            return run
        return [in_chip.start] + [step(n) for n in range(len(bits) + 1)]

    block2 = [reduction(0), reduction(1)]
    block1 = [reduction(2), reduction(3)]
    small = small_sum(slice(SMALL, PACK), small_land, small_send, small_recv)
    taps_sum = small_sum(slice(0, SMALL), conv_land, conv_send, conv_recv)

    plan = {}

    def put(places, pair):
        left = [list(pair[0]), list(pair[1])]
        plan.setdefault(places[0], []).append(left[0].pop(0))
        plan.setdefault(places[1], []).append(left[1].pop(0))
        turn = 0
        for place in places[2:]:
            if left[turn]:
                plan.setdefault(place, []).append(left[turn].pop(0))
            turn = 1 - turn
        rest = []
        while left[0] or left[1]:
            if left[turn]:
                rest.append(left[turn].pop(0))
            turn = 1 - turn
        return rest

    inner = [7, 8, 9, 0, 1, 2, 3, 4, 5, 6]
    tail = put([(1, 3), (1, 4), (1, 5), (1, 6)] + [(2, p) for p in inner] + [(3, p) for p in inner], block2)
    assert not tail
    tail = put([(3, 3), (3, 4), (3, 5), (3, 6)] + [(4, 7), (4, 8), (4, 9), (5, 7), (5, 8), (5, 9)], block1)
    for place, step in zip([(4, 7), (4, 8), (4, 9), (5, 7), (5, 8), (5, 9)], small):
        plan.setdefault(place, []).append(step)
    tail += small[6:]

    pack_over.wait()
    for t in range(2):
        image_in[t].wait()

    def widen_image(t):
        def widen(i, inner):
            uf[t, pl.ds(pl.multiple_of(i * SIDE + SIDE, SIDE), SIDE), :] = ub[t, i].astype(F32)
            return inner
        lax.fori_loop(0, SIDE, widen, 0)

    def start_image(t, carry):
        widen_image(t)
        conv_stage(t, 0)
        return carry
    lax.fori_loop(0, 2, start_image, 0)
    for t in range(2):
        grad_in[t].start()

    for copy in weights_in + weights_over:
        copy.wait()
    for k in range(2):
        wmid[k] = wm[k, :, C : 2 * C]

    def forward_block(k, carry):
        mixers(k, False)

        def one(t, inner):
            forward_stage(t, k)

            @pl.when(k == 0)
            def _():
                for copy in spill(t):
                    copy.start()
                conv_stage(t, 1)
            return inner
        lax.fori_loop(0, 2, one, 0)
        return carry
    lax.fori_loop(0, 2, forward_block, 0)

    for t in range(2):
        grad_in[t].wait()
        pltpu.make_async_copy(ybuf.at[t], so_h.at[0, t], so_local.at[t]).wait()
        across(ybuf.at[t], so_h.at[0, t], so_send.at[t], so_recv.at[t]).wait_send()

    def load_grad(t, carry):
        def widen(i, inner):
            gf[t, pl.ds(pl.multiple_of(i * SIDE, SIDE), SIDE), :] = ub[t, i].astype(F32)
            return inner
        lax.fori_loop(0, SIDE, widen, 0)
        return carry
    lax.fori_loop(0, 2, load_grad, 0)
    for t in range(2):
        image_copy(t, again_sems.at[t]).start()

    def turn(s, carry):
        t = lax.rem(s, 2)

        def tick(place):
            for n in range(6):
                steps = plan.get((n, place), [])
                if steps:
                    @pl.when(s == n)
                    def _():
                        for step in steps:
                            step()

        @pl.when(lax.rem(s, 2) == 0)
        def _():
            @pl.when(s > 0)
            def _():
                close_mix(2 - lax.div(s, 2))

            @pl.when(s < 4)
            def _():
                mixers(1 - lax.div(s, 2), True)
                clear_mix()

        @pl.when(s > 1)
        def _():
            @pl.when(s > 3)
            def _():
                image_copy(t, again_sems.at[t]).wait()
                widen_image(t)
            tick(7)
            input_stage(t, 2 - lax.div(s, 2), tick)
            tick(9)

        @pl.when(s < 4)
        def _():
            @pl.when(s > 1)
            def _():
                for copy in fetch(t):
                    copy.wait()
            tick(0)
            backward_stage(t, 1 - lax.div(s, 2), tick)
            tick(6)

            @pl.when(s < 2)
            def _():
                for copy in fetch(t):
                    copy.start()
        return carry
    lax.fori_loop(0, 6, turn, 0)

    taps_left = list(taps_sum)
    taps_left.pop(0)()
    while tail or taps_left:
        if tail:
            tail.pop(0)()
        if taps_left:
            taps_left.pop(0)()

    gs_out = pltpu.make_async_copy(gs.at[me_p], gs_h, gs_sem.at[0])
    gs_out.start()
    for t in range(2):
        pltpu.make_async_copy(igbuf.at[t], ig_h.at[0, t], ig_local.at[t]).wait()
        across(ybuf.at[t], so_h.at[0, t], so_send.at[t], so_recv.at[t]).wait_recv()
        across(igbuf.at[t], ig_h.at[0, t], ig_send.at[t], ig_recv.at[t]).wait()
    for lb, out_h, n in ((lb_a, ga_h, 0), (lb_b, gb_h, 1)):
        pltpu.make_async_copy(lb.at[0], out_h.at[0], out_local.at[n]).wait()
        across(lb.at[0], out_h.at[0], out_send.at[n], out_recv.at[n]).wait()
    gs_out.wait()


def finish_kernel(
    so_in, ig_in, ga, gb, gs,
    so, ig, conv, bgain, bbias, ww, wb, hw, hb, gm, mbias, ngain, nbias, gu, ubias, gd, dbias, sems,
):
    copies = [pltpu.make_async_copy(so_in, so, sems.at[0]), pltpu.make_async_copy(ig_in, ig, sems.at[1])]
    for copy in copies:
        copy.start()
    for p in range(2):
        for q in range(SHARDS):
            start = p * HALF + (q % 2) * SHARD
            rows = slice(start, start + SHARD)
            out, at = (gd, gu)[q // 4], WIDE * (q // 2 % 2)
            out[rows, at : at + WIDE] = ga[p, q].astype(F32)
            at = FT * (q // 2)
            width = min(FT, 3 * C - at)
            gm[rows, at : at + width] = gb[p, q, :, 0:width].astype(F32)
    for n in range(9):
        conv[n] = gs[CONV + n : CONV + n + 1, :]
    for row, ref in ((BGAIN, bgain), (BBIAS, bbias), (MBIAS, mbias), (NGAIN, ngain), (NBIAS, nbias), (DBIAS, dbias)):
        ref[...] = gs[row : row + 1, :]
    for row, ref in ((WBIAS, wb), (HBIAS, hb)):
        ref[...] = gs[row : row + 1, 0:SIDE]
    for n in range(FF // FT):
        ubias[:, n * FT : n * FT + FT] = gs[UBIAS + n : UBIAS + n + 1, 0:FT]
    for row, ref in ((WW, ww), (HW, hw)):
        ref[0] = gs[row : row + SIDE, 0:SIDE]
    for copy in copies:
        copy.wait()


def on_device(
    images, masks, conv_weight, batch_gain, batch_bias, width_weight, width_bias,
    height_weight, height_bias, merge_weight, merge_bias, norm_gain, norm_bias,
    up_weight, up_bias, down_weight, down_bias, out_grad,
):
    n_dp = lax.axis_size("dp")
    micro = images.shape[0]
    steps = max(n_dp.bit_length() - 1, 4)
    any_space = pl.BlockSpec(memory_space=pl.ANY)
    vmem = pl.BlockSpec(memory_space=pltpu.VMEM)
    dma = pltpu.SemaphoreType.DMA
    grid = (SIDE, SIDE, C)
    shape = jax.ShapeDtypeStruct
    outs = pl.pallas_call(
        functools.partial(kernel, n_dp),
        out_shape=(
            shape((1, micro) + grid, BF16),
            shape((1, micro) + grid, BF16),
            shape((2, SHARDS, SHARD, WIDE), BF16),
            shape((2, SHARDS, SHARD, FT), BF16),
            shape((PACK, C), F32),
            shape((2, ROWS, FF), BF16),
            shape((2, ROWS, FF), BF16),
            shape((2, ROWS, 3 * C), BF16),
            shape((2, ROWS, C), BF16),
            shape((2, ROWS, C), BF16),
        ),
        in_specs=[any_space] + [vmem] * 8 + [any_space] + [vmem] * 3 + [any_space, vmem, any_space, vmem, any_space],
        out_specs=(any_space,) * 10,
        scratch_shapes=[
            pltpu.VMEM((2, ROWS, 1), F32),
            pltpu.VMEM((2, PACK, C), F32),
            pltpu.VMEM((2, C, 3 * C), BF16),
            pltpu.VMEM((2, C, C), BF16),
            pltpu.VMEM((2, C, FF), BF16),
            pltpu.VMEM((2, C, FF), BF16),
            pltpu.VMEM((2,) + grid, BF16),
            pltpu.VMEM((2, ROWS + 2 * SIDE, C), F32),
            pltpu.VMEM((4, ROWS, C), F32),
            pltpu.VMEM((2, ROWS, 3 * C), BF16),
            pltpu.VMEM((2, ROWS, C), BF16),
            pltpu.VMEM((2, ROWS, C), BF16),
            pltpu.VMEM((4, ROWS, 1), F32),
            pltpu.VMEM((2, ROWS, FF), BF16),
            pltpu.VMEM((2, ROWS, FF), BF16),
            pltpu.VMEM((2, ROWS, C), F32),
            pltpu.VMEM((ROWS, C), BF16),
            pltpu.VMEM((ROWS, C), BF16),
            pltpu.VMEM((GROUP, C), BF16),
            pltpu.VMEM((C, ROWS), BF16),
            pltpu.VMEM((ROWS, FF), BF16),
            pltpu.VMEM((2, ROWS, C), F32),
            pltpu.VMEM((ROWS, C), BF16),
            pltpu.VMEM((3, ROWS + 2 * SIDE, C), F32),
            pltpu.VMEM((GROUP, GROUP), BF16),
            pltpu.VMEM((ROWS, ROWS), BF16),
            pltpu.VMEM((ROWS, 1), F32),
            pltpu.VMEM((ROWS, 1), F32),
            pltpu.VMEM((GROUP, GROUP), F32),
            pltpu.VMEM((ROWS, ROWS), F32),
            pltpu.VMEM((ROWS, 1), F32),
            pltpu.VMEM((ROWS, 1), F32),
            pltpu.VMEM((4,) + grid, BF16),
            pltpu.VMEM((8, 2, CP), F32),
            pltpu.VMEM((8, n_dp - 1, 2, CP), F32),
            pltpu.VMEM((2, 4, C, WIDE), F32),
            pltpu.VMEM((2, 4, C, FT), F32),
            pltpu.VMEM((2, PACK, C), F32),
            pltpu.VMEM((2, 4 + steps, SHARD, WIDE), BF16),
            pltpu.VMEM((2, SHARDS, SHARD, WIDE), BF16),
            pltpu.VMEM((2, 4 + steps, SHARD, WIDE), BF16),
            pltpu.VMEM((2, 4 + steps, SHARD, FT), BF16),
            pltpu.VMEM((2, SHARDS, SHARD, FT), BF16),
            pltpu.VMEM((2, 4 + steps, SHARD, FT), BF16),
            pltpu.VMEM((1 + steps, PACK - SMALL, C), F32),
            pltpu.VMEM((1 + steps, SMALL, C), F32),
            dma((9,)), dma((2,)), dma((2,)), dma((3,)), dma((3,)), dma((8,)), dma((8,)),
            dma((2,)), dma((2,)), dma((2,)), dma((2,)), dma((2,)), dma((2,)), dma((2, 5)), dma((2, 5)),
            dma((4, 4 + steps)), dma((4, 4 + steps)), dma((1 + steps,)), dma((1 + steps,)),
            dma((1 + steps,)), dma((1 + steps,)), dma((2,)), dma((2,)), dma((2,)), dma((1,)),
        ],
        compiler_params=pltpu.CompilerParams(
            collective_id=0, has_side_effects=True, vmem_limit_bytes=65400 * 1024),
    )(
        images, masks, conv_weight, batch_gain, batch_bias, width_weight, width_bias, height_weight, height_bias,
        merge_weight[0].T, merge_bias, norm_gain, norm_bias, up_weight[0], up_bias, down_weight[0].T, down_bias, out_grad)

    row = shape((1, C), F32)
    square, line = shape((1, SIDE, SIDE), F32), shape((1, SIDE), F32)
    so, ig, conv, bgain, bbias, ww, wb, hw, hb, gm, mbias, ngain, nbias, gu, ubias, gd, dbias = pl.pallas_call(
        finish_kernel,
        out_shape=(
            shape((1, micro) + grid, BF16), shape((1, micro) + grid, BF16), shape((9, 1, C), F32), row, row,
            square, line, square, line, shape((C, 3 * C), F32), row, row, row,
            shape((C, FF), F32), shape((1, FF), F32), shape((C, FF), F32), row),
        in_specs=[any_space] * 2 + [vmem] * 3,
        out_specs=(any_space,) * 2 + (vmem,) * 15,
        scratch_shapes=[dma((2,))],
        compiler_params=pltpu.CompilerParams(vmem_limit_bytes=65400 * 1024),
    )(*outs[:5])
    return (
        so, ig, jnp.swapaxes(conv, 0, 1), bgain, bbias, ww, wb, hw, hb, gm.T[None], mbias, ngain, nbias,
        gu[None], ubias, gd.T[None], dbias)


def solution(mesh):
    data4 = P("dp", None, None, None)
    p1, p2, p3 = P("pipe"), P("pipe", None), P("pipe", None, None)
    out5 = P("pipe", "dp", None, None, None)
    return jax.shard_map(
        on_device,
        mesh=mesh,
        in_specs=(data4, P("dp", None, None), p3, p2, p2, p3, p2, p3, p2, p3, p2, p2, p2, p3, p2, p3, p2, data4),
        out_specs=(out5, out5, p3, p2, p2, p3, p2, p3, p2, p3, p2, p2, p2, p3, p2, p3, p2),
        check_vma=False,
    )
```

```python
import functools

import jax
import jax.numpy as jnp
from jax import lax
from jax.experimental import pallas as pl
from jax.experimental.pallas import tpu as pltpu
from jax.sharding import PartitionSpec as P

EPS = 1e-05
MESH = pl.DeviceIdType.MESH
F32 = jnp.float32
BF16 = jnp.bfloat16

SIDE = 24
ROWS = SIDE * SIDE
C = 320
CP = 384
FF = 1280
FT = 256
CHUNK = 48
TILE = 32
LANES = ((0, 128), (128, 256), (256, 320))
GROUP = 8 * SIDE

HALF = C // 2
SHARD = HALF // 2
WIDE = FF // 2
SHARDS = 4
MT = 512
STEP = 8

CONV, BGAIN, BBIAS, MBIAS, NGAIN, NBIAS, DBIAS, WBIAS, HBIAS, UBIAS, WW, HW, PACK = (
    0, 16, 17, 18, 19, 20, 21, 22, 23, 24, 32, 56, 80)
SMALL = 16


def dot(a, b, contract=(1, 0), precision=None):
    return lax.dot_general(
        a, b, (((contract[0],), (contract[1],)), ((), ())),
        preferred_element_type=F32, precision=precision)


def fold(value):
    rows = value.shape[0]
    return jnp.sum(value.reshape(rows // 8, 8, value.shape[1]), 0)


def total(partial):
    return jnp.sum(partial, 0, keepdims=True)


def grid_row(index):
    return (index * 2731) >> 16


def one_hots(rows):
    place = lax.broadcasted_iota(jnp.int32, (rows, SIDE), 0)
    lane = lax.broadcasted_iota(jnp.int32, (rows, SIDE), 1)
    i = grid_row(place)
    return i == lane, place - SIDE * i == lane


def gelu_both(x):
    e = jnp.exp2(x * x * -0.7213475204444817)
    d = 1.0 + 0.23164189 * jnp.abs(x)
    t = pl.reciprocal(d, approx=True)
    t = t * (2.0 - d * t)
    poly = t * (0.127414796 + t * (-0.142248368 + t * (0.7107068705 + t * (-0.7265760135 + t * 0.5307027145))))
    tail = poly * e
    phi = jnp.where(x >= 0, 1.0 - tail, tail)
    return x * phi, phi + x * e * 0.3989422804014327


def kernel(
    n_dp,
    images, masks, conv_w, bgain, bbias, wwt, wb, hwt, hb, wm_h, mbias, ngain, nbias, wu_h, ubias, wd_h, dbias, og_h,
    so_h, ig_h, gd_h, gu_h, gm_h, gs_h, sp_hidden, sp_gp, sp_joined, sp_normal, sp_xl,
    mask_cols, stat, own_column, i_hot, pack, wm, wmid, wu, wd, ub, uf, cv, joined, normal, xl, rstd, hidden, gp,
    gf, gb, gmb, gwb, gbt, gpre, gmix, gwh, gsh, kw, kh, wbcol, hbcol,
    gw_acc, gh_acc, wcol, hcol, ybuf, msg, land, acc_d, acc_u, acc_m, gs,
    sb_d, lb_d, rl_d, sb_u, lb_u, rl_u, sb_m, lb_m, rl_m, small_land, conv_land,
    local_sems, again_sems, pack_sems, w_send, w_recv, st_send, st_recv,
    so_local, so_send, so_recv, ig_local, ig_send, ig_recv, spill_sems, fetch_sems,
    red_send, red_recv, small_send, small_recv, conv_send, conv_recv, out_local, out_send, out_recv, gs_sem,
):
    me_p = lax.axis_index("pipe")
    me_d = lax.axis_index("dp")
    other = 1 - me_p
    first = gsh.at[2, pl.ds(SIDE, ROWS)]
    igbuf = ybuf
    gnorm = gsh.at[0, pl.ds(SIDE, ROWS)]

    def image_copy(t, sems):
        return pltpu.make_async_copy(images.at[2 * me_p + t], ub.at[t], sems)

    image_in = [image_copy(t, local_sems.at[5 + t]) for t in range(2)]
    grad_in = [pltpu.make_async_copy(og_h.at[2 * me_p + t], ub.at[t], local_sems.at[7 + t]) for t in range(2)]
    weights = ((wm_h, wm), (wu_h, wu), (wd_h, wd))
    weights_in = [pltpu.make_async_copy(src, dst.at[me_p], local_sems.at[n]) for n, (src, dst) in enumerate(weights)]
    for copy in image_in + weights_in:
        copy.start()

    barrier = pltpu.get_barrier_semaphore()

    def greet(step, carry):
        pl.semaphore_signal(barrier, inc=1, device_id={"dp": lax.rem(me_d + step, n_dp)}, device_id_type=MESH)
        return carry

    lax.fori_loop(1, n_dp, greet, 0)
    pl.semaphore_signal(barrier, inc=1, device_id={"pipe": other}, device_id_type=MESH)

    pack[me_p] = jnp.zeros(pack.shape[1:], F32)
    pack[me_p, CONV : CONV + 9, :] = conv_w[0].astype(F32)
    for row, ref in ((BGAIN, bgain), (BBIAS, bbias), (MBIAS, mbias), (NGAIN, ngain), (NBIAS, nbias), (DBIAS, dbias)):
        pack[me_p, row : row + 1, :] = ref[...]
    for row, ref in ((WBIAS, wb), (HBIAS, hb)):
        pack[me_p, row : row + 1, 0:SIDE] = ref[...]
    for n in range(FF // FT):
        pack[me_p, UBIAS + n : UBIAS + n + 1, 0:FT] = ubias[:, n * FT : n * FT + FT]
    for row, ref in ((WW, wwt), (HW, hwt)):
        pack[me_p, row : row + SIDE, 0:SIDE] = ref[0].astype(F32)

    pl.semaphore_wait(barrier, n_dp)

    def across(src, dst, send, recv):
        return pltpu.make_async_remote_copy(
            src_ref=src, dst_ref=dst, send_sem=send, recv_sem=recv,
            device_id={"pipe": other}, device_id_type=MESH)

    pack_over = across(pack.at[me_p], pack.at[me_p], pack_sems.at[0], pack_sems.at[1])
    weights_over = [across(src, dst.at[me_p], w_send.at[n], w_recv.at[n]) for n, (src, dst) in enumerate(weights)]
    pack_over.start()
    for copy in weights_over:
        copy.start()

    msg[...] = jnp.zeros(msg.shape, F32)
    for k in range(2):
        for acc in (acc_d, acc_u, acc_m):
            for n in range(2):
                acc[k, n] = jnp.zeros(acc.shape[2:], F32)
        gs[k] = jnp.zeros(gs.shape[1:], F32)
    for n in range(2):
        uf[n, 0:SIDE, :] = jnp.zeros((SIDE, C), F32)
        uf[n, SIDE + ROWS : 2 * SIDE + ROWS, :] = jnp.zeros((SIDE, C), F32)
    for n in range(3):
        gsh[n, 0:SIDE, :] = jnp.zeros((SIDE, C), F32)
        gsh[n, SIDE + ROWS : 2 * SIDE + ROWS, :] = jnp.zeros((SIDE, C), F32)

    i_r, j_r = one_hots(ROWS)
    i_hot[...] = jnp.where(i_r, 1.0, 0.0).astype(BF16)
    q = lax.broadcasted_iota(jnp.int32, (SIDE, ROWS), 1)
    q = q - SIDE * grid_row(q)
    own_column[...] = jnp.where(lax.broadcasted_iota(jnp.int32, (SIDE, ROWS), 0) == q, 1.0, 0.0)
    for t in range(2):
        chosen = dot(i_hot[...], masks[2 * me_p + t].astype(F32).astype(BF16))
        mask_cols[t] = jnp.sum(jnp.where(j_r, chosen, 0.0), 1, keepdims=True)

    def later(value):
        at = lax.broadcasted_iota(jnp.int32, value.shape, 0)
        return jnp.where(at != 0, pltpu.roll(value, 1, 0), 0.0)

    def sooner(value):
        at = lax.broadcasted_iota(jnp.int32, value.shape, 0)
        return jnp.where(at != SIDE - 1, pltpu.roll(value, SIDE - 1, 0), 0.0)

    def grid_rows(body, init):
        def step(c, carry):
            for row in range(STEP):
                carry = body(pl.multiple_of(c * (STEP * SIDE), STEP * SIDE) + row * SIDE, carry)
            return carry
        return lax.fori_loop(0, SIDE // STEP, step, init)

    def groups(body, init):
        for g in range(ROWS // GROUP):
            init = body(g * GROUP, init)
        return init

    def send_stats(r):
        def one(step, carry):
            pltpu.make_async_remote_copy(
                src_ref=msg.at[r], dst_ref=land.at[r, n_dp - 1 - step],
                send_sem=st_send.at[r], recv_sem=st_recv.at[r],
                device_id={"dp": lax.rem(me_d + step, n_dp)}, device_id_type=MESH).start()
            return carry
        lax.fori_loop(1, n_dp, one, 0)

    def wait_stats(r):
        whole = pltpu.make_async_remote_copy(
            src_ref=land.at[r], dst_ref=land.at[r], send_sem=st_send.at[r], recv_sem=st_recv.at[r],
            device_id={"dp": lax.rem(me_d + 1, n_dp)}, device_id_type=MESH)
        whole.wait_send()
        whole.wait_recv()

    def conv_stage(t, k):
        z = 2 * k + t
        n_own = total(mask_cols[t])
        taps = [[pack[k, CONV + n : CONV + n + 1, l:m] for n in range(9)] for l, m in LANES]

        def conv(start, acc):
            at = pl.ds(start, SIDE)
            new = []
            for (l, m), tap, one in zip(LANES, taps, acc):
                rows = [uf[t, pl.ds(start + SIDE * r, SIDE), l:m] for r in range(3)]
                part = [rows[0] * tap[s] + rows[1] * tap[3 + s] + rows[2] * tap[6 + s] for s in range(3)]
                out = part[1] + later(part[0]) + sooner(part[2])
                cv[z, at, l:m] = out
                new.append(one + fold(out * mask_cols[t, at, :]))
            return new
        acc = grid_rows(conv, [jnp.zeros((8, m - l), F32) for l, m in LANES])
        sums = jnp.concatenate([total(one) for one in acc], 1)
        mean = sums / n_own

        def centred(start, acc):
            rows = pl.ds(start, SIDE)
            d = cv[z, rows, :] - mean
            return acc + fold(d * d * mask_cols[t, rows, :])

        m2 = total(grid_rows(centred, jnp.zeros((8, C), F32)))
        msg[z, 0:1, 0:C] = sums
        msg[z, 0:1, C:CP] = jnp.broadcast_to(n_own, (1, CP - C))
        msg[z, 1:2, 0:C] = m2
        send_stats(z)

    def peers(body, init):
        if n_dp > 16:
            return lax.fori_loop(0, n_dp - 1, body, init)
        for d in range(n_dp - 1):
            init = body(d, init)
        return init

    def gather_stats(r):
        def add(d, carry):
            return carry + land[r, d]
        return peers(add, msg[r])

    def norm_stats(z):
        sums = gather_stats(z)[0:1, :]
        count = sums[:, CP - 1 : CP]
        mean = sums[:, 0:C] / count

        def spread(values):
            n = values[0:1, CP - 1 : CP]
            off = values[0:1, 0:C] / n - mean
            return values[1:2, 0:C] + n * off * off

        def add(d, carry):
            return carry + spread(land[z, d])
        m2 = peers(add, spread(msg[z]))
        scale = lax.rsqrt(m2 / count + EPS)
        stat[z, 0:1, :] = scale
        stat[z, 1:2, :] = jnp.broadcast_to(count, (1, C))
        return mean, scale

    def mixers(k, backward):
        _, j_g = one_hots(GROUP)
        ww = pack[k, WW : WW + SIDE, 0:SIDE].astype(BF16)
        hw = pack[k, HW : HW + SIDE, 0:SIDE].astype(BF16)
        side_of = 0 if backward else 1
        j_b = jnp.where(j_g, 1.0, 0.0).astype(BF16)
        left = dot(j_b, ww, (1, 1 - side_of)).astype(BF16)
        p = grid_row(lax.broadcasted_iota(jnp.int32, (GROUP, GROUP), 0))
        q = grid_row(lax.broadcasted_iota(jnp.int32, (GROUP, GROUP), 1))
        kw[...] = jnp.where(p == q, dot(left, j_b, (1, 1)), 0.0).astype(BF16)
        spread = dot(hw, i_hot[...], (side_of, 1))
        own = own_column[...]
        for i in range(0, SIDE, 2):
            two = jnp.concatenate([spread[i : i + 1, :] * own, spread[i + 1 : i + 2, :] * own], 0)
            kh[i * SIDE : i * SIDE + 2 * SIDE, :] = two.astype(BF16)
        if not backward:
            i_r, j_r = one_hots(ROWS)
            wb = pack[k, WBIAS : WBIAS + 1, 0:SIDE]
            hb = pack[k, HBIAS : HBIAS + 1, 0:SIDE]
            wbcol[...] = jnp.sum(jnp.where(j_r, wb, 0.0), 1, keepdims=True)
            hbcol[...] = jnp.sum(jnp.where(i_r, hb, 0.0), 1, keepdims=True)

    stored = ((hidden, sp_hidden), (gp, sp_gp), (joined, sp_joined), (normal, sp_normal), (xl, sp_xl))

    def spill(t):
        return [pltpu.make_async_copy(v.at[t], h.at[t], spill_sems.at[t, n]) for n, (v, h) in enumerate(stored)]

    def fetch(t):
        return [pltpu.make_async_copy(h.at[t], v.at[t], fetch_sems.at[t, n]) for n, (v, h) in enumerate(stored)]

    def forward_stage(t, k):
        z = 2 * k + t

        @pl.when(k == 1)
        def _():
            for copy in spill(t):
                copy.wait()

        wait_stats(z)
        mean, scale = norm_stats(z)
        gain = pack[k, BGAIN : BGAIN + 1, :]
        bias = pack[k, BBIAS : BBIAS + 1, :]

        def standardize(start, carry):
            for o in range(0, GROUP, TILE):
                rows = pl.ds(start + o, TILE)
                x = (cv[z, rows, :] - mean) * scale
                cv[z, rows, :] = x
                joined[t, rows, 2 * C : 3 * C] = ((x * gain + bias) * mask_cols[t, rows, :]).astype(BF16)
            along = dot(kw[...], joined[t, pl.ds(start, GROUP), 2 * C : 3 * C])
            for o in range(0, GROUP, TILE):
                rows = pl.ds(start + o, TILE)
                joined[t, rows, 0:C] = (along[o : o + TILE] + wbcol[rows, :]).astype(BF16)
            return carry
        groups(standardize, 0)

        m_bias = pack[k, MBIAS : MBIAS + 1, :]
        n_gain = pack[k, NGAIN : NGAIN + 1, :]
        n_bias = pack[k, NBIAS : NBIAS + 1, :]
        d_bias = pack[k, DBIAS : DBIAS + 1, :]
        u_bias = [pack[k, UBIAS + n : UBIAS + n + 1, 0:FT] for n in range(FF // FT)]

        def rest(start, carry):
            rows = pl.ds(start, GROUP)
            along = dot(kh[rows, :], joined[t, :, 2 * C : 3 * C])
            for o in range(0, GROUP, TILE):
                part = pl.ds(start + o, TILE)
                joined[t, part, C : 2 * C] = (along[o : o + TILE] + hbcol[part, :]).astype(BF16)
            merged = dot(joined[t, rows, :], wm[k], (1, 1))
            for o in range(0, GROUP, TILE):
                part = pl.ds(start + o, TILE)
                f = uf[t, pl.ds(start + SIDE + o, TILE), :] + merged[o : o + TILE] + m_bias
                d = f - jnp.mean(f, 1, keepdims=True)
                rs = lax.rsqrt(jnp.mean(d * d, 1, keepdims=True) + EPS)
                x = d * rs
                first[part, :] = f
                rstd[z, part, :] = rs
                xl[t, part, :] = x.astype(BF16)
                normal[t, part, :] = (x * n_gain + n_bias).astype(BF16)
            norm = normal[t, rows, :]
            pre = dot(norm, wu[k, :, 0:FT])
            for n in range(FF // FT):
                cols = slice(n * FT, n * FT + FT)
                now = pre
                if n + 1 < FF // FT:
                    pre = dot(norm, wu[k, :, n * FT + FT : n * FT + 2 * FT])
                for o in range(0, GROUP, TILE):
                    part = pl.ds(start + o, TILE)
                    h, dh = gelu_both(now[o : o + TILE] + u_bias[n])
                    hidden[t, part, cols] = h.astype(BF16)
                    gp[t, part, cols] = dh.astype(BF16)
            down = dot(hidden[t, rows, :], wd[k], (1, 1))
            i = start // SIDE
            for r in range(GROUP // SIDE):
                y = first[pl.ds(start + r * SIDE, SIDE), :] + down[r * SIDE : r * SIDE + SIDE] + d_bias
                ybuf[z, i + r] = y.astype(BF16)
            return carry
        groups(rest, 0)

        @pl.when(k == 0)
        def _():
            def reread(start, carry):
                uf[t, pl.ds(start + SIDE, SIDE), :] = ybuf[z, lax.div(start, SIDE)].astype(F32)
                return carry
            grid_rows(reread, 0)

        @pl.when(me_p == k)
        def _():
            pltpu.make_async_copy(ybuf.at[z], so_h.at[0, 2 * me_p + t], so_local.at[t]).start()

        @pl.when(me_p != k)
        def _():
            across(ybuf.at[z], so_h.at[0, 2 * me_p + t], so_send.at[t], so_recv.at[t]).start()

    def backward_stage(t, k, tick):
        z = 2 * k + t
        zero = jnp.zeros((8, C), F32)
        n_gain = pack[k, NGAIN : NGAIN + 1, :]

        d_acc = zero
        for o in range(0, ROWS, TILE):
            g = gf[t, o : o + TILE, :]
            gb[o : o + TILE, :] = g.astype(BF16)
            d_acc = d_acc + fold(g)
        gs[k, DBIAS : DBIAS + 1, :] += total(d_acc)
        gbt[...] = gb[...].T
        for n in range(2):
            acc_d[k, n] += dot(gbt[...], hidden[t, :, n * WIDE : n * WIDE + WIDE])
        tick(1)

        def chain(start, acc):
            rows = pl.ds(start, GROUP)
            x_acc, n_acc, m_acc, u_acc = acc
            u_acc = list(u_acc)
            low = gb[rows, :]
            raw = dot(low, wd[k, :, 0:FT])
            for n in range(FF // FT):
                cols = slice(n * FT, n * FT + FT)
                now = raw
                if n + 1 < FF // FT:
                    raw = dot(low, wd[k, :, n * FT + FT : n * FT + 2 * FT])
                for o in range(0, GROUP, TILE):
                    part = pl.ds(start + o, TILE)
                    gpn = (now[o : o + TILE] * gp[t, part, cols].astype(F32)).astype(BF16)
                    gpre[part, cols] = gpn
                    u_acc[n] = u_acc[n] + fold(gpn.astype(F32))
            back = dot(gpre[rows, :], wu[k], (1, 1))
            for o in range(0, GROUP, TILE):
                part = pl.ds(start + o, TILE)
                g = back[o : o + TILE]
                x = xl[t, part, :].astype(F32)
                gn = g * n_gain
                mean_g = jnp.mean(gn, 1, keepdims=True)
                mean_gx = jnp.mean(gn * x, 1, keepdims=True)
                out = gf[t, part, :] + rstd[z, part, :] * (gn - mean_g - x * mean_gx)
                gf[t, part, :] = out
                low = out.astype(BF16)
                gmb[part, :] = low
                x_acc = x_acc + fold(g * x)
                n_acc = n_acc + fold(g)
                m_acc = m_acc + fold(low.astype(F32))
            low = gmb[rows, :]
            g_w = dot(low, wm[k, :, 0:C])
            g_h = dot(low, wmid[k])
            for o in range(0, GROUP, TILE):
                part = pl.ds(start + o, TILE)
                one = g_w[o : o + TILE].astype(BF16)
                gwb[o : o + TILE, :] = one
                wcol[part, :] += jnp.sum(one.astype(F32), 1, keepdims=True)
                one = g_h[o : o + TILE].astype(BF16)
                gwh[part, :] = one
                hcol[part, :] += jnp.sum(one.astype(F32), 1, keepdims=True)
            third = dot(low, wm[k, :, 2 * C : 3 * C])
            crossed = dot(kw[...], gwb[...])
            for o in range(0, GROUP, TILE):
                gmix[t, pl.ds(start + o, TILE), :] = third[o : o + TILE] + crossed[o : o + TILE]
            gw_acc[...] += dot(gwb[...], joined[t, rows, 2 * C : 3 * C], (1, 1))
            return (x_acc, n_acc, m_acc, u_acc)
        acc = groups(chain, (zero, zero, zero, [jnp.zeros((8, FT), F32) for _ in range(FF // FT)]))
        tick(4)
        gs[k, NGAIN : NGAIN + 1, :] += total(acc[0])
        gs[k, NBIAS : NBIAS + 1, :] += total(acc[1])
        gs[k, MBIAS : MBIAS + 1, :] += total(acc[2])
        for n in range(FF // FT):
            gs[k, UBIAS + n : UBIAS + n + 1, 0:FT] += total(acc[3][n])
        gbt[...] = normal[t].T
        for n in range(2):
            acc_u[k, n] += dot(gbt[...], gpre[:, n * WIDE : n * WIDE + WIDE])
        tick(5)
        gbt[...] = gmb[...].T
        for n in range(2):
            width = min(MT, 3 * C - n * MT)
            acc_m[k, n, :, 0:width] += dot(gbt[...], joined[t, :, n * MT : n * MT + width])
        tick(6)
        gh_acc[...] += dot(gwh[...], joined[t, :, 2 * C : 3 * C], (1, 1))
        tick(10)

        def batch_sums(start, acc):
            plain, cross = acc
            crossed = dot(kh[pl.ds(start, GROUP), :], gwh[...])
            for o in range(0, GROUP, TILE):
                rows = pl.ds(start + o, TILE)
                g = (gmix[t, rows, :] + crossed[o : o + TILE]) * mask_cols[t, rows, :]
                gmix[t, rows, :] = g
                plain = plain + fold(g)
                cross = cross + fold(g * cv[z, rows, :])
            return plain, cross
        acc = groups(batch_sums, (zero, zero))
        plain, cross = total(acc[0]), total(acc[1])
        gs[k, BBIAS : BBIAS + 1, :] += plain
        gs[k, BGAIN : BGAIN + 1, :] += cross
        r = 4 + z
        msg[r, 0:1, 0:C] = plain
        msg[r, 1:2, 0:C] = cross
        send_stats(r)

    def input_stage(t, k, tick):
        z = 2 * k + t
        r = 4 + z
        wait_stats(r)
        scale, count = stat[z, 0:1, :], stat[z, 1:2, :]
        both = gather_stats(r)
        plain, cross = both[0:1, 0:C], both[1:2, 0:C]
        gain = pack[k, BGAIN : BGAIN + 1, :]
        out_scale = gain * scale
        plain = plain / count
        cross = cross / count

        def shifted(start, carry):
            rows = pl.ds(start, SIDE)
            g = (gmix[t, rows, :] - plain - cv[z, rows, :] * cross) * (mask_cols[t, rows, :] * out_scale)
            rows = pl.ds(start + SIDE, SIDE)
            gsh[0, rows, :] = sooner(g)
            gsh[1, rows, :] = g
            gsh[2, rows, :] = later(g)
            return carry
        grid_rows(shifted, 0)
        tick(8)
        taps = [[pack[k, CONV + n : CONV + n + 1, l:m] for n in range(9)] for l, m in LANES]

        def pull(start, acc):
            new = []
            for (l, m), tap, one in zip(LANES, taps, acc):
                u = [uf[t, pl.ds(start + SIDE * r, SIDE), l:m] for r in range(3)]
                out = gf[t, pl.ds(start, SIDE), l:m]
                sums = []
                for s in range(3):
                    around = [gsh[s, pl.ds(start + SIDE * r, SIDE), l:m] for r in range(3)]
                    out = out + around[2] * tap[s] + around[1] * tap[3 + s] + around[0] * tap[6 + s]
                    sums.append([one[s][r] + fold(around[1] * u[r]) for r in range(3)])
                new.append(sums)
                igbuf[z, lax.div(start, SIDE), :, l:m] = out.astype(BF16)
            return new
        acc = grid_rows(pull, [[[jnp.zeros((8, m - l), F32) for _ in range(3)] for _ in range(3)] for l, m in LANES])
        for (l, m), one in zip(LANES, acc):
            for r in range(3):
                for s in range(3):
                    row = CONV + 3 * r + s
                    gs[k, row : row + 1, l:m] += total(one[s][r])

        @pl.when(k == 1)
        def _():
            def reread(start, carry):
                gf[t, pl.ds(start, SIDE), :] = igbuf[z, lax.div(start, SIDE)].astype(F32)
                return carry
            grid_rows(reread, 0)

        @pl.when(me_p == k)
        def _():
            pltpu.make_async_copy(igbuf.at[z], ig_h.at[0, 2 * me_p + t], ig_local.at[t]).start()

        @pl.when(me_p != k)
        def _():
            across(igbuf.at[z], ig_h.at[0, 2 * me_p + t], ig_send.at[t], ig_recv.at[t]).start()

    def clear_mix():
        gw_acc[...] = jnp.zeros(gw_acc.shape, F32)
        gh_acc[...] = jnp.zeros(gh_acc.shape, F32)
        wcol[...] = jnp.zeros(wcol.shape, F32)
        hcol[...] = jnp.zeros(hcol.shape, F32)

    def close_mix(k):
        i_r, j_r = one_hots(ROWS)
        _, j_g = one_hots(GROUP)
        gs[k, WBIAS : WBIAS + 1, 0:SIDE] = total(jnp.where(j_r, wcol[...], 0.0))
        gs[k, HBIAS : HBIAS + 1, 0:SIDE] = total(jnp.where(i_r, hcol[...], 0.0))
        highest = lax.Precision.HIGHEST
        p = grid_row(lax.broadcasted_iota(jnp.int32, (GROUP, GROUP), 0))
        q = grid_row(lax.broadcasted_iota(jnp.int32, (GROUP, GROUP), 1))
        own = jnp.where(p == q, gw_acc[...], 0.0)
        own = jnp.sum(own.reshape(GROUP // SIDE, SIDE, GROUP), 0)
        gs[k, WW : WW + SIDE, 0:SIDE] = dot(own, jnp.where(j_g, 1.0, 0.0), precision=highest)
        i_f = jnp.where(i_r, 1.0, 0.0)
        for i in range(SIDE):
            rows = slice(i * SIDE, i * SIDE + SIDE)
            own = total(fold(own_column[...] * gh_acc[rows, :]))
            first[i : i + 1, :] = own[:, 0:C]
            gnorm[i : i + 1, 0 : ROWS - C] = own[:, C:ROWS]
        value = dot(first[0:SIDE, :], i_f[0:C, :], precision=highest)
        value += dot(gnorm[0:SIDE, 0 : ROWS - C], i_f[C:ROWS, :], precision=highest)
        gs[k, HW : HW + SIDE, 0:SIDE] = value

    bits = [1, 2]
    while 2 * bits[-1] < n_dp:
        bits.append(2 * bits[-1])
    n_swaps = len(bits) - 2
    n_steps = 1 + 2 + n_swaps + 2

    def partner(bit):
        return me_d + bit * (1 - 2 * lax.rem(me_d // bit, 2))

    def side(bit):
        return lax.rem(me_d // bit, 2)

    def along(bit, src, dst, send, recv):
        return pltpu.make_async_remote_copy(
            src_ref=src, dst_ref=dst, send_sem=send, recv_sem=recv,
            device_id={"dp": partner(bit)}, device_id_type=MESH)

    streams = (
        (acc_d, gd_h, sb_d, lb_d, rl_d), (acc_u, gu_h, sb_u, lb_u, rl_u), (acc_m, gm_h, sb_m, lb_m, rl_m))

    def reduction(k, which):
        acc, out_h, sb, lb, rl = streams[which]
        sb, lb, rl = sb.at[k], lb.at[k], rl.at[k]
        halving = [1 + me_p, 2 - me_p] if which != 1 else [2 - me_p, 1 + me_p]

        def sems(step):
            return red_send.at[3 * k + which, step], red_recv.at[3 * k + which, step]

        def own(q):
            return k, lax.div(q, 2), pl.ds(pl.multiple_of(me_p * HALF + lax.rem(q, 2) * SHARD, 16), SHARD), slice(None)

        def each(count, body):
            if count == 1:
                body(0)
                return

            def step(n, carry):
                body(n)
                return carry
            lax.fori_loop(0, count, step, 0)

        in_chip = across(sb.at[pl.ds(0, SHARDS)], lb, *sems(0))
        base = [0]
        for n, bit in enumerate(halving):
            base.append(base[n] + side(bit) * (2 >> n))
        mine = base[2]

        def half_copy(n):
            count, at = 2 >> n, 2 * n
            return along(halving[n], sb.at[pl.ds(at, count)], rl.at[pl.ds(at, count)], *sems(1 + n))

        def swap_copy(n):
            return along(bits[2 + n], sb.at[3 + n], rl.at[3 + n], *sems(3 + n))

        def double_copy(n):
            count = 2 >> n
            here = lb.at[pl.ds(base[n + 1], count)]
            return along(halving[n], here, here, *sems(n_steps - 1 - n))

        def send_half(n, landed):
            count, at = 2 >> n, 2 * n
            give = base[n] + (1 - side(halving[n])) * count
            keep = base[n + 1]

            def one(q):
                sb[at + q] = (acc[own(give + q)] + landed(give + q).astype(F32)).astype(BF16)
            each(count, one)
            half_copy(n).start()

            def two(q):
                acc[own(keep + q)] += landed(keep + q).astype(F32)
            each(count, two)

        def start():
            def one(q):
                rows = pl.ds(pl.multiple_of(other * HALF + lax.rem(q, 2) * SHARD, 16), SHARD)
                sb[q] = acc[k, lax.div(q, 2), rows, :].astype(BF16)
            each(SHARDS, one)
            in_chip.start()

        def first_half():
            in_chip.wait()
            send_half(0, lambda q: lb[q])

        def second_half():
            half_copy(0).wait()
            send_half(1, lambda q: rl[q - base[1]])

        def swap(n):
            def run():
                if n == 0:
                    half_copy(1).wait()
                    sb[3] = (acc[own(mine)] + rl[2].astype(F32)).astype(BF16)
                else:
                    swap_copy(n - 1).wait()
                    sb[3 + n] = (sb[2 + n].astype(F32) + rl[2 + n].astype(F32)).astype(BF16)
                swap_copy(n).start()
            return run

        def double(n):
            def run():
                if n == 1:
                    last = n_swaps - 1
                    swap_copy(last).wait()
                    lb[mine] = (sb[3 + last].astype(F32) + rl[3 + last].astype(F32)).astype(BF16)
                else:
                    double_copy(n + 1).wait()
                double_copy(n).start()
            return run

        def hand_over():
            double_copy(0).wait()

            @pl.when(me_p == k)
            def _():
                pltpu.make_async_copy(lb, out_h.at[me_p], out_local.at[which]).start()

            @pl.when(me_p != k)
            def _():
                across(lb, out_h.at[me_p], out_send.at[which], out_recv.at[which]).start()

        return [start, first_half, second_half] + [swap(n) for n in range(n_swaps)] + [double(1), double(0), hand_over]

    def small_sum(rows, landing, send, recv):
        count = rows.stop - rows.start
        rows = pl.ds(rows.start, count)
        in_chip = across(gs.at[other, rows], landing.at[0], send.at[0], recv.at[0])

        def swap_copy(n):
            return along(bits[n], gs.at[me_p, rows], landing.at[1 + n], send.at[1 + n], recv.at[1 + n])

        def step(n):
            def run():
                (swap_copy(n - 1) if n else in_chip).wait()
                gs[me_p, rows, :] += landing[n]
                if n < len(bits):
                    swap_copy(n).start()
            return run
        return [in_chip.start] + [step(n) for n in range(len(bits) + 1)]

    small = small_sum(slice(SMALL, PACK), small_land, small_send, small_recv)
    taps_sum = small_sum(slice(0, SMALL), conv_land, conv_send, conv_recv)

    plan = {}
    backward_places, input_places = [0, 1, 4, 5, 6, 10, 11], [7, 8, 9]
    order = []
    for n in range(6):
        order += [(n, p) for p in input_places] if n > 1 else []
        order += [(n, p) for p in backward_places] if n < 4 else []

    def put(start, steps, gap):
        at = order.index(start)
        steps = list(steps)
        while steps and at < len(order):
            plan.setdefault(order[at], []).append(steps.pop(0))
            at += gap
        return steps

    for which, place in enumerate((1, 5, 6)):
        assert not put((1, place), reduction(1, which), 2 if n_swaps < 3 else 1)
    tails = [put((3, place), reduction(0, which), 1) for which, place in enumerate((1, 5, 6))]
    tails.append(put((4, 7), small, 1))
    tails.append(list(taps_sum))

    pack_over.wait()
    for t in range(2):
        image_in[t].wait()

    def widen_image(t):
        def widen(i, inner):
            uf[t, pl.ds(pl.multiple_of(i * SIDE + SIDE, SIDE), SIDE), :] = ub[t, i].astype(F32)
            return inner
        lax.fori_loop(0, SIDE, widen, 0)

    def start_image(t, carry):
        widen_image(t)
        conv_stage(t, 0)
        return carry
    lax.fori_loop(0, 2, start_image, 0)
    for t in range(2):
        grad_in[t].start()

    for copy in weights_in + weights_over:
        copy.wait()
    for k in range(2):
        wmid[k] = wm[k, :, C : 2 * C]

    def forward_block(k, carry):
        mixers(k, False)

        def one(t, inner):
            forward_stage(t, k)

            @pl.when(k == 0)
            def _():
                for copy in spill(t):
                    copy.start()
                conv_stage(t, 1)
            return inner
        lax.fori_loop(0, 2, one, 0)
        return carry
    lax.fori_loop(0, 2, forward_block, 0)

    for t in range(2):
        grad_in[t].wait()
        pltpu.make_async_copy(ybuf.at[t], so_h.at[0, t], so_local.at[t]).wait()
        across(ybuf.at[t], so_h.at[0, t], so_send.at[t], so_recv.at[t]).wait_send()

    def load_grad(t, carry):
        def widen(i, inner):
            gf[t, pl.ds(pl.multiple_of(i * SIDE, SIDE), SIDE), :] = ub[t, i].astype(F32)
            return inner
        lax.fori_loop(0, SIDE, widen, 0)
        return carry
    lax.fori_loop(0, 2, load_grad, 0)
    for t in range(2):
        image_copy(t, again_sems.at[t]).start()

    def turn(s, carry):
        t = lax.rem(s, 2)

        def tick(place):
            for n in range(6):
                steps = plan.get((n, place), [])
                if steps:
                    @pl.when(s == n)
                    def _():
                        for step in steps:
                            step()

        @pl.when(lax.rem(s, 2) == 0)
        def _():
            @pl.when(s > 0)
            def _():
                close_mix(2 - lax.div(s, 2))

            @pl.when(s < 4)
            def _():
                mixers(1 - lax.div(s, 2), True)
                clear_mix()

        @pl.when(s > 1)
        def _():
            @pl.when(s > 3)
            def _():
                image_copy(t, again_sems.at[t]).wait()
                widen_image(t)
            tick(7)
            input_stage(t, 2 - lax.div(s, 2), tick)
            tick(9)

        @pl.when(s < 4)
        def _():
            @pl.when(s > 1)
            def _():
                for copy in fetch(t):
                    copy.wait()
            tick(0)
            backward_stage(t, 1 - lax.div(s, 2), tick)
            tick(11)

            @pl.when(s < 2)
            def _():
                for copy in fetch(t):
                    copy.start()
        return carry
    lax.fori_loop(0, 6, turn, 0)

    while any(tails):
        for steps in tails:
            if steps:
                steps.pop(0)()

    gs_out = pltpu.make_async_copy(gs.at[me_p], gs_h, gs_sem.at[0])
    gs_out.start()
    for t in range(2):
        pltpu.make_async_copy(igbuf.at[t], ig_h.at[0, t], ig_local.at[t]).wait()
        across(ybuf.at[t], so_h.at[0, t], so_send.at[t], so_recv.at[t]).wait_recv()
        across(igbuf.at[t], ig_h.at[0, t], ig_send.at[t], ig_recv.at[t]).wait()
    for n, (_, out_h, _, lb, _) in enumerate(streams):
        pltpu.make_async_copy(lb.at[0], out_h.at[0], out_local.at[n]).wait()
        across(lb.at[0], out_h.at[0], out_send.at[n], out_recv.at[n]).wait()
    gs_out.wait()


def finish_kernel(
    so_in, ig_in, gd_in, gu_in, gm_in, gs,
    so, ig, conv, bgain, bbias, ww, wb, hw, hb, gm, mbias, ngain, nbias, gu, ubias, gd, dbias,
    large, d_in, u_in, m_in, d_out, u_out, m_out, in_sems, out_sems,
):
    moved = ((gd_in, d_in), (gu_in, u_in), (gm_in, m_in), (so_in, large.at[0]), (ig_in, large.at[1]))
    arrive = [pltpu.make_async_copy(src, dst, in_sems.at[n]) for n, (src, dst) in enumerate(moved)]
    for copy in arrive:
        copy.start()
    moved = ((d_out, gd), (u_out, gu), (m_out, gm), (large.at[0], so), (large.at[1], ig))
    leave = [pltpu.make_async_copy(src, dst, out_sems.at[n]) for n, (src, dst) in enumerate(moved)]
    for n in range(9):
        conv[n] = gs[CONV + n : CONV + n + 1, :]
    for row, ref in ((BGAIN, bgain), (BBIAS, bbias), (MBIAS, mbias), (NGAIN, ngain), (NBIAS, nbias), (DBIAS, dbias)):
        ref[...] = gs[row : row + 1, :]
    for row, ref in ((WBIAS, wb), (HBIAS, hb)):
        ref[...] = gs[row : row + 1, 0:SIDE]
    for n in range(FF // FT):
        ubias[:, n * FT : n * FT + FT] = gs[UBIAS + n : UBIAS + n + 1, 0:FT]
    for row, ref in ((WW, ww), (HW, hw)):
        ref[0] = gs[row : row + SIDE, 0:SIDE]
    for n, (src, dst, piece) in enumerate(((d_in, d_out, WIDE), (u_in, u_out, WIDE), (m_in, m_out, MT))):
        arrive[n].wait()
        for p in range(2):
            for q in range(SHARDS):
                start, at = p * HALF + (q % 2) * SHARD, piece * (q // 2)
                width = min(piece, dst.shape[1] - at)
                dst[start : start + SHARD, at : at + width] = src[p, q, :, 0:width].astype(F32)
        leave[n].start()
    for n in (3, 4):
        arrive[n].wait()
        leave[n].start()
    for copy in leave:
        copy.wait()


def on_device(
    images, masks, conv_weight, batch_gain, batch_bias, width_weight, width_bias,
    height_weight, height_bias, merge_weight, merge_bias, norm_gain, norm_bias,
    up_weight, up_bias, down_weight, down_bias, out_grad,
):
    n_dp = lax.axis_size("dp")
    micro = images.shape[0]
    steps = max(n_dp.bit_length() - 1, 4)
    any_space = pl.BlockSpec(memory_space=pl.ANY)
    vmem = pl.BlockSpec(memory_space=pltpu.VMEM)
    dma = pltpu.SemaphoreType.DMA
    grid = (SIDE, SIDE, C)
    shape = jax.ShapeDtypeStruct
    outs = pl.pallas_call(
        functools.partial(kernel, n_dp),
        out_shape=(
            shape((1, micro) + grid, BF16),
            shape((1, micro) + grid, BF16),
            shape((2, SHARDS, SHARD, WIDE), BF16),
            shape((2, SHARDS, SHARD, WIDE), BF16),
            shape((2, SHARDS, SHARD, MT), BF16),
            shape((PACK, C), F32),
            shape((2, ROWS, FF), BF16),
            shape((2, ROWS, FF), BF16),
            shape((2, ROWS, 3 * C), BF16),
            shape((2, ROWS, C), BF16),
            shape((2, ROWS, C), BF16),
        ),
        in_specs=[any_space] + [vmem] * 8 + [any_space] + [vmem] * 3 + [any_space, vmem, any_space, vmem, any_space],
        out_specs=(any_space,) * 11,
        scratch_shapes=[
            pltpu.VMEM((2, ROWS, 1), F32),
            pltpu.VMEM((4, 2, C), F32),
            pltpu.VMEM((SIDE, ROWS), F32),
            pltpu.VMEM((ROWS, SIDE), BF16),
            pltpu.VMEM((2, PACK, C), F32),
            pltpu.VMEM((2, C, 3 * C), BF16),
            pltpu.VMEM((2, C, C), BF16),
            pltpu.VMEM((2, C, FF), BF16),
            pltpu.VMEM((2, C, FF), BF16),
            pltpu.VMEM((2,) + grid, BF16),
            pltpu.VMEM((2, ROWS + 2 * SIDE, C), F32),
            pltpu.VMEM((4, ROWS, C), F32),
            pltpu.VMEM((2, ROWS, 3 * C), BF16),
            pltpu.VMEM((2, ROWS, C), BF16),
            pltpu.VMEM((2, ROWS, C), BF16),
            pltpu.VMEM((4, ROWS, 1), F32),
            pltpu.VMEM((2, ROWS, FF), BF16),
            pltpu.VMEM((2, ROWS, FF), BF16),
            pltpu.VMEM((2, ROWS, C), F32),
            pltpu.VMEM((ROWS, C), BF16),
            pltpu.VMEM((ROWS, C), BF16),
            pltpu.VMEM((GROUP, C), BF16),
            pltpu.VMEM((C, ROWS), BF16),
            pltpu.VMEM((ROWS, FF), BF16),
            pltpu.VMEM((2, ROWS, C), F32),
            pltpu.VMEM((ROWS, C), BF16),
            pltpu.VMEM((3, ROWS + 2 * SIDE, C), F32),
            pltpu.VMEM((GROUP, GROUP), BF16),
            pltpu.VMEM((ROWS, ROWS), BF16),
            pltpu.VMEM((ROWS, 1), F32),
            pltpu.VMEM((ROWS, 1), F32),
            pltpu.VMEM((GROUP, GROUP), F32),
            pltpu.VMEM((ROWS, ROWS), F32),
            pltpu.VMEM((ROWS, 1), F32),
            pltpu.VMEM((ROWS, 1), F32),
            pltpu.VMEM((4,) + grid, BF16),
            pltpu.VMEM((8, 2, CP), F32),
            pltpu.VMEM((8, n_dp - 1, 2, CP), F32),
            pltpu.VMEM((2, 2, C, WIDE), F32),
            pltpu.VMEM((2, 2, C, WIDE), F32),
            pltpu.VMEM((2, 2, C, MT), F32),
            pltpu.VMEM((2, PACK, C), F32),
            pltpu.VMEM((2, 1 + steps, SHARD, WIDE), BF16),
            pltpu.VMEM((2, SHARDS, SHARD, WIDE), BF16),
            pltpu.VMEM((2, 1 + steps, SHARD, WIDE), BF16),
            pltpu.VMEM((2, 1 + steps, SHARD, WIDE), BF16),
            pltpu.VMEM((2, SHARDS, SHARD, WIDE), BF16),
            pltpu.VMEM((2, 1 + steps, SHARD, WIDE), BF16),
            pltpu.VMEM((2, 1 + steps, SHARD, MT), BF16),
            pltpu.VMEM((2, SHARDS, SHARD, MT), BF16),
            pltpu.VMEM((2, 1 + steps, SHARD, MT), BF16),
            pltpu.VMEM((1 + steps, PACK - SMALL, C), F32),
            pltpu.VMEM((1 + steps, SMALL, C), F32),
            dma((9,)), dma((2,)), dma((2,)), dma((3,)), dma((3,)), dma((8,)), dma((8,)),
            dma((2,)), dma((2,)), dma((2,)), dma((2,)), dma((2,)), dma((2,)), dma((2, 5)), dma((2, 5)),
            dma((6, 3 + steps)), dma((6, 3 + steps)), dma((1 + steps,)), dma((1 + steps,)),
            dma((1 + steps,)), dma((1 + steps,)), dma((3,)), dma((3,)), dma((3,)), dma((1,)),
        ],
        compiler_params=pltpu.CompilerParams(
            collective_id=0, has_side_effects=True, vmem_limit_bytes=65400 * 1024),
    )(
        images, masks, conv_weight, batch_gain, batch_bias, width_weight, width_bias, height_weight, height_bias,
        merge_weight[0].T, merge_bias, norm_gain, norm_bias, up_weight[0], up_bias, down_weight[0].T, down_bias, out_grad)

    row = shape((1, C), F32)
    square, line = shape((1, SIDE, SIDE), F32), shape((1, SIDE), F32)
    so, ig, conv, bgain, bbias, ww, wb, hw, hb, gm, mbias, ngain, nbias, gu, ubias, gd, dbias = pl.pallas_call(
        finish_kernel,
        out_shape=(
            shape((1, micro) + grid, BF16), shape((1, micro) + grid, BF16), shape((9, 1, C), F32), row, row,
            square, line, square, line, shape((C, 3 * C), F32), row, row, row,
            shape((C, FF), F32), shape((1, FF), F32), shape((C, FF), F32), row),
        in_specs=[any_space] * 5 + [vmem],
        out_specs=(any_space,) * 2 + (vmem,) * 7 + (any_space,) + (vmem,) * 3 + (any_space, vmem, any_space, vmem),
        scratch_shapes=[
            pltpu.VMEM((2, 1, micro) + grid, BF16),
            pltpu.VMEM((2, SHARDS, SHARD, WIDE), BF16),
            pltpu.VMEM((2, SHARDS, SHARD, WIDE), BF16),
            pltpu.VMEM((2, SHARDS, SHARD, MT), BF16),
            pltpu.VMEM((C, FF), F32),
            pltpu.VMEM((C, FF), F32),
            pltpu.VMEM((C, 3 * C), F32),
            dma((5,)), dma((5,)),
        ],
        compiler_params=pltpu.CompilerParams(vmem_limit_bytes=65400 * 1024),
    )(*outs[:6])
    return (
        so, ig, jnp.swapaxes(conv, 0, 1), bgain, bbias, ww, wb, hw, hb, gm.T[None], mbias, ngain, nbias,
        gu[None], ubias, gd.T[None], dbias)


def solution(mesh):
    data4 = P("dp", None, None, None)
    p1, p2, p3 = P("pipe"), P("pipe", None), P("pipe", None, None)
    out5 = P("pipe", "dp", None, None, None)
    return jax.shard_map(
        on_device,
        mesh=mesh,
        in_specs=(data4, P("dp", None, None), p3, p2, p2, p3, p2, p3, p2, p3, p2, p2, p2, p3, p2, p3, p2, data4),
        out_specs=(out5, out5, p3, p2, p2, p3, p2, p3, p2, p3, p2, p2, p2, p3, p2, p3, p2),
        check_vma=False,
    )
```

```python
import functools

import jax
import jax.numpy as jnp
from jax import lax
from jax.experimental import pallas as pl
from jax.experimental.pallas import tpu as pltpu
from jax.sharding import PartitionSpec as P

EPS = 1e-05
MESH = pl.DeviceIdType.MESH
F32 = jnp.float32
BF16 = jnp.bfloat16

SIDE = 24
ROWS = SIDE * SIDE
C = 320
CP = 384
FF = 1280
FT = 256
CHUNK = 48
TILE = 32
LANES = ((0, 128), (128, 256), (256, 320))
GROUP = 8 * SIDE

HALF = C // 2
SHARD = HALF // 2
WIDE = FF // 2
SHARDS = 4
MT = 512
STEP = 8

CONV, BGAIN, BBIAS, MBIAS, NGAIN, NBIAS, DBIAS, WBIAS, HBIAS, UBIAS, WW, HW, PACK = (
    0, 16, 17, 18, 19, 20, 21, 22, 23, 24, 32, 56, 80)
SMALL = 16


def dot(a, b, contract=(1, 0), precision=None):
    return lax.dot_general(
        a, b, (((contract[0],), (contract[1],)), ((), ())),
        preferred_element_type=F32, precision=precision)


def fold(value):
    rows = value.shape[0]
    return jnp.sum(value.reshape(rows // 8, 8, value.shape[1]), 0)


def total(partial):
    return jnp.sum(partial, 0, keepdims=True)


def grid_row(index):
    return (index * 2731) >> 16


def one_hots(rows):
    place = lax.broadcasted_iota(jnp.int32, (rows, SIDE), 0)
    lane = lax.broadcasted_iota(jnp.int32, (rows, SIDE), 1)
    i = grid_row(place)
    return i == lane, place - SIDE * i == lane


def gelu_both(x):
    e = jnp.exp2(x * x * -0.7213475204444817)
    d = 1.0 + 0.23164189 * jnp.abs(x)
    t = pl.reciprocal(d, approx=True)
    t = t * (2.0 - d * t)
    poly = t * (0.127414796 + t * (-0.142248368 + t * (0.7107068705 + t * (-0.7265760135 + t * 0.5307027145))))
    tail = poly * e
    phi = jnp.where(x >= 0, 1.0 - tail, tail)
    return x * phi, phi + x * e * 0.3989422804014327


def kernel(
    n_dp,
    images, masks, conv_w, bgain, bbias, wwt, wb, hwt, hb, wm_h, mbias, ngain, nbias, wu_h, ubias, wd_h, dbias, og_h,
    so_h, ig_h, gd_h, gu_h, gm_h, gs_h, sp_hidden, sp_gp, sp_joined, sp_normal, sp_xl,
    mask_cols, stat, own_column, i_hot, pack, wm, wmid, wu, wd, ub, uf, cv, joined, normal, xl, rstd, hidden, gp,
    gf, gb, gmb, gwb, gbt, gpre, gmix, gwh, gsh, kw, kh, wbcol, hbcol,
    gw_acc, gh_acc, wcol, hcol, ybuf, msg, land, acc_d, acc_u, acc_m, gs,
    sb_d, lb_d, rl_d, sb_u, lb_u, rl_u, sb_m, lb_m, rl_m, small_land, conv_land,
    local_sems, again_sems, pack_sems, w_send, w_recv, st_send, st_recv,
    so_local, so_send, so_recv, ig_local, ig_send, ig_recv, spill_sems, fetch_sems,
    red_send, red_recv, small_send, small_recv, conv_send, conv_recv, out_local, out_send, out_recv, gs_sem,
):
    me_p = lax.axis_index("pipe")
    me_d = lax.axis_index("dp")
    other = 1 - me_p
    first = gsh.at[2, pl.ds(SIDE, ROWS)]
    igbuf = ybuf
    gnorm = gsh.at[0, pl.ds(SIDE, ROWS)]

    def image_copy(t, sems):
        return pltpu.make_async_copy(images.at[2 * me_p + t], ub.at[t], sems)

    image_in = [image_copy(t, local_sems.at[5 + t]) for t in range(2)]
    grad_in = [pltpu.make_async_copy(og_h.at[2 * me_p + t], ub.at[t], local_sems.at[7 + t]) for t in range(2)]
    weights = ((wm_h, wm), (wu_h, wu), (wd_h, wd))
    weights_in = [pltpu.make_async_copy(src, dst.at[me_p], local_sems.at[n]) for n, (src, dst) in enumerate(weights)]
    for copy in image_in + weights_in:
        copy.start()

    barrier = pltpu.get_barrier_semaphore()

    def greet(step, carry):
        pl.semaphore_signal(barrier, inc=1, device_id={"dp": lax.rem(me_d + step, n_dp)}, device_id_type=MESH)
        return carry

    lax.fori_loop(1, n_dp, greet, 0)
    pl.semaphore_signal(barrier, inc=1, device_id={"pipe": other}, device_id_type=MESH)

    pack[me_p] = jnp.zeros(pack.shape[1:], F32)
    pack[me_p, CONV : CONV + 9, :] = conv_w[0].astype(F32)
    for row, ref in ((BGAIN, bgain), (BBIAS, bbias), (MBIAS, mbias), (NGAIN, ngain), (NBIAS, nbias), (DBIAS, dbias)):
        pack[me_p, row : row + 1, :] = ref[...]
    for row, ref in ((WBIAS, wb), (HBIAS, hb)):
        pack[me_p, row : row + 1, 0:SIDE] = ref[...]
    for n in range(FF // FT):
        pack[me_p, UBIAS + n : UBIAS + n + 1, 0:FT] = ubias[:, n * FT : n * FT + FT]
    for row, ref in ((WW, wwt), (HW, hwt)):
        pack[me_p, row : row + SIDE, 0:SIDE] = ref[0].astype(F32)

    pl.semaphore_wait(barrier, n_dp)

    def across(src, dst, send, recv):
        return pltpu.make_async_remote_copy(
            src_ref=src, dst_ref=dst, send_sem=send, recv_sem=recv,
            device_id={"pipe": other}, device_id_type=MESH)

    pack_over = across(pack.at[me_p], pack.at[me_p], pack_sems.at[0], pack_sems.at[1])
    weights_over = [across(src, dst.at[me_p], w_send.at[n], w_recv.at[n]) for n, (src, dst) in enumerate(weights)]
    pack_over.start()
    for copy in weights_over:
        copy.start()

    msg[...] = jnp.zeros(msg.shape, F32)
    for k in range(2):
        for acc in (acc_d, acc_u, acc_m):
            for n in range(2):
                acc[k, n] = jnp.zeros(acc.shape[2:], F32)
        gs[k] = jnp.zeros(gs.shape[1:], F32)
    for n in range(2):
        uf[n, 0:SIDE, :] = jnp.zeros((SIDE, C), F32)
        uf[n, SIDE + ROWS : 2 * SIDE + ROWS, :] = jnp.zeros((SIDE, C), F32)
    for n in range(3):
        gsh[n, 0:SIDE, :] = jnp.zeros((SIDE, C), F32)
        gsh[n, SIDE + ROWS : 2 * SIDE + ROWS, :] = jnp.zeros((SIDE, C), F32)

    i_r, j_r = one_hots(ROWS)
    i_hot[...] = jnp.where(i_r, 1.0, 0.0).astype(BF16)
    q = lax.broadcasted_iota(jnp.int32, (SIDE, ROWS), 1)
    q = q - SIDE * grid_row(q)
    own_column[...] = jnp.where(lax.broadcasted_iota(jnp.int32, (SIDE, ROWS), 0) == q, 1.0, 0.0)
    for t in range(2):
        chosen = dot(i_hot[...], masks[2 * me_p + t].astype(F32).astype(BF16))
        mask_cols[t] = jnp.sum(jnp.where(j_r, chosen, 0.0), 1, keepdims=True)

    def later(value):
        at = lax.broadcasted_iota(jnp.int32, value.shape, 0)
        return jnp.where(at != 0, pltpu.roll(value, 1, 0), 0.0)

    def sooner(value):
        at = lax.broadcasted_iota(jnp.int32, value.shape, 0)
        return jnp.where(at != SIDE - 1, pltpu.roll(value, SIDE - 1, 0), 0.0)

    def grid_rows(body, init):
        def step(c, carry):
            for row in range(STEP):
                carry = body(pl.multiple_of(c * (STEP * SIDE), STEP * SIDE) + row * SIDE, carry)
            return carry
        return lax.fori_loop(0, SIDE // STEP, step, init)

    def groups(body, init):
        def step(g, carry):
            return body(pl.multiple_of(g * GROUP, GROUP), carry)
        return lax.fori_loop(0, ROWS // GROUP, step, init)

    def send_stats(r):
        def one(step, carry):
            pltpu.make_async_remote_copy(
                src_ref=msg.at[r], dst_ref=land.at[r, n_dp - 1 - step],
                send_sem=st_send.at[r], recv_sem=st_recv.at[r],
                device_id={"dp": lax.rem(me_d + step, n_dp)}, device_id_type=MESH).start()
            return carry
        lax.fori_loop(1, n_dp, one, 0)

    def wait_stats(r):
        whole = pltpu.make_async_remote_copy(
            src_ref=land.at[r], dst_ref=land.at[r], send_sem=st_send.at[r], recv_sem=st_recv.at[r],
            device_id={"dp": lax.rem(me_d + 1, n_dp)}, device_id_type=MESH)
        whole.wait_send()
        whole.wait_recv()

    def conv_stage(t, k):
        z = 2 * k + t
        n_own = total(mask_cols[t])
        taps = [[pack[k, CONV + n : CONV + n + 1, l:m] for n in range(9)] for l, m in LANES]

        def conv(start, acc):
            at = pl.ds(start, SIDE)
            new = []
            for (l, m), tap, one in zip(LANES, taps, acc):
                rows = [uf[t, pl.ds(start + SIDE * r, SIDE), l:m] for r in range(3)]
                part = [rows[0] * tap[s] + rows[1] * tap[3 + s] + rows[2] * tap[6 + s] for s in range(3)]
                out = part[1] + later(part[0]) + sooner(part[2])
                cv[z, at, l:m] = out
                new.append(one + fold(out * mask_cols[t, at, :]))
            return new
        acc = grid_rows(conv, [jnp.zeros((8, m - l), F32) for l, m in LANES])
        sums = jnp.concatenate([total(one) for one in acc], 1)
        mean = sums / n_own

        def centred(start, acc):
            rows = pl.ds(start, SIDE)
            d = cv[z, rows, :] - mean
            return acc + fold(d * d * mask_cols[t, rows, :])

        m2 = total(grid_rows(centred, jnp.zeros((8, C), F32)))
        msg[z, 0:1, 0:C] = sums
        msg[z, 0:1, C:CP] = jnp.broadcast_to(n_own, (1, CP - C))
        msg[z, 1:2, 0:C] = m2
        send_stats(z)

    def peers(body, init):
        if n_dp > 16:
            return lax.fori_loop(0, n_dp - 1, body, init)
        for d in range(n_dp - 1):
            init = body(d, init)
        return init

    def gather_stats(r):
        def add(d, carry):
            return carry + land[r, d]
        return peers(add, msg[r])

    def norm_stats(z):
        sums = gather_stats(z)[0:1, :]
        count = sums[:, CP - 1 : CP]
        mean = sums[:, 0:C] / count

        def spread(values):
            n = values[0:1, CP - 1 : CP]
            off = values[0:1, 0:C] / n - mean
            return values[1:2, 0:C] + n * off * off

        def add(d, carry):
            return carry + spread(land[z, d])
        m2 = peers(add, spread(msg[z]))
        scale = lax.rsqrt(m2 / count + EPS)
        stat[z, 0:1, :] = scale
        stat[z, 1:2, :] = jnp.broadcast_to(count, (1, C))
        return mean, scale

    def mixers(k, backward):
        _, j_g = one_hots(GROUP)
        ww = pack[k, WW : WW + SIDE, 0:SIDE].astype(BF16)
        hw = pack[k, HW : HW + SIDE, 0:SIDE].astype(BF16)
        side_of = 0 if backward else 1
        j_b = jnp.where(j_g, 1.0, 0.0).astype(BF16)
        left = dot(j_b, ww, (1, 1 - side_of)).astype(BF16)
        p = grid_row(lax.broadcasted_iota(jnp.int32, (GROUP, GROUP), 0))
        q = grid_row(lax.broadcasted_iota(jnp.int32, (GROUP, GROUP), 1))
        kw[...] = jnp.where(p == q, dot(left, j_b, (1, 1)), 0.0).astype(BF16)
        spread = dot(hw, i_hot[...], (side_of, 1))
        own = own_column[...]
        for i in range(0, SIDE, 2):
            two = jnp.concatenate([spread[i : i + 1, :] * own, spread[i + 1 : i + 2, :] * own], 0)
            kh[i * SIDE : i * SIDE + 2 * SIDE, :] = two.astype(BF16)
        if not backward:
            i_r, j_r = one_hots(ROWS)
            wb = pack[k, WBIAS : WBIAS + 1, 0:SIDE]
            hb = pack[k, HBIAS : HBIAS + 1, 0:SIDE]
            wbcol[...] = jnp.sum(jnp.where(j_r, wb, 0.0), 1, keepdims=True)
            hbcol[...] = jnp.sum(jnp.where(i_r, hb, 0.0), 1, keepdims=True)

    stored = ((hidden, sp_hidden), (gp, sp_gp), (joined, sp_joined), (normal, sp_normal), (xl, sp_xl))

    def spill(t):
        return [pltpu.make_async_copy(v.at[t], h.at[t], spill_sems.at[t, n]) for n, (v, h) in enumerate(stored)]

    def fetch(t):
        return [pltpu.make_async_copy(h.at[t], v.at[t], fetch_sems.at[t, n]) for n, (v, h) in enumerate(stored)]

    def forward_stage(t, k):
        z = 2 * k + t

        @pl.when(k == 1)
        def _():
            for copy in spill(t):
                copy.wait()

        wait_stats(z)
        mean, scale = norm_stats(z)
        gain = pack[k, BGAIN : BGAIN + 1, :]
        bias = pack[k, BBIAS : BBIAS + 1, :]

        def standardize(start, carry):
            for o in range(0, GROUP, TILE):
                rows = pl.ds(start + o, TILE)
                x = (cv[z, rows, :] - mean) * scale
                cv[z, rows, :] = x
                joined[t, rows, 2 * C : 3 * C] = ((x * gain + bias) * mask_cols[t, rows, :]).astype(BF16)
            along = dot(kw[...], joined[t, pl.ds(start, GROUP), 2 * C : 3 * C])
            for o in range(0, GROUP, TILE):
                rows = pl.ds(start + o, TILE)
                joined[t, rows, 0:C] = (along[o : o + TILE] + wbcol[rows, :]).astype(BF16)
            return carry
        groups(standardize, 0)

        m_bias = pack[k, MBIAS : MBIAS + 1, :]
        n_gain = pack[k, NGAIN : NGAIN + 1, :]
        n_bias = pack[k, NBIAS : NBIAS + 1, :]
        d_bias = pack[k, DBIAS : DBIAS + 1, :]
        u_bias = [pack[k, UBIAS + n : UBIAS + n + 1, 0:FT] for n in range(FF // FT)]

        def rest(start, carry):
            rows = pl.ds(start, GROUP)
            along = dot(kh[rows, :], joined[t, :, 2 * C : 3 * C])
            for o in range(0, GROUP, TILE):
                part = pl.ds(start + o, TILE)
                joined[t, part, C : 2 * C] = (along[o : o + TILE] + hbcol[part, :]).astype(BF16)
            merged = dot(joined[t, rows, :], wm[k], (1, 1))
            for o in range(0, GROUP, TILE):
                part = pl.ds(start + o, TILE)
                f = uf[t, pl.ds(start + SIDE + o, TILE), :] + merged[o : o + TILE] + m_bias
                d = f - jnp.mean(f, 1, keepdims=True)
                rs = lax.rsqrt(jnp.mean(d * d, 1, keepdims=True) + EPS)
                x = d * rs
                first[part, :] = f
                rstd[z, part, :] = rs
                xl[t, part, :] = x.astype(BF16)
                normal[t, part, :] = (x * n_gain + n_bias).astype(BF16)
            norm = normal[t, rows, :]
            pre = dot(norm, wu[k, :, 0:FT])
            for n in range(FF // FT):
                cols = slice(n * FT, n * FT + FT)
                now = pre
                if n + 1 < FF // FT:
                    pre = dot(norm, wu[k, :, n * FT + FT : n * FT + 2 * FT])
                for o in range(0, GROUP, TILE):
                    part = pl.ds(start + o, TILE)
                    h, dh = gelu_both(now[o : o + TILE] + u_bias[n])
                    hidden[t, part, cols] = h.astype(BF16)
                    gp[t, part, cols] = dh.astype(BF16)
            down = dot(hidden[t, rows, :], wd[k], (1, 1))
            i = lax.div(start, SIDE)
            for r in range(GROUP // SIDE):
                y = first[pl.ds(start + r * SIDE, SIDE), :] + down[r * SIDE : r * SIDE + SIDE] + d_bias
                ybuf[z, i + r] = y.astype(BF16)
            return carry
        groups(rest, 0)

        @pl.when(k == 0)
        def _():
            def reread(start, carry):
                uf[t, pl.ds(start + SIDE, SIDE), :] = ybuf[z, lax.div(start, SIDE)].astype(F32)
                return carry
            grid_rows(reread, 0)

        @pl.when(me_p == k)
        def _():
            pltpu.make_async_copy(ybuf.at[z], so_h.at[0, 2 * me_p + t], so_local.at[t]).start()

        @pl.when(me_p != k)
        def _():
            across(ybuf.at[z], so_h.at[0, 2 * me_p + t], so_send.at[t], so_recv.at[t]).start()

    def backward_stage(t, k, tick):
        z = 2 * k + t
        zero = jnp.zeros((8, C), F32)
        n_gain = pack[k, NGAIN : NGAIN + 1, :]

        d_acc = zero
        for o in range(0, ROWS, TILE):
            g = gf[t, o : o + TILE, :]
            gb[o : o + TILE, :] = g.astype(BF16)
            d_acc = d_acc + fold(g)
        gs[k, DBIAS : DBIAS + 1, :] += total(d_acc)
        gbt[...] = gb[...].T
        for n in range(2):
            acc_d[k, n] += dot(gbt[...], hidden[t, :, n * WIDE : n * WIDE + WIDE])
        tick(1)

        def chain(start, acc):
            rows = pl.ds(start, GROUP)
            x_acc, n_acc, m_acc, u_acc = acc
            u_acc = list(u_acc)
            low = gb[rows, :]
            raw = dot(low, wd[k, :, 0:FT])
            for n in range(FF // FT):
                cols = slice(n * FT, n * FT + FT)
                now = raw
                if n + 1 < FF // FT:
                    raw = dot(low, wd[k, :, n * FT + FT : n * FT + 2 * FT])
                for o in range(0, GROUP, TILE):
                    part = pl.ds(start + o, TILE)
                    gpn = (now[o : o + TILE] * gp[t, part, cols].astype(F32)).astype(BF16)
                    gpre[part, cols] = gpn
                    u_acc[n] = u_acc[n] + fold(gpn.astype(F32))
            back = dot(gpre[rows, :], wu[k], (1, 1))
            for o in range(0, GROUP, TILE):
                part = pl.ds(start + o, TILE)
                g = back[o : o + TILE]
                x = xl[t, part, :].astype(F32)
                gn = g * n_gain
                mean_g = jnp.mean(gn, 1, keepdims=True)
                mean_gx = jnp.mean(gn * x, 1, keepdims=True)
                out = gf[t, part, :] + rstd[z, part, :] * (gn - mean_g - x * mean_gx)
                gf[t, part, :] = out
                low = out.astype(BF16)
                gmb[part, :] = low
                x_acc = x_acc + fold(g * x)
                n_acc = n_acc + fold(g)
                m_acc = m_acc + fold(low.astype(F32))
            low = gmb[rows, :]
            g_w = dot(low, wm[k, :, 0:C])
            g_h = dot(low, wmid[k])
            for o in range(0, GROUP, TILE):
                part = pl.ds(start + o, TILE)
                one = g_w[o : o + TILE].astype(BF16)
                gwb[o : o + TILE, :] = one
                wcol[part, :] += jnp.sum(one.astype(F32), 1, keepdims=True)
                one = g_h[o : o + TILE].astype(BF16)
                gwh[part, :] = one
                hcol[part, :] += jnp.sum(one.astype(F32), 1, keepdims=True)
            third = dot(low, wm[k, :, 2 * C : 3 * C])
            crossed = dot(kw[...], gwb[...])
            for o in range(0, GROUP, TILE):
                gmix[t, pl.ds(start + o, TILE), :] = third[o : o + TILE] + crossed[o : o + TILE]
            gw_acc[...] += dot(gwb[...], joined[t, rows, 2 * C : 3 * C], (1, 1))
            return (x_acc, n_acc, m_acc, u_acc)
        acc = groups(chain, (zero, zero, zero, [jnp.zeros((8, FT), F32) for _ in range(FF // FT)]))
        tick(4)
        gs[k, NGAIN : NGAIN + 1, :] += total(acc[0])
        gs[k, NBIAS : NBIAS + 1, :] += total(acc[1])
        gs[k, MBIAS : MBIAS + 1, :] += total(acc[2])
        for n in range(FF // FT):
            gs[k, UBIAS + n : UBIAS + n + 1, 0:FT] += total(acc[3][n])
        gbt[...] = normal[t].T
        for n in range(2):
            acc_u[k, n] += dot(gbt[...], gpre[:, n * WIDE : n * WIDE + WIDE])
        tick(5)
        gbt[...] = gmb[...].T
        for n in range(2):
            width = min(MT, 3 * C - n * MT)
            acc_m[k, n, :, 0:width] += dot(gbt[...], joined[t, :, n * MT : n * MT + width])
        tick(6)
        gh_acc[...] += dot(gwh[...], joined[t, :, 2 * C : 3 * C], (1, 1))
        tick(10)

        def batch_sums(start, acc):
            plain, cross = acc
            crossed = dot(kh[pl.ds(start, GROUP), :], gwh[...])
            for o in range(0, GROUP, TILE):
                rows = pl.ds(start + o, TILE)
                g = (gmix[t, rows, :] + crossed[o : o + TILE]) * mask_cols[t, rows, :]
                gmix[t, rows, :] = g
                plain = plain + fold(g)
                cross = cross + fold(g * cv[z, rows, :])
            return plain, cross
        acc = groups(batch_sums, (zero, zero))
        plain, cross = total(acc[0]), total(acc[1])
        gs[k, BBIAS : BBIAS + 1, :] += plain
        gs[k, BGAIN : BGAIN + 1, :] += cross
        r = 4 + z
        msg[r, 0:1, 0:C] = plain
        msg[r, 1:2, 0:C] = cross
        send_stats(r)

    def input_stage(t, k, tick):
        z = 2 * k + t
        r = 4 + z
        wait_stats(r)
        scale, count = stat[z, 0:1, :], stat[z, 1:2, :]
        both = gather_stats(r)
        plain, cross = both[0:1, 0:C], both[1:2, 0:C]
        gain = pack[k, BGAIN : BGAIN + 1, :]
        out_scale = gain * scale
        plain = plain / count
        cross = cross / count

        def shifted(start, carry):
            rows = pl.ds(start, SIDE)
            g = (gmix[t, rows, :] - plain - cv[z, rows, :] * cross) * (mask_cols[t, rows, :] * out_scale)
            rows = pl.ds(start + SIDE, SIDE)
            gsh[0, rows, :] = sooner(g)
            gsh[1, rows, :] = g
            gsh[2, rows, :] = later(g)
            return carry
        grid_rows(shifted, 0)
        tick(8)
        taps = [[pack[k, CONV + n : CONV + n + 1, l:m] for n in range(9)] for l, m in LANES]

        def pull(start, acc):
            new = []
            for (l, m), tap, one in zip(LANES, taps, acc):
                u = [uf[t, pl.ds(start + SIDE * r, SIDE), l:m] for r in range(3)]
                out = gf[t, pl.ds(start, SIDE), l:m]
                sums = []
                for s in range(3):
                    around = [gsh[s, pl.ds(start + SIDE * r, SIDE), l:m] for r in range(3)]
                    out = out + around[2] * tap[s] + around[1] * tap[3 + s] + around[0] * tap[6 + s]
                    sums.append([one[s][r] + fold(around[1] * u[r]) for r in range(3)])
                new.append(sums)
                igbuf[z, lax.div(start, SIDE), :, l:m] = out.astype(BF16)
            return new
        acc = grid_rows(pull, [[[jnp.zeros((8, m - l), F32) for _ in range(3)] for _ in range(3)] for l, m in LANES])
        for (l, m), one in zip(LANES, acc):
            for r in range(3):
                for s in range(3):
                    row = CONV + 3 * r + s
                    gs[k, row : row + 1, l:m] += total(one[s][r])

        @pl.when(k == 1)
        def _():
            def reread(start, carry):
                gf[t, pl.ds(start, SIDE), :] = igbuf[z, lax.div(start, SIDE)].astype(F32)
                return carry
            grid_rows(reread, 0)

        @pl.when(me_p == k)
        def _():
            pltpu.make_async_copy(igbuf.at[z], ig_h.at[0, 2 * me_p + t], ig_local.at[t]).start()

        @pl.when(me_p != k)
        def _():
            across(igbuf.at[z], ig_h.at[0, 2 * me_p + t], ig_send.at[t], ig_recv.at[t]).start()

    def clear_mix():
        gw_acc[...] = jnp.zeros(gw_acc.shape, F32)
        gh_acc[...] = jnp.zeros(gh_acc.shape, F32)
        wcol[...] = jnp.zeros(wcol.shape, F32)
        hcol[...] = jnp.zeros(hcol.shape, F32)

    def close_mix(k):
        i_r, j_r = one_hots(ROWS)
        _, j_g = one_hots(GROUP)
        gs[k, WBIAS : WBIAS + 1, 0:SIDE] = total(jnp.where(j_r, wcol[...], 0.0))
        gs[k, HBIAS : HBIAS + 1, 0:SIDE] = total(jnp.where(i_r, hcol[...], 0.0))
        highest = lax.Precision.HIGHEST
        p = grid_row(lax.broadcasted_iota(jnp.int32, (GROUP, GROUP), 0))
        q = grid_row(lax.broadcasted_iota(jnp.int32, (GROUP, GROUP), 1))
        own = jnp.where(p == q, gw_acc[...], 0.0)
        own = jnp.sum(own.reshape(GROUP // SIDE, SIDE, GROUP), 0)
        gs[k, WW : WW + SIDE, 0:SIDE] = dot(own, jnp.where(j_g, 1.0, 0.0), precision=highest)
        i_f = jnp.where(i_r, 1.0, 0.0)
        for i in range(SIDE):
            rows = slice(i * SIDE, i * SIDE + SIDE)
            own = total(fold(own_column[...] * gh_acc[rows, :]))
            first[i : i + 1, :] = own[:, 0:C]
            gnorm[i : i + 1, 0 : ROWS - C] = own[:, C:ROWS]
        value = dot(first[0:SIDE, :], i_f[0:C, :], precision=highest)
        value += dot(gnorm[0:SIDE, 0 : ROWS - C], i_f[C:ROWS, :], precision=highest)
        gs[k, HW : HW + SIDE, 0:SIDE] = value

    bits = [1, 2]
    while 2 * bits[-1] < n_dp:
        bits.append(2 * bits[-1])
    n_swaps = len(bits) - 2
    n_steps = 1 + 2 + n_swaps + 2

    def partner(bit):
        return me_d + bit * (1 - 2 * lax.rem(me_d // bit, 2))

    def side(bit):
        return lax.rem(me_d // bit, 2)

    def along(bit, src, dst, send, recv):
        return pltpu.make_async_remote_copy(
            src_ref=src, dst_ref=dst, send_sem=send, recv_sem=recv,
            device_id={"dp": partner(bit)}, device_id_type=MESH)

    streams = (
        (acc_d, gd_h, sb_d, lb_d, rl_d), (acc_u, gu_h, sb_u, lb_u, rl_u), (acc_m, gm_h, sb_m, lb_m, rl_m))

    def reduction(k, which):
        acc, out_h, sb, lb, rl = streams[which]
        sb, lb, rl = sb.at[k], lb.at[k], rl.at[k]
        halving = [1 + me_p, 2 - me_p] if which != 1 else [2 - me_p, 1 + me_p]

        def sems(step):
            return red_send.at[3 * k + which, step], red_recv.at[3 * k + which, step]

        def own(q):
            return k, lax.div(q, 2), pl.ds(pl.multiple_of(me_p * HALF + lax.rem(q, 2) * SHARD, 16), SHARD), slice(None)

        def each(count, body):
            if count == 1:
                body(0)
                return

            def step(n, carry):
                body(n)
                return carry
            lax.fori_loop(0, count, step, 0)

        in_chip = across(sb.at[pl.ds(0, SHARDS)], lb, *sems(0))
        base = [0]
        for n, bit in enumerate(halving):
            base.append(base[n] + side(bit) * (2 >> n))
        mine = base[2]

        def half_copy(n):
            count, at = 2 >> n, 2 * n
            return along(halving[n], sb.at[pl.ds(at, count)], rl.at[pl.ds(at, count)], *sems(1 + n))

        def swap_copy(n):
            return along(bits[2 + n], sb.at[3 + n], rl.at[3 + n], *sems(3 + n))

        def double_copy(n):
            count = 2 >> n
            here = lb.at[pl.ds(base[n + 1], count)]
            return along(halving[n], here, here, *sems(n_steps - 1 - n))

        def send_half(n, landed):
            count, at = 2 >> n, 2 * n
            give = base[n] + (1 - side(halving[n])) * count
            keep = base[n + 1]

            def one(q):
                sb[at + q] = (acc[own(give + q)] + landed(give + q).astype(F32)).astype(BF16)
            each(count, one)
            half_copy(n).start()

            def two(q):
                acc[own(keep + q)] += landed(keep + q).astype(F32)
            each(count, two)

        def start():
            def one(q):
                rows = pl.ds(pl.multiple_of(other * HALF + lax.rem(q, 2) * SHARD, 16), SHARD)
                sb[q] = acc[k, lax.div(q, 2), rows, :].astype(BF16)
            each(SHARDS, one)
            in_chip.start()

        def first_half():
            in_chip.wait()
            send_half(0, lambda q: lb[q])

        def second_half():
            half_copy(0).wait()
            send_half(1, lambda q: rl[q - base[1]])

        def swap(n):
            def run():
                if n == 0:
                    half_copy(1).wait()
                    sb[3] = (acc[own(mine)] + rl[2].astype(F32)).astype(BF16)
                else:
                    swap_copy(n - 1).wait()
                    sb[3 + n] = (sb[2 + n].astype(F32) + rl[2 + n].astype(F32)).astype(BF16)
                swap_copy(n).start()
            return run

        def double(n):
            def run():
                if n == 1:
                    last = n_swaps - 1
                    swap_copy(last).wait()
                    lb[mine] = (sb[3 + last].astype(F32) + rl[3 + last].astype(F32)).astype(BF16)
                else:
                    double_copy(n + 1).wait()
                double_copy(n).start()
            return run

        def hand_over():
            double_copy(0).wait()

            @pl.when(me_p == k)
            def _():
                pltpu.make_async_copy(lb, out_h.at[me_p], out_local.at[which]).start()

            @pl.when(me_p != k)
            def _():
                across(lb, out_h.at[me_p], out_send.at[which], out_recv.at[which]).start()

        return [start, first_half, second_half] + [swap(n) for n in range(n_swaps)] + [double(1), double(0), hand_over]

    def small_sum(rows, landing, send, recv):
        count = rows.stop - rows.start
        rows = pl.ds(rows.start, count)
        in_chip = across(gs.at[other, rows], landing.at[0], send.at[0], recv.at[0])

        def swap_copy(n):
            return along(bits[n], gs.at[me_p, rows], landing.at[1 + n], send.at[1 + n], recv.at[1 + n])

        def step(n):
            def run():
                (swap_copy(n - 1) if n else in_chip).wait()
                gs[me_p, rows, :] += landing[n]
                if n < len(bits):
                    swap_copy(n).start()
            return run
        return [in_chip.start] + [step(n) for n in range(len(bits) + 1)]

    small = small_sum(slice(SMALL, PACK), small_land, small_send, small_recv)
    taps_sum = small_sum(slice(0, SMALL), conv_land, conv_send, conv_recv)

    plan = {}
    backward_places, input_places = [0, 1, 4, 5, 6, 10, 11], [7, 8, 9]
    order = []
    for n in range(6):
        order += [(n, p) for p in input_places] if n > 1 else []
        order += [(n, p) for p in backward_places] if n < 4 else []

    def put(start, steps, gap):
        at = order.index(start)
        steps = list(steps)
        while steps and at < len(order):
            plan.setdefault(order[at], []).append(steps.pop(0))
            at += gap
        return steps

    for which, place in enumerate((1, 5, 6)):
        assert not put((1, place), reduction(1, which), 2 if n_swaps < 3 else 1)
    tails = [put((3, place), reduction(0, which), 1) for which, place in enumerate((1, 5, 6))]
    tails.append(put((4, 7), small, 1))
    tails.append(list(taps_sum))

    pack_over.wait()
    for t in range(2):
        image_in[t].wait()

    def widen_image(t):
        def widen(i, inner):
            uf[t, pl.ds(pl.multiple_of(i * SIDE + SIDE, SIDE), SIDE), :] = ub[t, i].astype(F32)
            return inner
        lax.fori_loop(0, SIDE, widen, 0)

    def start_image(t, carry):
        widen_image(t)
        conv_stage(t, 0)
        return carry
    lax.fori_loop(0, 2, start_image, 0)
    for t in range(2):
        grad_in[t].start()

    for copy in weights_in + weights_over:
        copy.wait()
    for k in range(2):
        wmid[k] = wm[k, :, C : 2 * C]

    def forward_block(k, carry):
        mixers(k, False)

        def one(t, inner):
            forward_stage(t, k)

            @pl.when(k == 0)
            def _():
                for copy in spill(t):
                    copy.start()
                conv_stage(t, 1)
            return inner
        lax.fori_loop(0, 2, one, 0)
        return carry
    lax.fori_loop(0, 2, forward_block, 0)

    for t in range(2):
        grad_in[t].wait()
        pltpu.make_async_copy(ybuf.at[t], so_h.at[0, t], so_local.at[t]).wait()
        across(ybuf.at[t], so_h.at[0, t], so_send.at[t], so_recv.at[t]).wait_send()

    def load_grad(t, carry):
        def widen(i, inner):
            gf[t, pl.ds(pl.multiple_of(i * SIDE, SIDE), SIDE), :] = ub[t, i].astype(F32)
            return inner
        lax.fori_loop(0, SIDE, widen, 0)
        return carry
    lax.fori_loop(0, 2, load_grad, 0)
    for t in range(2):
        image_copy(t, again_sems.at[t]).start()

    def turn(s, carry):
        t = lax.rem(s, 2)

        def tick(place):
            for n in range(6):
                steps = plan.get((n, place), [])
                if steps:
                    @pl.when(s == n)
                    def _():
                        for step in steps:
                            step()

        @pl.when(lax.rem(s, 2) == 0)
        def _():
            @pl.when(s > 0)
            def _():
                close_mix(2 - lax.div(s, 2))

            @pl.when(s < 4)
            def _():
                mixers(1 - lax.div(s, 2), True)
                clear_mix()

        @pl.when(s > 1)
        def _():
            @pl.when(s > 3)
            def _():
                image_copy(t, again_sems.at[t]).wait()
                widen_image(t)
            tick(7)
            input_stage(t, 2 - lax.div(s, 2), tick)
            tick(9)

        @pl.when(s < 4)
        def _():
            @pl.when(s > 1)
            def _():
                for copy in fetch(t):
                    copy.wait()
            tick(0)
            backward_stage(t, 1 - lax.div(s, 2), tick)
            tick(11)

            @pl.when(s < 2)
            def _():
                for copy in fetch(t):
                    copy.start()
        return carry
    lax.fori_loop(0, 6, turn, 0)

    while any(tails):
        for steps in tails:
            if steps:
                steps.pop(0)()

    gs_out = pltpu.make_async_copy(gs.at[me_p], gs_h, gs_sem.at[0])
    gs_out.start()
    for t in range(2):
        pltpu.make_async_copy(igbuf.at[t], ig_h.at[0, t], ig_local.at[t]).wait()
        across(ybuf.at[t], so_h.at[0, t], so_send.at[t], so_recv.at[t]).wait_recv()
        across(igbuf.at[t], ig_h.at[0, t], ig_send.at[t], ig_recv.at[t]).wait()
    for n, (_, out_h, _, lb, _) in enumerate(streams):
        pltpu.make_async_copy(lb.at[0], out_h.at[0], out_local.at[n]).wait()
        across(lb.at[0], out_h.at[0], out_send.at[n], out_recv.at[n]).wait()
    gs_out.wait()


def finish_kernel(
    so_in, ig_in, gd_in, gu_in, gm_in, gs,
    so, ig, conv, bgain, bbias, ww, wb, hw, hb, gm, mbias, ngain, nbias, gu, ubias, gd, dbias,
    large, d_in, u_in, m_in, d_out, u_out, m_out, in_sems, out_sems,
):
    images = [(n, i) for i in range(so_in.shape[1]) for n in range(2)]
    moved = [(gd_in, d_in), (gu_in, u_in), (gm_in, m_in)] + [
        ((so_in, ig_in)[n].at[0, i], large.at[n, 0, i]) for n, i in images]
    arrive = [pltpu.make_async_copy(src, dst, in_sems.at[n]) for n, (src, dst) in enumerate(moved)]
    for copy in arrive[3:] + arrive[:3]:
        copy.start()
    moved = [(d_out, gd), (u_out, gu), (m_out, gm)] + [(large.at[n, 0, i], (so, ig)[n].at[0, i]) for n, i in images]
    leave = [pltpu.make_async_copy(src, dst, out_sems.at[n]) for n, (src, dst) in enumerate(moved)]
    for n in range(9):
        conv[n] = gs[CONV + n : CONV + n + 1, :]
    for row, ref in ((BGAIN, bgain), (BBIAS, bbias), (MBIAS, mbias), (NGAIN, ngain), (NBIAS, nbias), (DBIAS, dbias)):
        ref[...] = gs[row : row + 1, :]
    for row, ref in ((WBIAS, wb), (HBIAS, hb)):
        ref[...] = gs[row : row + 1, 0:SIDE]
    for n in range(FF // FT):
        ubias[:, n * FT : n * FT + FT] = gs[UBIAS + n : UBIAS + n + 1, 0:FT]
    for row, ref in ((WW, ww), (HW, hw)):
        ref[0] = gs[row : row + SIDE, 0:SIDE]
    for n in range(3, len(arrive)):
        arrive[n].wait()
        leave[n].start()
    for n, (src, dst, piece) in enumerate(((d_in, d_out, WIDE), (u_in, u_out, WIDE), (m_in, m_out, MT))):
        arrive[n].wait()
        for p in range(2):
            for q in range(SHARDS):
                start, at = p * HALF + (q % 2) * SHARD, piece * (q // 2)
                width = min(piece, dst.shape[1] - at)
                dst[start : start + SHARD, at : at + width] = src[p, q, :, 0:width].astype(F32)
        leave[n].start()
    for copy in leave:
        copy.wait()


def on_device(
    images, masks, conv_weight, batch_gain, batch_bias, width_weight, width_bias,
    height_weight, height_bias, merge_weight, merge_bias, norm_gain, norm_bias,
    up_weight, up_bias, down_weight, down_bias, out_grad,
):
    n_dp = lax.axis_size("dp")
    micro = images.shape[0]
    steps = max(n_dp.bit_length() - 1, 4)
    any_space = pl.BlockSpec(memory_space=pl.ANY)
    vmem = pl.BlockSpec(memory_space=pltpu.VMEM)
    dma = pltpu.SemaphoreType.DMA
    grid = (SIDE, SIDE, C)
    shape = jax.ShapeDtypeStruct
    outs = pl.pallas_call(
        functools.partial(kernel, n_dp),
        out_shape=(
            shape((1, micro) + grid, BF16),
            shape((1, micro) + grid, BF16),
            shape((2, SHARDS, SHARD, WIDE), BF16),
            shape((2, SHARDS, SHARD, WIDE), BF16),
            shape((2, SHARDS, SHARD, MT), BF16),
            shape((PACK, C), F32),
            shape((2, ROWS, FF), BF16),
            shape((2, ROWS, FF), BF16),
            shape((2, ROWS, 3 * C), BF16),
            shape((2, ROWS, C), BF16),
            shape((2, ROWS, C), BF16),
        ),
        in_specs=[any_space] + [vmem] * 8 + [any_space] + [vmem] * 3 + [any_space, vmem, any_space, vmem, any_space],
        out_specs=(any_space,) * 11,
        scratch_shapes=[
            pltpu.VMEM((2, ROWS, 1), F32),
            pltpu.VMEM((4, 2, C), F32),
            pltpu.VMEM((SIDE, ROWS), F32),
            pltpu.VMEM((ROWS, SIDE), BF16),
            pltpu.VMEM((2, PACK, C), F32),
            pltpu.VMEM((2, C, 3 * C), BF16),
            pltpu.VMEM((2, C, C), BF16),
            pltpu.VMEM((2, C, FF), BF16),
            pltpu.VMEM((2, C, FF), BF16),
            pltpu.VMEM((2,) + grid, BF16),
            pltpu.VMEM((2, ROWS + 2 * SIDE, C), F32),
            pltpu.VMEM((4, ROWS, C), F32),
            pltpu.VMEM((2, ROWS, 3 * C), BF16),
            pltpu.VMEM((2, ROWS, C), BF16),
            pltpu.VMEM((2, ROWS, C), BF16),
            pltpu.VMEM((4, ROWS, 1), F32),
            pltpu.VMEM((2, ROWS, FF), BF16),
            pltpu.VMEM((2, ROWS, FF), BF16),
            pltpu.VMEM((2, ROWS, C), F32),
            pltpu.VMEM((ROWS, C), BF16),
            pltpu.VMEM((ROWS, C), BF16),
            pltpu.VMEM((GROUP, C), BF16),
            pltpu.VMEM((C, ROWS), BF16),
            pltpu.VMEM((ROWS, FF), BF16),
            pltpu.VMEM((2, ROWS, C), F32),
            pltpu.VMEM((ROWS, C), BF16),
            pltpu.VMEM((3, ROWS + 2 * SIDE, C), F32),
            pltpu.VMEM((GROUP, GROUP), BF16),
            pltpu.VMEM((ROWS, ROWS), BF16),
            pltpu.VMEM((ROWS, 1), F32),
            pltpu.VMEM((ROWS, 1), F32),
            pltpu.VMEM((GROUP, GROUP), F32),
            pltpu.VMEM((ROWS, ROWS), F32),
            pltpu.VMEM((ROWS, 1), F32),
            pltpu.VMEM((ROWS, 1), F32),
            pltpu.VMEM((4,) + grid, BF16),
            pltpu.VMEM((8, 2, CP), F32),
            pltpu.VMEM((8, n_dp - 1, 2, CP), F32),
            pltpu.VMEM((2, 2, C, WIDE), F32),
            pltpu.VMEM((2, 2, C, WIDE), F32),
            pltpu.VMEM((2, 2, C, MT), F32),
            pltpu.VMEM((2, PACK, C), F32),
            pltpu.VMEM((2, 1 + steps, SHARD, WIDE), BF16),
            pltpu.VMEM((2, SHARDS, SHARD, WIDE), BF16),
            pltpu.VMEM((2, 1 + steps, SHARD, WIDE), BF16),
            pltpu.VMEM((2, 1 + steps, SHARD, WIDE), BF16),
            pltpu.VMEM((2, SHARDS, SHARD, WIDE), BF16),
            pltpu.VMEM((2, 1 + steps, SHARD, WIDE), BF16),
            pltpu.VMEM((2, 1 + steps, SHARD, MT), BF16),
            pltpu.VMEM((2, SHARDS, SHARD, MT), BF16),
            pltpu.VMEM((2, 1 + steps, SHARD, MT), BF16),
            pltpu.VMEM((1 + steps, PACK - SMALL, C), F32),
            pltpu.VMEM((1 + steps, SMALL, C), F32),
            dma((9,)), dma((2,)), dma((2,)), dma((3,)), dma((3,)), dma((8,)), dma((8,)),
            dma((2,)), dma((2,)), dma((2,)), dma((2,)), dma((2,)), dma((2,)), dma((2, 5)), dma((2, 5)),
            dma((6, 3 + steps)), dma((6, 3 + steps)), dma((1 + steps,)), dma((1 + steps,)),
            dma((1 + steps,)), dma((1 + steps,)), dma((3,)), dma((3,)), dma((3,)), dma((1,)),
        ],
        compiler_params=pltpu.CompilerParams(
            collective_id=0, has_side_effects=True, vmem_limit_bytes=65400 * 1024),
    )(
        images, masks, conv_weight, batch_gain, batch_bias, width_weight, width_bias, height_weight, height_bias,
        merge_weight[0].T, merge_bias, norm_gain, norm_bias, up_weight[0], up_bias, down_weight[0].T, down_bias, out_grad)

    row = shape((1, C), F32)
    square, line = shape((1, SIDE, SIDE), F32), shape((1, SIDE), F32)
    so, ig, conv, bgain, bbias, ww, wb, hw, hb, gm, mbias, ngain, nbias, gu, ubias, gd, dbias = pl.pallas_call(
        finish_kernel,
        out_shape=(
            shape((1, micro) + grid, BF16), shape((1, micro) + grid, BF16), shape((9, 1, C), F32), row, row,
            square, line, square, line, shape((C, 3 * C), F32), row, row, row,
            shape((C, FF), F32), shape((1, FF), F32), shape((C, FF), F32), row),
        in_specs=[any_space] * 5 + [vmem],
        out_specs=(any_space,) * 2 + (vmem,) * 7 + (any_space,) + (vmem,) * 3 + (any_space, vmem, any_space, vmem),
        scratch_shapes=[
            pltpu.VMEM((2, 1, micro) + grid, BF16),
            pltpu.VMEM((2, SHARDS, SHARD, WIDE), BF16),
            pltpu.VMEM((2, SHARDS, SHARD, WIDE), BF16),
            pltpu.VMEM((2, SHARDS, SHARD, MT), BF16),
            pltpu.VMEM((C, FF), F32),
            pltpu.VMEM((C, FF), F32),
            pltpu.VMEM((C, 3 * C), F32),
            dma((3 + 2 * micro,)), dma((3 + 2 * micro,)),
        ],
        compiler_params=pltpu.CompilerParams(vmem_limit_bytes=65400 * 1024),
    )(*outs[:6])
    return (
        so, ig, jnp.swapaxes(conv, 0, 1), bgain, bbias, ww, wb, hw, hb, gm.T[None], mbias, ngain, nbias,
        gu[None], ubias, gd.T[None], dbias)


def solution(mesh):
    data4 = P("dp", None, None, None)
    p1, p2, p3 = P("pipe"), P("pipe", None), P("pipe", None, None)
    out5 = P("pipe", "dp", None, None, None)
    return jax.shard_map(
        on_device,
        mesh=mesh,
        in_specs=(data4, P("dp", None, None), p3, p2, p2, p3, p2, p3, p2, p3, p2, p2, p2, p3, p2, p3, p2, data4),
        out_specs=(out5, out5, p3, p2, p2, p3, p2, p3, p2, p3, p2, p2, p2, p3, p2, p3, p2),
        check_vma=False,
    )
```

```python
import functools

import jax
import jax.numpy as jnp
from jax import lax
from jax.experimental import pallas as pl
from jax.experimental.pallas import tpu as pltpu
from jax.sharding import PartitionSpec as P

EPS = 1e-05
MESH = pl.DeviceIdType.MESH
F32 = jnp.float32
BF16 = jnp.bfloat16

SIDE = 24
ROWS = SIDE * SIDE
C = 320
CP = 384
FF = 1280
FT = 256
CHUNK = 48
TILE = 32
LANES = ((0, 128), (128, 256), (256, 320))
GROUP = 8 * SIDE

HALF = C // 2
SHARD = HALF // 2
WIDE = FF // 2
SHARDS = 4
MT = 512
STEP = 24

CONV, BGAIN, BBIAS, MBIAS, NGAIN, NBIAS, DBIAS, WBIAS, HBIAS, UBIAS, WW, HW, PACK = (
    0, 16, 17, 18, 19, 20, 21, 22, 23, 24, 32, 56, 80)
SMALL = 16


def dot(a, b, contract=(1, 0), precision=None):
    return lax.dot_general(
        a, b, (((contract[0],), (contract[1],)), ((), ())),
        preferred_element_type=F32, precision=precision)


def in_turn(phases, starts):
    for step in range(len(phases) + len(starts) - 1):
        for g, start in enumerate(starts):
            if 0 <= step - g < len(phases):
                phases[step - g](start)


def fold(value):
    rows = value.shape[0]
    return jnp.sum(value.reshape(rows // 8, 8, value.shape[1]), 0)


def total(partial):
    return jnp.sum(partial, 0, keepdims=True)


def grid_row(index):
    return (index * 2731) >> 16


def one_hots(rows):
    place = lax.broadcasted_iota(jnp.int32, (rows, SIDE), 0)
    lane = lax.broadcasted_iota(jnp.int32, (rows, SIDE), 1)
    i = grid_row(place)
    return i == lane, place - SIDE * i == lane


def gelu_both(x):
    e = jnp.exp2(x * x * -0.7213475204444817)
    d = 1.0 + 0.23164189 * jnp.abs(x)
    t = pl.reciprocal(d, approx=True)
    t = t * (2.0 - d * t)
    poly = t * (0.127414796 + t * (-0.142248368 + t * (0.7107068705 + t * (-0.7265760135 + t * 0.5307027145))))
    tail = poly * e
    phi = jnp.where(x >= 0, 1.0 - tail, tail)
    return x * phi, phi + x * e * 0.3989422804014327


def kernel(
    n_dp,
    images, masks, conv_w, bgain, bbias, wwt, wb, hwt, hb, wm_h, mbias, ngain, nbias, wu_h, ubias, wd_h, dbias, og_h,
    so_h, ig_h, gd_h, gu_h, gm_h, gs_h, sp_hidden, sp_gp, sp_joined, sp_normal, sp_xl,
    mask_cols, stat, own_column, i_hot, pack, wm, wmid, wu, wd, ub, uf, cv, joined, normal, xl, rstd, hidden, gp,
    gf, gb, gmb, gwb, gbt, gmt, gpre, gmix, gwh, gsh, kw, kh, wbcol, hbcol,
    gw_acc, gh_acc, wcol, hcol, ybuf, msg, land, acc_d, acc_u, acc_m, gs,
    sb_d, lb_d, rl_d, sb_u, lb_u, rl_u, sb_m, lb_m, rl_m, small_land, conv_land,
    local_sems, again_sems, pack_sems, w_send, w_recv, st_send, st_recv,
    so_local, so_send, so_recv, ig_local, ig_send, ig_recv, spill_sems, fetch_sems,
    red_send, red_recv, small_send, small_recv, conv_send, conv_recv, out_local, out_send, out_recv, gs_sem,
):
    me_p = lax.axis_index("pipe")
    me_d = lax.axis_index("dp")
    other = 1 - me_p
    first = gsh.at[2, pl.ds(SIDE, ROWS)]
    igbuf = ybuf
    gnorm = gsh.at[0, pl.ds(SIDE, ROWS)]

    def image_copy(t, sems):
        return pltpu.make_async_copy(images.at[2 * me_p + t], ub.at[t], sems)

    image_in = [image_copy(t, local_sems.at[5 + t]) for t in range(2)]
    grad_in = [pltpu.make_async_copy(og_h.at[2 * me_p + t], ub.at[t], local_sems.at[7 + t]) for t in range(2)]
    weights = ((wm_h, wm), (wu_h, wu), (wd_h, wd))
    weights_in = [pltpu.make_async_copy(src, dst.at[me_p], local_sems.at[n]) for n, (src, dst) in enumerate(weights)]
    for copy in image_in + weights_in:
        copy.start()

    barrier = pltpu.get_barrier_semaphore()

    def greet(step, carry):
        pl.semaphore_signal(barrier, inc=1, device_id={"dp": lax.rem(me_d + step, n_dp)}, device_id_type=MESH)
        return carry

    lax.fori_loop(1, n_dp, greet, 0)
    pl.semaphore_signal(barrier, inc=1, device_id={"pipe": other}, device_id_type=MESH)

    pack[me_p] = jnp.zeros(pack.shape[1:], F32)
    pack[me_p, CONV : CONV + 9, :] = conv_w[0].astype(F32)
    for row, ref in ((BGAIN, bgain), (BBIAS, bbias), (MBIAS, mbias), (NGAIN, ngain), (NBIAS, nbias), (DBIAS, dbias)):
        pack[me_p, row : row + 1, :] = ref[...]
    for row, ref in ((WBIAS, wb), (HBIAS, hb)):
        pack[me_p, row : row + 1, 0:SIDE] = ref[...]
    for n in range(FF // FT):
        pack[me_p, UBIAS + n : UBIAS + n + 1, 0:FT] = ubias[:, n * FT : n * FT + FT]
    for row, ref in ((WW, wwt), (HW, hwt)):
        pack[me_p, row : row + SIDE, 0:SIDE] = ref[0].astype(F32)

    pl.semaphore_wait(barrier, n_dp)

    def across(src, dst, send, recv):
        return pltpu.make_async_remote_copy(
            src_ref=src, dst_ref=dst, send_sem=send, recv_sem=recv,
            device_id={"pipe": other}, device_id_type=MESH)

    pack_over = across(pack.at[me_p], pack.at[me_p], pack_sems.at[0], pack_sems.at[1])
    weights_over = [across(src, dst.at[me_p], w_send.at[n], w_recv.at[n]) for n, (src, dst) in enumerate(weights)]
    pack_over.start()
    for copy in weights_over:
        copy.start()

    msg[...] = jnp.zeros(msg.shape, F32)
    for k in range(2):
        for acc in (acc_d, acc_u, acc_m):
            for n in range(2):
                acc[k, n] = jnp.zeros(acc.shape[2:], F32)
        gs[k] = jnp.zeros(gs.shape[1:], F32)
    for n in range(2):
        uf[n, 0:SIDE, :] = jnp.zeros((SIDE, C), F32)
        uf[n, SIDE + ROWS : 2 * SIDE + ROWS, :] = jnp.zeros((SIDE, C), F32)
    for n in range(3):
        gsh[n, 0:SIDE, :] = jnp.zeros((SIDE, C), F32)
        gsh[n, SIDE + ROWS : 2 * SIDE + ROWS, :] = jnp.zeros((SIDE, C), F32)

    i_r, j_r = one_hots(ROWS)
    i_hot[...] = jnp.where(i_r, 1.0, 0.0).astype(BF16)
    q = lax.broadcasted_iota(jnp.int32, (SIDE, ROWS), 1)
    q = q - SIDE * grid_row(q)
    own_column[...] = jnp.where(lax.broadcasted_iota(jnp.int32, (SIDE, ROWS), 0) == q, 1.0, 0.0)
    for t in range(2):
        chosen = dot(i_hot[...], masks[2 * me_p + t].astype(F32).astype(BF16))
        mask_cols[t] = jnp.sum(jnp.where(j_r, chosen, 0.0), 1, keepdims=True)

    def later(value):
        at = lax.broadcasted_iota(jnp.int32, value.shape, 0)
        return jnp.where(at != 0, pltpu.roll(value, 1, 0), 0.0)

    def sooner(value):
        at = lax.broadcasted_iota(jnp.int32, value.shape, 0)
        return jnp.where(at != SIDE - 1, pltpu.roll(value, SIDE - 1, 0), 0.0)

    def grid_rows(body, init):
        def step(c, carry):
            for row in range(STEP):
                carry = body(pl.multiple_of(c * (STEP * SIDE), STEP * SIDE) + row * SIDE, carry)
            return carry
        return lax.fori_loop(0, SIDE // STEP, step, init)

    def groups(body, init):
        for g in range(ROWS // GROUP):
            init = body(g * GROUP, init)
        return init

    def send_stats(r):
        def one(step, carry):
            pltpu.make_async_remote_copy(
                src_ref=msg.at[r], dst_ref=land.at[r, n_dp - 1 - step],
                send_sem=st_send.at[r], recv_sem=st_recv.at[r],
                device_id={"dp": lax.rem(me_d + step, n_dp)}, device_id_type=MESH).start()
            return carry
        lax.fori_loop(1, n_dp, one, 0)

    def wait_stats(r):
        whole = pltpu.make_async_remote_copy(
            src_ref=land.at[r], dst_ref=land.at[r], send_sem=st_send.at[r], recv_sem=st_recv.at[r],
            device_id={"dp": lax.rem(me_d + 1, n_dp)}, device_id_type=MESH)
        whole.wait_send()
        whole.wait_recv()

    def conv_stage(t, k):
        z = 2 * k + t
        n_own = total(mask_cols[t])
        taps = [[pack[k, CONV + n : CONV + n + 1, l:m] for n in range(9)] for l, m in LANES]

        def conv(start, acc):
            at = pl.ds(start, SIDE)
            new = []
            for (l, m), tap, one in zip(LANES, taps, acc):
                rows = [uf[t, pl.ds(start + SIDE * r, SIDE), l:m] for r in range(3)]
                part = [rows[0] * tap[s] + rows[1] * tap[3 + s] + rows[2] * tap[6 + s] for s in range(3)]
                out = part[1] + later(part[0]) + sooner(part[2])
                cv[z, at, l:m] = out
                new.append(one + fold(out * mask_cols[t, at, :]))
            return new
        acc = grid_rows(conv, [jnp.zeros((8, m - l), F32) for l, m in LANES])
        sums = jnp.concatenate([total(one) for one in acc], 1)
        mean = sums / n_own

        def centred(start, acc):
            rows = pl.ds(start, SIDE)
            d = cv[z, rows, :] - mean
            return acc + fold(d * d * mask_cols[t, rows, :])

        m2 = total(grid_rows(centred, jnp.zeros((8, C), F32)))
        msg[z, 0:1, 0:C] = sums
        msg[z, 0:1, C:CP] = jnp.broadcast_to(n_own, (1, CP - C))
        msg[z, 1:2, 0:C] = m2
        send_stats(z)

    def peers(body, init):
        if n_dp > 16:
            return lax.fori_loop(0, n_dp - 1, body, init)
        for d in range(n_dp - 1):
            init = body(d, init)
        return init

    def gather_stats(r):
        def add(d, carry):
            return carry + land[r, d]
        return peers(add, msg[r])

    def norm_stats(z):
        sums = gather_stats(z)[0:1, :]
        count = sums[:, CP - 1 : CP]
        mean = sums[:, 0:C] / count

        def spread(values):
            n = values[0:1, CP - 1 : CP]
            off = values[0:1, 0:C] / n - mean
            return values[1:2, 0:C] + n * off * off

        def add(d, carry):
            return carry + spread(land[z, d])
        m2 = peers(add, spread(msg[z]))
        scale = lax.rsqrt(m2 / count + EPS)
        stat[z, 0:1, :] = scale
        stat[z, 1:2, :] = jnp.broadcast_to(count, (1, C))
        return mean, scale

    def mixers(k, backward):
        _, j_g = one_hots(GROUP)
        ww = pack[k, WW : WW + SIDE, 0:SIDE].astype(BF16)
        hw = pack[k, HW : HW + SIDE, 0:SIDE].astype(BF16)
        side_of = 0 if backward else 1
        j_b = jnp.where(j_g, 1.0, 0.0).astype(BF16)
        left = dot(j_b, ww, (1, 1 - side_of)).astype(BF16)
        p = grid_row(lax.broadcasted_iota(jnp.int32, (GROUP, GROUP), 0))
        q = grid_row(lax.broadcasted_iota(jnp.int32, (GROUP, GROUP), 1))
        kw[...] = jnp.where(p == q, dot(left, j_b, (1, 1)), 0.0).astype(BF16)
        spread = dot(hw, i_hot[...], (side_of, 1))
        own = own_column[...]
        for i in range(0, SIDE, 2):
            two = jnp.concatenate([spread[i : i + 1, :] * own, spread[i + 1 : i + 2, :] * own], 0)
            kh[i * SIDE : i * SIDE + 2 * SIDE, :] = two.astype(BF16)
        if not backward:
            i_r, j_r = one_hots(ROWS)
            wb = pack[k, WBIAS : WBIAS + 1, 0:SIDE]
            hb = pack[k, HBIAS : HBIAS + 1, 0:SIDE]
            wbcol[...] = jnp.sum(jnp.where(j_r, wb, 0.0), 1, keepdims=True)
            hbcol[...] = jnp.sum(jnp.where(i_r, hb, 0.0), 1, keepdims=True)

    stored = ((hidden, sp_hidden), (gp, sp_gp), (joined, sp_joined), (normal, sp_normal), (xl, sp_xl))

    def spill(t):
        return [pltpu.make_async_copy(v.at[t], h.at[t], spill_sems.at[t, n]) for n, (v, h) in enumerate(stored)]

    def fetch(t):
        return [pltpu.make_async_copy(h.at[t], v.at[t], fetch_sems.at[t, n]) for n, (v, h) in enumerate(stored)]

    def forward_stage(t, k):
        z = 2 * k + t

        @pl.when(k == 1)
        def _():
            for copy in spill(t):
                copy.wait()

        wait_stats(z)
        mean, scale = norm_stats(z)
        gain = pack[k, BGAIN : BGAIN + 1, :]
        bias = pack[k, BBIAS : BBIAS + 1, :]

        def standardize(start, carry):
            for o in range(0, GROUP, TILE):
                rows = pl.ds(start + o, TILE)
                x = (cv[z, rows, :] - mean) * scale
                cv[z, rows, :] = x
                joined[t, rows, 2 * C : 3 * C] = ((x * gain + bias) * mask_cols[t, rows, :]).astype(BF16)
            along = dot(kw[...], joined[t, pl.ds(start, GROUP), 2 * C : 3 * C])
            for o in range(0, GROUP, TILE):
                rows = pl.ds(start + o, TILE)
                joined[t, rows, 0:C] = (along[o : o + TILE] + wbcol[rows, :]).astype(BF16)
            return carry
        groups(standardize, 0)

        m_bias = pack[k, MBIAS : MBIAS + 1, :]
        n_gain = pack[k, NGAIN : NGAIN + 1, :]
        n_bias = pack[k, NBIAS : NBIAS + 1, :]
        d_bias = pack[k, DBIAS : DBIAS + 1, :]
        u_bias = [pack[k, UBIAS + n : UBIAS + n + 1, 0:FT] for n in range(FF // FT)]

        starts = [g * GROUP for g in range(ROWS // GROUP)]
        merged, down = {}, {}

        def mix(start):
            rows = slice(start, start + GROUP)
            along = dot(kh[rows, :], joined[t, :, 2 * C : 3 * C])
            for o in range(0, GROUP, TILE):
                part = slice(start + o, start + o + TILE)
                joined[t, part, C : 2 * C] = (along[o : o + TILE] + hbcol[part, :]).astype(BF16)
            merged[start] = dot(joined[t, rows, :], wm[k], (1, 1))

        def layer_norm(start):
            for o in range(0, GROUP, TILE):
                part = slice(start + o, start + o + TILE)
                f = uf[t, start + SIDE + o : start + SIDE + o + TILE, :] + merged[start][o : o + TILE] + m_bias
                d = f - jnp.mean(f, 1, keepdims=True)
                rs = lax.rsqrt(jnp.mean(d * d, 1, keepdims=True) + EPS)
                x = d * rs
                first[part, :] = f
                rstd[z, part, :] = rs
                xl[t, part, :] = x.astype(BF16)
                normal[t, part, :] = (x * n_gain + n_bias).astype(BF16)

        def activate(start):
            rows = slice(start, start + GROUP)
            norm = normal[t, rows, :]
            pre = dot(norm, wu[k, :, 0:FT])
            for n in range(FF // FT):
                cols = slice(n * FT, n * FT + FT)
                now = pre
                if n + 1 < FF // FT:
                    pre = dot(norm, wu[k, :, n * FT + FT : n * FT + 2 * FT])
                for o in range(0, GROUP, TILE):
                    part = slice(start + o, start + o + TILE)
                    h, dh = gelu_both(now[o : o + TILE] + u_bias[n])
                    hidden[t, part, cols] = h.astype(BF16)
                    gp[t, part, cols] = dh.astype(BF16)

        def project(start):
            down[start] = dot(hidden[t, start : start + GROUP, :], wd[k], (1, 1))

        def finish(start):
            for r in range(GROUP // SIDE):
                part = slice(start + r * SIDE, start + r * SIDE + SIDE)
                y = first[part, :] + down[start][r * SIDE : r * SIDE + SIDE] + d_bias
                ybuf[z, start // SIDE + r] = y.astype(BF16)

        in_turn([mix, layer_norm, activate, project, finish], starts)

        @pl.when(k == 0)
        def _():
            def reread(start, carry):
                uf[t, pl.ds(start + SIDE, SIDE), :] = ybuf[z, lax.div(start, SIDE)].astype(F32)
                return carry
            grid_rows(reread, 0)

        @pl.when(me_p == k)
        def _():
            pltpu.make_async_copy(ybuf.at[z], so_h.at[0, 2 * me_p + t], so_local.at[t]).start()

        @pl.when(me_p != k)
        def _():
            across(ybuf.at[z], so_h.at[0, 2 * me_p + t], so_send.at[t], so_recv.at[t]).start()

    def backward_stage(t, k, tick):
        z = 2 * k + t
        zero = jnp.zeros((8, C), F32)
        n_gain = pack[k, NGAIN : NGAIN + 1, :]

        d_acc = zero
        for o in range(0, ROWS, TILE):
            g = gf[t, o : o + TILE, :]
            gb[o : o + TILE, :] = g.astype(BF16)
            d_acc = d_acc + fold(g)
        gs[k, DBIAS : DBIAS + 1, :] += total(d_acc)
        gbt[...] = gb[...].T
        for n in range(2):
            acc_d[k, n] += dot(gbt[...], hidden[t, :, n * WIDE : n * WIDE + WIDE])
        tick(1)

        starts = [g * GROUP for g in range(ROWS // GROUP)]
        sums = {"x": zero, "n": zero, "m": zero, "u": [jnp.zeros((8, FT), F32) for _ in range(FF // FT)]}
        kept = {}

        def through_gelu(start):
            low = gb[start : start + GROUP, :]
            raw = dot(low, wd[k, :, 0:FT])
            for n in range(FF // FT):
                cols = slice(n * FT, n * FT + FT)
                now = raw
                if n + 1 < FF // FT:
                    raw = dot(low, wd[k, :, n * FT + FT : n * FT + 2 * FT])
                for o in range(0, GROUP, TILE):
                    part = slice(start + o, start + o + TILE)
                    gpn = (now[o : o + TILE] * gp[t, part, cols].astype(F32)).astype(BF16)
                    gpre[part, cols] = gpn
                    sums["u"][n] = sums["u"][n] + fold(gpn.astype(F32))

        def through_up(start):
            kept["back", start] = dot(gpre[start : start + GROUP, :], wu[k], (1, 1))

        def through_norm(start):
            for o in range(0, GROUP, TILE):
                part = slice(start + o, start + o + TILE)
                g = kept["back", start][o : o + TILE]
                x = xl[t, part, :].astype(F32)
                gn = g * n_gain
                mean_g = jnp.mean(gn, 1, keepdims=True)
                mean_gx = jnp.mean(gn * x, 1, keepdims=True)
                out = gf[t, part, :] + rstd[z, part, :] * (gn - mean_g - x * mean_gx)
                gf[t, part, :] = out
                low = out.astype(BF16)
                gmb[part, :] = low
                sums["x"] = sums["x"] + fold(g * x)
                sums["n"] = sums["n"] + fold(g)
                sums["m"] = sums["m"] + fold(low.astype(F32))

        def through_merge(start):
            low = gmb[start : start + GROUP, :]
            kept["w", start] = dot(low, wm[k, :, 0:C])
            kept["h", start] = dot(low, wmid[k])
            kept["third", start] = dot(low, wm[k, :, 2 * C : 3 * C])

        def round_branches(start):
            for o in range(0, GROUP, TILE):
                part = slice(start + o, start + o + TILE)
                one = kept["w", start][o : o + TILE].astype(BF16)
                gwb[part, :] = one
                wcol[part, :] += jnp.sum(one.astype(F32), 1, keepdims=True)
                one = kept["h", start][o : o + TILE].astype(BF16)
                gwh[part, :] = one
                hcol[part, :] += jnp.sum(one.astype(F32), 1, keepdims=True)

        def across_width(start):
            rows = slice(start, start + GROUP)
            crossed = dot(kw[...], gwb[rows, :])
            for o in range(0, GROUP, TILE):
                part = slice(start + o, start + o + TILE)
                gmix[t, part, :] = kept["third", start][o : o + TILE] + crossed[o : o + TILE]
            gw_acc[...] += dot(gwb[rows, :], joined[t, rows, 2 * C : 3 * C], (1, 1))

        in_turn([through_gelu, through_up, through_norm, through_merge, round_branches, across_width], starts)
        gs[k, NGAIN : NGAIN + 1, :] += total(sums["x"])
        gs[k, NBIAS : NBIAS + 1, :] += total(sums["n"])
        gs[k, MBIAS : MBIAS + 1, :] += total(sums["m"])
        for n in range(FF // FT):
            gs[k, UBIAS + n : UBIAS + n + 1, 0:FT] += total(sums["u"][n])
        tick(4)
        gbt[...] = normal[t].T
        for n in range(2):
            acc_u[k, n] += dot(gbt[...], gpre[:, n * WIDE : n * WIDE + WIDE])
        gmt[...] = gmb[...].T
        for n in range(2):
            width = min(MT, 3 * C - n * MT)
            acc_m[k, n, :, 0:width] += dot(gmt[...], joined[t, :, n * MT : n * MT + width])
        tick(6)
        gh_acc[...] += dot(gwh[...], joined[t, :, 2 * C : 3 * C], (1, 1))

        def batch_sums(start, acc):
            plain, cross = acc
            crossed = dot(kh[pl.ds(start, GROUP), :], gwh[...])
            for o in range(0, GROUP, TILE):
                rows = pl.ds(start + o, TILE)
                g = (gmix[t, rows, :] + crossed[o : o + TILE]) * mask_cols[t, rows, :]
                gmix[t, rows, :] = g
                plain = plain + fold(g)
                cross = cross + fold(g * cv[z, rows, :])
            return plain, cross
        acc = groups(batch_sums, (zero, zero))
        plain, cross = total(acc[0]), total(acc[1])
        gs[k, BBIAS : BBIAS + 1, :] += plain
        gs[k, BGAIN : BGAIN + 1, :] += cross
        r = 4 + z
        msg[r, 0:1, 0:C] = plain
        msg[r, 1:2, 0:C] = cross
        send_stats(r)

    def input_stage(t, k, tick):
        z = 2 * k + t
        r = 4 + z
        wait_stats(r)
        scale, count = stat[z, 0:1, :], stat[z, 1:2, :]
        both = gather_stats(r)
        plain, cross = both[0:1, 0:C], both[1:2, 0:C]
        gain = pack[k, BGAIN : BGAIN + 1, :]
        out_scale = gain * scale
        plain = plain / count
        cross = cross / count

        def shifted(start, carry):
            rows = pl.ds(start, SIDE)
            g = (gmix[t, rows, :] - plain - cv[z, rows, :] * cross) * (mask_cols[t, rows, :] * out_scale)
            rows = pl.ds(start + SIDE, SIDE)
            gsh[0, rows, :] = sooner(g)
            gsh[1, rows, :] = g
            gsh[2, rows, :] = later(g)
            return carry
        grid_rows(shifted, 0)
        tick(8)
        taps = [[pack[k, CONV + n : CONV + n + 1, l:m] for n in range(9)] for l, m in LANES]

        def pull(start, acc):
            new = []
            for (l, m), tap, one in zip(LANES, taps, acc):
                u = [uf[t, pl.ds(start + SIDE * r, SIDE), l:m] for r in range(3)]
                out = gf[t, pl.ds(start, SIDE), l:m]
                sums = []
                for s in range(3):
                    around = [gsh[s, pl.ds(start + SIDE * r, SIDE), l:m] for r in range(3)]
                    out = out + around[2] * tap[s] + around[1] * tap[3 + s] + around[0] * tap[6 + s]
                    sums.append([one[s][r] + fold(around[1] * u[r]) for r in range(3)])
                new.append(sums)
                igbuf[z, lax.div(start, SIDE), :, l:m] = out.astype(BF16)
            return new
        acc = grid_rows(pull, [[[jnp.zeros((8, m - l), F32) for _ in range(3)] for _ in range(3)] for l, m in LANES])
        for (l, m), one in zip(LANES, acc):
            for r in range(3):
                for s in range(3):
                    row = CONV + 3 * r + s
                    gs[k, row : row + 1, l:m] += total(one[s][r])

        @pl.when(k == 1)
        def _():
            def reread(start, carry):
                gf[t, pl.ds(start, SIDE), :] = igbuf[z, lax.div(start, SIDE)].astype(F32)
                return carry
            grid_rows(reread, 0)

        @pl.when(me_p == k)
        def _():
            pltpu.make_async_copy(igbuf.at[z], ig_h.at[0, 2 * me_p + t], ig_local.at[t]).start()

        @pl.when(me_p != k)
        def _():
            across(igbuf.at[z], ig_h.at[0, 2 * me_p + t], ig_send.at[t], ig_recv.at[t]).start()

    def clear_mix():
        gw_acc[...] = jnp.zeros(gw_acc.shape, F32)
        gh_acc[...] = jnp.zeros(gh_acc.shape, F32)
        wcol[...] = jnp.zeros(wcol.shape, F32)
        hcol[...] = jnp.zeros(hcol.shape, F32)

    def close_mix(k):
        i_r, j_r = one_hots(ROWS)
        _, j_g = one_hots(GROUP)
        gs[k, WBIAS : WBIAS + 1, 0:SIDE] = total(jnp.where(j_r, wcol[...], 0.0))
        gs[k, HBIAS : HBIAS + 1, 0:SIDE] = total(jnp.where(i_r, hcol[...], 0.0))
        highest = lax.Precision.HIGHEST
        p = grid_row(lax.broadcasted_iota(jnp.int32, (GROUP, GROUP), 0))
        q = grid_row(lax.broadcasted_iota(jnp.int32, (GROUP, GROUP), 1))
        own = jnp.where(p == q, gw_acc[...], 0.0)
        own = jnp.sum(own.reshape(GROUP // SIDE, SIDE, GROUP), 0)
        gs[k, WW : WW + SIDE, 0:SIDE] = dot(own, jnp.where(j_g, 1.0, 0.0), precision=highest)
        i_f = jnp.where(i_r, 1.0, 0.0)
        for i in range(SIDE):
            rows = slice(i * SIDE, i * SIDE + SIDE)
            own = total(fold(own_column[...] * gh_acc[rows, :]))
            first[i : i + 1, :] = own[:, 0:C]
            gnorm[i : i + 1, 0 : ROWS - C] = own[:, C:ROWS]
        value = dot(first[0:SIDE, :], i_f[0:C, :], precision=highest)
        value += dot(gnorm[0:SIDE, 0 : ROWS - C], i_f[C:ROWS, :], precision=highest)
        gs[k, HW : HW + SIDE, 0:SIDE] = value

    bits = [1, 2]
    while 2 * bits[-1] < n_dp:
        bits.append(2 * bits[-1])
    n_swaps = len(bits) - 2
    n_steps = 1 + 2 + n_swaps + 2

    def partner(bit):
        return me_d + bit * (1 - 2 * lax.rem(me_d // bit, 2))

    def side(bit):
        return lax.rem(me_d // bit, 2)

    def along(bit, src, dst, send, recv):
        return pltpu.make_async_remote_copy(
            src_ref=src, dst_ref=dst, send_sem=send, recv_sem=recv,
            device_id={"dp": partner(bit)}, device_id_type=MESH)

    streams = (
        (acc_d, gd_h, sb_d, lb_d, rl_d), (acc_u, gu_h, sb_u, lb_u, rl_u), (acc_m, gm_h, sb_m, lb_m, rl_m))

    def reduction(k, which):
        acc, out_h, sb, lb, rl = streams[which]
        sb, lb, rl = sb.at[k], lb.at[k], rl.at[k]
        halving = [1 + me_p, 2 - me_p] if which != 1 else [2 - me_p, 1 + me_p]

        def sems(step):
            return red_send.at[3 * k + which, step], red_recv.at[3 * k + which, step]

        def own(q):
            return k, lax.div(q, 2), pl.ds(pl.multiple_of(me_p * HALF + lax.rem(q, 2) * SHARD, 16), SHARD), slice(None)

        def each(count, body):
            if count == 1:
                body(0)
                return

            def step(n, carry):
                body(n)
                return carry
            lax.fori_loop(0, count, step, 0)

        in_chip = across(sb.at[pl.ds(0, SHARDS)], lb, *sems(0))
        base = [0]
        for n, bit in enumerate(halving):
            base.append(base[n] + side(bit) * (2 >> n))
        mine = base[2]

        def half_copy(n):
            count, at = 2 >> n, 2 * n
            return along(halving[n], sb.at[pl.ds(at, count)], rl.at[pl.ds(at, count)], *sems(1 + n))

        def swap_copy(n):
            return along(bits[2 + n], sb.at[3 + n], rl.at[3 + n], *sems(3 + n))

        def double_copy(n):
            count = 2 >> n
            here = lb.at[pl.ds(base[n + 1], count)]
            return along(halving[n], here, here, *sems(n_steps - 1 - n))

        def send_half(n, landed):
            count, at = 2 >> n, 2 * n
            give = base[n] + (1 - side(halving[n])) * count
            keep = base[n + 1]

            def one(q):
                sb[at + q] = (acc[own(give + q)] + landed(give + q).astype(F32)).astype(BF16)
            each(count, one)
            half_copy(n).start()

            def two(q):
                acc[own(keep + q)] += landed(keep + q).astype(F32)
            each(count, two)

        def start():
            def one(q):
                rows = pl.ds(pl.multiple_of(other * HALF + lax.rem(q, 2) * SHARD, 16), SHARD)
                sb[q] = acc[k, lax.div(q, 2), rows, :].astype(BF16)
            each(SHARDS, one)
            in_chip.start()

        def first_half():
            in_chip.wait()
            send_half(0, lambda q: lb[q])

        def second_half():
            half_copy(0).wait()
            send_half(1, lambda q: rl[q - base[1]])

        def swap(n):
            def run():
                if n == 0:
                    half_copy(1).wait()
                    sb[3] = (acc[own(mine)] + rl[2].astype(F32)).astype(BF16)
                else:
                    swap_copy(n - 1).wait()
                    sb[3 + n] = (sb[2 + n].astype(F32) + rl[2 + n].astype(F32)).astype(BF16)
                swap_copy(n).start()
            return run

        def double(n):
            def run():
                if n == 1:
                    last = n_swaps - 1
                    swap_copy(last).wait()
                    lb[mine] = (sb[3 + last].astype(F32) + rl[3 + last].astype(F32)).astype(BF16)
                else:
                    double_copy(n + 1).wait()
                double_copy(n).start()
            return run

        def hand_over():
            double_copy(0).wait()

            @pl.when(me_p == k)
            def _():
                pltpu.make_async_copy(lb, out_h.at[me_p], out_local.at[which]).start()

            @pl.when(me_p != k)
            def _():
                across(lb, out_h.at[me_p], out_send.at[which], out_recv.at[which]).start()

        return [start, first_half, second_half] + [swap(n) for n in range(n_swaps)] + [double(1), double(0), hand_over]

    def small_sum(rows, landing, send, recv):
        count = rows.stop - rows.start
        rows = pl.ds(rows.start, count)
        in_chip = across(gs.at[other, rows], landing.at[0], send.at[0], recv.at[0])

        def swap_copy(n):
            return along(bits[n], gs.at[me_p, rows], landing.at[1 + n], send.at[1 + n], recv.at[1 + n])

        def step(n):
            def run():
                (swap_copy(n - 1) if n else in_chip).wait()
                gs[me_p, rows, :] += landing[n]
                if n < len(bits):
                    swap_copy(n).start()
            return run
        return [in_chip.start] + [step(n) for n in range(len(bits) + 1)]

    small = small_sum(slice(SMALL, PACK), small_land, small_send, small_recv)
    taps_sum = small_sum(slice(0, SMALL), conv_land, conv_send, conv_recv)

    plan = {}
    backward_places, input_places = [0, 1, 4, 6, 11], [7, 8, 9]
    order = []
    for n in range(6):
        order += [(n, p) for p in input_places] if n > 1 else []
        order += [(n, p) for p in backward_places] if n < 4 else []

    def put(start, steps, gap):
        at = order.index(start)
        steps = list(steps)
        while steps and at < len(order):
            plan.setdefault(order[at], []).append(steps.pop(0))
            at += gap
        return steps

    for which, place in enumerate((1, 6, 6)):
        assert not put((1, place), reduction(1, which), 1)
    tails = [put((3, place), reduction(0, which), 1) for which, place in enumerate((1, 6, 6))]
    tails.append(put((4, 7), small, 1))
    tails.append(list(taps_sum))

    pack_over.wait()
    for t in range(2):
        image_in[t].wait()

    def widen_image(t):
        def widen(i, inner):
            uf[t, pl.ds(pl.multiple_of(i * SIDE + SIDE, SIDE), SIDE), :] = ub[t, i].astype(F32)
            return inner
        lax.fori_loop(0, SIDE, widen, 0)

    def start_image(t, carry):
        widen_image(t)
        conv_stage(t, 0)
        return carry
    lax.fori_loop(0, 2, start_image, 0)
    for t in range(2):
        grad_in[t].start()

    for copy in weights_in + weights_over:
        copy.wait()
    for k in range(2):
        wmid[k] = wm[k, :, C : 2 * C]

    def forward_block(k, carry):
        mixers(k, False)

        def one(t, inner):
            forward_stage(t, k)

            @pl.when(k == 0)
            def _():
                for copy in spill(t):
                    copy.start()
                conv_stage(t, 1)
            return inner
        lax.fori_loop(0, 2, one, 0)
        return carry
    lax.fori_loop(0, 2, forward_block, 0)

    for t in range(2):
        grad_in[t].wait()
        pltpu.make_async_copy(ybuf.at[t], so_h.at[0, t], so_local.at[t]).wait()
        across(ybuf.at[t], so_h.at[0, t], so_send.at[t], so_recv.at[t]).wait_send()

    def load_grad(t, carry):
        def widen(i, inner):
            gf[t, pl.ds(pl.multiple_of(i * SIDE, SIDE), SIDE), :] = ub[t, i].astype(F32)
            return inner
        lax.fori_loop(0, SIDE, widen, 0)
        return carry
    lax.fori_loop(0, 2, load_grad, 0)
    for t in range(2):
        image_copy(t, again_sems.at[t]).start()

    def turn(s, carry):
        t = lax.rem(s, 2)

        def tick(place):
            for n in range(6):
                steps = plan.get((n, place), [])
                if steps:
                    @pl.when(s == n)
                    def _():
                        for step in steps:
                            step()

        @pl.when(lax.rem(s, 2) == 0)
        def _():
            @pl.when(s > 0)
            def _():
                close_mix(2 - lax.div(s, 2))

            @pl.when(s < 4)
            def _():
                mixers(1 - lax.div(s, 2), True)
                clear_mix()

        @pl.when(s > 1)
        def _():
            @pl.when(s > 3)
            def _():
                image_copy(t, again_sems.at[t]).wait()
                widen_image(t)
            tick(7)
            input_stage(t, 2 - lax.div(s, 2), tick)
            tick(9)

        @pl.when(s < 4)
        def _():
            @pl.when(s > 1)
            def _():
                for copy in fetch(t):
                    copy.wait()
            tick(0)
            backward_stage(t, 1 - lax.div(s, 2), tick)
            tick(11)

            @pl.when(s < 2)
            def _():
                for copy in fetch(t):
                    copy.start()
        return carry
    lax.fori_loop(0, 6, turn, 0)

    while any(tails):
        for steps in tails:
            if steps:
                steps.pop(0)()

    gs_out = pltpu.make_async_copy(gs.at[me_p], gs_h, gs_sem.at[0])
    gs_out.start()
    for t in range(2):
        pltpu.make_async_copy(igbuf.at[t], ig_h.at[0, t], ig_local.at[t]).wait()
        across(ybuf.at[t], so_h.at[0, t], so_send.at[t], so_recv.at[t]).wait_recv()
        across(igbuf.at[t], ig_h.at[0, t], ig_send.at[t], ig_recv.at[t]).wait()
    for n, (_, out_h, _, lb, _) in enumerate(streams):
        pltpu.make_async_copy(lb.at[0], out_h.at[0], out_local.at[n]).wait()
        across(lb.at[0], out_h.at[0], out_send.at[n], out_recv.at[n]).wait()
    gs_out.wait()


def finish_kernel(
    so_in, ig_in, gd_in, gu_in, gm_in, gs,
    so, ig, conv, bgain, bbias, ww, wb, hw, hb, gm, mbias, ngain, nbias, gu, ubias, gd, dbias,
    large, d_in, u_in, m_in, d_out, u_out, m_out, in_sems, out_sems,
):
    moved = ((gd_in, d_in), (gu_in, u_in), (gm_in, m_in), (so_in, large.at[0]), (ig_in, large.at[1]))
    arrive = [pltpu.make_async_copy(src, dst, in_sems.at[n]) for n, (src, dst) in enumerate(moved)]
    for copy in arrive:
        copy.start()
    moved = ((d_out, gd), (u_out, gu), (m_out, gm), (large.at[0], so), (large.at[1], ig))
    leave = [pltpu.make_async_copy(src, dst, out_sems.at[n]) for n, (src, dst) in enumerate(moved)]
    for n in range(9):
        conv[n] = gs[CONV + n : CONV + n + 1, :]
    for row, ref in ((BGAIN, bgain), (BBIAS, bbias), (MBIAS, mbias), (NGAIN, ngain), (NBIAS, nbias), (DBIAS, dbias)):
        ref[...] = gs[row : row + 1, :]
    for row, ref in ((WBIAS, wb), (HBIAS, hb)):
        ref[...] = gs[row : row + 1, 0:SIDE]
    for n in range(FF // FT):
        ubias[:, n * FT : n * FT + FT] = gs[UBIAS + n : UBIAS + n + 1, 0:FT]
    for row, ref in ((WW, ww), (HW, hw)):
        ref[0] = gs[row : row + SIDE, 0:SIDE]
    for n, (src, dst, piece) in enumerate(((d_in, d_out, WIDE), (u_in, u_out, WIDE), (m_in, m_out, MT))):
        arrive[n].wait()
        for p in range(2):
            for q in range(SHARDS):
                start, at = p * HALF + (q % 2) * SHARD, piece * (q // 2)
                width = min(piece, dst.shape[1] - at)
                dst[start : start + SHARD, at : at + width] = src[p, q, :, 0:width].astype(F32)
        leave[n].start()
    for n in (3, 4):
        arrive[n].wait()
        leave[n].start()
    for copy in leave:
        copy.wait()


def on_device(
    images, masks, conv_weight, batch_gain, batch_bias, width_weight, width_bias,
    height_weight, height_bias, merge_weight, merge_bias, norm_gain, norm_bias,
    up_weight, up_bias, down_weight, down_bias, out_grad,
):
    n_dp = lax.axis_size("dp")
    micro = images.shape[0]
    steps = max(n_dp.bit_length() - 1, 4)
    any_space = pl.BlockSpec(memory_space=pl.ANY)
    vmem = pl.BlockSpec(memory_space=pltpu.VMEM)
    dma = pltpu.SemaphoreType.DMA
    grid = (SIDE, SIDE, C)
    shape = jax.ShapeDtypeStruct
    outs = pl.pallas_call(
        functools.partial(kernel, n_dp),
        out_shape=(
            shape((1, micro) + grid, BF16),
            shape((1, micro) + grid, BF16),
            shape((2, SHARDS, SHARD, WIDE), BF16),
            shape((2, SHARDS, SHARD, WIDE), BF16),
            shape((2, SHARDS, SHARD, MT), BF16),
            shape((PACK, C), F32),
            shape((2, ROWS, FF), BF16),
            shape((2, ROWS, FF), BF16),
            shape((2, ROWS, 3 * C), BF16),
            shape((2, ROWS, C), BF16),
            shape((2, ROWS, C), BF16),
        ),
        in_specs=[any_space] + [vmem] * 8 + [any_space] + [vmem] * 3 + [any_space, vmem, any_space, vmem, any_space],
        out_specs=(any_space,) * 11,
        scratch_shapes=[
            pltpu.VMEM((2, ROWS, 1), F32),
            pltpu.VMEM((4, 2, C), F32),
            pltpu.VMEM((SIDE, ROWS), F32),
            pltpu.VMEM((ROWS, SIDE), BF16),
            pltpu.VMEM((2, PACK, C), F32),
            pltpu.VMEM((2, C, 3 * C), BF16),
            pltpu.VMEM((2, C, C), BF16),
            pltpu.VMEM((2, C, FF), BF16),
            pltpu.VMEM((2, C, FF), BF16),
            pltpu.VMEM((2,) + grid, BF16),
            pltpu.VMEM((2, ROWS + 2 * SIDE, C), F32),
            pltpu.VMEM((4, ROWS, C), F32),
            pltpu.VMEM((2, ROWS, 3 * C), BF16),
            pltpu.VMEM((2, ROWS, C), BF16),
            pltpu.VMEM((2, ROWS, C), BF16),
            pltpu.VMEM((4, ROWS, 1), F32),
            pltpu.VMEM((2, ROWS, FF), BF16),
            pltpu.VMEM((2, ROWS, FF), BF16),
            pltpu.VMEM((2, ROWS, C), F32),
            pltpu.VMEM((ROWS, C), BF16),
            pltpu.VMEM((ROWS, C), BF16),
            pltpu.VMEM((ROWS, C), BF16),
            pltpu.VMEM((C, ROWS), BF16),
            pltpu.VMEM((C, ROWS), BF16),
            pltpu.VMEM((ROWS, FF), BF16),
            pltpu.VMEM((2, ROWS, C), F32),
            pltpu.VMEM((ROWS, C), BF16),
            pltpu.VMEM((3, ROWS + 2 * SIDE, C), F32),
            pltpu.VMEM((GROUP, GROUP), BF16),
            pltpu.VMEM((ROWS, ROWS), BF16),
            pltpu.VMEM((ROWS, 1), F32),
            pltpu.VMEM((ROWS, 1), F32),
            pltpu.VMEM((GROUP, GROUP), F32),
            pltpu.VMEM((ROWS, ROWS), F32),
            pltpu.VMEM((ROWS, 1), F32),
            pltpu.VMEM((ROWS, 1), F32),
            pltpu.VMEM((4,) + grid, BF16),
            pltpu.VMEM((8, 2, CP), F32),
            pltpu.VMEM((8, n_dp - 1, 2, CP), F32),
            pltpu.VMEM((2, 2, C, WIDE), F32),
            pltpu.VMEM((2, 2, C, WIDE), F32),
            pltpu.VMEM((2, 2, C, MT), F32),
            pltpu.VMEM((2, PACK, C), F32),
            pltpu.VMEM((2, 1 + steps, SHARD, WIDE), BF16),
            pltpu.VMEM((2, SHARDS, SHARD, WIDE), BF16),
            pltpu.VMEM((2, 1 + steps, SHARD, WIDE), BF16),
            pltpu.VMEM((2, 1 + steps, SHARD, WIDE), BF16),
            pltpu.VMEM((2, SHARDS, SHARD, WIDE), BF16),
            pltpu.VMEM((2, 1 + steps, SHARD, WIDE), BF16),
            pltpu.VMEM((2, 1 + steps, SHARD, MT), BF16),
            pltpu.VMEM((2, SHARDS, SHARD, MT), BF16),
            pltpu.VMEM((2, 1 + steps, SHARD, MT), BF16),
            pltpu.VMEM((1 + steps, PACK - SMALL, C), F32),
            pltpu.VMEM((1 + steps, SMALL, C), F32),
            dma((9,)), dma((2,)), dma((2,)), dma((3,)), dma((3,)), dma((8,)), dma((8,)),
            dma((2,)), dma((2,)), dma((2,)), dma((2,)), dma((2,)), dma((2,)), dma((2, 5)), dma((2, 5)),
            dma((6, 3 + steps)), dma((6, 3 + steps)), dma((1 + steps,)), dma((1 + steps,)),
            dma((1 + steps,)), dma((1 + steps,)), dma((3,)), dma((3,)), dma((3,)), dma((1,)),
        ],
        compiler_params=pltpu.CompilerParams(
            collective_id=0, has_side_effects=True, vmem_limit_bytes=65400 * 1024),
    )(
        images, masks, conv_weight, batch_gain, batch_bias, width_weight, width_bias, height_weight, height_bias,
        merge_weight[0].T, merge_bias, norm_gain, norm_bias, up_weight[0], up_bias, down_weight[0].T, down_bias, out_grad)

    row = shape((1, C), F32)
    square, line = shape((1, SIDE, SIDE), F32), shape((1, SIDE), F32)
    so, ig, conv, bgain, bbias, ww, wb, hw, hb, gm, mbias, ngain, nbias, gu, ubias, gd, dbias = pl.pallas_call(
        finish_kernel,
        out_shape=(
            shape((1, micro) + grid, BF16), shape((1, micro) + grid, BF16), shape((9, 1, C), F32), row, row,
            square, line, square, line, shape((C, 3 * C), F32), row, row, row,
            shape((C, FF), F32), shape((1, FF), F32), shape((C, FF), F32), row),
        in_specs=[any_space] * 5 + [vmem],
        out_specs=(any_space,) * 2 + (vmem,) * 7 + (any_space,) + (vmem,) * 3 + (any_space, vmem, any_space, vmem),
        scratch_shapes=[
            pltpu.VMEM((2, 1, micro) + grid, BF16),
            pltpu.VMEM((2, SHARDS, SHARD, WIDE), BF16),
            pltpu.VMEM((2, SHARDS, SHARD, WIDE), BF16),
            pltpu.VMEM((2, SHARDS, SHARD, MT), BF16),
            pltpu.VMEM((C, FF), F32),
            pltpu.VMEM((C, FF), F32),
            pltpu.VMEM((C, 3 * C), F32),
            dma((5,)), dma((5,)),
        ],
        compiler_params=pltpu.CompilerParams(vmem_limit_bytes=65400 * 1024),
    )(*outs[:6])
    return (
        so, ig, jnp.swapaxes(conv, 0, 1), bgain, bbias, ww, wb, hw, hb, gm.T[None], mbias, ngain, nbias,
        gu[None], ubias, gd.T[None], dbias)


def solution(mesh):
    data4 = P("dp", None, None, None)
    p1, p2, p3 = P("pipe"), P("pipe", None), P("pipe", None, None)
    out5 = P("pipe", "dp", None, None, None)
    return jax.shard_map(
        on_device,
        mesh=mesh,
        in_specs=(data4, P("dp", None, None), p3, p2, p2, p3, p2, p3, p2, p3, p2, p2, p2, p3, p2, p3, p2, data4),
        out_specs=(out5, out5, p3, p2, p2, p3, p2, p3, p2, p3, p2, p2, p2, p3, p2, p3, p2),
        check_vma=False,
    )
```

```python
import functools

import jax
import jax.numpy as jnp
from jax import lax
from jax.experimental import pallas as pl
from jax.experimental.pallas import tpu as pltpu
from jax.sharding import PartitionSpec as P

EPS = 1e-05
MESH = pl.DeviceIdType.MESH
F32 = jnp.float32
BF16 = jnp.bfloat16

SIDE = 24
ROWS = SIDE * SIDE
C = 320
CP = 384
FF = 1280
FT = 256
CHUNK = 48
TILE = 32
LANES = ((0, 128), (128, 256), (256, 320))
GROUP = 8 * SIDE

HALF = C // 2
SHARD = HALF // 2
WIDE = FF // 2
SHARDS = 4
MT = 512
STEP = 24

CONV, BGAIN, BBIAS, MBIAS, NGAIN, NBIAS, DBIAS, WBIAS, HBIAS, UBIAS, WW, HW, PACK = (
    0, 16, 17, 18, 19, 20, 21, 22, 23, 24, 32, 56, 80)
SMALL = 16


def dot(a, b, contract=(1, 0), precision=None):
    return lax.dot_general(
        a, b, (((contract[0],), (contract[1],)), ((), ())),
        preferred_element_type=F32, precision=precision)


def in_turn(phases, starts):
    for step in range(len(phases) + len(starts) - 1):
        for g, start in enumerate(starts):
            if 0 <= step - g < len(phases):
                phases[step - g](start)


def fold(value):
    rows = value.shape[0]
    return jnp.sum(value.reshape(rows // 8, 8, value.shape[1]), 0)


def total(partial):
    return jnp.sum(partial, 0, keepdims=True)


def grid_row(index):
    return (index * 2731) >> 16


def one_hots(rows):
    place = lax.broadcasted_iota(jnp.int32, (rows, SIDE), 0)
    lane = lax.broadcasted_iota(jnp.int32, (rows, SIDE), 1)
    i = grid_row(place)
    return i == lane, place - SIDE * i == lane


def gelu_both(x):
    e = jnp.exp2(x * x * -0.7213475204444817)
    d = 1.0 + 0.23164189 * jnp.abs(x)
    t = pl.reciprocal(d, approx=True)
    poly = t * (0.127414796 + t * (-0.142248368 + t * (0.7107068705 + t * (-0.7265760135 + t * 0.5307027145))))
    tail = poly * e
    phi = jnp.where(x >= 0, 1.0 - tail, tail)
    return x * phi, phi + x * e * 0.3989422804014327


def kernel(
    n_dp,
    images, masks, conv_w, bgain, bbias, wwt, wb, hwt, hb, wm_h, mbias, ngain, nbias, wu_h, ubias, wd_h, dbias, og_h,
    so_h, ig_h, gd_h, gu_h, gm_h, gs_h, sp_hidden, sp_gp, sp_joined, sp_normal, sp_xl,
    mask_cols, stat, own_column, i_hot, pack, wm, wmid, wu, wd, ub, uf, cv, joined, normal, xl, rstd, hidden, gp,
    gf, gb, gmb, gwb, gbt, gmt, gpre, gmix, gwh, gsh, kw, kh, wbcol, hbcol,
    gw_acc, gh_acc, wcol, hcol, ybuf, msg, land, acc_d, acc_u, acc_m, gs,
    sb_d, lb_d, rl_d, sb_u, lb_u, rl_u, sb_m, lb_m, rl_m, small_land, conv_land,
    local_sems, again_sems, pack_sems, w_send, w_recv, st_send, st_recv,
    so_local, so_send, so_recv, ig_local, ig_send, ig_recv, spill_sems, fetch_sems,
    red_send, red_recv, small_send, small_recv, conv_send, conv_recv, out_local, out_send, out_recv, gs_sem,
):
    me_p = lax.axis_index("pipe")
    me_d = lax.axis_index("dp")
    other = 1 - me_p
    first = gsh.at[2, pl.ds(SIDE, ROWS)]
    igbuf = ybuf
    gnorm = gsh.at[0, pl.ds(SIDE, ROWS)]

    def image_copy(t, sems):
        return pltpu.make_async_copy(images.at[2 * me_p + t], ub.at[t], sems)

    image_in = [image_copy(t, local_sems.at[5 + t]) for t in range(2)]
    grad_in = [pltpu.make_async_copy(og_h.at[2 * me_p + t], ub.at[t], local_sems.at[7 + t]) for t in range(2)]
    weights = ((wm_h, wm), (wu_h, wu), (wd_h, wd))
    weights_in = [pltpu.make_async_copy(src, dst.at[me_p], local_sems.at[n]) for n, (src, dst) in enumerate(weights)]
    for copy in image_in + weights_in:
        copy.start()

    barrier = pltpu.get_barrier_semaphore()

    def greet(step, carry):
        pl.semaphore_signal(barrier, inc=1, device_id={"dp": lax.rem(me_d + step, n_dp)}, device_id_type=MESH)
        return carry

    lax.fori_loop(1, n_dp, greet, 0)
    pl.semaphore_signal(barrier, inc=1, device_id={"pipe": other}, device_id_type=MESH)

    pack[me_p] = jnp.zeros(pack.shape[1:], F32)
    pack[me_p, CONV : CONV + 9, :] = conv_w[0].astype(F32)
    for row, ref in ((BGAIN, bgain), (BBIAS, bbias), (MBIAS, mbias), (NGAIN, ngain), (NBIAS, nbias), (DBIAS, dbias)):
        pack[me_p, row : row + 1, :] = ref[...]
    for row, ref in ((WBIAS, wb), (HBIAS, hb)):
        pack[me_p, row : row + 1, 0:SIDE] = ref[...]
    for n in range(FF // FT):
        pack[me_p, UBIAS + n : UBIAS + n + 1, 0:FT] = ubias[:, n * FT : n * FT + FT]
    for row, ref in ((WW, wwt), (HW, hwt)):
        pack[me_p, row : row + SIDE, 0:SIDE] = ref[0].astype(F32)

    pl.semaphore_wait(barrier, n_dp)

    def across(src, dst, send, recv):
        return pltpu.make_async_remote_copy(
            src_ref=src, dst_ref=dst, send_sem=send, recv_sem=recv,
            device_id={"pipe": other}, device_id_type=MESH)

    pack_over = across(pack.at[me_p], pack.at[me_p], pack_sems.at[0], pack_sems.at[1])
    weights_over = [across(src, dst.at[me_p], w_send.at[n], w_recv.at[n]) for n, (src, dst) in enumerate(weights)]
    pack_over.start()
    for copy in weights_over:
        copy.start()

    msg[...] = jnp.zeros(msg.shape, F32)
    for k in range(2):
        for acc in (acc_d, acc_u, acc_m):
            for n in range(2):
                acc[k, n] = jnp.zeros(acc.shape[2:], F32)
        gs[k] = jnp.zeros(gs.shape[1:], F32)
    for n in range(2):
        uf[n, 0:SIDE, :] = jnp.zeros((SIDE, C), F32)
        uf[n, SIDE + ROWS : 2 * SIDE + ROWS, :] = jnp.zeros((SIDE, C), F32)
    for n in range(3):
        gsh[n, 0:SIDE, :] = jnp.zeros((SIDE, C), F32)
        gsh[n, SIDE + ROWS : 2 * SIDE + ROWS, :] = jnp.zeros((SIDE, C), F32)

    i_r, j_r = one_hots(ROWS)
    i_hot[...] = jnp.where(i_r, 1.0, 0.0).astype(BF16)
    q = lax.broadcasted_iota(jnp.int32, (SIDE, ROWS), 1)
    q = q - SIDE * grid_row(q)
    own_column[...] = jnp.where(lax.broadcasted_iota(jnp.int32, (SIDE, ROWS), 0) == q, 1.0, 0.0)
    for t in range(2):
        chosen = dot(i_hot[...], masks[2 * me_p + t].astype(F32).astype(BF16))
        mask_cols[t] = jnp.sum(jnp.where(j_r, chosen, 0.0), 1, keepdims=True)

    def later(value):
        at = lax.broadcasted_iota(jnp.int32, value.shape, 0)
        return jnp.where(at != 0, pltpu.roll(value, 1, 0), 0.0)

    def sooner(value):
        at = lax.broadcasted_iota(jnp.int32, value.shape, 0)
        return jnp.where(at != SIDE - 1, pltpu.roll(value, SIDE - 1, 0), 0.0)

    def grid_rows(body, init):
        def step(c, carry):
            for row in range(STEP):
                carry = body(pl.multiple_of(c * (STEP * SIDE), STEP * SIDE) + row * SIDE, carry)
            return carry
        return lax.fori_loop(0, SIDE // STEP, step, init)

    def groups(body, init):
        for g in range(ROWS // GROUP):
            init = body(g * GROUP, init)
        return init

    def send_stats(r):
        def one(step, carry):
            pltpu.make_async_remote_copy(
                src_ref=msg.at[r], dst_ref=land.at[r, n_dp - 1 - step],
                send_sem=st_send.at[r], recv_sem=st_recv.at[r],
                device_id={"dp": lax.rem(me_d + step, n_dp)}, device_id_type=MESH).start()
            return carry
        lax.fori_loop(1, n_dp, one, 0)

    def wait_stats(r):
        whole = pltpu.make_async_remote_copy(
            src_ref=land.at[r], dst_ref=land.at[r], send_sem=st_send.at[r], recv_sem=st_recv.at[r],
            device_id={"dp": lax.rem(me_d + 1, n_dp)}, device_id_type=MESH)
        whole.wait_send()
        whole.wait_recv()

    def conv_stage(t, k):
        z = 2 * k + t
        n_own = total(mask_cols[t])
        taps = [[pack[k, CONV + n : CONV + n + 1, l:m] for n in range(9)] for l, m in LANES]

        def conv(start, acc):
            at = pl.ds(start, SIDE)
            new = []
            for (l, m), tap, one in zip(LANES, taps, acc):
                rows = [uf[t, pl.ds(start + SIDE * r, SIDE), l:m] for r in range(3)]
                part = [rows[0] * tap[s] + rows[1] * tap[3 + s] + rows[2] * tap[6 + s] for s in range(3)]
                out = part[1] + later(part[0]) + sooner(part[2])
                cv[z, at, l:m] = out
                new.append(one + fold(out * mask_cols[t, at, :]))
            return new
        acc = grid_rows(conv, [jnp.zeros((8, m - l), F32) for l, m in LANES])
        sums = jnp.concatenate([total(one) for one in acc], 1)
        mean = sums / n_own

        def centred(start, acc):
            rows = pl.ds(start, SIDE)
            d = cv[z, rows, :] - mean
            return acc + fold(d * d * mask_cols[t, rows, :])

        m2 = total(grid_rows(centred, jnp.zeros((8, C), F32)))
        msg[z, 0:1, 0:C] = sums
        msg[z, 0:1, C:CP] = jnp.broadcast_to(n_own, (1, CP - C))
        msg[z, 1:2, 0:C] = m2
        send_stats(z)

    def peers(body, init):
        if n_dp > 16:
            return lax.fori_loop(0, n_dp - 1, body, init)
        for d in range(n_dp - 1):
            init = body(d, init)
        return init

    def gather_stats(r):
        def add(d, carry):
            return carry + land[r, d]
        return peers(add, msg[r])

    def norm_stats(z):
        sums = gather_stats(z)[0:1, :]
        count = sums[:, CP - 1 : CP]
        mean = sums[:, 0:C] / count

        def spread(values):
            n = values[0:1, CP - 1 : CP]
            off = values[0:1, 0:C] / n - mean
            return values[1:2, 0:C] + n * off * off

        def add(d, carry):
            return carry + spread(land[z, d])
        m2 = peers(add, spread(msg[z]))
        scale = lax.rsqrt(m2 / count + EPS)
        stat[z, 0:1, :] = scale
        stat[z, 1:2, :] = jnp.broadcast_to(count, (1, C))
        return mean, scale

    def mixers(k, backward):
        _, j_g = one_hots(GROUP)
        ww = pack[k, WW : WW + SIDE, 0:SIDE].astype(BF16)
        hw = pack[k, HW : HW + SIDE, 0:SIDE].astype(BF16)
        side_of = 0 if backward else 1
        j_b = jnp.where(j_g, 1.0, 0.0).astype(BF16)
        left = dot(j_b, ww, (1, 1 - side_of)).astype(BF16)
        p = grid_row(lax.broadcasted_iota(jnp.int32, (GROUP, GROUP), 0))
        q = grid_row(lax.broadcasted_iota(jnp.int32, (GROUP, GROUP), 1))
        kw[...] = jnp.where(p == q, dot(left, j_b, (1, 1)), 0.0).astype(BF16)
        spread = dot(hw, i_hot[...], (side_of, 1))
        own = own_column[...]
        for i in range(0, SIDE, 2):
            two = jnp.concatenate([spread[i : i + 1, :] * own, spread[i + 1 : i + 2, :] * own], 0)
            kh[i * SIDE : i * SIDE + 2 * SIDE, :] = two.astype(BF16)
        if not backward:
            i_r, j_r = one_hots(ROWS)
            wb = pack[k, WBIAS : WBIAS + 1, 0:SIDE]
            hb = pack[k, HBIAS : HBIAS + 1, 0:SIDE]
            wbcol[...] = jnp.sum(jnp.where(j_r, wb, 0.0), 1, keepdims=True)
            hbcol[...] = jnp.sum(jnp.where(i_r, hb, 0.0), 1, keepdims=True)

    stored = ((hidden, sp_hidden), (gp, sp_gp), (joined, sp_joined), (normal, sp_normal), (xl, sp_xl))

    def spill(t):
        return [pltpu.make_async_copy(v.at[t], h.at[t], spill_sems.at[t, n]) for n, (v, h) in enumerate(stored)]

    def fetch(t):
        return [pltpu.make_async_copy(h.at[t], v.at[t], fetch_sems.at[t, n]) for n, (v, h) in enumerate(stored)]

    def forward_stage(t, k):
        z = 2 * k + t

        @pl.when(k == 1)
        def _():
            for copy in spill(t):
                copy.wait()

        wait_stats(z)
        mean, scale = norm_stats(z)
        gain = pack[k, BGAIN : BGAIN + 1, :]
        bias = pack[k, BBIAS : BBIAS + 1, :]

        def standardize(start, carry):
            for o in range(0, GROUP, TILE):
                rows = pl.ds(start + o, TILE)
                x = (cv[z, rows, :] - mean) * scale
                cv[z, rows, :] = x
                joined[t, rows, 2 * C : 3 * C] = ((x * gain + bias) * mask_cols[t, rows, :]).astype(BF16)
            along = dot(kw[...], joined[t, pl.ds(start, GROUP), 2 * C : 3 * C])
            for o in range(0, GROUP, TILE):
                rows = pl.ds(start + o, TILE)
                joined[t, rows, 0:C] = (along[o : o + TILE] + wbcol[rows, :]).astype(BF16)
            return carry
        groups(standardize, 0)

        m_bias = pack[k, MBIAS : MBIAS + 1, :]
        n_gain = pack[k, NGAIN : NGAIN + 1, :]
        n_bias = pack[k, NBIAS : NBIAS + 1, :]
        d_bias = pack[k, DBIAS : DBIAS + 1, :]
        u_bias = [pack[k, UBIAS + n : UBIAS + n + 1, 0:FT] for n in range(FF // FT)]

        starts = [g * GROUP for g in range(ROWS // GROUP)]
        merged, down = {}, {}

        def mix(start):
            rows = slice(start, start + GROUP)
            along = dot(kh[rows, :], joined[t, :, 2 * C : 3 * C])
            for o in range(0, GROUP, TILE):
                part = slice(start + o, start + o + TILE)
                joined[t, part, C : 2 * C] = (along[o : o + TILE] + hbcol[part, :]).astype(BF16)
            merged[start] = dot(joined[t, rows, :], wm[k], (1, 1))

        def layer_norm(start):
            for o in range(0, GROUP, TILE):
                part = slice(start + o, start + o + TILE)
                f = uf[t, start + SIDE + o : start + SIDE + o + TILE, :] + merged[start][o : o + TILE] + m_bias
                d = f - jnp.mean(f, 1, keepdims=True)
                rs = lax.rsqrt(jnp.mean(d * d, 1, keepdims=True) + EPS)
                x = d * rs
                first[part, :] = f
                rstd[z, part, :] = rs
                xl[t, part, :] = x.astype(BF16)
                normal[t, part, :] = (x * n_gain + n_bias).astype(BF16)

        def activate(start):
            rows = slice(start, start + GROUP)
            norm = normal[t, rows, :]
            pre = dot(norm, wu[k, :, 0:FT])
            for n in range(FF // FT):
                cols = slice(n * FT, n * FT + FT)
                now = pre
                if n + 1 < FF // FT:
                    pre = dot(norm, wu[k, :, n * FT + FT : n * FT + 2 * FT])
                for o in range(0, GROUP, TILE):
                    part = slice(start + o, start + o + TILE)
                    h, dh = gelu_both(now[o : o + TILE] + u_bias[n])
                    hidden[t, part, cols] = h.astype(BF16)
                    gp[t, part, cols] = dh.astype(BF16)

        def project(start):
            down[start] = dot(hidden[t, start : start + GROUP, :], wd[k], (1, 1))

        def finish(start):
            for r in range(GROUP // SIDE):
                part = slice(start + r * SIDE, start + r * SIDE + SIDE)
                y = first[part, :] + down[start][r * SIDE : r * SIDE + SIDE] + d_bias
                ybuf[z, start // SIDE + r] = y.astype(BF16)

        in_turn([mix, layer_norm, activate, project, finish], starts)

        @pl.when(k == 0)
        def _():
            def reread(start, carry):
                uf[t, pl.ds(start + SIDE, SIDE), :] = ybuf[z, lax.div(start, SIDE)].astype(F32)
                return carry
            grid_rows(reread, 0)

        @pl.when(me_p == k)
        def _():
            pltpu.make_async_copy(ybuf.at[z], so_h.at[0, 2 * me_p + t], so_local.at[t]).start()

        @pl.when(me_p != k)
        def _():
            across(ybuf.at[z], so_h.at[0, 2 * me_p + t], so_send.at[t], so_recv.at[t]).start()

    def backward_stage(t, k, tick):
        z = 2 * k + t
        zero = jnp.zeros((8, C), F32)
        n_gain = pack[k, NGAIN : NGAIN + 1, :]

        d_acc = zero
        for o in range(0, ROWS, TILE):
            g = gf[t, o : o + TILE, :]
            gb[o : o + TILE, :] = g.astype(BF16)
            d_acc = d_acc + fold(g)
        gs[k, DBIAS : DBIAS + 1, :] += total(d_acc)
        gbt[...] = gb[...].T
        for n in range(2):
            acc_d[k, n] += dot(gbt[...], hidden[t, :, n * WIDE : n * WIDE + WIDE])
        tick(1)

        starts = [g * GROUP for g in range(ROWS // GROUP)]
        sums = {"x": zero, "n": zero, "m": zero, "u": [jnp.zeros((8, FT), F32) for _ in range(FF // FT)]}
        kept = {}

        def through_gelu(start):
            low = gb[start : start + GROUP, :]
            raw = dot(low, wd[k, :, 0:FT])
            for n in range(FF // FT):
                cols = slice(n * FT, n * FT + FT)
                now = raw
                if n + 1 < FF // FT:
                    raw = dot(low, wd[k, :, n * FT + FT : n * FT + 2 * FT])
                for o in range(0, GROUP, TILE):
                    part = slice(start + o, start + o + TILE)
                    gpn = (now[o : o + TILE] * gp[t, part, cols].astype(F32)).astype(BF16)
                    gpre[part, cols] = gpn
                    sums["u"][n] = sums["u"][n] + fold(gpn.astype(F32))

        def through_up(start):
            kept["back", start] = dot(gpre[start : start + GROUP, :], wu[k], (1, 1))

        def through_norm(start):
            for o in range(0, GROUP, TILE):
                part = slice(start + o, start + o + TILE)
                g = kept["back", start][o : o + TILE]
                x = xl[t, part, :].astype(F32)
                gn = g * n_gain
                mean_g = jnp.mean(gn, 1, keepdims=True)
                mean_gx = jnp.mean(gn * x, 1, keepdims=True)
                out = gf[t, part, :] + rstd[z, part, :] * (gn - mean_g - x * mean_gx)
                gf[t, part, :] = out
                low = out.astype(BF16)
                gmb[part, :] = low
                sums["x"] = sums["x"] + fold(g * x)
                sums["n"] = sums["n"] + fold(g)
                sums["m"] = sums["m"] + fold(low.astype(F32))

        def through_merge(start):
            low = gmb[start : start + GROUP, :]
            kept["w", start] = dot(low, wm[k, :, 0:C])
            kept["h", start] = dot(low, wmid[k])
            kept["third", start] = dot(low, wm[k, :, 2 * C : 3 * C])

        def round_branches(start):
            for o in range(0, GROUP, TILE):
                part = slice(start + o, start + o + TILE)
                one = kept["w", start][o : o + TILE].astype(BF16)
                gwb[part, :] = one
                wcol[part, :] += jnp.sum(one.astype(F32), 1, keepdims=True)
                one = kept["h", start][o : o + TILE].astype(BF16)
                gwh[part, :] = one
                hcol[part, :] += jnp.sum(one.astype(F32), 1, keepdims=True)

        def across_width(start):
            rows = slice(start, start + GROUP)
            crossed = dot(kw[...], gwb[rows, :])
            for o in range(0, GROUP, TILE):
                part = slice(start + o, start + o + TILE)
                gmix[t, part, :] = kept["third", start][o : o + TILE] + crossed[o : o + TILE]
            gw_acc[...] += dot(gwb[rows, :], joined[t, rows, 2 * C : 3 * C], (1, 1))

        def up_grad(start):
            if start == starts[-1]:
                gbt[...] = normal[t].T
                for n in range(2):
                    acc_u[k, n] += dot(gbt[...], gpre[:, n * WIDE : n * WIDE + WIDE])

        def merge_grad(start):
            if start == starts[-1]:
                gmt[...] = gmb[...].T
                for n in range(2):
                    width = min(MT, 3 * C - n * MT)
                    acc_m[k, n, :, 0:width] += dot(gmt[...], joined[t, :, n * MT : n * MT + width])

        in_turn([
            through_gelu, through_up, up_grad, through_norm, through_merge, merge_grad, round_branches, across_width,
        ], starts)
        gs[k, NGAIN : NGAIN + 1, :] += total(sums["x"])
        gs[k, NBIAS : NBIAS + 1, :] += total(sums["n"])
        gs[k, MBIAS : MBIAS + 1, :] += total(sums["m"])
        for n in range(FF // FT):
            gs[k, UBIAS + n : UBIAS + n + 1, 0:FT] += total(sums["u"][n])
        tick(6)
        gh_acc[...] += dot(gwh[...], joined[t, :, 2 * C : 3 * C], (1, 1))

        def batch_sums(start, acc):
            plain, cross = acc
            crossed = dot(kh[pl.ds(start, GROUP), :], gwh[...])
            for o in range(0, GROUP, TILE):
                rows = pl.ds(start + o, TILE)
                g = (gmix[t, rows, :] + crossed[o : o + TILE]) * mask_cols[t, rows, :]
                gmix[t, rows, :] = g
                plain = plain + fold(g)
                cross = cross + fold(g * cv[z, rows, :])
            return plain, cross
        acc = groups(batch_sums, (zero, zero))
        plain, cross = total(acc[0]), total(acc[1])
        gs[k, BBIAS : BBIAS + 1, :] += plain
        gs[k, BGAIN : BGAIN + 1, :] += cross
        r = 4 + z
        msg[r, 0:1, 0:C] = plain
        msg[r, 1:2, 0:C] = cross
        send_stats(r)

    def input_stage(t, k, tick):
        z = 2 * k + t
        r = 4 + z
        wait_stats(r)
        scale, count = stat[z, 0:1, :], stat[z, 1:2, :]
        both = gather_stats(r)
        plain, cross = both[0:1, 0:C], both[1:2, 0:C]
        gain = pack[k, BGAIN : BGAIN + 1, :]
        out_scale = gain * scale
        plain = plain / count
        cross = cross / count

        def shifted(start, carry):
            rows = pl.ds(start, SIDE)
            g = (gmix[t, rows, :] - plain - cv[z, rows, :] * cross) * (mask_cols[t, rows, :] * out_scale)
            rows = pl.ds(start + SIDE, SIDE)
            gsh[0, rows, :] = sooner(g)
            gsh[1, rows, :] = g
            gsh[2, rows, :] = later(g)
            return carry
        grid_rows(shifted, 0)
        tick(8)
        taps = [[pack[k, CONV + n : CONV + n + 1, l:m] for n in range(9)] for l, m in LANES]

        def pull(start, acc):
            new = []
            for (l, m), tap, one in zip(LANES, taps, acc):
                u = [uf[t, pl.ds(start + SIDE * r, SIDE), l:m] for r in range(3)]
                out = gf[t, pl.ds(start, SIDE), l:m]
                sums = []
                for s in range(3):
                    around = [gsh[s, pl.ds(start + SIDE * r, SIDE), l:m] for r in range(3)]
                    out = out + around[2] * tap[s] + around[1] * tap[3 + s] + around[0] * tap[6 + s]
                    sums.append([one[s][r] + fold(around[1] * u[r]) for r in range(3)])
                new.append(sums)
                igbuf[z, lax.div(start, SIDE), :, l:m] = out.astype(BF16)
            return new
        acc = grid_rows(pull, [[[jnp.zeros((8, m - l), F32) for _ in range(3)] for _ in range(3)] for l, m in LANES])
        for (l, m), one in zip(LANES, acc):
            for r in range(3):
                for s in range(3):
                    row = CONV + 3 * r + s
                    gs[k, row : row + 1, l:m] += total(one[s][r])

        @pl.when(k == 1)
        def _():
            def reread(start, carry):
                gf[t, pl.ds(start, SIDE), :] = igbuf[z, lax.div(start, SIDE)].astype(F32)
                return carry
            grid_rows(reread, 0)

        @pl.when(me_p == k)
        def _():
            pltpu.make_async_copy(igbuf.at[z], ig_h.at[0, 2 * me_p + t], ig_local.at[t]).start()

        @pl.when(me_p != k)
        def _():
            across(igbuf.at[z], ig_h.at[0, 2 * me_p + t], ig_send.at[t], ig_recv.at[t]).start()

    def clear_mix():
        gw_acc[...] = jnp.zeros(gw_acc.shape, F32)
        gh_acc[...] = jnp.zeros(gh_acc.shape, F32)
        wcol[...] = jnp.zeros(wcol.shape, F32)
        hcol[...] = jnp.zeros(hcol.shape, F32)

    def close_mix(k):
        i_r, j_r = one_hots(ROWS)
        _, j_g = one_hots(GROUP)
        gs[k, WBIAS : WBIAS + 1, 0:SIDE] = total(jnp.where(j_r, wcol[...], 0.0))
        gs[k, HBIAS : HBIAS + 1, 0:SIDE] = total(jnp.where(i_r, hcol[...], 0.0))
        highest = lax.Precision.HIGHEST
        p = grid_row(lax.broadcasted_iota(jnp.int32, (GROUP, GROUP), 0))
        q = grid_row(lax.broadcasted_iota(jnp.int32, (GROUP, GROUP), 1))
        own = jnp.where(p == q, gw_acc[...], 0.0)
        own = jnp.sum(own.reshape(GROUP // SIDE, SIDE, GROUP), 0)
        gs[k, WW : WW + SIDE, 0:SIDE] = dot(own, jnp.where(j_g, 1.0, 0.0), precision=highest)
        i_f = jnp.where(i_r, 1.0, 0.0)
        for i in range(SIDE):
            rows = slice(i * SIDE, i * SIDE + SIDE)
            own = total(fold(own_column[...] * gh_acc[rows, :]))
            first[i : i + 1, :] = own[:, 0:C]
            gnorm[i : i + 1, 0 : ROWS - C] = own[:, C:ROWS]
        value = dot(first[0:SIDE, :], i_f[0:C, :], precision=highest)
        value += dot(gnorm[0:SIDE, 0 : ROWS - C], i_f[C:ROWS, :], precision=highest)
        gs[k, HW : HW + SIDE, 0:SIDE] = value

    bits = [1, 2]
    while 2 * bits[-1] < n_dp:
        bits.append(2 * bits[-1])
    n_swaps = len(bits) - 2
    n_steps = 1 + 2 + n_swaps + 2

    def partner(bit):
        return me_d + bit * (1 - 2 * lax.rem(me_d // bit, 2))

    def side(bit):
        return lax.rem(me_d // bit, 2)

    def along(bit, src, dst, send, recv):
        return pltpu.make_async_remote_copy(
            src_ref=src, dst_ref=dst, send_sem=send, recv_sem=recv,
            device_id={"dp": partner(bit)}, device_id_type=MESH)

    streams = (
        (acc_d, gd_h, sb_d, lb_d, rl_d), (acc_u, gu_h, sb_u, lb_u, rl_u), (acc_m, gm_h, sb_m, lb_m, rl_m))

    def reduction(k, which):
        acc, out_h, sb, lb, rl = streams[which]
        sb, lb, rl = sb.at[k], lb.at[k], rl.at[k]
        halving = [1 + me_p, 2 - me_p] if which != 1 else [2 - me_p, 1 + me_p]

        def sems(step):
            return red_send.at[3 * k + which, step], red_recv.at[3 * k + which, step]

        def own(q):
            return k, lax.div(q, 2), pl.ds(pl.multiple_of(me_p * HALF + lax.rem(q, 2) * SHARD, 16), SHARD), slice(None)

        def each(count, body):
            if count == 1:
                body(0)
                return

            def step(n, carry):
                body(n)
                return carry
            lax.fori_loop(0, count, step, 0)

        in_chip = across(sb.at[pl.ds(0, SHARDS)], lb, *sems(0))
        base = [0]
        for n, bit in enumerate(halving):
            base.append(base[n] + side(bit) * (2 >> n))
        mine = base[2]

        def half_copy(n):
            count, at = 2 >> n, 2 * n
            return along(halving[n], sb.at[pl.ds(at, count)], rl.at[pl.ds(at, count)], *sems(1 + n))

        def swap_copy(n):
            return along(bits[2 + n], sb.at[3 + n], rl.at[3 + n], *sems(3 + n))

        def double_copy(n):
            count = 2 >> n
            here = lb.at[pl.ds(base[n + 1], count)]
            return along(halving[n], here, here, *sems(n_steps - 1 - n))

        def send_half(n, landed):
            count, at = 2 >> n, 2 * n
            give = base[n] + (1 - side(halving[n])) * count
            keep = base[n + 1]

            def one(q):
                sb[at + q] = (acc[own(give + q)] + landed(give + q).astype(F32)).astype(BF16)
            each(count, one)
            half_copy(n).start()

            def two(q):
                acc[own(keep + q)] += landed(keep + q).astype(F32)
            each(count, two)

        def start():
            def one(q):
                rows = pl.ds(pl.multiple_of(other * HALF + lax.rem(q, 2) * SHARD, 16), SHARD)
                sb[q] = acc[k, lax.div(q, 2), rows, :].astype(BF16)
            each(SHARDS, one)
            in_chip.start()

        def first_half():
            in_chip.wait()
            send_half(0, lambda q: lb[q])

        def second_half():
            half_copy(0).wait()
            send_half(1, lambda q: rl[q - base[1]])

        def swap(n):
            def run():
                if n == 0:
                    half_copy(1).wait()
                    sb[3] = (acc[own(mine)] + rl[2].astype(F32)).astype(BF16)
                else:
                    swap_copy(n - 1).wait()
                    sb[3 + n] = (sb[2 + n].astype(F32) + rl[2 + n].astype(F32)).astype(BF16)
                swap_copy(n).start()
            return run

        def double(n):
            def run():
                if n == 1:
                    last = n_swaps - 1
                    swap_copy(last).wait()
                    lb[mine] = (sb[3 + last].astype(F32) + rl[3 + last].astype(F32)).astype(BF16)
                else:
                    double_copy(n + 1).wait()
                double_copy(n).start()
            return run

        def hand_over():
            double_copy(0).wait()

            @pl.when(me_p == k)
            def _():
                pltpu.make_async_copy(lb, out_h.at[me_p], out_local.at[which]).start()

            @pl.when(me_p != k)
            def _():
                across(lb, out_h.at[me_p], out_send.at[which], out_recv.at[which]).start()

        return [start, first_half, second_half] + [swap(n) for n in range(n_swaps)] + [double(1), double(0), hand_over]

    def small_sum(rows, landing, send, recv):
        count = rows.stop - rows.start
        rows = pl.ds(rows.start, count)
        in_chip = across(gs.at[other, rows], landing.at[0], send.at[0], recv.at[0])

        def swap_copy(n):
            return along(bits[n], gs.at[me_p, rows], landing.at[1 + n], send.at[1 + n], recv.at[1 + n])

        def step(n):
            def run():
                (swap_copy(n - 1) if n else in_chip).wait()
                gs[me_p, rows, :] += landing[n]
                if n < len(bits):
                    swap_copy(n).start()
            return run
        return [in_chip.start] + [step(n) for n in range(len(bits) + 1)]

    small = small_sum(slice(SMALL, PACK), small_land, small_send, small_recv)
    taps_sum = small_sum(slice(0, SMALL), conv_land, conv_send, conv_recv)

    plan = {}
    backward_places, input_places = [0, 1, 6, 11], [7, 8, 9]
    order = []
    for n in range(6):
        order += [(n, p) for p in input_places] if n > 1 else []
        order += [(n, p) for p in backward_places] if n < 4 else []

    def put(start, steps, gap):
        at = order.index(start)
        steps = list(steps)
        while steps and at < len(order):
            plan.setdefault(order[at], []).append(steps.pop(0))
            at += gap
        return steps

    for which, place in enumerate((1, 6, 6)):
        assert not put((1, place), reduction(1, which), 1)
    tails = [put((3, place), reduction(0, which), 2 if which else 1) for which, place in enumerate((1, 6, 6))]
    tails.append(put((4, 7), small, 2))
    tails.append(list(taps_sum))

    pack_over.wait()
    for t in range(2):
        image_in[t].wait()

    def widen_image(t):
        def widen(i, inner):
            uf[t, pl.ds(pl.multiple_of(i * SIDE + SIDE, SIDE), SIDE), :] = ub[t, i].astype(F32)
            return inner
        lax.fori_loop(0, SIDE, widen, 0)

    def start_image(t, carry):
        widen_image(t)
        conv_stage(t, 0)
        return carry
    lax.fori_loop(0, 2, start_image, 0)
    for t in range(2):
        grad_in[t].start()

    for copy in weights_in + weights_over:
        copy.wait()
    for k in range(2):
        wmid[k] = wm[k, :, C : 2 * C]

    def forward_block(k, carry):
        mixers(k, False)

        def one(t, inner):
            forward_stage(t, k)

            @pl.when(k == 0)
            def _():
                for copy in spill(t):
                    copy.start()
                conv_stage(t, 1)
            return inner
        lax.fori_loop(0, 2, one, 0)
        return carry
    lax.fori_loop(0, 2, forward_block, 0)

    for t in range(2):
        grad_in[t].wait()
        pltpu.make_async_copy(ybuf.at[t], so_h.at[0, t], so_local.at[t]).wait()
        across(ybuf.at[t], so_h.at[0, t], so_send.at[t], so_recv.at[t]).wait_send()

    def load_grad(t, carry):
        def widen(i, inner):
            gf[t, pl.ds(pl.multiple_of(i * SIDE, SIDE), SIDE), :] = ub[t, i].astype(F32)
            return inner
        lax.fori_loop(0, SIDE, widen, 0)
        return carry
    lax.fori_loop(0, 2, load_grad, 0)
    for t in range(2):
        image_copy(t, again_sems.at[t]).start()

    def turn(s, carry):
        t = lax.rem(s, 2)

        def tick(place):
            for n in range(6):
                steps = plan.get((n, place), [])
                if steps:
                    @pl.when(s == n)
                    def _():
                        for step in steps:
                            step()

        @pl.when(lax.rem(s, 2) == 0)
        def _():
            @pl.when(s > 0)
            def _():
                close_mix(2 - lax.div(s, 2))

            @pl.when(s < 4)
            def _():
                mixers(1 - lax.div(s, 2), True)
                clear_mix()

        @pl.when(s > 1)
        def _():
            @pl.when(s > 3)
            def _():
                image_copy(t, again_sems.at[t]).wait()
                widen_image(t)
            tick(7)
            input_stage(t, 2 - lax.div(s, 2), tick)
            tick(9)

        @pl.when(s < 4)
        def _():
            @pl.when(s > 1)
            def _():
                for copy in fetch(t):
                    copy.wait()
            tick(0)
            backward_stage(t, 1 - lax.div(s, 2), tick)
            tick(11)

            @pl.when(s < 2)
            def _():
                for copy in fetch(t):
                    copy.start()
        return carry
    lax.fori_loop(0, 6, turn, 0)

    while any(tails):
        for steps in tails:
            if steps:
                steps.pop(0)()

    gs_out = pltpu.make_async_copy(gs.at[me_p], gs_h, gs_sem.at[0])
    gs_out.start()
    for t in range(2):
        pltpu.make_async_copy(igbuf.at[t], ig_h.at[0, t], ig_local.at[t]).wait()
        across(ybuf.at[t], so_h.at[0, t], so_send.at[t], so_recv.at[t]).wait_recv()
        across(igbuf.at[t], ig_h.at[0, t], ig_send.at[t], ig_recv.at[t]).wait()
    for n, (_, out_h, _, lb, _) in enumerate(streams):
        pltpu.make_async_copy(lb.at[0], out_h.at[0], out_local.at[n]).wait()
        across(lb.at[0], out_h.at[0], out_send.at[n], out_recv.at[n]).wait()
    gs_out.wait()


def finish_kernel(
    so_in, ig_in, gd_in, gu_in, gm_in, gs,
    so, ig, conv, bgain, bbias, ww, wb, hw, hb, gm, mbias, ngain, nbias, gu, ubias, gd, dbias,
    large, d_in, u_in, m_in, d_out, u_out, m_out, in_sems, out_sems,
):
    moved = ((gd_in, d_in), (gu_in, u_in), (gm_in, m_in), (so_in, large.at[0]), (ig_in, large.at[1]))
    arrive = [pltpu.make_async_copy(src, dst, in_sems.at[n]) for n, (src, dst) in enumerate(moved)]
    for copy in arrive:
        copy.start()
    moved = ((d_out, gd), (u_out, gu), (m_out, gm), (large.at[0], so), (large.at[1], ig))
    leave = [pltpu.make_async_copy(src, dst, out_sems.at[n]) for n, (src, dst) in enumerate(moved)]
    for n in range(9):
        conv[n] = gs[CONV + n : CONV + n + 1, :]
    for row, ref in ((BGAIN, bgain), (BBIAS, bbias), (MBIAS, mbias), (NGAIN, ngain), (NBIAS, nbias), (DBIAS, dbias)):
        ref[...] = gs[row : row + 1, :]
    for row, ref in ((WBIAS, wb), (HBIAS, hb)):
        ref[...] = gs[row : row + 1, 0:SIDE]
    for n in range(FF // FT):
        ubias[:, n * FT : n * FT + FT] = gs[UBIAS + n : UBIAS + n + 1, 0:FT]
    for row, ref in ((WW, ww), (HW, hw)):
        ref[0] = gs[row : row + SIDE, 0:SIDE]
    for n, (src, dst, piece) in enumerate(((d_in, d_out, WIDE), (u_in, u_out, WIDE), (m_in, m_out, MT))):
        arrive[n].wait()
        for p in range(2):
            for q in range(SHARDS):
                start, at = p * HALF + (q % 2) * SHARD, piece * (q // 2)
                width = min(piece, dst.shape[1] - at)
                dst[start : start + SHARD, at : at + width] = src[p, q, :, 0:width].astype(F32)
        leave[n].start()
    for n in (3, 4):
        arrive[n].wait()
        leave[n].start()
    for copy in leave:
        copy.wait()


def on_device(
    images, masks, conv_weight, batch_gain, batch_bias, width_weight, width_bias,
    height_weight, height_bias, merge_weight, merge_bias, norm_gain, norm_bias,
    up_weight, up_bias, down_weight, down_bias, out_grad,
):
    n_dp = lax.axis_size("dp")
    micro = images.shape[0]
    steps = max(n_dp.bit_length() - 1, 4)
    any_space = pl.BlockSpec(memory_space=pl.ANY)
    vmem = pl.BlockSpec(memory_space=pltpu.VMEM)
    dma = pltpu.SemaphoreType.DMA
    grid = (SIDE, SIDE, C)
    shape = jax.ShapeDtypeStruct
    outs = pl.pallas_call(
        functools.partial(kernel, n_dp),
        out_shape=(
            shape((1, micro) + grid, BF16),
            shape((1, micro) + grid, BF16),
            shape((2, SHARDS, SHARD, WIDE), BF16),
            shape((2, SHARDS, SHARD, WIDE), BF16),
            shape((2, SHARDS, SHARD, MT), BF16),
            shape((PACK, C), F32),
            shape((2, ROWS, FF), BF16),
            shape((2, ROWS, FF), BF16),
            shape((2, ROWS, 3 * C), BF16),
            shape((2, ROWS, C), BF16),
            shape((2, ROWS, C), BF16),
        ),
        in_specs=[any_space] + [vmem] * 8 + [any_space] + [vmem] * 3 + [any_space, vmem, any_space, vmem, any_space],
        out_specs=(any_space,) * 11,
        scratch_shapes=[
            pltpu.VMEM((2, ROWS, 1), F32),
            pltpu.VMEM((4, 2, C), F32),
            pltpu.VMEM((SIDE, ROWS), F32),
            pltpu.VMEM((ROWS, SIDE), BF16),
            pltpu.VMEM((2, PACK, C), F32),
            pltpu.VMEM((2, C, 3 * C), BF16),
            pltpu.VMEM((2, C, C), BF16),
            pltpu.VMEM((2, C, FF), BF16),
            pltpu.VMEM((2, C, FF), BF16),
            pltpu.VMEM((2,) + grid, BF16),
            pltpu.VMEM((2, ROWS + 2 * SIDE, C), F32),
            pltpu.VMEM((4, ROWS, C), F32),
            pltpu.VMEM((2, ROWS, 3 * C), BF16),
            pltpu.VMEM((2, ROWS, C), BF16),
            pltpu.VMEM((2, ROWS, C), BF16),
            pltpu.VMEM((4, ROWS, 1), F32),
            pltpu.VMEM((2, ROWS, FF), BF16),
            pltpu.VMEM((2, ROWS, FF), BF16),
            pltpu.VMEM((2, ROWS, C), F32),
            pltpu.VMEM((ROWS, C), BF16),
            pltpu.VMEM((ROWS, C), BF16),
            pltpu.VMEM((ROWS, C), BF16),
            pltpu.VMEM((C, ROWS), BF16),
            pltpu.VMEM((C, ROWS), BF16),
            pltpu.VMEM((ROWS, FF), BF16),
            pltpu.VMEM((2, ROWS, C), F32),
            pltpu.VMEM((ROWS, C), BF16),
            pltpu.VMEM((3, ROWS + 2 * SIDE, C), F32),
            pltpu.VMEM((GROUP, GROUP), BF16),
            pltpu.VMEM((ROWS, ROWS), BF16),
            pltpu.VMEM((ROWS, 1), F32),
            pltpu.VMEM((ROWS, 1), F32),
            pltpu.VMEM((GROUP, GROUP), F32),
            pltpu.VMEM((ROWS, ROWS), F32),
            pltpu.VMEM((ROWS, 1), F32),
            pltpu.VMEM((ROWS, 1), F32),
            pltpu.VMEM((4,) + grid, BF16),
            pltpu.VMEM((8, 2, CP), F32),
            pltpu.VMEM((8, n_dp - 1, 2, CP), F32),
            pltpu.VMEM((2, 2, C, WIDE), F32),
            pltpu.VMEM((2, 2, C, WIDE), F32),
            pltpu.VMEM((2, 2, C, MT), F32),
            pltpu.VMEM((2, PACK, C), F32),
            pltpu.VMEM((2, 1 + steps, SHARD, WIDE), BF16),
            pltpu.VMEM((2, SHARDS, SHARD, WIDE), BF16),
            pltpu.VMEM((2, 1 + steps, SHARD, WIDE), BF16),
            pltpu.VMEM((2, 1 + steps, SHARD, WIDE), BF16),
            pltpu.VMEM((2, SHARDS, SHARD, WIDE), BF16),
            pltpu.VMEM((2, 1 + steps, SHARD, WIDE), BF16),
            pltpu.VMEM((2, 1 + steps, SHARD, MT), BF16),
            pltpu.VMEM((2, SHARDS, SHARD, MT), BF16),
            pltpu.VMEM((2, 1 + steps, SHARD, MT), BF16),
            pltpu.VMEM((1 + steps, PACK - SMALL, C), F32),
            pltpu.VMEM((1 + steps, SMALL, C), F32),
            dma((9,)), dma((2,)), dma((2,)), dma((3,)), dma((3,)), dma((8,)), dma((8,)),
            dma((2,)), dma((2,)), dma((2,)), dma((2,)), dma((2,)), dma((2,)), dma((2, 5)), dma((2, 5)),
            dma((6, 3 + steps)), dma((6, 3 + steps)), dma((1 + steps,)), dma((1 + steps,)),
            dma((1 + steps,)), dma((1 + steps,)), dma((3,)), dma((3,)), dma((3,)), dma((1,)),
        ],
        compiler_params=pltpu.CompilerParams(
            collective_id=0, has_side_effects=True, vmem_limit_bytes=65400 * 1024),
    )(
        images, masks, conv_weight, batch_gain, batch_bias, width_weight, width_bias, height_weight, height_bias,
        merge_weight[0].T, merge_bias, norm_gain, norm_bias, up_weight[0], up_bias, down_weight[0].T, down_bias, out_grad)

    row = shape((1, C), F32)
    square, line = shape((1, SIDE, SIDE), F32), shape((1, SIDE), F32)
    so, ig, conv, bgain, bbias, ww, wb, hw, hb, gm, mbias, ngain, nbias, gu, ubias, gd, dbias = pl.pallas_call(
        finish_kernel,
        out_shape=(
            shape((1, micro) + grid, BF16), shape((1, micro) + grid, BF16), shape((9, 1, C), F32), row, row,
            square, line, square, line, shape((C, 3 * C), F32), row, row, row,
            shape((C, FF), F32), shape((1, FF), F32), shape((C, FF), F32), row),
        in_specs=[any_space] * 5 + [vmem],
        out_specs=(any_space,) * 2 + (vmem,) * 7 + (any_space,) + (vmem,) * 3 + (any_space, vmem, any_space, vmem),
        scratch_shapes=[
            pltpu.VMEM((2, 1, micro) + grid, BF16),
            pltpu.VMEM((2, SHARDS, SHARD, WIDE), BF16),
            pltpu.VMEM((2, SHARDS, SHARD, WIDE), BF16),
            pltpu.VMEM((2, SHARDS, SHARD, MT), BF16),
            pltpu.VMEM((C, FF), F32),
            pltpu.VMEM((C, FF), F32),
            pltpu.VMEM((C, 3 * C), F32),
            dma((5,)), dma((5,)),
        ],
        compiler_params=pltpu.CompilerParams(vmem_limit_bytes=65400 * 1024),
    )(*outs[:6])
    return (
        so, ig, jnp.swapaxes(conv, 0, 1), bgain, bbias, ww, wb, hw, hb, gm.T[None], mbias, ngain, nbias,
        gu[None], ubias, gd.T[None], dbias)


def solution(mesh):
    data4 = P("dp", None, None, None)
    p1, p2, p3 = P("pipe"), P("pipe", None), P("pipe", None, None)
    out5 = P("pipe", "dp", None, None, None)
    return jax.shard_map(
        on_device,
        mesh=mesh,
        in_specs=(data4, P("dp", None, None), p3, p2, p2, p3, p2, p3, p2, p3, p2, p2, p2, p3, p2, p3, p2, data4),
        out_specs=(out5, out5, p3, p2, p2, p3, p2, p3, p2, p3, p2, p2, p2, p3, p2, p3, p2),
        check_vma=False,
    )
```

```python
import functools

import jax
import jax.numpy as jnp
from jax import lax
from jax.experimental import pallas as pl
from jax.experimental.pallas import tpu as pltpu
from jax.sharding import PartitionSpec as P

EPS = 1e-05
MESH = pl.DeviceIdType.MESH
F32 = jnp.float32
BF16 = jnp.bfloat16

SIDE = 24
ROWS = SIDE * SIDE
C = 320
CP = 384
FF = 1280
FT = 256
CHUNK = 48
TILE = 32
LANES = ((0, 128), (128, 256), (256, 320))
GROUP = 8 * SIDE

HALF = C // 2
SHARD = HALF // 2
WIDE = FF // 2
SHARDS = 4
MT = 512
STEP = 24

CONV, BGAIN, BBIAS, MBIAS, NGAIN, NBIAS, DBIAS, WBIAS, HBIAS, UBIAS, WW, HW, PACK = (
    0, 16, 17, 18, 19, 20, 21, 22, 23, 24, 32, 56, 80)
SMALL = 16


def dot(a, b, contract=(1, 0), precision=None):
    return lax.dot_general(
        a, b, (((contract[0],), (contract[1],)), ((), ())),
        preferred_element_type=F32, precision=precision)


def in_turn(phases, starts):
    for step in range(len(phases) + len(starts) - 1):
        for g, start in enumerate(starts):
            if 0 <= step - g < len(phases):
                phases[step - g](start)


def fold(value):
    rows = value.shape[0]
    return jnp.sum(value.reshape(rows // 8, 8, value.shape[1]), 0)


def total(partial):
    return jnp.sum(partial, 0, keepdims=True)


def grid_row(index):
    return (index * 2731) >> 16


def one_hots(rows):
    place = lax.broadcasted_iota(jnp.int32, (rows, SIDE), 0)
    lane = lax.broadcasted_iota(jnp.int32, (rows, SIDE), 1)
    i = grid_row(place)
    return i == lane, place - SIDE * i == lane


def gelu_both(x):
    e = jnp.exp2(x * x * -0.7213475204444817)
    d = 1.0 + 0.23164189 * jnp.abs(x)
    t = pl.reciprocal(d, approx=True)
    poly = t * (0.127414796 + t * (-0.142248368 + t * (0.7107068705 + t * (-0.7265760135 + t * 0.5307027145))))
    tail = poly * e
    phi = jnp.where(x >= 0, 1.0 - tail, tail)
    return x * phi, phi + x * e * 0.3989422804014327


def kernel(
    n_dp,
    images, masks, conv_w, bgain, bbias, wwt, wb, hwt, hb, wm_h, mbias, ngain, nbias, wu_h, ubias, wd_h, dbias, og_h,
    so_h, ig_h, gd_h, gu_h, gm_h, gs_h, sp_hidden, sp_gp, sp_joined, sp_normal, sp_xl,
    mask_cols, stat, own_column, i_hot, pack, wm, wmid, wu, wd, ub, uf, cv, joined, normal, xl, rstd, hidden, gp,
    gf, gb, gmb, gwb, gbt, gmt, gpre, gmix, gwh, gsh, kw, kh, wbcol, hbcol,
    gw_acc, gh_acc, wcol, hcol, ybuf, msg, land, acc_d, acc_u, acc_m, gs,
    sb_d, lb_d, rl_d, sb_u, lb_u, rl_u, sb_m, lb_m, rl_m, small_land, conv_land,
    local_sems, again_sems, pack_sems, w_send, w_recv, st_send, st_recv,
    so_local, so_send, so_recv, ig_local, ig_send, ig_recv, spill_sems, fetch_sems,
    red_send, red_recv, small_send, small_recv, conv_send, conv_recv, out_local, out_send, out_recv, gs_sem,
):
    me_p = lax.axis_index("pipe")
    me_d = lax.axis_index("dp")
    other = 1 - me_p
    first = gsh.at[2, pl.ds(SIDE, ROWS)]
    igbuf = ybuf
    gnorm = gsh.at[0, pl.ds(SIDE, ROWS)]

    def image_copy(t, sems):
        return pltpu.make_async_copy(images.at[2 * me_p + t], ub.at[t], sems)

    image_in = [image_copy(t, local_sems.at[5 + t]) for t in range(2)]
    grad_in = [pltpu.make_async_copy(og_h.at[2 * me_p + t], ub.at[t], local_sems.at[7 + t]) for t in range(2)]
    weights = ((wm_h, wm), (wu_h, wu), (wd_h, wd))
    weights_in = [pltpu.make_async_copy(src, dst.at[me_p], local_sems.at[n]) for n, (src, dst) in enumerate(weights)]
    for copy in image_in + weights_in:
        copy.start()

    barrier = pltpu.get_barrier_semaphore()

    def greet(step, carry):
        pl.semaphore_signal(barrier, inc=1, device_id={"dp": lax.rem(me_d + step, n_dp)}, device_id_type=MESH)
        return carry

    lax.fori_loop(1, n_dp, greet, 0)
    pl.semaphore_signal(barrier, inc=1, device_id={"pipe": other}, device_id_type=MESH)

    pack[me_p] = jnp.zeros(pack.shape[1:], F32)
    pack[me_p, CONV : CONV + 9, :] = conv_w[0].astype(F32)
    for row, ref in ((BGAIN, bgain), (BBIAS, bbias), (MBIAS, mbias), (NGAIN, ngain), (NBIAS, nbias), (DBIAS, dbias)):
        pack[me_p, row : row + 1, :] = ref[...]
    for row, ref in ((WBIAS, wb), (HBIAS, hb)):
        pack[me_p, row : row + 1, 0:SIDE] = ref[...]
    for n in range(FF // FT):
        pack[me_p, UBIAS + n : UBIAS + n + 1, 0:FT] = ubias[:, n * FT : n * FT + FT]
    for row, ref in ((WW, wwt), (HW, hwt)):
        pack[me_p, row : row + SIDE, 0:SIDE] = ref[0].astype(F32)

    pl.semaphore_wait(barrier, n_dp)

    def across(src, dst, send, recv):
        return pltpu.make_async_remote_copy(
            src_ref=src, dst_ref=dst, send_sem=send, recv_sem=recv,
            device_id={"pipe": other}, device_id_type=MESH)

    pack_over = across(pack.at[me_p], pack.at[me_p], pack_sems.at[0], pack_sems.at[1])
    weights_over = [across(src, dst.at[me_p], w_send.at[n], w_recv.at[n]) for n, (src, dst) in enumerate(weights)]
    pack_over.start()
    for copy in weights_over:
        copy.start()

    msg[...] = jnp.zeros(msg.shape, F32)
    for k in range(2):
        for acc in (acc_d, acc_u, acc_m):
            for n in range(2):
                acc[k, n] = jnp.zeros(acc.shape[2:], F32)
        gs[k] = jnp.zeros(gs.shape[1:], F32)
    for n in range(2):
        uf[n, 0:SIDE, :] = jnp.zeros((SIDE, C), F32)
        uf[n, SIDE + ROWS : 2 * SIDE + ROWS, :] = jnp.zeros((SIDE, C), F32)
    for n in range(3):
        gsh[n, 0:SIDE, :] = jnp.zeros((SIDE, C), F32)
        gsh[n, SIDE + ROWS : 2 * SIDE + ROWS, :] = jnp.zeros((SIDE, C), F32)

    i_r, j_r = one_hots(ROWS)
    i_hot[...] = jnp.where(i_r, 1.0, 0.0).astype(BF16)
    q = lax.broadcasted_iota(jnp.int32, (SIDE, ROWS), 1)
    q = q - SIDE * grid_row(q)
    own_column[...] = jnp.where(lax.broadcasted_iota(jnp.int32, (SIDE, ROWS), 0) == q, 1.0, 0.0)
    for t in range(2):
        chosen = dot(i_hot[...], masks[2 * me_p + t].astype(F32).astype(BF16))
        mask_cols[t] = jnp.sum(jnp.where(j_r, chosen, 0.0), 1, keepdims=True)

    def later(value):
        at = lax.broadcasted_iota(jnp.int32, value.shape, 0)
        return jnp.where(at != 0, pltpu.roll(value, 1, 0), 0.0)

    def sooner(value):
        at = lax.broadcasted_iota(jnp.int32, value.shape, 0)
        return jnp.where(at != SIDE - 1, pltpu.roll(value, SIDE - 1, 0), 0.0)

    def grid_rows(body, init):
        def step(c, carry):
            for row in range(STEP):
                carry = body(pl.multiple_of(c * (STEP * SIDE), STEP * SIDE) + row * SIDE, carry)
            return carry
        return lax.fori_loop(0, SIDE // STEP, step, init)

    def groups(body, init):
        for g in range(ROWS // GROUP):
            init = body(g * GROUP, init)
        return init

    def send_stats(r):
        def one(step, carry):
            pltpu.make_async_remote_copy(
                src_ref=msg.at[r], dst_ref=land.at[r, n_dp - 1 - step],
                send_sem=st_send.at[r], recv_sem=st_recv.at[r],
                device_id={"dp": lax.rem(me_d + step, n_dp)}, device_id_type=MESH).start()
            return carry
        lax.fori_loop(1, n_dp, one, 0)

    def wait_stats(r):
        whole = pltpu.make_async_remote_copy(
            src_ref=land.at[r], dst_ref=land.at[r], send_sem=st_send.at[r], recv_sem=st_recv.at[r],
            device_id={"dp": lax.rem(me_d + 1, n_dp)}, device_id_type=MESH)
        whole.wait_send()
        whole.wait_recv()

    def conv_stage(t, k):
        z = 2 * k + t
        n_own = total(mask_cols[t])
        taps = [[pack[k, CONV + n : CONV + n + 1, l:m] for n in range(9)] for l, m in LANES]

        def conv(start, acc):
            at = pl.ds(start, SIDE)
            new = []
            for (l, m), tap, one in zip(LANES, taps, acc):
                rows = [uf[t, pl.ds(start + SIDE * r, SIDE), l:m] for r in range(3)]
                part = [rows[0] * tap[s] + rows[1] * tap[3 + s] + rows[2] * tap[6 + s] for s in range(3)]
                out = part[1] + later(part[0]) + sooner(part[2])
                cv[z, at, l:m] = out
                new.append(one + fold(out * mask_cols[t, at, :]))
            return new
        acc = grid_rows(conv, [jnp.zeros((8, m - l), F32) for l, m in LANES])
        sums = jnp.concatenate([total(one) for one in acc], 1)
        mean = sums / n_own

        def centred(start, acc):
            rows = pl.ds(start, SIDE)
            d = cv[z, rows, :] - mean
            return acc + fold(d * d * mask_cols[t, rows, :])

        m2 = total(grid_rows(centred, jnp.zeros((8, C), F32)))
        msg[z, 0:1, 0:C] = sums
        msg[z, 0:1, C:CP] = jnp.broadcast_to(n_own, (1, CP - C))
        msg[z, 1:2, 0:C] = m2
        send_stats(z)

    def peers(body, init):
        if n_dp > 16:
            return lax.fori_loop(0, n_dp - 1, body, init)
        for d in range(n_dp - 1):
            init = body(d, init)
        return init

    def gather_stats(r):
        def add(d, carry):
            return carry + land[r, d]
        return peers(add, msg[r])

    def norm_stats(z):
        sums = gather_stats(z)[0:1, :]
        count = sums[:, CP - 1 : CP]
        mean = sums[:, 0:C] / count

        def spread(values):
            n = values[0:1, CP - 1 : CP]
            off = values[0:1, 0:C] / n - mean
            return values[1:2, 0:C] + n * off * off

        def add(d, carry):
            return carry + spread(land[z, d])
        m2 = peers(add, spread(msg[z]))
        scale = lax.rsqrt(m2 / count + EPS)
        stat[z, 0:1, :] = scale
        stat[z, 1:2, :] = jnp.broadcast_to(count, (1, C))
        return mean, scale

    def mixers(k, backward):
        _, j_g = one_hots(GROUP)
        ww = pack[k, WW : WW + SIDE, 0:SIDE].astype(BF16)
        hw = pack[k, HW : HW + SIDE, 0:SIDE].astype(BF16)
        side_of = 0 if backward else 1
        j_b = jnp.where(j_g, 1.0, 0.0).astype(BF16)
        left = dot(j_b, ww, (1, 1 - side_of)).astype(BF16)
        p = grid_row(lax.broadcasted_iota(jnp.int32, (GROUP, GROUP), 0))
        q = grid_row(lax.broadcasted_iota(jnp.int32, (GROUP, GROUP), 1))
        kw[...] = jnp.where(p == q, dot(left, j_b, (1, 1)), 0.0).astype(BF16)
        spread = dot(hw, i_hot[...], (side_of, 1))
        own = own_column[...]
        for i in range(0, SIDE, 2):
            two = jnp.concatenate([spread[i : i + 1, :] * own, spread[i + 1 : i + 2, :] * own], 0)
            kh[i * SIDE : i * SIDE + 2 * SIDE, :] = two.astype(BF16)
        if not backward:
            i_r, j_r = one_hots(ROWS)
            wb = pack[k, WBIAS : WBIAS + 1, 0:SIDE]
            hb = pack[k, HBIAS : HBIAS + 1, 0:SIDE]
            wbcol[...] = jnp.sum(jnp.where(j_r, wb, 0.0), 1, keepdims=True)
            hbcol[...] = jnp.sum(jnp.where(i_r, hb, 0.0), 1, keepdims=True)

    stored = ((hidden, sp_hidden), (gp, sp_gp), (joined, sp_joined), (normal, sp_normal), (xl, sp_xl))

    def spill(t):
        return [pltpu.make_async_copy(v.at[t], h.at[t], spill_sems.at[t, n]) for n, (v, h) in enumerate(stored)]

    def fetch(t):
        return [pltpu.make_async_copy(h.at[t], v.at[t], fetch_sems.at[t, n]) for n, (v, h) in enumerate(stored)]

    def forward_stage(t, k):
        z = 2 * k + t

        @pl.when(k == 1)
        def _():
            for copy in spill(t):
                copy.wait()

        wait_stats(z)
        mean, scale = norm_stats(z)
        gain = pack[k, BGAIN : BGAIN + 1, :]
        bias = pack[k, BBIAS : BBIAS + 1, :]

        def standardize(start, carry):
            for o in range(0, GROUP, TILE):
                rows = pl.ds(start + o, TILE)
                x = (cv[z, rows, :] - mean) * scale
                cv[z, rows, :] = x
                joined[t, rows, 2 * C : 3 * C] = ((x * gain + bias) * mask_cols[t, rows, :]).astype(BF16)
            along = dot(kw[...], joined[t, pl.ds(start, GROUP), 2 * C : 3 * C])
            for o in range(0, GROUP, TILE):
                rows = pl.ds(start + o, TILE)
                joined[t, rows, 0:C] = (along[o : o + TILE] + wbcol[rows, :]).astype(BF16)
            return carry
        groups(standardize, 0)

        m_bias = pack[k, MBIAS : MBIAS + 1, :]
        n_gain = pack[k, NGAIN : NGAIN + 1, :]
        n_bias = pack[k, NBIAS : NBIAS + 1, :]
        d_bias = pack[k, DBIAS : DBIAS + 1, :]
        u_bias = [pack[k, UBIAS + n : UBIAS + n + 1, 0:FT] for n in range(FF // FT)]

        starts = [g * GROUP for g in range(ROWS // GROUP)]
        merged, down = {}, {}

        def mix(start):
            rows = slice(start, start + GROUP)
            along = dot(kh[rows, :], joined[t, :, 2 * C : 3 * C])
            for o in range(0, GROUP, TILE):
                part = slice(start + o, start + o + TILE)
                joined[t, part, C : 2 * C] = (along[o : o + TILE] + hbcol[part, :]).astype(BF16)
            merged[start] = dot(joined[t, rows, :], wm[k], (1, 1))

        def layer_norm(start):
            for o in range(0, GROUP, TILE):
                part = slice(start + o, start + o + TILE)
                f = uf[t, start + SIDE + o : start + SIDE + o + TILE, :] + merged[start][o : o + TILE] + m_bias
                d = f - jnp.mean(f, 1, keepdims=True)
                rs = lax.rsqrt(jnp.mean(d * d, 1, keepdims=True) + EPS)
                x = d * rs
                first[part, :] = f
                rstd[z, part, :] = rs
                xl[t, part, :] = x.astype(BF16)
                normal[t, part, :] = (x * n_gain + n_bias).astype(BF16)

        def activate(start):
            rows = slice(start, start + GROUP)
            norm = normal[t, rows, :]
            pre = dot(norm, wu[k, :, 0:FT])
            for n in range(FF // FT):
                cols = slice(n * FT, n * FT + FT)
                now = pre
                if n + 1 < FF // FT:
                    pre = dot(norm, wu[k, :, n * FT + FT : n * FT + 2 * FT])
                for o in range(0, GROUP, TILE):
                    part = slice(start + o, start + o + TILE)
                    h, dh = gelu_both(now[o : o + TILE] + u_bias[n])
                    hidden[t, part, cols] = h.astype(BF16)
                    gp[t, part, cols] = dh.astype(BF16)

        def project(start):
            down[start] = dot(hidden[t, start : start + GROUP, :], wd[k], (1, 1))

        def finish(start):
            for r in range(GROUP // SIDE):
                part = slice(start + r * SIDE, start + r * SIDE + SIDE)
                y = first[part, :] + down[start][r * SIDE : r * SIDE + SIDE] + d_bias
                ybuf[z, start // SIDE + r] = y.astype(BF16)

        in_turn([mix, layer_norm, activate, project, finish], starts)

        @pl.when(k == 0)
        def _():
            def reread(start, carry):
                uf[t, pl.ds(start + SIDE, SIDE), :] = ybuf[z, lax.div(start, SIDE)].astype(F32)
                return carry
            grid_rows(reread, 0)

        @pl.when(me_p == k)
        def _():
            pltpu.make_async_copy(ybuf.at[z], so_h.at[0, 2 * me_p + t], so_local.at[t]).start()

        @pl.when(me_p != k)
        def _():
            across(ybuf.at[z], so_h.at[0, 2 * me_p + t], so_send.at[t], so_recv.at[t]).start()

    def backward_stage(t, k, tick):
        z = 2 * k + t
        zero = jnp.zeros((8, C), F32)
        n_gain = pack[k, NGAIN : NGAIN + 1, :]

        d_acc = zero
        for o in range(0, ROWS, TILE):
            g = gf[t, o : o + TILE, :]
            gb[o : o + TILE, :] = g.astype(BF16)
            d_acc = d_acc + fold(g)
        gs[k, DBIAS : DBIAS + 1, :] += total(d_acc)
        gbt[...] = gb[...].T
        for n in range(2):
            acc_d[k, n] += dot(gbt[...], hidden[t, :, n * WIDE : n * WIDE + WIDE])
        tick(1)

        starts = [g * GROUP for g in range(ROWS // GROUP)]
        sums = {"x": zero, "n": zero, "m": zero, "u": [jnp.zeros((8, FT), F32) for _ in range(FF // FT)]}
        kept = {}

        def through_gelu(start):
            low = gb[start : start + GROUP, :]
            raw = dot(low, wd[k, :, 0:FT])
            for n in range(FF // FT):
                cols = slice(n * FT, n * FT + FT)
                now = raw
                if n + 1 < FF // FT:
                    raw = dot(low, wd[k, :, n * FT + FT : n * FT + 2 * FT])
                for o in range(0, GROUP, TILE):
                    part = slice(start + o, start + o + TILE)
                    gpn = (now[o : o + TILE] * gp[t, part, cols].astype(F32)).astype(BF16)
                    gpre[part, cols] = gpn
                    sums["u"][n] = sums["u"][n] + fold(gpn.astype(F32))

        def through_up(start):
            kept["back", start] = dot(gpre[start : start + GROUP, :], wu[k], (1, 1))

        def through_norm(start):
            for o in range(0, GROUP, TILE):
                part = slice(start + o, start + o + TILE)
                g = kept["back", start][o : o + TILE]
                x = xl[t, part, :].astype(F32)
                gn = g * n_gain
                mean_g = jnp.mean(gn, 1, keepdims=True)
                mean_gx = jnp.mean(gn * x, 1, keepdims=True)
                out = gf[t, part, :] + rstd[z, part, :] * (gn - mean_g - x * mean_gx)
                gf[t, part, :] = out
                low = out.astype(BF16)
                gmb[part, :] = low
                sums["x"] = sums["x"] + fold(g * x)
                sums["n"] = sums["n"] + fold(g)
                sums["m"] = sums["m"] + fold(low.astype(F32))

        def through_merge(start):
            low = gmb[start : start + GROUP, :]
            kept["w", start] = dot(low, wm[k, :, 0:C])
            kept["h", start] = dot(low, wmid[k])
            kept["third", start] = dot(low, wm[k, :, 2 * C : 3 * C])

        def round_branches(start):
            for o in range(0, GROUP, TILE):
                part = slice(start + o, start + o + TILE)
                one = kept["w", start][o : o + TILE].astype(BF16)
                gwb[part, :] = one
                wcol[part, :] += jnp.sum(one.astype(F32), 1, keepdims=True)
                one = kept["h", start][o : o + TILE].astype(BF16)
                gwh[part, :] = one
                hcol[part, :] += jnp.sum(one.astype(F32), 1, keepdims=True)

        def across_width(start):
            rows = slice(start, start + GROUP)
            crossed = dot(kw[...], gwb[rows, :])
            for o in range(0, GROUP, TILE):
                part = slice(start + o, start + o + TILE)
                gmix[t, part, :] = kept["third", start][o : o + TILE] + crossed[o : o + TILE]
            gw_acc[...] += dot(gwb[rows, :], joined[t, rows, 2 * C : 3 * C], (1, 1))

        def up_grad(start):
            if start == starts[-1]:
                gbt[...] = normal[t].T
                for n in range(2):
                    acc_u[k, n] += dot(gbt[...], gpre[:, n * WIDE : n * WIDE + WIDE])

        def merge_grad(start):
            if start == starts[-1]:
                gmt[...] = gmb[...].T
                for n in range(2):
                    width = min(MT, 3 * C - n * MT)
                    acc_m[k, n, :, 0:width] += dot(gmt[...], joined[t, :, n * MT : n * MT + width])

        in_turn([
            through_gelu, through_up, up_grad, through_norm, through_merge, merge_grad, round_branches, across_width,
        ], starts)
        gs[k, NGAIN : NGAIN + 1, :] += total(sums["x"])
        gs[k, NBIAS : NBIAS + 1, :] += total(sums["n"])
        gs[k, MBIAS : MBIAS + 1, :] += total(sums["m"])
        for n in range(FF // FT):
            gs[k, UBIAS + n : UBIAS + n + 1, 0:FT] += total(sums["u"][n])
        tick(6)
        gh_acc[...] += dot(gwh[...], joined[t, :, 2 * C : 3 * C], (1, 1))

        def batch_sums(start, acc):
            plain, cross = acc
            crossed = dot(kh[pl.ds(start, GROUP), :], gwh[...])
            for o in range(0, GROUP, TILE):
                rows = pl.ds(start + o, TILE)
                g = (gmix[t, rows, :] + crossed[o : o + TILE]) * mask_cols[t, rows, :]
                gmix[t, rows, :] = g
                plain = plain + fold(g)
                cross = cross + fold(g * cv[z, rows, :])
            return plain, cross
        acc = groups(batch_sums, (zero, zero))
        plain, cross = total(acc[0]), total(acc[1])
        gs[k, BBIAS : BBIAS + 1, :] += plain
        gs[k, BGAIN : BGAIN + 1, :] += cross
        r = 4 + z
        msg[r, 0:1, 0:C] = plain
        msg[r, 1:2, 0:C] = cross
        send_stats(r)

    def input_stage(t, k, tick):
        z = 2 * k + t
        r = 4 + z
        wait_stats(r)
        scale, count = stat[z, 0:1, :], stat[z, 1:2, :]
        both = gather_stats(r)
        plain, cross = both[0:1, 0:C], both[1:2, 0:C]
        gain = pack[k, BGAIN : BGAIN + 1, :]
        out_scale = gain * scale
        plain = plain / count
        cross = cross / count

        def shifted(start, carry):
            rows = pl.ds(start, SIDE)
            g = (gmix[t, rows, :] - plain - cv[z, rows, :] * cross) * (mask_cols[t, rows, :] * out_scale)
            rows = pl.ds(start + SIDE, SIDE)
            gsh[0, rows, :] = sooner(g)
            gsh[1, rows, :] = g
            gsh[2, rows, :] = later(g)
            return carry
        grid_rows(shifted, 0)
        tick(8)
        taps = [[pack[k, CONV + n : CONV + n + 1, l:m] for n in range(9)] for l, m in LANES]

        def pull(start, acc):
            new = []
            for (l, m), tap, one in zip(LANES, taps, acc):
                u = [uf[t, pl.ds(start + SIDE * r, SIDE), l:m] for r in range(3)]
                out = gf[t, pl.ds(start, SIDE), l:m]
                sums = []
                for s in range(3):
                    around = [gsh[s, pl.ds(start + SIDE * r, SIDE), l:m] for r in range(3)]
                    out = out + around[2] * tap[s] + around[1] * tap[3 + s] + around[0] * tap[6 + s]
                    sums.append([one[s][r] + fold(around[1] * u[r]) for r in range(3)])
                new.append(sums)
                igbuf[z, lax.div(start, SIDE), :, l:m] = out.astype(BF16)
            return new
        acc = grid_rows(pull, [[[jnp.zeros((8, m - l), F32) for _ in range(3)] for _ in range(3)] for l, m in LANES])
        for (l, m), one in zip(LANES, acc):
            for r in range(3):
                for s in range(3):
                    row = CONV + 3 * r + s
                    gs[k, row : row + 1, l:m] += total(one[s][r])

        @pl.when(k == 1)
        def _():
            def reread(start, carry):
                gf[t, pl.ds(start, SIDE), :] = igbuf[z, lax.div(start, SIDE)].astype(F32)
                return carry
            grid_rows(reread, 0)

        @pl.when(me_p == k)
        def _():
            pltpu.make_async_copy(igbuf.at[z], ig_h.at[0, 2 * me_p + t], ig_local.at[t]).start()

        @pl.when(me_p != k)
        def _():
            across(igbuf.at[z], ig_h.at[0, 2 * me_p + t], ig_send.at[t], ig_recv.at[t]).start()

    def clear_mix():
        gw_acc[...] = jnp.zeros(gw_acc.shape, F32)
        gh_acc[...] = jnp.zeros(gh_acc.shape, F32)
        wcol[...] = jnp.zeros(wcol.shape, F32)
        hcol[...] = jnp.zeros(hcol.shape, F32)

    def close_mix(k):
        i_r, j_r = one_hots(ROWS)
        _, j_g = one_hots(GROUP)
        gs[k, WBIAS : WBIAS + 1, 0:SIDE] = total(jnp.where(j_r, wcol[...], 0.0))
        gs[k, HBIAS : HBIAS + 1, 0:SIDE] = total(jnp.where(i_r, hcol[...], 0.0))
        highest = lax.Precision.HIGHEST
        p = grid_row(lax.broadcasted_iota(jnp.int32, (GROUP, GROUP), 0))
        q = grid_row(lax.broadcasted_iota(jnp.int32, (GROUP, GROUP), 1))
        own = jnp.where(p == q, gw_acc[...], 0.0)
        own = jnp.sum(own.reshape(GROUP // SIDE, SIDE, GROUP), 0)
        gs[k, WW : WW + SIDE, 0:SIDE] = dot(own, jnp.where(j_g, 1.0, 0.0), precision=highest)
        i_f = jnp.where(i_r, 1.0, 0.0)
        for i in range(SIDE):
            rows = slice(i * SIDE, i * SIDE + SIDE)
            own = total(fold(own_column[...] * gh_acc[rows, :]))
            first[i : i + 1, :] = own[:, 0:C]
            gnorm[i : i + 1, 0 : ROWS - C] = own[:, C:ROWS]
        value = dot(first[0:SIDE, :], i_f[0:C, :], precision=highest)
        value += dot(gnorm[0:SIDE, 0 : ROWS - C], i_f[C:ROWS, :], precision=highest)
        gs[k, HW : HW + SIDE, 0:SIDE] = value

    bits = [1, 2]
    while 2 * bits[-1] < n_dp:
        bits.append(2 * bits[-1])
    n_swaps = len(bits) - 2
    n_steps = 1 + 2 + n_swaps + 2

    def partner(bit):
        return me_d + bit * (1 - 2 * lax.rem(me_d // bit, 2))

    def side(bit):
        return lax.rem(me_d // bit, 2)

    def along(bit, src, dst, send, recv):
        return pltpu.make_async_remote_copy(
            src_ref=src, dst_ref=dst, send_sem=send, recv_sem=recv,
            device_id={"dp": partner(bit)}, device_id_type=MESH)

    streams = (
        (acc_d, gd_h, sb_d, lb_d, rl_d), (acc_u, gu_h, sb_u, lb_u, rl_u), (acc_m, gm_h, sb_m, lb_m, rl_m))

    def reduction(k, which):
        acc, out_h, sb, lb, rl = streams[which]
        sb, lb, rl = sb.at[k], lb.at[k], rl.at[k]
        halving = [1 + me_p, 2 - me_p] if which != 1 else [2 - me_p, 1 + me_p]

        def sems(step):
            return red_send.at[3 * k + which, step], red_recv.at[3 * k + which, step]

        def own(q):
            return k, lax.div(q, 2), pl.ds(pl.multiple_of(me_p * HALF + lax.rem(q, 2) * SHARD, 16), SHARD), slice(None)

        def each(count, body):
            if count == 1:
                body(0)
                return

            def step(n, carry):
                body(n)
                return carry
            lax.fori_loop(0, count, step, 0)

        in_chip = across(sb.at[pl.ds(0, SHARDS)], lb, *sems(0))
        base = [0]
        for n, bit in enumerate(halving):
            base.append(base[n] + side(bit) * (2 >> n))
        mine = base[2]

        def half_copy(n):
            count, at = 2 >> n, 2 * n
            return along(halving[n], sb.at[pl.ds(at, count)], rl.at[pl.ds(at, count)], *sems(1 + n))

        def swap_copy(n):
            return along(bits[2 + n], sb.at[3 + n], rl.at[3 + n], *sems(3 + n))

        def double_copy(n):
            count = 2 >> n
            here = lb.at[pl.ds(base[n + 1], count)]
            return along(halving[n], here, here, *sems(n_steps - 1 - n))

        def send_half(n, landed):
            count, at = 2 >> n, 2 * n
            give = base[n] + (1 - side(halving[n])) * count
            keep = base[n + 1]

            def one(q):
                sb[at + q] = (acc[own(give + q)] + landed(give + q).astype(F32)).astype(BF16)
            each(count, one)
            half_copy(n).start()

            def two(q):
                acc[own(keep + q)] += landed(keep + q).astype(F32)
            each(count, two)

        def start():
            def one(q):
                rows = pl.ds(pl.multiple_of(other * HALF + lax.rem(q, 2) * SHARD, 16), SHARD)
                sb[q] = acc[k, lax.div(q, 2), rows, :].astype(BF16)
            each(SHARDS, one)
            in_chip.start()

        def first_half():
            in_chip.wait()
            send_half(0, lambda q: lb[q])

        def second_half():
            half_copy(0).wait()
            send_half(1, lambda q: rl[q - base[1]])

        def swap(n):
            def run():
                if n == 0:
                    half_copy(1).wait()
                    sb[3] = (acc[own(mine)] + rl[2].astype(F32)).astype(BF16)
                else:
                    swap_copy(n - 1).wait()
                    sb[3 + n] = (sb[2 + n].astype(F32) + rl[2 + n].astype(F32)).astype(BF16)
                swap_copy(n).start()
            return run

        def double(n):
            def run():
                if n == 1:
                    last = n_swaps - 1
                    swap_copy(last).wait()
                    lb[mine] = (sb[3 + last].astype(F32) + rl[3 + last].astype(F32)).astype(BF16)
                else:
                    double_copy(n + 1).wait()
                double_copy(n).start()
            return run

        def hand_over():
            double_copy(0).wait()

            @pl.when(me_p == k)
            def _():
                pltpu.make_async_copy(lb, out_h.at[me_p], out_local.at[which]).start()

            @pl.when(me_p != k)
            def _():
                across(lb, out_h.at[me_p], out_send.at[which], out_recv.at[which]).start()

        return [start, first_half, second_half] + [swap(n) for n in range(n_swaps)] + [double(1), double(0), hand_over]

    def small_sum(rows, landing, send, recv):
        count = rows.stop - rows.start
        rows = pl.ds(rows.start, count)
        in_chip = across(gs.at[other, rows], landing.at[0], send.at[0], recv.at[0])

        def swap_copy(n):
            return along(bits[n], gs.at[me_p, rows], landing.at[1 + n], send.at[1 + n], recv.at[1 + n])

        def step(n):
            def run():
                (swap_copy(n - 1) if n else in_chip).wait()
                gs[me_p, rows, :] += landing[n]
                if n < len(bits):
                    swap_copy(n).start()
            return run
        return [in_chip.start] + [step(n) for n in range(len(bits) + 1)]

    small = small_sum(slice(SMALL, PACK), small_land, small_send, small_recv)
    taps_sum = small_sum(slice(0, SMALL), conv_land, conv_send, conv_recv)

    plan = {}
    backward_places, input_places = [0, 1, 6, 11], [7, 8, 9]
    order = []
    for n in range(6):
        order += [(n, p) for p in input_places] if n > 1 else []
        order += [(n, p) for p in backward_places] if n < 4 else []

    def put(start, steps, gap):
        at = order.index(start)
        steps = list(steps)
        while steps and at < len(order):
            plan.setdefault(order[at], []).append(steps.pop(0))
            at += gap
        return steps

    for which, place in enumerate(((1, 1), (1, 6), (2, 7))):
        assert not put(place, reduction(1, which), 1)
    tails = [put(place, reduction(0, which), 1) for which, place in enumerate(((3, 1), (3, 6), (4, 7)))]
    tails.append(put((4, 7), small, 2))
    tails.append(list(taps_sum))

    pack_over.wait()
    for t in range(2):
        image_in[t].wait()

    def widen_image(t):
        def widen(i, inner):
            uf[t, pl.ds(pl.multiple_of(i * SIDE + SIDE, SIDE), SIDE), :] = ub[t, i].astype(F32)
            return inner
        lax.fori_loop(0, SIDE, widen, 0)

    def start_image(t, carry):
        widen_image(t)
        conv_stage(t, 0)
        return carry
    lax.fori_loop(0, 2, start_image, 0)
    for t in range(2):
        grad_in[t].start()

    for copy in weights_in + weights_over:
        copy.wait()
    for k in range(2):
        wmid[k] = wm[k, :, C : 2 * C]

    def forward_block(k, carry):
        mixers(k, False)

        def one(t, inner):
            forward_stage(t, k)

            @pl.when(k == 0)
            def _():
                for copy in spill(t):
                    copy.start()
                conv_stage(t, 1)
            return inner
        lax.fori_loop(0, 2, one, 0)
        return carry
    lax.fori_loop(0, 2, forward_block, 0)

    for t in range(2):
        grad_in[t].wait()
        pltpu.make_async_copy(ybuf.at[t], so_h.at[0, t], so_local.at[t]).wait()
        across(ybuf.at[t], so_h.at[0, t], so_send.at[t], so_recv.at[t]).wait_send()

    def load_grad(t, carry):
        def widen(i, inner):
            gf[t, pl.ds(pl.multiple_of(i * SIDE, SIDE), SIDE), :] = ub[t, i].astype(F32)
            return inner
        lax.fori_loop(0, SIDE, widen, 0)
        return carry
    lax.fori_loop(0, 2, load_grad, 0)
    for t in range(2):
        image_copy(t, again_sems.at[t]).start()

    def turn(s, carry):
        t = lax.rem(s, 2)

        def tick(place):
            for n in range(6):
                steps = plan.get((n, place), [])
                if steps:
                    @pl.when(s == n)
                    def _():
                        for step in steps:
                            step()

        @pl.when(lax.rem(s, 2) == 0)
        def _():
            @pl.when(s > 0)
            def _():
                close_mix(2 - lax.div(s, 2))

            @pl.when(s < 4)
            def _():
                mixers(1 - lax.div(s, 2), True)
                clear_mix()

        @pl.when(s > 1)
        def _():
            @pl.when(s > 3)
            def _():
                image_copy(t, again_sems.at[t]).wait()
                widen_image(t)
            tick(7)
            input_stage(t, 2 - lax.div(s, 2), tick)
            tick(9)

        @pl.when(s < 4)
        def _():
            @pl.when(s > 1)
            def _():
                for copy in fetch(t):
                    copy.wait()
            tick(0)
            backward_stage(t, 1 - lax.div(s, 2), tick)
            tick(11)

            @pl.when(s < 2)
            def _():
                for copy in fetch(t):
                    copy.start()
        return carry
    lax.fori_loop(0, 6, turn, 0)

    while any(tails):
        for steps in tails:
            if steps:
                steps.pop(0)()

    gs_out = pltpu.make_async_copy(gs.at[me_p], gs_h, gs_sem.at[0])
    gs_out.start()
    for t in range(2):
        pltpu.make_async_copy(igbuf.at[t], ig_h.at[0, t], ig_local.at[t]).wait()
        across(ybuf.at[t], so_h.at[0, t], so_send.at[t], so_recv.at[t]).wait_recv()
        across(igbuf.at[t], ig_h.at[0, t], ig_send.at[t], ig_recv.at[t]).wait()
    for n, (_, out_h, _, lb, _) in enumerate(streams):
        pltpu.make_async_copy(lb.at[0], out_h.at[0], out_local.at[n]).wait()
        across(lb.at[0], out_h.at[0], out_send.at[n], out_recv.at[n]).wait()
    gs_out.wait()


def finish_kernel(
    so_in, ig_in, gd_in, gu_in, gm_in, gs,
    so, ig, conv, bgain, bbias, ww, wb, hw, hb, gm, mbias, ngain, nbias, gu, ubias, gd, dbias,
    large, d_in, u_in, m_in, d_out, u_out, m_out, in_sems, out_sems,
):
    moved = ((gd_in, d_in), (gu_in, u_in), (gm_in, m_in), (so_in, large.at[0]), (ig_in, large.at[1]))
    arrive = [pltpu.make_async_copy(src, dst, in_sems.at[n]) for n, (src, dst) in enumerate(moved)]
    for copy in arrive:
        copy.start()
    moved = ((d_out, gd), (u_out, gu), (m_out, gm), (large.at[0], so), (large.at[1], ig))
    leave = [pltpu.make_async_copy(src, dst, out_sems.at[n]) for n, (src, dst) in enumerate(moved)]
    for n in range(9):
        conv[n] = gs[CONV + n : CONV + n + 1, :]
    for row, ref in ((BGAIN, bgain), (BBIAS, bbias), (MBIAS, mbias), (NGAIN, ngain), (NBIAS, nbias), (DBIAS, dbias)):
        ref[...] = gs[row : row + 1, :]
    for row, ref in ((WBIAS, wb), (HBIAS, hb)):
        ref[...] = gs[row : row + 1, 0:SIDE]
    for n in range(FF // FT):
        ubias[:, n * FT : n * FT + FT] = gs[UBIAS + n : UBIAS + n + 1, 0:FT]
    for row, ref in ((WW, ww), (HW, hw)):
        ref[0] = gs[row : row + SIDE, 0:SIDE]
    for n, (src, dst, piece) in enumerate(((d_in, d_out, WIDE), (u_in, u_out, WIDE), (m_in, m_out, MT))):
        arrive[n].wait()
        for p in range(2):
            for q in range(SHARDS):
                start, at = p * HALF + (q % 2) * SHARD, piece * (q // 2)
                width = min(piece, dst.shape[1] - at)
                dst[start : start + SHARD, at : at + width] = src[p, q, :, 0:width].astype(F32)
        leave[n].start()
    for n in (3, 4):
        arrive[n].wait()
        leave[n].start()
    for copy in leave:
        copy.wait()


def on_device(
    images, masks, conv_weight, batch_gain, batch_bias, width_weight, width_bias,
    height_weight, height_bias, merge_weight, merge_bias, norm_gain, norm_bias,
    up_weight, up_bias, down_weight, down_bias, out_grad,
):
    n_dp = lax.axis_size("dp")
    micro = images.shape[0]
    steps = max(n_dp.bit_length() - 1, 4)
    any_space = pl.BlockSpec(memory_space=pl.ANY)
    vmem = pl.BlockSpec(memory_space=pltpu.VMEM)
    dma = pltpu.SemaphoreType.DMA
    grid = (SIDE, SIDE, C)
    shape = jax.ShapeDtypeStruct
    outs = pl.pallas_call(
        functools.partial(kernel, n_dp),
        out_shape=(
            shape((1, micro) + grid, BF16),
            shape((1, micro) + grid, BF16),
            shape((2, SHARDS, SHARD, WIDE), BF16),
            shape((2, SHARDS, SHARD, WIDE), BF16),
            shape((2, SHARDS, SHARD, MT), BF16),
            shape((PACK, C), F32),
            shape((2, ROWS, FF), BF16),
            shape((2, ROWS, FF), BF16),
            shape((2, ROWS, 3 * C), BF16),
            shape((2, ROWS, C), BF16),
            shape((2, ROWS, C), BF16),
        ),
        in_specs=[any_space] + [vmem] * 8 + [any_space] + [vmem] * 3 + [any_space, vmem, any_space, vmem, any_space],
        out_specs=(any_space,) * 11,
        scratch_shapes=[
            pltpu.VMEM((2, ROWS, 1), F32),
            pltpu.VMEM((4, 2, C), F32),
            pltpu.VMEM((SIDE, ROWS), F32),
            pltpu.VMEM((ROWS, SIDE), BF16),
            pltpu.VMEM((2, PACK, C), F32),
            pltpu.VMEM((2, C, 3 * C), BF16),
            pltpu.VMEM((2, C, C), BF16),
            pltpu.VMEM((2, C, FF), BF16),
            pltpu.VMEM((2, C, FF), BF16),
            pltpu.VMEM((2,) + grid, BF16),
            pltpu.VMEM((2, ROWS + 2 * SIDE, C), F32),
            pltpu.VMEM((4, ROWS, C), F32),
            pltpu.VMEM((2, ROWS, 3 * C), BF16),
            pltpu.VMEM((2, ROWS, C), BF16),
            pltpu.VMEM((2, ROWS, C), BF16),
            pltpu.VMEM((4, ROWS, 1), F32),
            pltpu.VMEM((2, ROWS, FF), BF16),
            pltpu.VMEM((2, ROWS, FF), BF16),
            pltpu.VMEM((2, ROWS, C), F32),
            pltpu.VMEM((ROWS, C), BF16),
            pltpu.VMEM((ROWS, C), BF16),
            pltpu.VMEM((ROWS, C), BF16),
            pltpu.VMEM((C, ROWS), BF16),
            pltpu.VMEM((C, ROWS), BF16),
            pltpu.VMEM((ROWS, FF), BF16),
            pltpu.VMEM((2, ROWS, C), F32),
            pltpu.VMEM((ROWS, C), BF16),
            pltpu.VMEM((3, ROWS + 2 * SIDE, C), F32),
            pltpu.VMEM((GROUP, GROUP), BF16),
            pltpu.VMEM((ROWS, ROWS), BF16),
            pltpu.VMEM((ROWS, 1), F32),
            pltpu.VMEM((ROWS, 1), F32),
            pltpu.VMEM((GROUP, GROUP), F32),
            pltpu.VMEM((ROWS, ROWS), F32),
            pltpu.VMEM((ROWS, 1), F32),
            pltpu.VMEM((ROWS, 1), F32),
            pltpu.VMEM((4,) + grid, BF16),
            pltpu.VMEM((8, 2, CP), F32),
            pltpu.VMEM((8, n_dp - 1, 2, CP), F32),
            pltpu.VMEM((2, 2, C, WIDE), F32),
            pltpu.VMEM((2, 2, C, WIDE), F32),
            pltpu.VMEM((2, 2, C, MT), F32),
            pltpu.VMEM((2, PACK, C), F32),
            pltpu.VMEM((2, 1 + steps, SHARD, WIDE), BF16),
            pltpu.VMEM((2, SHARDS, SHARD, WIDE), BF16),
            pltpu.VMEM((2, 1 + steps, SHARD, WIDE), BF16),
            pltpu.VMEM((2, 1 + steps, SHARD, WIDE), BF16),
            pltpu.VMEM((2, SHARDS, SHARD, WIDE), BF16),
            pltpu.VMEM((2, 1 + steps, SHARD, WIDE), BF16),
            pltpu.VMEM((2, 1 + steps, SHARD, MT), BF16),
            pltpu.VMEM((2, SHARDS, SHARD, MT), BF16),
            pltpu.VMEM((2, 1 + steps, SHARD, MT), BF16),
            pltpu.VMEM((1 + steps, PACK - SMALL, C), F32),
            pltpu.VMEM((1 + steps, SMALL, C), F32),
            dma((9,)), dma((2,)), dma((2,)), dma((3,)), dma((3,)), dma((8,)), dma((8,)),
            dma((2,)), dma((2,)), dma((2,)), dma((2,)), dma((2,)), dma((2,)), dma((2, 5)), dma((2, 5)),
            dma((6, 3 + steps)), dma((6, 3 + steps)), dma((1 + steps,)), dma((1 + steps,)),
            dma((1 + steps,)), dma((1 + steps,)), dma((3,)), dma((3,)), dma((3,)), dma((1,)),
        ],
        compiler_params=pltpu.CompilerParams(
            collective_id=0, has_side_effects=True, vmem_limit_bytes=65400 * 1024),
    )(
        images, masks, conv_weight, batch_gain, batch_bias, width_weight, width_bias, height_weight, height_bias,
        merge_weight[0].T, merge_bias, norm_gain, norm_bias, up_weight[0], up_bias, down_weight[0].T, down_bias, out_grad)

    row = shape((1, C), F32)
    square, line = shape((1, SIDE, SIDE), F32), shape((1, SIDE), F32)
    so, ig, conv, bgain, bbias, ww, wb, hw, hb, gm, mbias, ngain, nbias, gu, ubias, gd, dbias = pl.pallas_call(
        finish_kernel,
        out_shape=(
            shape((1, micro) + grid, BF16), shape((1, micro) + grid, BF16), shape((9, 1, C), F32), row, row,
            square, line, square, line, shape((C, 3 * C), F32), row, row, row,
            shape((C, FF), F32), shape((1, FF), F32), shape((C, FF), F32), row),
        in_specs=[any_space] * 5 + [vmem],
        out_specs=(any_space,) * 2 + (vmem,) * 7 + (any_space,) + (vmem,) * 3 + (any_space, vmem, any_space, vmem),
        scratch_shapes=[
            pltpu.VMEM((2, 1, micro) + grid, BF16),
            pltpu.VMEM((2, SHARDS, SHARD, WIDE), BF16),
            pltpu.VMEM((2, SHARDS, SHARD, WIDE), BF16),
            pltpu.VMEM((2, SHARDS, SHARD, MT), BF16),
            pltpu.VMEM((C, FF), F32),
            pltpu.VMEM((C, FF), F32),
            pltpu.VMEM((C, 3 * C), F32),
            dma((5,)), dma((5,)),
        ],
        compiler_params=pltpu.CompilerParams(vmem_limit_bytes=65400 * 1024),
    )(*outs[:6])
    return (
        so, ig, jnp.swapaxes(conv, 0, 1), bgain, bbias, ww, wb, hw, hb, gm.T[None], mbias, ngain, nbias,
        gu[None], ubias, gd.T[None], dbias)


def solution(mesh):
    data4 = P("dp", None, None, None)
    p1, p2, p3 = P("pipe"), P("pipe", None), P("pipe", None, None)
    out5 = P("pipe", "dp", None, None, None)
    return jax.shard_map(
        on_device,
        mesh=mesh,
        in_specs=(data4, P("dp", None, None), p3, p2, p2, p3, p2, p3, p2, p3, p2, p2, p2, p3, p2, p3, p2, data4),
        out_specs=(out5, out5, p3, p2, p2, p3, p2, p3, p2, p3, p2, p2, p2, p3, p2, p3, p2),
        check_vma=False,
    )
```

```python
import functools

import jax
import jax.numpy as jnp
from jax import lax
from jax.experimental import pallas as pl
from jax.experimental.pallas import tpu as pltpu
from jax.sharding import PartitionSpec as P

EPS = 1e-05
MESH = pl.DeviceIdType.MESH
F32 = jnp.float32
BF16 = jnp.bfloat16

SIDE = 24
ROWS = SIDE * SIDE
C = 320
CP = 384
FF = 1280
FT = 256
CHUNK = 48
TILE = 32
LANES = ((0, 128), (128, 256), (256, 320))
GROUP = 8 * SIDE

HALF = C // 2
SHARD = HALF // 2
WIDE = FF // 2
SHARDS = 4
MT = 512
STEP = 24

CONV, BGAIN, BBIAS, MBIAS, NGAIN, NBIAS, DBIAS, WBIAS, HBIAS, UBIAS, WW, HW, PACK = (
    0, 16, 17, 18, 19, 20, 21, 22, 23, 24, 32, 56, 80)
SMALL = 16


def dot(a, b, contract=(1, 0), precision=None):
    return lax.dot_general(
        a, b, (((contract[0],), (contract[1],)), ((), ())),
        preferred_element_type=F32, precision=precision)


def in_turn(phases, starts):
    for step in range(len(phases) + len(starts) - 1):
        for g, start in enumerate(starts):
            if 0 <= step - g < len(phases):
                phases[step - g](start)


def fold(value):
    rows = value.shape[0]
    return jnp.sum(value.reshape(rows // 8, 8, value.shape[1]), 0)


def total(partial):
    return jnp.sum(partial, 0, keepdims=True)


def grid_row(index):
    return (index * 2731) >> 16


def one_hots(rows):
    place = lax.broadcasted_iota(jnp.int32, (rows, SIDE), 0)
    lane = lax.broadcasted_iota(jnp.int32, (rows, SIDE), 1)
    i = grid_row(place)
    return i == lane, place - SIDE * i == lane


def gelu_both(x):
    e = jnp.exp2(x * x * -0.7213475204444817)
    d = 1.0 + 0.23164189 * jnp.abs(x)
    t = pl.reciprocal(d, approx=True)
    poly = t * (0.127414796 + t * (-0.142248368 + t * (0.7107068705 + t * (-0.7265760135 + t * 0.5307027145))))
    tail = poly * e
    phi = jnp.where(x >= 0, 1.0 - tail, tail)
    return x * phi, phi + x * e * 0.3989422804014327


def kernel(
    n_dp,
    images, masks, conv_w, bgain, bbias, wwt, wb, hwt, hb, wm_h, mbias, ngain, nbias, wu_h, ubias, wd_h, dbias, og_h,
    so_h, ig_h, gd_h, gu_h, gm_h, gs_h, sp_hidden, sp_gp, sp_joined, sp_normal, sp_xl,
    mask_cols, stat, own_column, i_hot, pack, wm, wmid, wu, wd, ub, uf, cv, joined, normal, xl, rstd, hidden, gp,
    gf, gb, gmb, gwb, gbt, gmt, gpre, gmix, gwh, gsh, kw, kh, wbcol, hbcol,
    gw_acc, gh_acc, wcol, hcol, ybuf, msg, land, acc_d, acc_u, acc_m, gs,
    sb_d, lb_d, rl_d, sb_u, lb_u, rl_u, sb_m, lb_m, rl_m, small_land, conv_land,
    local_sems, again_sems, pack_sems, w_send, w_recv, st_send, st_recv,
    so_local, so_send, so_recv, ig_local, ig_send, ig_recv, spill_sems, fetch_sems,
    red_send, red_recv, small_send, small_recv, conv_send, conv_recv, out_local, out_send, out_recv, gs_sem,
):
    me_p = lax.axis_index("pipe")
    me_d = lax.axis_index("dp")
    other = 1 - me_p
    first = gsh.at[2, pl.ds(SIDE, ROWS)]
    igbuf = ybuf
    gnorm = gsh.at[0, pl.ds(SIDE, ROWS)]

    def image_copy(t, sems):
        return pltpu.make_async_copy(images.at[2 * me_p + t], ub.at[t], sems)

    image_in = [image_copy(t, local_sems.at[5 + t]) for t in range(2)]
    grad_in = [pltpu.make_async_copy(og_h.at[2 * me_p + t], ub.at[t], local_sems.at[7 + t]) for t in range(2)]
    weights = ((wm_h, wm), (wu_h, wu), (wd_h, wd))
    weights_in = [pltpu.make_async_copy(src, dst.at[me_p], local_sems.at[n]) for n, (src, dst) in enumerate(weights)]
    for copy in image_in + weights_in:
        copy.start()

    barrier = pltpu.get_barrier_semaphore()

    def greet(step, carry):
        pl.semaphore_signal(barrier, inc=1, device_id={"dp": lax.rem(me_d + step, n_dp)}, device_id_type=MESH)
        return carry

    lax.fori_loop(1, n_dp, greet, 0)
    pl.semaphore_signal(barrier, inc=1, device_id={"pipe": other}, device_id_type=MESH)

    pack[me_p] = jnp.zeros(pack.shape[1:], F32)
    pack[me_p, CONV : CONV + 9, :] = conv_w[0].astype(F32)
    for row, ref in ((BGAIN, bgain), (BBIAS, bbias), (MBIAS, mbias), (NGAIN, ngain), (NBIAS, nbias), (DBIAS, dbias)):
        pack[me_p, row : row + 1, :] = ref[...]
    for row, ref in ((WBIAS, wb), (HBIAS, hb)):
        pack[me_p, row : row + 1, 0:SIDE] = ref[...]
    for n in range(FF // FT):
        pack[me_p, UBIAS + n : UBIAS + n + 1, 0:FT] = ubias[:, n * FT : n * FT + FT]
    for row, ref in ((WW, wwt), (HW, hwt)):
        pack[me_p, row : row + SIDE, 0:SIDE] = ref[0].astype(F32)

    pl.semaphore_wait(barrier, n_dp)

    def across(src, dst, send, recv):
        return pltpu.make_async_remote_copy(
            src_ref=src, dst_ref=dst, send_sem=send, recv_sem=recv,
            device_id={"pipe": other}, device_id_type=MESH)

    pack_over = across(pack.at[me_p], pack.at[me_p], pack_sems.at[0], pack_sems.at[1])
    weights_over = [across(src, dst.at[me_p], w_send.at[n], w_recv.at[n]) for n, (src, dst) in enumerate(weights)]
    pack_over.start()
    for copy in weights_over:
        copy.start()

    msg[...] = jnp.zeros(msg.shape, F32)
    for k in range(2):
        for acc in (acc_d, acc_u, acc_m):
            for n in range(2):
                acc[k, n] = jnp.zeros(acc.shape[2:], F32)
        gs[k] = jnp.zeros(gs.shape[1:], F32)
    for n in range(2):
        uf[n, 0:SIDE, :] = jnp.zeros((SIDE, C), F32)
        uf[n, SIDE + ROWS : 2 * SIDE + ROWS, :] = jnp.zeros((SIDE, C), F32)
    for n in range(3):
        gsh[n, 0:SIDE, :] = jnp.zeros((SIDE, C), F32)
        gsh[n, SIDE + ROWS : 2 * SIDE + ROWS, :] = jnp.zeros((SIDE, C), F32)

    i_r, j_r = one_hots(ROWS)
    i_hot[...] = jnp.where(i_r, 1.0, 0.0).astype(BF16)
    q = lax.broadcasted_iota(jnp.int32, (SIDE, ROWS), 1)
    q = q - SIDE * grid_row(q)
    own_column[...] = jnp.where(lax.broadcasted_iota(jnp.int32, (SIDE, ROWS), 0) == q, 1.0, 0.0)
    for t in range(2):
        chosen = dot(i_hot[...], masks[2 * me_p + t].astype(F32).astype(BF16))
        mask_cols[t] = jnp.sum(jnp.where(j_r, chosen, 0.0), 1, keepdims=True)

    def later(value):
        at = lax.broadcasted_iota(jnp.int32, value.shape, 0)
        return jnp.where(at != 0, pltpu.roll(value, 1, 0), 0.0)

    def sooner(value):
        at = lax.broadcasted_iota(jnp.int32, value.shape, 0)
        return jnp.where(at != SIDE - 1, pltpu.roll(value, SIDE - 1, 0), 0.0)

    def grid_rows(body, init):
        def step(c, carry):
            for row in range(STEP):
                carry = body(pl.multiple_of(c * (STEP * SIDE), STEP * SIDE) + row * SIDE, carry)
            return carry
        return lax.fori_loop(0, SIDE // STEP, step, init)

    def groups(body, init):
        for g in range(ROWS // GROUP):
            init = body(g * GROUP, init)
        return init

    def send_stats(r):
        def one(step, carry):
            pltpu.make_async_remote_copy(
                src_ref=msg.at[r], dst_ref=land.at[r, n_dp - 1 - step],
                send_sem=st_send.at[r], recv_sem=st_recv.at[r],
                device_id={"dp": lax.rem(me_d + step, n_dp)}, device_id_type=MESH).start()
            return carry
        lax.fori_loop(1, n_dp, one, 0)

    def wait_stats(r):
        whole = pltpu.make_async_remote_copy(
            src_ref=land.at[r], dst_ref=land.at[r], send_sem=st_send.at[r], recv_sem=st_recv.at[r],
            device_id={"dp": lax.rem(me_d + 1, n_dp)}, device_id_type=MESH)
        whole.wait_send()
        whole.wait_recv()

    def conv_stage(t, k):
        z = 2 * k + t
        n_own = total(mask_cols[t])
        taps = [[pack[k, CONV + n : CONV + n + 1, l:m] for n in range(9)] for l, m in LANES]

        def conv(start, acc):
            at = pl.ds(start, SIDE)
            new = []
            for (l, m), tap, one in zip(LANES, taps, acc):
                rows = [uf[t, pl.ds(start + SIDE * r, SIDE), l:m] for r in range(3)]
                part = [rows[0] * tap[s] + rows[1] * tap[3 + s] + rows[2] * tap[6 + s] for s in range(3)]
                out = part[1] + later(part[0]) + sooner(part[2])
                cv[z, at, l:m] = out
                new.append(one + fold(out * mask_cols[t, at, :]))
            return new
        acc = grid_rows(conv, [jnp.zeros((8, m - l), F32) for l, m in LANES])
        sums = jnp.concatenate([total(one) for one in acc], 1)
        mean = sums / n_own

        def centred(start, acc):
            rows = pl.ds(start, SIDE)
            d = cv[z, rows, :] - mean
            return acc + fold(d * d * mask_cols[t, rows, :])

        m2 = total(grid_rows(centred, jnp.zeros((8, C), F32)))
        msg[z, 0:1, 0:C] = sums
        msg[z, 0:1, C:CP] = jnp.broadcast_to(n_own, (1, CP - C))
        msg[z, 1:2, 0:C] = m2
        send_stats(z)

    def peers(body, init):
        if n_dp > 16:
            return lax.fori_loop(0, n_dp - 1, body, init)
        for d in range(n_dp - 1):
            init = body(d, init)
        return init

    def gather_stats(r):
        def add(d, carry):
            return carry + land[r, d]
        return peers(add, msg[r])

    def norm_stats(z):
        sums = gather_stats(z)[0:1, :]
        count = sums[:, CP - 1 : CP]
        mean = sums[:, 0:C] / count

        def spread(values):
            n = values[0:1, CP - 1 : CP]
            off = values[0:1, 0:C] / n - mean
            return values[1:2, 0:C] + n * off * off

        def add(d, carry):
            return carry + spread(land[z, d])
        m2 = peers(add, spread(msg[z]))
        scale = lax.rsqrt(m2 / count + EPS)
        stat[z, 0:1, :] = scale
        stat[z, 1:2, :] = jnp.broadcast_to(count, (1, C))
        return mean, scale

    def mixers(k, backward):
        _, j_g = one_hots(GROUP)
        ww = pack[k, WW : WW + SIDE, 0:SIDE].astype(BF16)
        hw = pack[k, HW : HW + SIDE, 0:SIDE].astype(BF16)
        side_of = 0 if backward else 1
        j_b = jnp.where(j_g, 1.0, 0.0).astype(BF16)
        left = dot(j_b, ww, (1, 1 - side_of)).astype(BF16)
        p = grid_row(lax.broadcasted_iota(jnp.int32, (GROUP, GROUP), 0))
        q = grid_row(lax.broadcasted_iota(jnp.int32, (GROUP, GROUP), 1))
        kw[...] = jnp.where(p == q, dot(left, j_b, (1, 1)), 0.0).astype(BF16)
        spread = dot(hw, i_hot[...], (side_of, 1))
        own = own_column[...]
        for i in range(0, SIDE, 2):
            two = jnp.concatenate([spread[i : i + 1, :] * own, spread[i + 1 : i + 2, :] * own], 0)
            kh[i * SIDE : i * SIDE + 2 * SIDE, :] = two.astype(BF16)
        if not backward:
            i_r, j_r = one_hots(ROWS)
            wb = pack[k, WBIAS : WBIAS + 1, 0:SIDE]
            hb = pack[k, HBIAS : HBIAS + 1, 0:SIDE]
            wbcol[...] = jnp.sum(jnp.where(j_r, wb, 0.0), 1, keepdims=True)
            hbcol[...] = jnp.sum(jnp.where(i_r, hb, 0.0), 1, keepdims=True)

    stored = ((hidden, sp_hidden), (gp, sp_gp), (joined, sp_joined), (normal, sp_normal), (xl, sp_xl))

    def spill(t):
        return [pltpu.make_async_copy(v.at[t], h.at[t], spill_sems.at[t, n]) for n, (v, h) in enumerate(stored)]

    def fetch(t):
        return [pltpu.make_async_copy(h.at[t], v.at[t], fetch_sems.at[t, n]) for n, (v, h) in enumerate(stored)]

    def forward_stage(t, k):
        z = 2 * k + t

        @pl.when(k == 1)
        def _():
            for copy in spill(t):
                copy.wait()

        wait_stats(z)
        mean, scale = norm_stats(z)
        gain = pack[k, BGAIN : BGAIN + 1, :]
        bias = pack[k, BBIAS : BBIAS + 1, :]

        def standardize(start, carry):
            for o in range(0, GROUP, TILE):
                rows = pl.ds(start + o, TILE)
                x = (cv[z, rows, :] - mean) * scale
                cv[z, rows, :] = x
                joined[t, rows, 2 * C : 3 * C] = ((x * gain + bias) * mask_cols[t, rows, :]).astype(BF16)
            along = dot(kw[...], joined[t, pl.ds(start, GROUP), 2 * C : 3 * C])
            for o in range(0, GROUP, TILE):
                rows = pl.ds(start + o, TILE)
                joined[t, rows, 0:C] = (along[o : o + TILE] + wbcol[rows, :]).astype(BF16)
            return carry
        groups(standardize, 0)

        m_bias = pack[k, MBIAS : MBIAS + 1, :]
        n_gain = pack[k, NGAIN : NGAIN + 1, :]
        n_bias = pack[k, NBIAS : NBIAS + 1, :]
        d_bias = pack[k, DBIAS : DBIAS + 1, :]
        u_bias = [pack[k, UBIAS + n : UBIAS + n + 1, 0:FT] for n in range(FF // FT)]

        starts = [g * GROUP for g in range(ROWS // GROUP)]
        merged, down = {}, {}

        def mix(start):
            rows = slice(start, start + GROUP)
            along = dot(kh[rows, :], joined[t, :, 2 * C : 3 * C])
            for o in range(0, GROUP, TILE):
                part = slice(start + o, start + o + TILE)
                joined[t, part, C : 2 * C] = (along[o : o + TILE] + hbcol[part, :]).astype(BF16)
            merged[start] = dot(joined[t, rows, :], wm[k], (1, 1))

        def layer_norm(start):
            for o in range(0, GROUP, TILE):
                part = slice(start + o, start + o + TILE)
                f = uf[t, start + SIDE + o : start + SIDE + o + TILE, :] + merged[start][o : o + TILE] + m_bias
                d = f - jnp.mean(f, 1, keepdims=True)
                rs = lax.rsqrt(jnp.mean(d * d, 1, keepdims=True) + EPS)
                x = d * rs
                first[part, :] = f
                rstd[z, part, :] = rs
                xl[t, part, :] = x.astype(BF16)
                normal[t, part, :] = (x * n_gain + n_bias).astype(BF16)

        def activate(start):
            rows = slice(start, start + GROUP)
            norm = normal[t, rows, :]
            pre = dot(norm, wu[k, :, 0:FT])
            for n in range(FF // FT):
                cols = slice(n * FT, n * FT + FT)
                now = pre
                if n + 1 < FF // FT:
                    pre = dot(norm, wu[k, :, n * FT + FT : n * FT + 2 * FT])
                for o in range(0, GROUP, TILE):
                    part = slice(start + o, start + o + TILE)
                    h, dh = gelu_both(now[o : o + TILE] + u_bias[n])
                    hidden[t, part, cols] = h.astype(BF16)
                    gp[t, part, cols] = dh.astype(BF16)

        def project(start):
            down[start] = dot(hidden[t, start : start + GROUP, :], wd[k], (1, 1))

        def finish(start):
            for r in range(GROUP // SIDE):
                part = slice(start + r * SIDE, start + r * SIDE + SIDE)
                y = first[part, :] + down[start][r * SIDE : r * SIDE + SIDE] + d_bias
                ybuf[z, start // SIDE + r] = y.astype(BF16)

        in_turn([mix, layer_norm, activate, project, finish], starts)

        @pl.when(k == 0)
        def _():
            def reread(start, carry):
                uf[t, pl.ds(start + SIDE, SIDE), :] = ybuf[z, lax.div(start, SIDE)].astype(F32)
                return carry
            grid_rows(reread, 0)

        @pl.when(me_p == k)
        def _():
            pltpu.make_async_copy(ybuf.at[z], so_h.at[0, 2 * me_p + t], so_local.at[t]).start()

        @pl.when(me_p != k)
        def _():
            across(ybuf.at[z], so_h.at[0, 2 * me_p + t], so_send.at[t], so_recv.at[t]).start()

    def backward_stage(t, k, tick):
        z = 2 * k + t
        zero = jnp.zeros((8, C), F32)
        n_gain = pack[k, NGAIN : NGAIN + 1, :]

        d_acc = zero
        for o in range(0, ROWS, TILE):
            g = gf[t, o : o + TILE, :]
            gb[o : o + TILE, :] = g.astype(BF16)
            d_acc = d_acc + fold(g)
        gs[k, DBIAS : DBIAS + 1, :] += total(d_acc)
        gbt[...] = gb[...].T
        for n in range(2):
            acc_d[k, n] += dot(gbt[...], hidden[t, :, n * WIDE : n * WIDE + WIDE])
        tick(1)

        starts = [g * GROUP for g in range(ROWS // GROUP)]
        sums = {"x": zero, "n": zero, "m": zero, "u": [jnp.zeros((8, FT), F32) for _ in range(FF // FT)]}
        kept = {}

        def through_gelu(start):
            low = gb[start : start + GROUP, :]
            raw = dot(low, wd[k, :, 0:FT])
            for n in range(FF // FT):
                cols = slice(n * FT, n * FT + FT)
                now = raw
                if n + 1 < FF // FT:
                    raw = dot(low, wd[k, :, n * FT + FT : n * FT + 2 * FT])
                for o in range(0, GROUP, TILE):
                    part = slice(start + o, start + o + TILE)
                    gpn = (now[o : o + TILE] * gp[t, part, cols].astype(F32)).astype(BF16)
                    gpre[part, cols] = gpn
                    sums["u"][n] = sums["u"][n] + fold(gpn.astype(F32))

        def through_up(start):
            kept["back", start] = dot(gpre[start : start + GROUP, :], wu[k], (1, 1))

        def through_norm(start):
            for o in range(0, GROUP, TILE):
                part = slice(start + o, start + o + TILE)
                g = kept["back", start][o : o + TILE]
                x = xl[t, part, :].astype(F32)
                gn = g * n_gain
                mean_g = jnp.mean(gn, 1, keepdims=True)
                mean_gx = jnp.mean(gn * x, 1, keepdims=True)
                out = gf[t, part, :] + rstd[z, part, :] * (gn - mean_g - x * mean_gx)
                gf[t, part, :] = out
                low = out.astype(BF16)
                gmb[part, :] = low
                sums["x"] = sums["x"] + fold(g * x)
                sums["n"] = sums["n"] + fold(g)
                sums["m"] = sums["m"] + fold(low.astype(F32))

        def through_merge(start):
            low = gmb[start : start + GROUP, :]
            kept["w", start] = dot(low, wm[k, :, 0:C])
            kept["h", start] = dot(low, wmid[k])
            kept["third", start] = dot(low, wm[k, :, 2 * C : 3 * C])

        def round_branches(start):
            for o in range(0, GROUP, TILE):
                part = slice(start + o, start + o + TILE)
                one = kept["w", start][o : o + TILE].astype(BF16)
                gwb[part, :] = one
                wcol[part, :] += jnp.sum(one.astype(F32), 1, keepdims=True)
                one = kept["h", start][o : o + TILE].astype(BF16)
                gwh[part, :] = one
                hcol[part, :] += jnp.sum(one.astype(F32), 1, keepdims=True)

        def across_width(start):
            rows = slice(start, start + GROUP)
            crossed = dot(kw[...], gwb[rows, :])
            for o in range(0, GROUP, TILE):
                part = slice(start + o, start + o + TILE)
                gmix[t, part, :] = kept["third", start][o : o + TILE] + crossed[o : o + TILE]
            gw_acc[...] += dot(gwb[rows, :], joined[t, rows, 2 * C : 3 * C], (1, 1))

        def up_grad(start):
            if start == starts[-1]:
                gbt[...] = normal[t].T
                for n in range(2):
                    acc_u[k, n] += dot(gbt[...], gpre[:, n * WIDE : n * WIDE + WIDE])

        def merge_grad(start):
            if start == starts[-1]:
                gmt[...] = gmb[...].T
                for n in range(2):
                    width = min(MT, 3 * C - n * MT)
                    acc_m[k, n, :, 0:width] += dot(gmt[...], joined[t, :, n * MT : n * MT + width])

        in_turn([
            through_gelu, through_up, up_grad, through_norm, through_merge, merge_grad, round_branches, across_width,
        ], starts)
        gs[k, NGAIN : NGAIN + 1, :] += total(sums["x"])
        gs[k, NBIAS : NBIAS + 1, :] += total(sums["n"])
        gs[k, MBIAS : MBIAS + 1, :] += total(sums["m"])
        for n in range(FF // FT):
            gs[k, UBIAS + n : UBIAS + n + 1, 0:FT] += total(sums["u"][n])
        tick(6)
        gh_acc[...] += dot(gwh[...], joined[t, :, 2 * C : 3 * C], (1, 1))

        def batch_sums(start, acc):
            plain, cross = acc
            crossed = dot(kh[pl.ds(start, GROUP), :], gwh[...])
            for o in range(0, GROUP, TILE):
                rows = pl.ds(start + o, TILE)
                g = (gmix[t, rows, :] + crossed[o : o + TILE]) * mask_cols[t, rows, :]
                gmix[t, rows, :] = g
                plain = plain + fold(g)
                cross = cross + fold(g * cv[z, rows, :])
            return plain, cross
        acc = groups(batch_sums, (zero, zero))
        plain, cross = total(acc[0]), total(acc[1])
        gs[k, BBIAS : BBIAS + 1, :] += plain
        gs[k, BGAIN : BGAIN + 1, :] += cross
        r = 4 + z
        msg[r, 0:1, 0:C] = plain
        msg[r, 1:2, 0:C] = cross
        send_stats(r)

    def input_stage(t, k, tick):
        z = 2 * k + t
        r = 4 + z
        wait_stats(r)
        scale, count = stat[z, 0:1, :], stat[z, 1:2, :]
        both = gather_stats(r)
        plain, cross = both[0:1, 0:C], both[1:2, 0:C]
        gain = pack[k, BGAIN : BGAIN + 1, :]
        out_scale = gain * scale
        plain = plain / count
        cross = cross / count

        def shifted(start, carry):
            rows = pl.ds(start, SIDE)
            g = (gmix[t, rows, :] - plain - cv[z, rows, :] * cross) * (mask_cols[t, rows, :] * out_scale)
            rows = pl.ds(start + SIDE, SIDE)
            gsh[0, rows, :] = sooner(g)
            gsh[1, rows, :] = g
            gsh[2, rows, :] = later(g)
            return carry
        grid_rows(shifted, 0)
        tick(8)
        taps = [[pack[k, CONV + n : CONV + n + 1, l:m] for n in range(9)] for l, m in LANES]

        def pull(start, acc):
            new = []
            for (l, m), tap, one in zip(LANES, taps, acc):
                u = [uf[t, pl.ds(start + SIDE * r, SIDE), l:m] for r in range(3)]
                out = gf[t, pl.ds(start, SIDE), l:m]
                sums = []
                for s in range(3):
                    around = [gsh[s, pl.ds(start + SIDE * r, SIDE), l:m] for r in range(3)]
                    out = out + around[2] * tap[s] + around[1] * tap[3 + s] + around[0] * tap[6 + s]
                    sums.append([one[s][r] + fold(around[1] * u[r]) for r in range(3)])
                new.append(sums)
                igbuf[z, lax.div(start, SIDE), :, l:m] = out.astype(BF16)
            return new
        acc = grid_rows(pull, [[[jnp.zeros((8, m - l), F32) for _ in range(3)] for _ in range(3)] for l, m in LANES])
        for (l, m), one in zip(LANES, acc):
            for r in range(3):
                for s in range(3):
                    row = CONV + 3 * r + s
                    gs[k, row : row + 1, l:m] += total(one[s][r])

        @pl.when(k == 1)
        def _():
            def reread(start, carry):
                gf[t, pl.ds(start, SIDE), :] = igbuf[z, lax.div(start, SIDE)].astype(F32)
                return carry
            grid_rows(reread, 0)

        @pl.when(me_p == k)
        def _():
            pltpu.make_async_copy(igbuf.at[z], ig_h.at[0, 2 * me_p + t], ig_local.at[t]).start()

        @pl.when(me_p != k)
        def _():
            across(igbuf.at[z], ig_h.at[0, 2 * me_p + t], ig_send.at[t], ig_recv.at[t]).start()

    def clear_mix():
        gw_acc[...] = jnp.zeros(gw_acc.shape, F32)
        gh_acc[...] = jnp.zeros(gh_acc.shape, F32)
        wcol[...] = jnp.zeros(wcol.shape, F32)
        hcol[...] = jnp.zeros(hcol.shape, F32)

    def close_mix(k):
        i_r, j_r = one_hots(ROWS)
        _, j_g = one_hots(GROUP)
        gs[k, WBIAS : WBIAS + 1, 0:SIDE] = total(jnp.where(j_r, wcol[...], 0.0))
        gs[k, HBIAS : HBIAS + 1, 0:SIDE] = total(jnp.where(i_r, hcol[...], 0.0))
        highest = lax.Precision.HIGHEST
        p = grid_row(lax.broadcasted_iota(jnp.int32, (GROUP, GROUP), 0))
        q = grid_row(lax.broadcasted_iota(jnp.int32, (GROUP, GROUP), 1))
        own = jnp.where(p == q, gw_acc[...], 0.0)
        own = jnp.sum(own.reshape(GROUP // SIDE, SIDE, GROUP), 0)
        gs[k, WW : WW + SIDE, 0:SIDE] = dot(own, jnp.where(j_g, 1.0, 0.0), precision=highest)
        i_f = jnp.where(i_r, 1.0, 0.0)
        for i in range(SIDE):
            rows = slice(i * SIDE, i * SIDE + SIDE)
            own = total(fold(own_column[...] * gh_acc[rows, :]))
            first[i : i + 1, :] = own[:, 0:C]
            gnorm[i : i + 1, 0 : ROWS - C] = own[:, C:ROWS]
        value = dot(first[0:SIDE, :], i_f[0:C, :], precision=highest)
        value += dot(gnorm[0:SIDE, 0 : ROWS - C], i_f[C:ROWS, :], precision=highest)
        gs[k, HW : HW + SIDE, 0:SIDE] = value

    bits = [1, 2]
    while 2 * bits[-1] < n_dp:
        bits.append(2 * bits[-1])
    n_swaps = len(bits) - 2
    n_steps = 1 + 2 + n_swaps + 2

    def partner(bit):
        return me_d + bit * (1 - 2 * lax.rem(me_d // bit, 2))

    def side(bit):
        return lax.rem(me_d // bit, 2)

    def along(bit, src, dst, send, recv):
        return pltpu.make_async_remote_copy(
            src_ref=src, dst_ref=dst, send_sem=send, recv_sem=recv,
            device_id={"dp": partner(bit)}, device_id_type=MESH)

    streams = (
        (acc_d, gd_h, sb_d, lb_d, rl_d), (acc_u, gu_h, sb_u, lb_u, rl_u), (acc_m, gm_h, sb_m, lb_m, rl_m))

    def reduction(k, which):
        acc, out_h, sb, lb, rl = streams[which]
        sb, lb, rl = sb.at[k], lb.at[k], rl.at[k]
        halving = [1 + me_p, 2 - me_p] if which != 1 else [2 - me_p, 1 + me_p]

        def sems(step):
            return red_send.at[3 * k + which, step], red_recv.at[3 * k + which, step]

        def own(q):
            return k, lax.div(q, 2), pl.ds(pl.multiple_of(me_p * HALF + lax.rem(q, 2) * SHARD, 16), SHARD), slice(None)

        def each(count, body):
            if count == 1:
                body(0)
                return

            def step(n, carry):
                body(n)
                return carry
            lax.fori_loop(0, count, step, 0)

        in_chip = across(sb.at[pl.ds(0, SHARDS)], lb, *sems(0))
        base = [0]
        for n, bit in enumerate(halving):
            base.append(base[n] + side(bit) * (2 >> n))
        mine = base[2]

        def half_copy(n):
            count, at = 2 >> n, 2 * n
            return along(halving[n], sb.at[pl.ds(at, count)], rl.at[pl.ds(at, count)], *sems(1 + n))

        def swap_copy(n):
            return along(bits[2 + n], sb.at[3 + n], rl.at[3 + n], *sems(3 + n))

        def double_copy(n):
            count = 2 >> n
            here = lb.at[pl.ds(base[n + 1], count)]
            return along(halving[n], here, here, *sems(n_steps - 1 - n))

        def send_half(n, landed):
            count, at = 2 >> n, 2 * n
            give = base[n] + (1 - side(halving[n])) * count
            keep = base[n + 1]

            def one(q):
                sb[at + q] = (acc[own(give + q)] + landed(give + q).astype(F32)).astype(BF16)
            each(count, one)
            half_copy(n).start()

            def two(q):
                acc[own(keep + q)] += landed(keep + q).astype(F32)
            each(count, two)

        def start():
            def one(q):
                rows = pl.ds(pl.multiple_of(other * HALF + lax.rem(q, 2) * SHARD, 16), SHARD)
                sb[q] = acc[k, lax.div(q, 2), rows, :].astype(BF16)
            each(SHARDS, one)
            in_chip.start()

        def first_half():
            in_chip.wait()
            send_half(0, lambda q: lb[q])

        def second_half():
            half_copy(0).wait()
            send_half(1, lambda q: rl[q - base[1]])

        def swap(n):
            def run():
                if n == 0:
                    half_copy(1).wait()
                    sb[3] = (acc[own(mine)] + rl[2].astype(F32)).astype(BF16)
                else:
                    swap_copy(n - 1).wait()
                    sb[3 + n] = (sb[2 + n].astype(F32) + rl[2 + n].astype(F32)).astype(BF16)
                swap_copy(n).start()
            return run

        def double(n):
            def run():
                if n == 1:
                    last = n_swaps - 1
                    swap_copy(last).wait()
                    lb[mine] = (sb[3 + last].astype(F32) + rl[3 + last].astype(F32)).astype(BF16)
                else:
                    double_copy(n + 1).wait()
                double_copy(n).start()
            return run

        def hand_over():
            double_copy(0).wait()

            @pl.when(me_p == k)
            def _():
                pltpu.make_async_copy(lb, out_h.at[me_p], out_local.at[which]).start()

            @pl.when(me_p != k)
            def _():
                across(lb, out_h.at[me_p], out_send.at[which], out_recv.at[which]).start()

        return [start, first_half, second_half] + [swap(n) for n in range(n_swaps)] + [double(1), double(0), hand_over]

    def small_sum(rows, landing, send, recv):
        count = rows.stop - rows.start
        rows = pl.ds(rows.start, count)
        in_chip = across(gs.at[other, rows], landing.at[0], send.at[0], recv.at[0])

        def swap_copy(n):
            return along(bits[n], gs.at[me_p, rows], landing.at[1 + n], send.at[1 + n], recv.at[1 + n])

        def step(n):
            def run():
                (swap_copy(n - 1) if n else in_chip).wait()
                gs[me_p, rows, :] += landing[n]
                if n < len(bits):
                    swap_copy(n).start()
            return run
        return [in_chip.start] + [step(n) for n in range(len(bits) + 1)]

    small = small_sum(slice(SMALL, PACK), small_land, small_send, small_recv)
    taps_sum = small_sum(slice(0, SMALL), conv_land, conv_send, conv_recv)

    plan = {}
    backward_places, input_places = [0, 1, 6, 11], [7, 8, 9]
    order = []
    for n in range(6):
        order += [(n, p) for p in input_places] if n > 1 else []
        order += [(n, p) for p in backward_places] if n < 4 else []

    def put(start, steps, gap):
        at = order.index(start)
        steps = list(steps)
        while steps and at < len(order):
            plan.setdefault(order[at], []).append(steps.pop(0))
            at += gap
        return steps

    for which, place in enumerate((1, 6, 6)):
        assert not put((1, place), reduction(1, which), 1)
    tails = [put((3, place), reduction(0, which), 1) for which, place in enumerate((1, 6, 6))]
    tails.append(put((4, 7), small, 1))
    tails.append(list(taps_sum))

    pack_over.wait()
    for t in range(2):
        image_in[t].wait()

    def widen_image(t):
        def widen(i, inner):
            uf[t, pl.ds(pl.multiple_of(i * SIDE + SIDE, SIDE), SIDE), :] = ub[t, i].astype(F32)
            return inner
        lax.fori_loop(0, SIDE, widen, 0)

    def start_image(t, carry):
        widen_image(t)
        conv_stage(t, 0)
        return carry
    lax.fori_loop(0, 2, start_image, 0)
    for t in range(2):
        grad_in[t].start()

    for copy in weights_in + weights_over:
        copy.wait()
    for k in range(2):
        wmid[k] = wm[k, :, C : 2 * C]

    def forward_block(k, carry):
        mixers(k, False)

        def one(t, inner):
            forward_stage(t, k)

            @pl.when(k == 0)
            def _():
                for copy in spill(t):
                    copy.start()
                conv_stage(t, 1)
            return inner
        lax.fori_loop(0, 2, one, 0)
        return carry
    lax.fori_loop(0, 2, forward_block, 0)

    for t in range(2):
        grad_in[t].wait()
        pltpu.make_async_copy(ybuf.at[t], so_h.at[0, t], so_local.at[t]).wait()
        across(ybuf.at[t], so_h.at[0, t], so_send.at[t], so_recv.at[t]).wait_send()

    def load_grad(t, carry):
        def widen(i, inner):
            gf[t, pl.ds(pl.multiple_of(i * SIDE, SIDE), SIDE), :] = ub[t, i].astype(F32)
            return inner
        lax.fori_loop(0, SIDE, widen, 0)
        return carry
    lax.fori_loop(0, 2, load_grad, 0)
    for t in range(2):
        image_copy(t, again_sems.at[t]).start()

    def turn(s, carry):
        t = lax.rem(s, 2)

        def tick(place):
            for n in range(6):
                steps = plan.get((n, place), [])
                if steps:
                    @pl.when(s == n)
                    def _():
                        for step in steps:
                            step()

        @pl.when(lax.rem(s, 2) == 0)
        def _():
            @pl.when(s > 0)
            def _():
                close_mix(2 - lax.div(s, 2))

            @pl.when(s < 4)
            def _():
                mixers(1 - lax.div(s, 2), True)
                clear_mix()

        @pl.when(s > 1)
        def _():
            @pl.when(s > 3)
            def _():
                image_copy(t, again_sems.at[t]).wait()
                widen_image(t)
            tick(7)
            input_stage(t, 2 - lax.div(s, 2), tick)
            tick(9)

        @pl.when(s < 4)
        def _():
            @pl.when(s > 1)
            def _():
                for copy in fetch(t):
                    copy.wait()
            tick(0)
            backward_stage(t, 1 - lax.div(s, 2), tick)
            tick(11)

            @pl.when(s < 2)
            def _():
                for copy in fetch(t):
                    copy.start()
        return carry
    lax.fori_loop(0, 6, turn, 0)

    while any(tails):
        for steps in tails:
            if steps:
                steps.pop(0)()

    gs_out = pltpu.make_async_copy(gs.at[me_p], gs_h, gs_sem.at[0])
    gs_out.start()
    for t in range(2):
        pltpu.make_async_copy(igbuf.at[t], ig_h.at[0, t], ig_local.at[t]).wait()
        across(ybuf.at[t], so_h.at[0, t], so_send.at[t], so_recv.at[t]).wait_recv()
        across(igbuf.at[t], ig_h.at[0, t], ig_send.at[t], ig_recv.at[t]).wait()
    for n, (_, out_h, _, lb, _) in enumerate(streams):
        pltpu.make_async_copy(lb.at[0], out_h.at[0], out_local.at[n]).wait()
        across(lb.at[0], out_h.at[0], out_send.at[n], out_recv.at[n]).wait()
    gs_out.wait()


def finish_kernel(
    so_in, ig_in, gd_in, gu_in, gm_in, gs,
    so, ig, conv, bgain, bbias, ww, wb, hw, hb, gm, mbias, ngain, nbias, gu, ubias, gd, dbias,
    large, d_in, u_in, m_in, d_out, u_out, m_out, in_sems, out_sems,
):
    moved = ((gd_in, d_in), (gu_in, u_in), (gm_in, m_in), (so_in, large.at[0]), (ig_in, large.at[1]))
    arrive = [pltpu.make_async_copy(src, dst, in_sems.at[n]) for n, (src, dst) in enumerate(moved)]
    for copy in arrive:
        copy.start()
    moved = ((d_out, gd), (u_out, gu), (m_out, gm), (large.at[0], so), (large.at[1], ig))
    leave = [pltpu.make_async_copy(src, dst, out_sems.at[n]) for n, (src, dst) in enumerate(moved)]
    for n in range(9):
        conv[n] = gs[CONV + n : CONV + n + 1, :]
    for row, ref in ((BGAIN, bgain), (BBIAS, bbias), (MBIAS, mbias), (NGAIN, ngain), (NBIAS, nbias), (DBIAS, dbias)):
        ref[...] = gs[row : row + 1, :]
    for row, ref in ((WBIAS, wb), (HBIAS, hb)):
        ref[...] = gs[row : row + 1, 0:SIDE]
    for n in range(FF // FT):
        ubias[:, n * FT : n * FT + FT] = gs[UBIAS + n : UBIAS + n + 1, 0:FT]
    for row, ref in ((WW, ww), (HW, hw)):
        ref[0] = gs[row : row + SIDE, 0:SIDE]
    for n, (src, dst, piece) in enumerate(((d_in, d_out, WIDE), (u_in, u_out, WIDE), (m_in, m_out, MT))):
        arrive[n].wait()
        for p in range(2):
            for q in range(SHARDS):
                start, at = p * HALF + (q % 2) * SHARD, piece * (q // 2)
                width = min(piece, dst.shape[1] - at)
                dst[start : start + SHARD, at : at + width] = src[p, q, :, 0:width].astype(F32)
        leave[n].start()
    for n in (3, 4):
        arrive[n].wait()
        leave[n].start()
    for copy in leave:
        copy.wait()


def on_device(
    images, masks, conv_weight, batch_gain, batch_bias, width_weight, width_bias,
    height_weight, height_bias, merge_weight, merge_bias, norm_gain, norm_bias,
    up_weight, up_bias, down_weight, down_bias, out_grad,
):
    n_dp = lax.axis_size("dp")
    micro = images.shape[0]
    steps = max(n_dp.bit_length() - 1, 4)
    any_space = pl.BlockSpec(memory_space=pl.ANY)
    vmem = pl.BlockSpec(memory_space=pltpu.VMEM)
    dma = pltpu.SemaphoreType.DMA
    grid = (SIDE, SIDE, C)
    shape = jax.ShapeDtypeStruct
    outs = pl.pallas_call(
        functools.partial(kernel, n_dp),
        out_shape=(
            shape((1, micro) + grid, BF16),
            shape((1, micro) + grid, BF16),
            shape((2, SHARDS, SHARD, WIDE), BF16),
            shape((2, SHARDS, SHARD, WIDE), BF16),
            shape((2, SHARDS, SHARD, MT), BF16),
            shape((PACK, C), F32),
            shape((2, ROWS, FF), BF16),
            shape((2, ROWS, FF), BF16),
            shape((2, ROWS, 3 * C), BF16),
            shape((2, ROWS, C), BF16),
            shape((2, ROWS, C), BF16),
        ),
        in_specs=[any_space] + [vmem] * 8 + [any_space] + [vmem] * 3 + [any_space, vmem, any_space, vmem, any_space],
        out_specs=(any_space,) * 11,
        scratch_shapes=[
            pltpu.VMEM((2, ROWS, 1), F32),
            pltpu.VMEM((4, 2, C), F32),
            pltpu.VMEM((SIDE, ROWS), F32),
            pltpu.VMEM((ROWS, SIDE), BF16),
            pltpu.VMEM((2, PACK, C), F32),
            pltpu.VMEM((2, C, 3 * C), BF16),
            pltpu.VMEM((2, C, C), BF16),
            pltpu.VMEM((2, C, FF), BF16),
            pltpu.VMEM((2, C, FF), BF16),
            pltpu.VMEM((2,) + grid, BF16),
            pltpu.VMEM((2, ROWS + 2 * SIDE, C), F32),
            pltpu.VMEM((4, ROWS, C), F32),
            pltpu.VMEM((2, ROWS, 3 * C), BF16),
            pltpu.VMEM((2, ROWS, C), BF16),
            pltpu.VMEM((2, ROWS, C), BF16),
            pltpu.VMEM((4, ROWS, 1), F32),
            pltpu.VMEM((2, ROWS, FF), BF16),
            pltpu.VMEM((2, ROWS, FF), BF16),
            pltpu.VMEM((2, ROWS, C), F32),
            pltpu.VMEM((ROWS, C), BF16),
            pltpu.VMEM((ROWS, C), BF16),
            pltpu.VMEM((ROWS, C), BF16),
            pltpu.VMEM((C, ROWS), BF16),
            pltpu.VMEM((C, ROWS), BF16),
            pltpu.VMEM((ROWS, FF), BF16),
            pltpu.VMEM((2, ROWS, C), F32),
            pltpu.VMEM((ROWS, C), BF16),
            pltpu.VMEM((3, ROWS + 2 * SIDE, C), F32),
            pltpu.VMEM((GROUP, GROUP), BF16),
            pltpu.VMEM((ROWS, ROWS), BF16),
            pltpu.VMEM((ROWS, 1), F32),
            pltpu.VMEM((ROWS, 1), F32),
            pltpu.VMEM((GROUP, GROUP), F32),
            pltpu.VMEM((ROWS, ROWS), F32),
            pltpu.VMEM((ROWS, 1), F32),
            pltpu.VMEM((ROWS, 1), F32),
            pltpu.VMEM((4,) + grid, BF16),
            pltpu.VMEM((8, 2, CP), F32),
            pltpu.VMEM((8, n_dp - 1, 2, CP), F32),
            pltpu.VMEM((2, 2, C, WIDE), F32),
            pltpu.VMEM((2, 2, C, WIDE), F32),
            pltpu.VMEM((2, 2, C, MT), F32),
            pltpu.VMEM((2, PACK, C), F32),
            pltpu.VMEM((2, 1 + steps, SHARD, WIDE), BF16),
            pltpu.VMEM((2, SHARDS, SHARD, WIDE), BF16),
            pltpu.VMEM((2, 1 + steps, SHARD, WIDE), BF16),
            pltpu.VMEM((2, 1 + steps, SHARD, WIDE), BF16),
            pltpu.VMEM((2, SHARDS, SHARD, WIDE), BF16),
            pltpu.VMEM((2, 1 + steps, SHARD, WIDE), BF16),
            pltpu.VMEM((2, 1 + steps, SHARD, MT), BF16),
            pltpu.VMEM((2, SHARDS, SHARD, MT), BF16),
            pltpu.VMEM((2, 1 + steps, SHARD, MT), BF16),
            pltpu.VMEM((1 + steps, PACK - SMALL, C), F32),
            pltpu.VMEM((1 + steps, SMALL, C), F32),
            dma((9,)), dma((2,)), dma((2,)), dma((3,)), dma((3,)), dma((8,)), dma((8,)),
            dma((2,)), dma((2,)), dma((2,)), dma((2,)), dma((2,)), dma((2,)), dma((2, 5)), dma((2, 5)),
            dma((6, 3 + steps)), dma((6, 3 + steps)), dma((1 + steps,)), dma((1 + steps,)),
            dma((1 + steps,)), dma((1 + steps,)), dma((3,)), dma((3,)), dma((3,)), dma((1,)),
        ],
        compiler_params=pltpu.CompilerParams(
            collective_id=0, has_side_effects=True, vmem_limit_bytes=65400 * 1024),
    )(
        images, masks, conv_weight, batch_gain, batch_bias, width_weight, width_bias, height_weight, height_bias,
        merge_weight[0].T, merge_bias, norm_gain, norm_bias, up_weight[0], up_bias, down_weight[0].T, down_bias, out_grad)

    row = shape((1, C), F32)
    square, line = shape((1, SIDE, SIDE), F32), shape((1, SIDE), F32)
    so, ig, conv, bgain, bbias, ww, wb, hw, hb, gm, mbias, ngain, nbias, gu, ubias, gd, dbias = pl.pallas_call(
        finish_kernel,
        out_shape=(
            shape((1, micro) + grid, BF16), shape((1, micro) + grid, BF16), shape((9, 1, C), F32), row, row,
            square, line, square, line, shape((C, 3 * C), F32), row, row, row,
            shape((C, FF), F32), shape((1, FF), F32), shape((C, FF), F32), row),
        in_specs=[any_space] * 5 + [vmem],
        out_specs=(any_space,) * 2 + (vmem,) * 7 + (any_space,) + (vmem,) * 3 + (any_space, vmem, any_space, vmem),
        scratch_shapes=[
            pltpu.VMEM((2, 1, micro) + grid, BF16),
            pltpu.VMEM((2, SHARDS, SHARD, WIDE), BF16),
            pltpu.VMEM((2, SHARDS, SHARD, WIDE), BF16),
            pltpu.VMEM((2, SHARDS, SHARD, MT), BF16),
            pltpu.VMEM((C, FF), F32),
            pltpu.VMEM((C, FF), F32),
            pltpu.VMEM((C, 3 * C), F32),
            dma((5,)), dma((5,)),
        ],
        compiler_params=pltpu.CompilerParams(vmem_limit_bytes=65400 * 1024),
    )(*outs[:6])
    return (
        so, ig, jnp.swapaxes(conv, 0, 1), bgain, bbias, ww, wb, hw, hb, gm.T[None], mbias, ngain, nbias,
        gu[None], ubias, gd.T[None], dbias)


def solution(mesh):
    data4 = P("dp", None, None, None)
    p1, p2, p3 = P("pipe"), P("pipe", None), P("pipe", None, None)
    out5 = P("pipe", "dp", None, None, None)
    return jax.shard_map(
        on_device,
        mesh=mesh,
        in_specs=(data4, P("dp", None, None), p3, p2, p2, p3, p2, p3, p2, p3, p2, p2, p2, p3, p2, p3, p2, data4),
        out_specs=(out5, out5, p3, p2, p2, p3, p2, p3, p2, p3, p2, p2, p2, p3, p2, p3, p2),
        check_vma=False,
    )
```
